32 devices in a mesh: dp: 4 (over z), row: 2 (over core), col: 4 (over y, x).
Axes of the slice: x: 2, y: 2, z: 4, core: 2. Of those that a mesh axis runs over, the one named last changes fastest.
Arguments:
- tokens: bfloat16 [12608, 768], P(('dp', 'row'), 'col'), may hold values from -6 to 6
- cotangent: bfloat16 [12608, 768], P(('dp', 'row'), 'col'), may hold values from -6 to 6
- routes: int32 [12608, 2], P('dp'), may hold values from 0 to 31, all different within a row; in each aligned block of 3152 rows (0 to 3151, 3152 to 6303, ...) at most 400 rows name the same one
- adapter_pick: int32 [64], replicated, may hold values from 0 to 7
- gain_attn: float32 [768], P('col'), may hold values from 0.5 to 1.5
- gain_moe: float32 [768], P('col'), may hold values from 0.5 to 1.5
- w_qkv: bfloat16 [3, 768, 768], P(None, 'col', 'row'), may hold values from -0.21875 to 0.21875
- w_out: bfloat16 [768, 768], P('row', 'col'), may hold values from -0.875 to 0.875
- w_router: bfloat16 [768, 32], replicated, may hold values from -0.15625 to 0.15625
- w_up: bfloat16 [32, 768, 3072], P(None, None, ('row', 'col')), may hold values from -0.21875 to 0.21875
- w_down: bfloat16 [32, 3072, 768], P(None, ('row', 'col')), may hold values from -1.75 to 1.75
- a_qkv: bfloat16 [3, 768, 128], P(None, 'col'), may hold values from -0.21875 to 0.21875
- b_qkv: bfloat16 [3, 128, 768], P(None, None, 'row'), may hold values from -0.75 to 0.75
- a_out: bfloat16 [768, 128], P('row'), may hold values from -0.875 to 0.875
- b_out: bfloat16 [128, 768], P(None, 'col'), may hold values from -0.75 to 0.75
- a_router: bfloat16 [768, 128], replicated, may hold values from -0.21875 to 0.21875
- b_router: bfloat16 [128, 32], replicated, may hold values from -0.5 to 0.5
- a_up: bfloat16 [768, 128], replicated, may hold values from -0.21875 to 0.21875
- b_up: bfloat16 [128, 3072], P(None, ('row', 'col')), may hold values from -0.75 to 0.75
- a_down: bfloat16 [3072, 128], P(('row', 'col')), may hold values from -0.109375 to 0.109375
- b_down: bfloat16 [128, 768], replicated, may hold values from -1.5 to 1.5
Outputs:
- block_out: bfloat16 [12608, 768], P(('dp', 'row'), 'col')
- grad_tokens: float32 [12608, 768], P(('dp', 'row'), 'col')
- grad_a_qkv: float32 [3, 768, 128], P(None, 'col')
- grad_b_qkv: float32 [3, 128, 768], P(None, None, 'row')
- grad_a_out: float32 [768, 128], P('row')
- grad_b_out: float32 [128, 768], P(None, 'col')
- grad_a_router: float32 [768, 128], replicated
- grad_b_router: float32 [128, 32], replicated
- grad_a_up: float32 [768, 128], replicated
- grad_b_up: float32 [128, 3072], P(None, ('row', 'col'))
- grad_a_down: float32 [3072, 128], P(('row', 'col'))
- grad_b_down: float32 [128, 768], replicated
The draws below stay inside these ranges and needn't reach their ends.
Inputs may be any that keep to these rules, and one draw needn't show every extreme that they name: `routes`: each token names two different experts. In each aligned block of 3152 rows (the tokens of one index of dp) no expert is named by more than 400 rows, and in some block one expert is named by exactly 400 rows.
All inputs are finite; a program needn't handle non-finite values.
Results may differ from the reference program's by a relative error of at most 0.035.
Values may be sent and summed in bfloat16 or wider, within the bound.
No kernel may reach another device: no remote copies, remote signals or barrier semaphores. Data moves between devices by JAX's collectives and lax.ppermute only.
A program may use at most 448 MiB of HBM per device.

```python
import math
import jax
import jax.numpy as jnp
import numpy as np
from jax import lax

D = 768
HEADS = 12
HEAD_DIM = 64
FF = 3072
EXPERTS = 32
SEQ = 197
RANK = 16
ADAPTERS = 8
IMG_GRP = 16
TOKG = 3152
CAP = 400
ADAPT = 128
IMAGES = 64
TOKENS = 12608
N_DP = 4


def set_ends(array, key, smallest, largest):
    extent = array.shape
    spot = [jax.random.randint(jax.random.fold_in(key, axis), (), 0, extent[axis]) for axis in range(len(extent))]
    array = array.at[tuple(spot)].set(smallest)
    longest = extent.index(max(extent))
    spot[longest] = (spot[longest] + 1) % extent[longest]
    return array.at[tuple(spot)].set(largest)


def shard_levels(key, shape, cuts, low, top_value):
    def one(dim, shards_of):
        draws = jax.random.uniform(jax.random.fold_in(jax.random.fold_in(key, 6), dim), (shards_of,), jnp.float32, low / len(cuts), top_value / len(cuts))
        return jnp.repeat(jnp.exp(draws), shape[dim] // shards_of).reshape((-1,) + (1,) * (len(shape) - dim - 1))

    factor_of = one(*cuts[0])
    for cut in cuts[1:]:
        factor_of = factor_of * one(*cut)
    return factor_of


def assign_block(key, own, number, rows, number_of, top, limit, slope):
    sequence = jax.random.permutation(key, number_of)
    packed, ordinary = shares(number_of, rows * top, limit, slope, True), shares(number_of, rows * top, limit, slope, False)
    places = jnp.arange(number_of)

    def named(sizes, turn):
        used = int((sizes > 0).sum())
        fixed = max(1, used // 4)
        moved = fixed + (places - fixed + turn * (used - fixed)) % max(1, number_of - fixed)
        return jnp.zeros((number_of,), jnp.int32).at[sequence[jnp.where(places < fixed, places, moved)]].set(jnp.asarray(sizes, jnp.int32))

    sizes = jnp.where(number % 4 == 0, named(packed, number // 4), named(ordinary, number - number // 4 - 1))
    mixed = jax.random.permutation(jax.random.fold_in(own, 3), number_of)
    giver, taker = mixed[0:number_of // 2 * 2:2], mixed[1:number_of // 2 * 2:2]
    margin = jnp.minimum(sizes[giver] - 1, limit - sizes[taker]) // 2
    margin = jnp.where((giver == sequence[0]) | (taker == sequence[0]) | (sizes[taker] == 0), 0, jnp.maximum(margin, 0))
    moved = jax.random.randint(jax.random.fold_in(own, 4), (number_of // 2,), 0, 1 << 20) % (margin + 1)
    sizes = sizes.at[giver].add(-moved).at[taker].add(moved)
    items = jnp.searchsorted(jnp.cumsum(sizes), jnp.arange(rows * top), side="right").astype(jnp.int32)
    grid = items.reshape(top, rows).T
    grid = grid[jax.random.permutation(jax.random.fold_in(own, 1), rows)]
    turn = jax.random.randint(jax.random.fold_in(own, 2), (rows, 1), 0, top)
    return jnp.take_along_axis(grid, (jnp.arange(top)[None, :] + turn) % top, axis=1)


def shares(number_of, total, reach, slope, full):
    loads = [(1 << 20) // math.isqrt(grade ** slope) + 1 for grade in range(1, number_of + 1)]
    largest = reach if full else min(reach, max(-(-total // number_of), total * loads[0] // sum(loads)))
    least = 1 if total - largest >= number_of - 1 else 0
    given, rest = [largest] + [least] * (number_of - 1), total - largest - least * (number_of - 1)
    while rest > 0:
        candidates = [i for i in range(1, number_of) if given[i] < largest] or [i for i in range(1, number_of) if given[i] < reach]
        pool, budget = sum([loads[i] for i in candidates]), rest
        for i in candidates:
            extra = min(reach - given[i], max(1, budget * loads[i] // pool), rest)
            given[i] = given[i] + extra
            rest = rest - extra
    return np.array(given)


def gaussian(rng, shape, width, reach, split=(), held_as=jnp.bfloat16):
    loudness = shard_levels(rng, shape, split, -0.22, 0.18) if split else 1.0
    values = jax.random.normal(rng, shape, jnp.float32) * width * loudness
    return jnp.minimum(jnp.maximum(values, -reach), reach).astype(held_as)


def setup_inputs(seed: int = 0) -> dict:
    keys = jax.random.split(jax.random.key(seed), 22)
    tokens = gaussian(keys[0], (TOKENS, D), 1.0, 6.0, ((0, 8), (1, 4)))
    cotangent = gaussian(keys[1], (TOKENS, D), 1.0, 6.0, ((0, 8), (1, 4)))
    routes_keys = jax.random.split(jax.random.fold_in(keys[2], 1), TOKENS // TOKG)
    routes_turns = jax.random.permutation(jax.random.fold_in(keys[2], 3), TOKENS // TOKG)
    routes = jax.vmap(lambda own, number: assign_block(jax.random.fold_in(keys[2], 2), own, number, TOKG, EXPERTS, 2, CAP, 1))(routes_keys, routes_turns).reshape((TOKENS, 2))
    adapter_pick = set_ends(jax.random.randint(keys[3], (IMAGES,), 0, ADAPTERS), jax.random.fold_in(keys[3], 1), 0, ADAPTERS - 1).astype(jnp.int32)
    gain_attn = jnp.clip(1.0 + 0.1 * jax.random.normal(keys[4], (D,), jnp.float32), 0.5, 1.5)
    gain_moe = jnp.clip(1.0 + 0.1 * jax.random.normal(keys[5], (D,), jnp.float32), 0.5, 1.5)
    w_qkv = gaussian(keys[6], (3, D, D), D ** -0.5, 0.21875, ((1, 4), (2, 2)))
    w_out = gaussian(keys[7], (D, D), (D // 16) ** -0.5, 0.875, ((0, 2), (1, 4)))
    w_router = gaussian(keys[8], (D, EXPERTS), (2 * D) ** -0.5, 0.15625)
    w_up = gaussian(keys[9], (EXPERTS, D, FF), D ** -0.5, 0.21875, ((2, 8),))
    w_down = gaussian(keys[10], (EXPERTS, FF, D), (max(4 * FF // (EXPERTS * EXPERTS), 1)) ** -0.5, 1.75, ((1, 8),))
    a_qkv = gaussian(keys[11], (3, D, ADAPT), D ** -0.5, 0.21875, ((1, 4),))
    b_qkv = gaussian(keys[12], (3, ADAPT, D), (4 * RANK) ** -0.5, 0.75, ((2, 2),))
    a_out = gaussian(keys[13], (D, ADAPT), (D // 16) ** -0.5, 0.875, ((0, 2),))
    b_out = gaussian(keys[14], (ADAPT, D), (4 * RANK) ** -0.5, 0.75, ((1, 4),))
    a_router = gaussian(keys[15], (D, ADAPT), D ** -0.5, 0.21875)
    b_router = gaussian(keys[16], (ADAPT, EXPERTS), (8 * RANK) ** -0.5, 0.5)
    a_up = gaussian(keys[17], (D, ADAPT), D ** -0.5, 0.21875)
    b_up = gaussian(keys[18], (ADAPT, FF), (4 * RANK) ** -0.5, 0.75, ((1, 8),))
    a_down = gaussian(keys[19], (FF, ADAPT), FF ** -0.5, 0.109375, ((0, 8),))
    b_down = gaussian(keys[20], (ADAPT, D), RANK ** -0.5, 1.5)
    return {"tokens": tokens, "cotangent": cotangent, "routes": routes, "adapter_pick": adapter_pick, "gain_attn": gain_attn, "gain_moe": gain_moe, "w_qkv": w_qkv, "w_out": w_out, "w_router": w_router, "w_up": w_up, "w_down": w_down, "a_qkv": a_qkv, "b_qkv": b_qkv, "a_out": a_out, "b_out": b_out, "a_router": a_router, "b_router": b_router, "a_up": a_up, "b_up": b_up, "a_down": a_down, "b_down": b_down}


@jax.custom_vjp
def low(v):
    return lax.optimization_barrier(v.astype(jnp.bfloat16)).astype(jnp.float32)

@jax.custom_vjp
def low_back(v):
    return v

def low_keep(v):
    return (low(v), None)

def low_pass(kept, grad):
    return (grad,)

def back_keep(v):
    return (v, None)

def back_low(kept, grad):
    return (low(grad),)
low.defvjp(low_keep, low_pass)
low_back.defvjp(back_keep, back_low)
highest = lax.Precision.HIGHEST

def product(left, right):
    return jnp.dot(left, right, precision=highest, preferred_element_type=jnp.float32)

def layer_norm(values, gain_vec):
    centre = lax.optimization_barrier(jnp.mean(values, axis=-1, keepdims=True))
    shifted = values - centre
    spread = lax.optimization_barrier(jnp.mean(shifted * shifted, axis=-1, keepdims=True))
    return shifted * lax.rsqrt(spread + 1e-06) * gain_vec

def adapter_mask(chosen):
    per_token = jnp.repeat(chosen.astype(jnp.int32), SEQ)
    columns = jnp.arange(ADAPT, dtype=jnp.int32) // RANK
    return (columns[None, :] == per_token[:, None]).astype(jnp.float32)

def expert_slots(routes_in):
    flattened = routes_in.reshape(-1).astype(jnp.int32)
    onehot = (flattened[:, None] == jnp.arange(EXPERTS, dtype=jnp.int32)[None, :]).astype(jnp.int32)
    earlier = jnp.cumsum(onehot, axis=0).astype(jnp.int32) - onehot
    position = lax.optimization_barrier(jnp.sum(earlier * onehot, axis=1)).astype(jnp.int32)
    slot_of = flattened * CAP + position
    counter = jnp.arange(flattened.shape[0], dtype=jnp.int32) + 1
    source = jnp.zeros((EXPERTS * CAP,), jnp.int32).at[slot_of].set(counter)
    return (slot_of.reshape(-1, 2), source)

def block_forward(frozen, tokens_in, adapters, routes_in, chosen):
    gain_attn, gain_moe, w_qkv, w_out, w_router, w_up, w_down = frozen
    a_qkv, b_qkv, a_out, b_out, a_router, b_router, a_up, b_up, a_down, b_down = adapters
    pick_mask = adapter_mask(chosen)
    normed = low(layer_norm(tokens_in, gain_attn))
    head_list = []
    for member in range(3):
        projected = product(normed, w_qkv[member]) + product(product(normed, a_qkv[member]) * pick_mask, b_qkv[member])
        head_list.append(low(low_back(projected)).reshape(IMG_GRP, SEQ, HEADS, HEAD_DIM))
    queries, keys_in, values_in = head_list
    scores = low_back(jnp.einsum('iqhd,ikhd->ihqk', queries, keys_in, precision=highest) * HEAD_DIM ** (-0.5))
    weights = low(jax.nn.softmax(scores, axis=-1))
    mixed_out = jnp.einsum('ihqk,ikhd->iqhd', weights, values_in, precision=highest)
    mixed_out = low(low_back(mixed_out)).reshape(TOKG, D)
    attention = low_back(product(mixed_out, w_out) + product(product(mixed_out, a_out) * pick_mask, b_out))
    resid_two = tokens_in + attention
    normed_two = low(layer_norm(resid_two, gain_moe))
    logits = product(normed_two, w_router) + product(product(normed_two, a_router) * pick_mask, b_router)
    router_probs = jax.nn.softmax(logits, axis=-1)
    gate_vals = jnp.take_along_axis(router_probs, routes_in, axis=1)
    slot_of, source = expert_slots(routes_in)
    token_src = jnp.where(source > 0, (source - 1) // 2 + 1, 0).astype(jnp.int32)
    padded = jnp.concatenate([jnp.zeros((1, D), jnp.float32), normed_two], axis=0)
    inputs = jnp.take(padded, token_src, axis=0).reshape(EXPERTS, CAP, D)
    slot_mask = jnp.take(jnp.concatenate([jnp.zeros((1, ADAPT), jnp.float32), pick_mask], axis=0), token_src, axis=0)
    low_up = jnp.concatenate([jnp.zeros((1, ADAPT), jnp.float32), product(normed_two, a_up)], axis=0)
    slot_low = jnp.take(low_up, token_src, axis=0) * slot_mask
    hidden = jnp.einsum('ecd,edf->ecf', inputs, w_up, precision=highest) + product(slot_low, b_up).reshape(EXPERTS, CAP, FF)
    activated = low(jax.nn.gelu(low_back(hidden), approximate=False))
    flat_act = activated.reshape(EXPERTS * CAP, FF)
    expert_out = jnp.einsum('ecf,efd->ecd', activated, w_down, precision=highest).reshape(EXPERTS * CAP, D)
    expert_out = low_back(expert_out + product(product(flat_act, a_down) * slot_mask, b_down))
    first_pick = jnp.take(expert_out, slot_of[:, 0], axis=0)
    second_pick = jnp.take(expert_out, slot_of[:, 1], axis=0)
    expert_sum = gate_vals[:, 0:1] * first_pick + gate_vals[:, 1:2] * second_pick
    return resid_two + expert_sum

def reference(tokens, cotangent, routes, adapter_pick, gain_attn, gain_moe, w_qkv, w_out, w_router, w_up, w_down, a_qkv, b_qkv, a_out, b_out, a_router, b_router, a_up, b_up, a_down, b_down):
    frozen = tuple((array_in.astype(jnp.float32) for array_in in (gain_attn, gain_moe, w_qkv, w_out, w_router, w_up, w_down)))
    adapters = tuple((array_in.astype(jnp.float32) for array_in in (a_qkv, b_qkv, a_out, b_out, a_router, b_router, a_up, b_up, a_down, b_down)))
    routes_grp = routes.reshape(N_DP, TOKG, 2)
    picks_grp = adapter_pick.reshape(N_DP, IMG_GRP)
    checked = jax.checkpoint(block_forward)

    def whole(tokens_f, adapt_in):

        def group_step(carried, group_in):
            tokens_grp, routes_in, chosen = group_in
            return (carried, checked(frozen, tokens_grp, adapt_in, routes_in, chosen))
        unused, outputs = lax.scan(group_step, jnp.zeros((), jnp.float32), (tokens_f.reshape(N_DP, TOKG, D), routes_grp, picks_grp))
        return outputs.reshape(TOKENS, D)
    result, pullback = jax.vjp(whole, tokens.astype(jnp.float32), adapters)
    grad_input, grads = pullback(cotangent.astype(jnp.float32))
    return (result.astype(jnp.bfloat16), grad_input, grads[0], grads[1], grads[2], grads[3], grads[4], grads[5], grads[6], grads[7], grads[8], grads[9])
```

```python
import jax
import jax.numpy as jnp
from jax import lax
from jax.experimental import pallas as pl
from jax.experimental.pallas import tpu as pltpu
from jax.sharding import PartitionSpec as P

D = 768
EXPERTS = 32
SEQ = 197
SEQP = 208
RANK = 16
ADAPT = 128
IMG_GRP = 16
TOK = IMG_GRP * SEQP
BLK = 2 * SEQP
DUMMY = SEQ
TILE = 128
f32 = jnp.float32
bf16 = jnp.bfloat16


def dot(left, right):
    return jnp.dot(left, right, preferred_element_type=f32)


def dot_nt(left, right):
    return lax.dot_general(left, right, (((1,), (1,)), ((), ())), preferred_element_type=f32)


def dot_tn(left, right):
    return lax.dot_general(left, right, (((0,), (0,)), ((), ())), preferred_element_type=f32)


def lane_iota(shape):
    return lax.broadcasted_iota(jnp.int32, shape, len(shape) - 1)


def moe_kernel(n_x, n_c, list_ref, offs_ref, picks_ref, *refs):
    x_blocks = refs[:n_x]
    c_blocks = refs[n_x : n_x + n_c]
    (
        w_up, w_down, b_up, a_down, a_up, b_down, w_router, a_router, b_router,
        ep_out, tg_out, gbu_out, gad_out, gau_out, gbd_out,
        xin, cin, gpin, table, acc, rows_in, rows_out, in_sem, ep_sem, tg_sem,
    ) = refs[n_x + n_c :]
    expert = pl.program_id(0)
    half = w_up.shape[2]
    acc_flat = acc.reshape(TOK * 16, 128)
    in_flat = rows_in.reshape(TILE * 16, 128)
    out_flat = rows_out.reshape(TILE * 16, 128)
    lane = lane_iota((1, 128))

    @pl.when(expert == 0)
    def prologue():
        copies = []
        for blocks, place in ((x_blocks, xin), (c_blocks, cin)):
            row = 0
            for block in blocks:
                rows = block.shape[0]
                copies.append(pltpu.make_async_copy(block, place.at[pl.ds(row, rows)], in_sem.at[len(copies)]))
                row += rows
        for copy in copies:
            copy.start()
        rows_in[...] = jnp.zeros_like(rows_in)
        rows_out[...] = jnp.zeros_like(rows_out)
        gbu_out[...] = jnp.zeros_like(gbu_out)
        gad_out[...] = jnp.zeros_like(gad_out)
        gau_out[...] = jnp.zeros_like(gau_out)
        gbd_out[...] = jnp.zeros_like(gbd_out)
        for copy in copies:
            copy.wait()

        def image(i, carry):
            row = pl.multiple_of(i * SEQP, 16)
            mask = (lane // RANK) == picks_ref[i]
            x = xin[pl.ds(row, SEQP), :]
            c = cin[pl.ds(row, SEQP), :]
            low_x = jnp.where(mask, dot(x, a_up[...]), 0.0)
            low_c = jnp.where(mask, dot_nt(c, b_down[...]), 0.0)
            low_r = jnp.where(mask, dot(x, a_router[...]), 0.0).astype(bf16)
            logits = dot(x, w_router[...]) + dot(low_r, b_router[...])
            logits = jnp.where(lane < 2 * EXPERTS, logits, -1e30)
            power = jnp.exp(logits - jnp.max(logits, axis=1, keepdims=True))
            total = jnp.sum(jnp.where(lane < EXPERTS, power, 0.0), axis=1, keepdims=True)
            probs = power / total
            lead = probs.astype(bf16).astype(f32)
            probs = jnp.where(lane < EXPERTS, lead, probs - lead)
            base = row * 16
            for j in range(6):
                acc_flat[pl.ds(base + j, SEQP, 16), :] = x[:, 128 * j : 128 * j + 128].astype(f32)
                acc_flat[pl.ds(base + 8 + j, SEQP, 16), :] = c[:, 128 * j : 128 * j + 128].astype(f32)
            acc_flat[pl.ds(base + 6, SEQP, 16), :] = low_x
            acc_flat[pl.ds(base + 14, SEQP, 16), :] = low_c
            acc_flat[pl.ds(base + 7, SEQP, 16), :] = probs
            acc_flat[pl.ds(base + 15, SEQP, 16), :] = jnp.zeros((SEQP, 128), f32)
            table[pl.ds(row, SEQP)] = acc[pl.ds(row, SEQP)].astype(bf16)
            acc[pl.ds(row, SEQP)] = jnp.zeros((SEQP, 16, 128), f32)
            return carry

        lax.fori_loop(0, IMG_GRP, image, 0)

    first = offs_ref[expert]
    count = offs_ref[expert + 1] - first

    def tile(t, carry):
        base = first + t * TILE
        rest = count - t * TILE
        batches = (jnp.minimum(rest, TILE) + 7) // 8

        def fetch(b, carry):
            for k in range(8):
                i = b * 8 + k
                token = jnp.where(i < rest, list_ref[base + i], DUMMY)
                rows_in[i] = table[token].astype(f32)
            return carry

        lax.fori_loop(0, batches, fetch, 0)

        def columns(start):
            return jnp.concatenate(
                [in_flat[pl.ds(start + j, TILE, 16), :].astype(bf16) for j in range(7)], axis=1
            )

        x = columns(0)
        c = columns(8)
        spread = in_flat[pl.ds(7, TILE, 16), :]
        inside = lax.broadcasted_iota(jnp.int32, (TILE, 1), 0) < rest
        mine = ((lane == expert) | (lane == expert + EXPERTS)) & inside
        gate = jnp.sum(jnp.where(mine, spread, 0.0), axis=1, keepdims=True)
        w_u = w_up[0]
        w_d = w_down[0]
        hidden = dot(x[:, :D], w_u) + dot(x[:, D:], b_up[...])
        cdf = 0.5 + 0.5 * lax.erf(hidden * 0.7071067811865476)
        slope = cdf + hidden * jnp.exp(hidden * hidden * -0.5) * 0.3989422804014327
        act = (hidden * cdf).astype(bf16)
        back = dot_nt(c[:, :D], w_d) + dot_nt(c[:, D:], a_down[...])
        act_f = act.astype(f32)
        gate_grad = jnp.sum(act_f * back, axis=1, keepdims=True)
        grad_hidden = (gate * back * slope).astype(bf16)
        act_gate = (gate * act_f).astype(bf16)
        out_main = dot(act_gate, w_d)
        out_low = dot(act_gate, a_down[...])
        in_main = dot_nt(grad_hidden, w_u)
        in_low = dot_nt(grad_hidden, b_up[...])
        gbu_out[...] += dot_tn(grad_hidden, x[:, D:])
        gad_out[...] += dot_tn(act_gate, c[:, D:])
        for j in range(6):
            out_flat[pl.ds(j, TILE, 16), :] = out_main[:, 128 * j : 128 * j + 128]
            out_flat[pl.ds(8 + j, TILE, 16), :] = in_main[:, 128 * j : 128 * j + 128]
        out_flat[pl.ds(6, TILE, 16), :] = out_low
        out_flat[pl.ds(14, TILE, 16), :] = in_low
        out_flat[pl.ds(15, TILE, 16), :] = jnp.where((lane == expert) & inside, gate_grad, 0.0)

        def give(b, carry):
            tokens = []
            sums = []
            for k in range(8):
                i = b * 8 + k
                token = jnp.where(i < rest, list_ref[base + i], DUMMY)
                tokens.append(token)
                sums.append(acc[token] + rows_out[i])
            for k in range(8):
                acc[tokens[k]] = sums[k]
            return carry

        lax.fori_loop(0, batches, give, 0)
        return carry

    lax.fori_loop(0, (count + TILE - 1) // TILE, tile, 0)

    @pl.when(expert == EXPERTS - 1)
    def epilogue():
        def image(i, carry):
            row = pl.multiple_of(i * SEQP, 16)
            base = row * 16
            mask = (lane // RANK) == picks_ref[i]

            def chunk(j):
                return acc_flat[pl.ds(base + j, SEQP, 16), :]

            x = xin[pl.ds(row, SEQP), :]
            c = cin[pl.ds(row, SEQP), :]
            low_in = jnp.where(mask, chunk(14), 0.0).astype(bf16)
            low_out = jnp.where(mask, chunk(6), 0.0).astype(bf16)
            gau_out[...] += dot_tn(x, low_in)
            gbd_out[...] += dot_tn(c, low_out)
            extra_in = dot_nt(low_in, a_up[...])
            extra_out = dot(low_out, b_down[...])
            for j in range(6):
                at = slice(128 * j, 128 * j + 128)
                cin[pl.ds(row, SEQP), at] = (chunk(8 + j) + extra_in[:, at]).astype(bf16)
                xin[pl.ds(row, SEQP), at] = (chunk(j) + extra_out[:, at]).astype(bf16)
            gpin[pl.ds(row, SEQP), :] = chunk(15).astype(bf16)
            rows = pl.ds(row, SEQP)
            pltpu.make_async_copy(cin.at[rows], tg_out.at[rows, pl.ds(0, D)], tg_sem).start()
            pltpu.make_async_copy(gpin.at[rows], tg_out.at[rows, pl.ds(D, 128)], tg_sem).start()
            pltpu.make_async_copy(xin.at[rows], ep_out.at[rows], ep_sem).start()
            return carry

        lax.fori_loop(0, IMG_GRP, image, 0)
        pltpu.make_async_copy(cin, tg_out.at[:, pl.ds(0, D)], tg_sem).wait()
        pltpu.make_async_copy(gpin, tg_out.at[:, pl.ds(D, 128)], tg_sem).wait()
        pltpu.make_async_copy(xin, ep_out, ep_sem).wait()


def moe_call(token_list, offs, picks, x_blocks, c_blocks, w_up, w_down, b_up, a_down, a_up, b_down, w_router, a_router, b_router):
    half = w_up.shape[2]
    n_x, n_c = len(x_blocks), len(c_blocks)

    def whole(*shape):
        return pl.BlockSpec(shape, lambda e, *_: (0,) * len(shape))

    anywhere = pl.BlockSpec(memory_space=pl.ANY)
    return pl.pallas_call(
        lambda *refs: moe_kernel(n_x, n_c, *refs),
        grid_spec=pltpu.PrefetchScalarGridSpec(
            num_scalar_prefetch=3,
            grid=(EXPERTS,),
            in_specs=[anywhere] * (n_x + n_c)
            + [
                pl.BlockSpec((1, D, half), lambda e, *_: (e, 0, 0)),
                pl.BlockSpec((1, half, D), lambda e, *_: (e, 0, 0)),
                whole(ADAPT, half),
                whole(half, ADAPT),
                whole(D, ADAPT),
                whole(ADAPT, D),
                whole(D, 128),
                whole(D, ADAPT),
                whole(ADAPT, 128),
            ],
            out_specs=[
                anywhere,
                anywhere,
                whole(half, ADAPT),
                whole(half, ADAPT),
                whole(D, ADAPT),
                whole(D, ADAPT),
            ],
            scratch_shapes=[
                pltpu.VMEM((TOK, D), bf16),
                pltpu.VMEM((TOK, D), bf16),
                pltpu.VMEM((TOK, 128), bf16),
                pltpu.VMEM((TOK, 16, 128), bf16),
                pltpu.VMEM((TOK, 16, 128), f32),
                pltpu.VMEM((TILE, 16, 128), f32),
                pltpu.VMEM((TILE, 16, 128), f32),
                pltpu.SemaphoreType.DMA((n_x + n_c,)),
                pltpu.SemaphoreType.DMA,
                pltpu.SemaphoreType.DMA,
            ],
        ),
        out_shape=[
            jax.ShapeDtypeStruct((TOK, D), bf16),
            jax.ShapeDtypeStruct((TOK, D + 128), bf16),
            jax.ShapeDtypeStruct((half, ADAPT), f32),
            jax.ShapeDtypeStruct((half, ADAPT), f32),
            jax.ShapeDtypeStruct((D, ADAPT), f32),
            jax.ShapeDtypeStruct((D, ADAPT), f32),
        ],
        compiler_params=pltpu.CompilerParams(vmem_limit_bytes=62 * 1024 * 1024),
        cost_estimate=pl.CostEstimate(flops=20_000_000_000, bytes_accessed=60_000_000, transcendentals=10_000_000),
    )(token_list, offs, picks, *x_blocks, *c_blocks, w_up, w_down, b_up, a_down, a_up, b_down, w_router, a_router, b_router)


HEADS = 12
HEAD_DIM = 64
PART_ROWS = 7168


def pick_mask(pick):
    return (lane_iota((1, ADAPT)) // RANK) == pick


def norm_stats(values):
    centre = jnp.sum(values, axis=1, keepdims=True) * (1.0 / D)
    shifted = values - centre
    spread = jnp.sum(shifted * shifted, axis=1, keepdims=True) * (1.0 / D)
    inverse = lax.rsqrt(spread + 1e-06)
    return shifted * inverse, inverse


def norm_back(grad, gain, unit, inverse):
    scaled = grad * gain
    total = jnp.sum(scaled, axis=1, keepdims=True) * (1.0 / D)
    along = jnp.sum(scaled * unit, axis=1, keepdims=True) * (1.0 / D)
    return inverse * (scaled - total - unit * along)


def load_weights(place_ref, blocks, scratch, sem):
    qkv, low_a, low_b, out_w, out_a = blocks
    w_qkv, a_qkv, b_qkv, w_out, a_out = scratch
    row, col = place_ref[0], place_ref[1]
    copies = []

    def copy(source, target):
        copies.append(pltpu.make_async_copy(source, target, sem.at[len(copies)]))

    for t in range(2):
        rows_at = pl.multiple_of((row ^ t) * 384, 128)
        for s in range(4):
            at = pl.multiple_of((col ^ s) * 192, 64)
            copy(qkv[4 * t + s], w_qkv.at[:, pl.ds(at, 192), pl.ds(rows_at, 384)])
        copy(low_b[t], b_qkv.at[:, :, pl.ds(rows_at, 384)])
        copy(out_w[t], w_out.at[pl.ds(rows_at, 384), :])
        copy(out_a[t], a_out.at[pl.ds(rows_at, 384), :])
    for s in range(4):
        at = pl.multiple_of((col ^ s) * 192, 64)
        copy(low_a[s], a_qkv.at[:, pl.ds(at, 192), :])
    for one in copies:
        one.start()
    for one in copies:
        one.wait()


N_COPIES = 18
WEIGHT_SCRATCH = [
    pltpu.VMEM((3, D, D), bf16),
    pltpu.VMEM((3, D, ADAPT), bf16),
    pltpu.VMEM((3, ADAPT, D), bf16),
    pltpu.VMEM((D, D), bf16),
    pltpu.VMEM((D, ADAPT), bf16),
    pltpu.SemaphoreType.DMA((N_COPIES,)),
]


def split_blocks(refs):
    qkv, refs = refs[:8], refs[8:]
    low_a, refs = refs[:4], refs[4:]
    low_b, refs = refs[:2], refs[2:]
    out_w, refs = refs[:2], refs[2:]
    out_a, refs = refs[:2], refs[2:]
    return (qkv, low_a, low_b, out_w, out_a), refs


def attend_kernel(picks_ref, place_ref, *refs):
    blocks, refs = split_blocks(refs)
    (
        x_ref, gain_one, gain_two, b_out,
        two_out, resid_out, normed_out, qkv_out, mixed_out, probs_out, lows_out,
        w_qkv, a_qkv, b_qkv, w_out, a_out, sem,
    ) = refs
    image = pl.program_id(0)

    @pl.when(image == 0)
    def start():
        load_weights(place_ref, blocks, (w_qkv, a_qkv, b_qkv, w_out, a_out), sem)

    mask = pick_mask(picks_ref[image])
    x = x_ref[...].astype(f32)
    unit, unused = norm_stats(x)
    normed = (unit * gain_one[...]).astype(bf16)
    normed_out[...] = normed
    for p in range(3):
        low = jnp.where(mask, dot(normed, a_qkv[p]), 0.0).astype(bf16)
        lows_out[:, 128 * p : 128 * p + 128] = low
        qkv_out[p] = (dot(normed, w_qkv[p]) + dot(low, b_qkv[p])).astype(bf16)
    lane = lane_iota((1, 128))
    key_lane = lane_iota((1, SEQP))
    for pair in range(HEADS // 2):
        at = slice(128 * pair, 128 * pair + 128)
        q = qkv_out[0, :, at]
        k = qkv_out[1, :, at]
        v = qkv_out[2, :, at]
        parts = []
        for side in range(2):
            own = (lane // HEAD_DIM) == side
            scores = dot_nt(jnp.where(own, q, jnp.zeros_like(q)), k) * (HEAD_DIM**-0.5)
            scores = jnp.where(key_lane < SEQ, scores, -1e30)
            power = jnp.exp(scores - jnp.max(scores, axis=1, keepdims=True))
            probs = (power / jnp.sum(power, axis=1, keepdims=True)).astype(bf16)
            probs_out[0, 2 * pair + side] = probs
            parts.append(dot(probs, v))
        mixed_out[:, at] = jnp.where(lane < HEAD_DIM, parts[0], parts[1]).astype(bf16)
    mixed = mixed_out[...]
    low = jnp.where(mask, dot(mixed, a_out[...]), 0.0).astype(bf16)
    lows_out[:, 384:512] = low
    resid = x + dot(mixed, w_out[...]) + dot(low, b_out[...])
    resid_out[...] = resid
    unit, unused = norm_stats(resid)
    two_out[...] = (unit * gain_two[...]).astype(bf16)


def image_rows(lanes):
    return pl.BlockSpec((SEQP, lanes), lambda i, *_: (i, 0))


def kept(*shape):
    return pl.BlockSpec(shape, lambda i, *_: (0,) * len(shape))


QKV_SPEC = pl.BlockSpec((3, SEQP, D), lambda i, *_: (0, i, 0))
PROBS_SPEC = pl.BlockSpec((1, HEADS, SEQP, SEQP), lambda i, *_: (i, 0, 0, 0))
ANYWHERE = pl.BlockSpec(memory_space=pl.ANY)


def attend_call(picks, place, blocks, x, gain_one, gain_two, b_out):
    rows = x.shape[0]
    return pl.pallas_call(
        attend_kernel,
        grid_spec=pltpu.PrefetchScalarGridSpec(
            num_scalar_prefetch=2,
            grid=(2,),
            in_specs=[ANYWHERE] * len(blocks)
            + [image_rows(D), kept(1, D), kept(1, D), kept(ADAPT, D)],
            out_specs=[
                image_rows(D), image_rows(D), image_rows(D), QKV_SPEC,
                image_rows(D), PROBS_SPEC, image_rows(512),
            ],
            scratch_shapes=WEIGHT_SCRATCH,
        ),
        out_shape=[
            jax.ShapeDtypeStruct((rows, D), bf16),
            jax.ShapeDtypeStruct((rows, D), f32),
            jax.ShapeDtypeStruct((rows, D), bf16),
            jax.ShapeDtypeStruct((3, rows, D), bf16),
            jax.ShapeDtypeStruct((rows, D), bf16),
            jax.ShapeDtypeStruct((2, HEADS, SEQP, SEQP), bf16),
            jax.ShapeDtypeStruct((rows, 512), bf16),
        ],
        compiler_params=pltpu.CompilerParams(vmem_limit_bytes=48 * 1024 * 1024),
        cost_estimate=pl.CostEstimate(flops=4_000_000_000, bytes_accessed=15_000_000, transcendentals=2_000_000),
    )(picks, place, *blocks, x, gain_one, gain_two, b_out)


def attend_back_kernel(picks_ref, place_ref, *refs):
    blocks, refs = split_blocks(refs)
    (
        x_ref, gain_one, gain_two, b_out,
        two_ref, resid_ref, normed_ref, qkv_ref, mixed_ref, probs_ref, lows_ref,
        cot_ref, grad_a, grad_b, w_router, a_router, b_router,
        tokens_out, parts_out,
        w_qkv, a_qkv, b_qkv, w_out, a_out, sem, parts, grads, grad_mixed,
    ) = refs
    image = pl.program_id(0)

    @pl.when(image == 0)
    def start():
        parts[...] = jnp.zeros_like(parts)
        load_weights(place_ref, blocks, (w_qkv, a_qkv, b_qkv, w_out, a_out), sem)

    mask = pick_mask(picks_ref[image])
    lane = lane_iota((1, 128))

    def add_part(row, value):
        at = slice(row, row + value.shape[0])
        parts[at, :] += value

    two = two_ref[...]
    received = grad_a[...].astype(f32) + grad_b[...].astype(f32)
    low_r = jnp.where(mask, dot(two, a_router[...]), 0.0).astype(bf16)
    logits = dot(two, w_router[...]) + dot(low_r, b_router[...])
    logits = jnp.where(lane < EXPERTS, logits, -1e30)
    power = jnp.exp(logits - jnp.max(logits, axis=1, keepdims=True))
    probs = power / jnp.sum(power, axis=1, keepdims=True)
    grad_probs = jnp.where(lane < EXPERTS, received[:, D:], 0.0)
    grad_logits = probs * (grad_probs - jnp.sum(probs * grad_probs, axis=1, keepdims=True))
    grad_logits = grad_logits.astype(bf16)
    grad_low = jnp.where(mask, dot_nt(grad_logits, b_router[...]), 0.0).astype(bf16)
    grad_two = received[:, :D] + dot_nt(grad_logits, w_router[...]) + dot_nt(grad_low, a_router[...])
    add_part(6144, dot_tn(two, grad_low))
    add_part(6912, dot_tn(grad_logits, low_r))
    unit, inverse = norm_stats(resid_ref[...])
    grad_resid = cot_ref[...].astype(f32) + norm_back(grad_two, gain_two[...], unit, inverse)
    grad_attn = grad_resid.astype(bf16)
    mixed = mixed_ref[...]
    grad_low = jnp.where(mask, dot_nt(grad_attn, b_out[...]), 0.0).astype(bf16)
    grad_mixed[...] = (dot_nt(grad_attn, w_out[...]) + dot_nt(grad_low, a_out[...])).astype(bf16)
    add_part(4608, dot_tn(mixed, grad_low))
    add_part(5376, dot_tn(grad_attn, lows_ref[:, 384:512]))
    for pair in range(HEADS // 2):
        at = slice(128 * pair, 128 * pair + 128)
        q = qkv_ref[0, :, at]
        k = qkv_ref[1, :, at]
        v = qkv_ref[2, :, at]
        gm = grad_mixed[:, at]
        found = []
        for side in range(2):
            own = (lane // HEAD_DIM) == side
            weights = probs_ref[0, 2 * pair + side]
            weights_f = weights.astype(f32)
            grad_w = dot_nt(jnp.where(own, gm, jnp.zeros_like(gm)), v)
            inner = jnp.sum(weights_f * grad_w, axis=1, keepdims=True)
            grad_s = (weights_f * (grad_w - inner)).astype(bf16)
            found.append(
                (
                    dot(grad_s, k) * (HEAD_DIM**-0.5),
                    dot_tn(grad_s, q) * (HEAD_DIM**-0.5),
                    dot_tn(weights, gm),
                )
            )
        for p in range(3):
            grads[p, :, at] = jnp.where(lane < HEAD_DIM, found[0][p], found[1][p]).astype(bf16)
    normed = normed_ref[...]
    grad_normed = jnp.zeros((SEQP, D), f32)
    for p in range(3):
        piece = grads[p]
        grad_low = jnp.where(mask, dot_nt(piece, b_qkv[p]), 0.0).astype(bf16)
        grad_normed = grad_normed + dot_nt(piece, w_qkv[p]) + dot_nt(grad_low, a_qkv[p])
        add_part(768 * p, dot_tn(normed, grad_low))
        add_part(2304 + 768 * p, dot_tn(piece, lows_ref[:, 128 * p : 128 * p + 128]))
    unit, inverse = norm_stats(x_ref[...].astype(f32))
    tokens_out[...] = (grad_resid + norm_back(grad_normed, gain_one[...], unit, inverse)).astype(bf16)

    @pl.when(image == 1)
    def finish():
        parts_out[...] = parts[...].astype(bf16)


def attend_back_call(picks, place, blocks, x, gain_one, gain_two, b_out, saved, cot, grad_a, grad_b, w_router, a_router, b_router):
    rows = x.shape[0]
    return pl.pallas_call(
        attend_back_kernel,
        grid_spec=pltpu.PrefetchScalarGridSpec(
            num_scalar_prefetch=2,
            grid=(2,),
            in_specs=[ANYWHERE] * len(blocks)
            + [image_rows(D), kept(1, D), kept(1, D), kept(ADAPT, D)]
            + [
                image_rows(D), image_rows(D), image_rows(D), QKV_SPEC,
                image_rows(D), PROBS_SPEC, image_rows(512),
            ]
            + [image_rows(D), image_rows(D + 128), image_rows(D + 128)]
            + [kept(D, 128), kept(D, ADAPT), kept(ADAPT, 128)],
            out_specs=[image_rows(D), kept(PART_ROWS, 128)],
            scratch_shapes=WEIGHT_SCRATCH
            + [
                pltpu.VMEM((PART_ROWS, 128), f32),
                pltpu.VMEM((3, SEQP, D), bf16),
                pltpu.VMEM((SEQP, D), bf16),
            ],
        ),
        out_shape=[
            jax.ShapeDtypeStruct((rows, D), bf16),
            jax.ShapeDtypeStruct((PART_ROWS, 128), bf16),
        ],
        compiler_params=pltpu.CompilerParams(vmem_limit_bytes=56 * 1024 * 1024),
        cost_estimate=pl.CostEstimate(flops=9_000_000_000, bytes_accessed=20_000_000, transcendentals=100_000),
    )(picks, place, *blocks, x, gain_one, gain_two, b_out, *saved, cot, grad_a, grad_b, w_router, a_router, b_router)


def across_row(value):
    return lax.ppermute(value, "row", [(0, 1), (1, 0)])


def across_col(value, step):
    return lax.ppermute(value, "col", [(i, i ^ step) for i in range(4)])


def by_place(blocks, col):
    found = []
    for place in range(4):
        value = blocks[place]
        for other in range(1, 4):
            value = jnp.where(col == other, blocks[place ^ other], value)
        found.append(value)
    return found


def gather_col(value, axis=0):
    middle = value.shape[axis] // 2
    from_x = across_col(value, 1)
    from_y = across_col(value, 2)
    head = across_col(lax.slice_in_dim(from_y, 0, middle, axis=axis), 1)
    tail = across_col(lax.slice_in_dim(from_x, middle, 2 * middle, axis=axis), 2)
    return [value, from_x, from_y, head, tail]


def joined(blocks, axis=0):
    return blocks[:3] + [jnp.concatenate(blocks[3:], axis=axis)]


def gather_group(value):
    own = gather_col(value)
    return own + [across_row(block) for block in own]


def added(*values):
    total = values[0].astype(f32)
    for value in values[1:]:
        total = total + value.astype(f32)
    return total


def scatter_group(value):
    lanes = value.shape[1]
    both = added(value[: TOK // 2], across_row(value[TOK // 2 :])).astype(bf16)
    both = both.reshape(4, 2, SEQP, lanes)
    from_x = across_col(jnp.stack([both[1, 0], both[3, 0]]), 1)
    from_y = across_col(jnp.stack([both[2, 1], both[3, 1]]), 2)
    last_y = across_col(added(both[2, 0], from_x[1]).astype(bf16), 2)
    last_x = across_col(added(both[1, 1], from_y[1]).astype(bf16), 1)
    mine = jnp.concatenate([added(both[0, 0], from_x[0]), added(both[0, 1], from_y[0])])
    return mine.astype(bf16), jnp.concatenate([last_y, last_x])


def reduce_parts(value, row, col):
    n = value.shape[0] // 8
    view = value.reshape(2, 4, n, 128)
    theirs = lax.dynamic_index_in_dim(view, 1 - row, 0, keepdims=False)
    ours = lax.dynamic_index_in_dim(view, row, 0, keepdims=False)
    both = added(ours, across_row(theirs)).astype(bf16)
    found = [lax.dynamic_index_in_dim(both, col, 0, keepdims=False)]
    for s in range(1, 4):
        found.append(across_col(lax.dynamic_index_in_dim(both, col ^ s, 0, keepdims=False), s))
    return added(*found).astype(bf16)


def reduce_dp(value):
    n_dp = lax.axis_size("dp")
    if n_dp != 4:
        return lax.psum(value, "dp")
    place = lax.axis_index("dp")

    def across(part, step):
        return lax.ppermute(part, "dp", [(i, i ^ step) for i in range(4)])

    view = value.reshape(4, -1, 128)
    found = [lax.dynamic_index_in_dim(view, place, 0, keepdims=False)]
    for s in range(1, 4):
        found.append(across(lax.dynamic_index_in_dim(view, place ^ s, 0, keepdims=False), s))
    total = added(*found).astype(bf16)
    blocks = [total] + [across(total, s) for s in range(1, 4)]
    return jnp.concatenate(by_place(blocks, place))


def spread_parts(value, row, col):
    blocks = [value] + [across_col(value, s) for s in range(1, 4)]
    half = jnp.concatenate(by_place(blocks, col))
    other = across_row(half)
    return jnp.where(row == 0, jnp.concatenate([half, other]), jnp.concatenate([other, half]))


def token_blocks(value):
    images = value.reshape(8, SEQ, value.shape[1])
    return jnp.pad(images, ((0, 0), (0, SEQP - SEQ), (0, 0))).reshape(4, BLK, value.shape[1])


def to_features(value, col):
    width = D // 4
    chunks = by_place([value[:, width * p : width * p + width] for p in range(4)], col)
    sent = [jnp.concatenate([chunk[:SEQP], chunk[SEQP:]], axis=1) for chunk in chunks]
    got = [sent[0]] + [across_col(sent[s], s) for s in range(1, 4)]
    rows = []
    for block in by_place(got, col):
        rows += [block[:SEQ, :width], block[:SEQ, width:]]
    return jnp.concatenate(rows, axis=0)


def on_device(
    tokens, cotangent, routes, adapter_pick, gain_attn, gain_moe, w_qkv, w_out, w_router, w_up, w_down,
    a_qkv, b_qkv, a_out, b_out, a_router, b_router, a_up, b_up, a_down, b_down,
):
    row = lax.axis_index("row")
    col = lax.axis_index("col")
    me = row * 4 + col
    place = jnp.stack([row, col]).astype(jnp.int32)

    both = jnp.concatenate([token_blocks(tokens), token_blocks(cotangent)], axis=2)
    pairs = [lax.dynamic_index_in_dim(both, col, 0, keepdims=False)]
    for s in range(1, 4):
        pairs.append(across_col(lax.dynamic_index_in_dim(both, col ^ s, 0, keepdims=False), s))
    pairs = by_place(pairs, col)
    width = D // 4
    x = jnp.concatenate([pair[:, :width] for pair in pairs], axis=1)
    cot = jnp.concatenate([pair[:, width:] for pair in pairs], axis=1)

    own_qkv = joined(gather_col(w_qkv, axis=1), axis=1)
    qkv_blocks = own_qkv + [across_row(block) for block in own_qkv]
    low_a = joined(gather_col(a_qkv, axis=1), axis=1)
    low_b = [b_qkv, across_row(b_qkv)]
    gains = []
    for gain in (gain_attn, gain_moe):
        left = gain
        for unused in range(3):
            lead = lax.reduce_precision(left, 8, 7)
            gains.append(lead.astype(bf16))
            left = left - lead
    small = jnp.concatenate([w_out, b_out, jnp.stack(gains), jnp.zeros((10, width), bf16)], axis=0)
    small = jnp.concatenate([small[:264], small[264:]], axis=1)
    small = by_place([small] + [across_col(small, s) for s in range(1, 4)], col)
    small = jnp.concatenate(
        [jnp.concatenate([block[:, :width] for block in small], axis=1),
         jnp.concatenate([block[:, width:] for block in small], axis=1)], axis=0
    )
    out_w = [small[:384], across_row(small[:384])]
    full_b_out = small[384:512]
    gain_rows = small[512:518].astype(f32)
    gain_one = jnp.sum(gain_rows[:3], axis=0, keepdims=True)
    gain_two = jnp.sum(gain_rows[3:], axis=0, keepdims=True)
    out_a = [a_out, across_row(a_out)]
    blocks = qkv_blocks + low_a + low_b + out_w + out_a

    picks_group = lax.dynamic_slice_in_dim(adapter_pick, lax.axis_index("dp") * IMG_GRP, IMG_GRP)
    order = jnp.arange(IMG_GRP, dtype=jnp.int32)
    picks = jnp.take(picks_group, ((order // 2) ^ me) * 2 + order % 2)
    token = jnp.arange(IMG_GRP * SEQ, dtype=jnp.int32)
    image = token // SEQ
    spot = ((image // 2) ^ me) * BLK + (image % 2) * SEQP + token % SEQ
    keys = (routes * 4096 + spot[:, None]).reshape(-1)
    token_list = jnp.concatenate([lax.sort(keys) & 4095, jnp.zeros((TILE,), jnp.int32)])
    offs = jnp.sum(
        (routes.reshape(-1)[:, None] < jnp.arange(EXPERTS + 1, dtype=jnp.int32)[None, :]).astype(jnp.int32), axis=0
    )
    wide_router = jnp.concatenate([w_router, w_router, jnp.zeros((D, 64), bf16)], axis=1)
    wide_b_router = jnp.concatenate([b_router, b_router, jnp.zeros((ADAPT, 64), bf16)], axis=1)
    slim_router = jnp.concatenate([w_router, jnp.zeros((D, 96), bf16)], axis=1)
    slim_b_router = jnp.concatenate([b_router, jnp.zeros((ADAPT, 96), bf16)], axis=1)

    saved = attend_call(picks, place, blocks, x, gain_one, gain_two, full_b_out)
    cot_blocks = gather_group(cot)
    two_blocks = gather_group(saved[0])
    sums, grads, part_b_up, part_a_down, part_a_up, part_b_down = moe_call(
        token_list, offs, picks, two_blocks, cot_blocks, w_up, w_down, b_up, a_down, a_up, b_down,
        wide_router, a_router, wide_b_router,
    )
    grad_a, grad_b = scatter_group(grads)
    grad_tokens, parts = attend_back_call(
        picks, place, blocks, x, gain_one, gain_two, full_b_out, saved, cot, grad_a, grad_b,
        slim_router, a_router, slim_b_router,
    )
    sum_a, sum_b = scatter_group(sums)
    block_out = to_features((saved[1] + added(sum_a, sum_b)).astype(bf16), col)
    grad_tokens = to_features(grad_tokens, col).astype(f32)

    early = reduce_parts(jnp.concatenate([part_a_up, part_b_down]).astype(bf16), row, col)
    n_early = early.shape[0]
    early = reduce_dp(jnp.concatenate([early, part_b_up.astype(bf16), part_a_down.astype(bf16)]))
    grad_b_up = early[n_early : n_early + 384].astype(f32).T
    grad_a_down = early[n_early + 384 :].astype(f32)
    early = spread_parts(early[:n_early], row, col).astype(f32)

    late = spread_parts(reduce_dp(reduce_parts(parts, row, col)), row, col)
    half = D // 2
    grad_a_qkv = lax.dynamic_slice_in_dim(late[:2304].reshape(3, D, ADAPT), col * width, width, axis=1)
    grad_b_qkv = lax.dynamic_slice_in_dim(late[2304:4608].reshape(3, D, ADAPT), row * half, half, axis=1)
    grad_a_out = lax.dynamic_slice_in_dim(late[4608:5376], row * half, half, axis=0)
    grad_b_out = lax.dynamic_slice_in_dim(late[5376:6144], col * width, width, axis=0)
    return (
        block_out,
        grad_tokens,
        grad_a_qkv.astype(f32),
        jnp.swapaxes(grad_b_qkv.astype(f32), 1, 2),
        grad_a_out.astype(f32),
        grad_b_out.astype(f32).T,
        late[6144:6912].astype(f32),
        late[6912:6944].astype(f32).T,
        early[:768],
        grad_b_up,
        grad_a_down,
        early[768:].T,
    )


def solution(mesh):
    return jax.shard_map(
        on_device,
        mesh=mesh,
        in_specs=(
            P(("dp", "row"), "col"),
            P(("dp", "row"), "col"),
            P("dp", None),
            P(),
            P("col"),
            P("col"),
            P(None, "col", "row"),
            P("row", "col"),
            P(),
            P(None, None, ("row", "col")),
            P(None, ("row", "col"), None),
            P(None, "col", None),
            P(None, None, "row"),
            P("row", None),
            P(None, "col"),
            P(),
            P(),
            P(),
            P(None, ("row", "col")),
            P(("row", "col"), None),
            P(),
        ),
        out_specs=(
            P(("dp", "row"), "col"),
            P(("dp", "row"), "col"),
            P(None, "col", None),
            P(None, None, "row"),
            P("row", None),
            P(None, "col"),
            P(),
            P(),
            P(),
            P(None, ("row", "col")),
            P(("row", "col"), None),
            P(),
        ),
        check_vma=False,
    )
```

```python
import jax
import jax.numpy as jnp
from jax import lax
from jax.experimental import pallas as pl
from jax.experimental.pallas import tpu as pltpu
from jax.sharding import PartitionSpec as P

D = 768
EXPERTS = 32
SEQ = 197
SEQP = 208
RANK = 16
ADAPT = 128
IMG_GRP = 16
TOK = IMG_GRP * SEQP
BLK = 2 * SEQP
DUMMY = SEQ
TILE = 192
f32 = jnp.float32
bf16 = jnp.bfloat16


def max_tiles():
    return (2 * IMG_GRP * SEQ) // TILE + EXPERTS + 1


def dot(left, right):
    return jnp.dot(left, right, preferred_element_type=f32)


def dot_nt(left, right):
    return lax.dot_general(left, right, (((1,), (1,)), ((), ())), preferred_element_type=f32)


def dot_tn(left, right):
    return lax.dot_general(left, right, (((0,), (0,)), ((), ())), preferred_element_type=f32)


def lane_iota(shape):
    return lax.broadcasted_iota(jnp.int32, shape, len(shape) - 1)


def repeat_lanes(value):
    for shift in (16, 32, 64):
        value = value + pltpu.roll(value, shift, 1)
    return value


def table_kernel(n_blocks, picks_ref, *refs):
    x_blocks = refs[:n_blocks]
    c_blocks = refs[n_blocks : 2 * n_blocks]
    a_up, b_down, w_router, a_router, b_router, table_out, xin, cin, rows_x, rows_c, sem = refs[2 * n_blocks :]
    image = pl.program_id(0)
    lane = lane_iota((1, 128))

    @pl.when(image == 0)
    def start():
        copies = []
        for blocks, place in ((x_blocks, xin), (c_blocks, cin)):
            for b, block in enumerate(blocks):
                copies.append(pltpu.make_async_copy(block, place.at[pl.ds(b * BLK, BLK)], sem.at[len(copies)]))
        for copy in copies:
            copy.start()
        for copy in copies:
            copy.wait()

    row = pl.multiple_of(image * SEQP, 16)
    mask = (lane // RANK) == picks_ref[image]
    x = xin[pl.ds(row, SEQP), :]
    c = cin[pl.ds(row, SEQP), :]
    flat_x = rows_x.reshape(SEQP * 8, 128)
    flat_c = rows_c.reshape(SEQP * 8, 128)
    low_x = jnp.where(mask, dot(x, a_up[...]), 0.0)
    low_c = jnp.where(mask, dot_nt(c, b_down[...]), 0.0)
    low_r = jnp.where(mask, dot(x, a_router[...]), 0.0).astype(bf16)
    logits = dot(x, w_router[...]) + dot(low_r, b_router[...])
    logits = jnp.where(lane < 2 * EXPERTS, logits, -1e30)
    power = jnp.exp(logits - jnp.max(logits, axis=1, keepdims=True))
    total = jnp.sum(jnp.where(lane < EXPERTS, power, 0.0), axis=1, keepdims=True)
    probs = power / total
    lead = probs.astype(bf16).astype(f32)
    probs = jnp.where(lane < EXPERTS, lead, probs - lead)
    for j in range(6):
        flat_x[pl.ds(j, SEQP, 8), :] = x[:, 128 * j : 128 * j + 128].astype(f32)
        flat_c[pl.ds(j, SEQP, 8), :] = c[:, 128 * j : 128 * j + 128].astype(f32)
    flat_x[pl.ds(6, SEQP, 8), :] = low_x
    flat_x[pl.ds(7, SEQP, 8), :] = probs
    flat_c[pl.ds(6, SEQP, 8), :] = low_c
    flat_c[pl.ds(7, SEQP, 8), :] = jnp.zeros((SEQP, 128), f32)
    table_out[...] = jnp.concatenate([rows_x[...], rows_c[...]], axis=1).astype(bf16)


def table_call(picks, x_blocks, c_blocks, a_up, b_down, w_router, a_router, b_router):
    n = len(x_blocks)

    def whole(*shape):
        return pl.BlockSpec(shape, lambda e, *_: (0,) * len(shape))

    anywhere = pl.BlockSpec(memory_space=pl.ANY)
    return pl.pallas_call(
        lambda *refs: table_kernel(n, *refs),
        grid_spec=pltpu.PrefetchScalarGridSpec(
            num_scalar_prefetch=1,
            grid=(2 * n,),
            in_specs=[anywhere] * (2 * n)
            + [whole(D, ADAPT), whole(ADAPT, D), whole(D, 128), whole(D, ADAPT), whole(ADAPT, 128)],
            out_specs=pl.BlockSpec((SEQP, 16, 128), lambda i, *_: (i, 0, 0)),
            scratch_shapes=[
                pltpu.VMEM((n * BLK, D), bf16),
                pltpu.VMEM((n * BLK, D), bf16),
                pltpu.VMEM((SEQP, 8, 128), f32),
                pltpu.VMEM((SEQP, 8, 128), f32),
                pltpu.SemaphoreType.DMA((2 * n,)),
            ],
        ),
        out_shape=jax.ShapeDtypeStruct((n * BLK, 16, 128), bf16),
        compiler_params=pltpu.CompilerParams(vmem_limit_bytes=32 * 1024 * 1024),
        cost_estimate=pl.CostEstimate(flops=n * 3_000_000_000, bytes_accessed=n * 3_000_000, transcendentals=n * 60_000),
    )(picks, *x_blocks, *c_blocks, a_up, b_down, w_router, a_router, b_router)


def moe_kernel(places, list_ref, expert_ref, picks_ref, *refs):
    n = len(places)
    tables = refs[:n]
    (
        w_up_hbm, w_down_hbm, b_up, a_down,
        ep_out, tg_out, gbu_out, gad_out,
        table, acc_e, acc_t, in_x, in_c, out_e, out_t, xb, cb, w_up, w_down, stage_ep, stage_tg,
        in_sem, up_sem, down_sem, ep_sem, tg_sem,
    ) = refs[n:]
    acc_e_flat = acc_e.reshape(TOK * 8, 128)
    acc_t_flat = acc_t.reshape(TOK * 8, 128)
    in_x_flat = in_x.reshape(TILE * 8, 128)
    in_c_flat = in_c.reshape(TILE * 8, 128)
    out_e_flat = out_e.reshape(TILE * 8, 128)
    out_t_flat = out_t.reshape(TILE * 8, 128)
    lane = lane_iota((1, 128))
    n_tiles = expert_ref[max_tiles()]

    copies = []
    for piece, spots in zip(tables, places):
        for b, spot in enumerate(spots):
            copies.append(
                pltpu.make_async_copy(
                    piece.at[pl.ds(b * BLK, BLK)], table.at[pl.ds(spot * BLK, BLK)], in_sem.at[len(copies)]
                )
            )
    for copy in copies:
        copy.start()

    def weights(expert):
        slot = expert % 2
        return (
            pltpu.make_async_copy(w_up_hbm.at[expert], w_up.at[slot], up_sem.at[slot]),
            pltpu.make_async_copy(w_down_hbm.at[expert], w_down.at[slot], down_sem.at[slot]),
        )

    for copy in weights(0):
        copy.start()
    out_e[...] = jnp.zeros_like(out_e)
    out_t[...] = jnp.zeros_like(out_t)
    gbu_out[...] = jnp.zeros_like(gbu_out)
    gad_out[...] = jnp.zeros_like(gad_out)

    def clear(i, carry):
        acc_e[pl.ds(i * 64, 64)] = jnp.zeros((64, 8, 128), f32)
        acc_t[pl.ds(i * 64, 64)] = jnp.zeros((64, 8, 128), f32)
        return carry

    lax.fori_loop(0, TOK // 64, clear, 0)
    for copy in copies:
        copy.wait()

    def fetch(t):
        for i in range(TILE):
            both = table[list_ref[t * TILE + i]].astype(f32)
            in_x[i] = both[:8]
            in_c[i] = both[8:]

    def give(t):
        for b in range(TILE // 8):
            tokens = [list_ref[t * TILE + 8 * b + k] for k in range(8)]
            sums_e = [acc_e[tokens[k]] + out_e[8 * b + k] for k in range(8)]
            sums_t = [acc_t[tokens[k]] + out_t[8 * b + k] for k in range(8)]
            for k in range(8):
                acc_e[tokens[k]] = sums_e[k]
                acc_t[tokens[k]] = sums_t[k]

    fetch(0)

    def tile(t, carry):
        expert = expert_ref[t]
        slot = expert % 2

        @pl.when((t == 0) | (expert_ref[jnp.maximum(t - 1, 0)] != expert))
        def arrive():
            for copy in weights(expert):
                copy.wait()

            @pl.when(expert + 1 < EXPERTS)
            def ahead():
                for copy in weights(expert + 1):
                    copy.start()

        for j in range(7):
            xb[:, 128 * j : 128 * j + 128] = in_x_flat[pl.ds(j, TILE, 8), :].astype(bf16)
            cb[:, 128 * j : 128 * j + 128] = in_c_flat[pl.ds(j, TILE, 8), :].astype(bf16)
        spread = in_x_flat[pl.ds(7, TILE, 8), :]
        mine = (lane == expert) | (lane == expert + EXPERTS)
        gate = jnp.sum(jnp.where(mine, spread, 0.0), axis=1, keepdims=True)
        fetch(t + 1)
        give(jnp.maximum(t - 1, 0))
        hidden = dot(xb[:, :D], w_up[slot]) + dot(xb[:, D:], b_up[...])
        back = dot_nt(cb[:, :D], w_down[slot]) + dot_nt(cb[:, D:], a_down[...])
        cdf = 0.5 + 0.5 * lax.erf(hidden * 0.7071067811865476)
        slope = cdf + hidden * jnp.exp(hidden * hidden * -0.5) * 0.3989422804014327
        act = (hidden * cdf).astype(bf16)
        act_f = act.astype(f32)
        gate_grad = jnp.sum(act_f * back, axis=1, keepdims=True)
        grad_hidden = (gate * back * slope).astype(bf16)
        act_gate = (gate * act_f).astype(bf16)
        out_main = dot(act_gate, w_down[slot])
        out_low = dot(act_gate, a_down[...])
        in_main = dot_nt(grad_hidden, w_up[slot])
        in_low = dot_nt(grad_hidden, b_up[...])
        gbu_out[...] += dot_tn(grad_hidden, xb[:, D:])
        gad_out[...] += dot_tn(act_gate, cb[:, D:])
        for j in range(6):
            out_e_flat[pl.ds(j, TILE, 8), :] = out_main[:, 128 * j : 128 * j + 128]
            out_t_flat[pl.ds(j, TILE, 8), :] = in_main[:, 128 * j : 128 * j + 128]
        out_e_flat[pl.ds(6, TILE, 8), :] = out_low
        out_t_flat[pl.ds(6, TILE, 8), :] = in_low
        out_t_flat[pl.ds(7, TILE, 8), :] = jnp.where(lane == expert, gate_grad, 0.0)
        return carry

    lax.fori_loop(0, n_tiles, tile, 0)
    give(n_tiles - 1)

    def image(i, carry):
        slot = i % 2
        row = pl.multiple_of(i * SEQP, 16)
        base = row * 8
        mask = (lane // RANK) == picks_ref[i]
        rows = pl.ds(row, SEQP)
        put_tg = pltpu.make_async_copy(stage_tg.at[slot], tg_out.at[rows], tg_sem.at[slot])
        put_ep = pltpu.make_async_copy(stage_ep.at[slot], ep_out.at[rows], ep_sem.at[slot])

        @pl.when(i >= 2)
        def drain():
            put_tg.wait()
            put_ep.wait()

        def chunk(j):
            flat = acc_e_flat if j < 8 else acc_t_flat
            return flat[pl.ds(base + j % 8, SEQP, 8), :]

        for j in range(6):
            at = slice(128 * j, 128 * j + 128)
            stage_tg[slot, :, at] = chunk(8 + j).astype(bf16)
            stage_ep[slot, :, at] = chunk(j).astype(bf16)
        low_in = repeat_lanes(jnp.where(mask, chunk(14), 0.0))
        low_out = repeat_lanes(jnp.where(mask, chunk(6), 0.0))
        last = jnp.where(lane < 32, chunk(15), jnp.where(lane < 48, low_in, jnp.where(lane < 64, low_out, 0.0)))
        stage_tg[slot, :, D:] = last.astype(bf16)
        put_tg.start()
        put_ep.start()
        return carry

    lax.fori_loop(0, IMG_GRP, image, 0)
    for i in range(IMG_GRP - 2, IMG_GRP):
        rows = pl.ds(i * SEQP, SEQP)
        pltpu.make_async_copy(stage_tg.at[i % 2], tg_out.at[rows], tg_sem.at[i % 2]).wait()
        pltpu.make_async_copy(stage_ep.at[i % 2], ep_out.at[rows], ep_sem.at[i % 2]).wait()


def moe_call(token_list, tile_experts, picks, tables, places, w_up, w_down, b_up, a_down):
    half = w_up.shape[2]
    n = len(tables)
    n_copies = sum(len(spots) for spots in places)
    anywhere = pl.BlockSpec(memory_space=pl.ANY)
    inside = pl.BlockSpec(memory_space=pltpu.VMEM)
    return pl.pallas_call(
        lambda *refs: moe_kernel(places, *refs),
        grid_spec=pltpu.PrefetchScalarGridSpec(
            num_scalar_prefetch=3,
            grid=(1,),
            in_specs=[anywhere] * (n + 2) + [inside, inside],
            out_specs=[anywhere, anywhere, inside, inside],
            scratch_shapes=[
                pltpu.VMEM((TOK, 16, 128), bf16),
                pltpu.VMEM((TOK, 8, 128), f32),
                pltpu.VMEM((TOK, 8, 128), f32),
                pltpu.VMEM((TILE, 8, 128), f32),
                pltpu.VMEM((TILE, 8, 128), f32),
                pltpu.VMEM((TILE, 8, 128), f32),
                pltpu.VMEM((TILE, 8, 128), f32),
                pltpu.VMEM((TILE, D + 128), bf16),
                pltpu.VMEM((TILE, D + 128), bf16),
                pltpu.VMEM((2, D, half), bf16),
                pltpu.VMEM((2, half, D), bf16),
                pltpu.VMEM((2, SEQP, D), bf16),
                pltpu.VMEM((2, SEQP, D + 128), bf16),
                pltpu.SemaphoreType.DMA((n_copies,)),
                pltpu.SemaphoreType.DMA((2,)),
                pltpu.SemaphoreType.DMA((2,)),
                pltpu.SemaphoreType.DMA((2,)),
                pltpu.SemaphoreType.DMA((2,)),
            ],
        ),
        out_shape=[
            jax.ShapeDtypeStruct((TOK, D), bf16),
            jax.ShapeDtypeStruct((TOK, D + 128), bf16),
            jax.ShapeDtypeStruct((half, ADAPT), f32),
            jax.ShapeDtypeStruct((half, ADAPT), f32),
        ],
        compiler_params=pltpu.CompilerParams(vmem_limit_bytes=58 * 1024 * 1024),
        cost_estimate=pl.CostEstimate(flops=20_000_000_000, bytes_accessed=60_000_000, transcendentals=10_000_000),
    )(token_list, tile_experts, picks, *tables, w_up, w_down, b_up, a_down)


def routing(routes, me):
    token = jnp.arange(IMG_GRP * SEQ, dtype=jnp.int32)
    image = token // SEQ
    spot = ((image // 2) ^ me) * BLK + (image % 2) * SEQP + token % SEQ
    keys = (routes * 4096 + spot[:, None]).reshape(-1)
    experts = jnp.arange(EXPERTS, dtype=jnp.int32)
    count = jnp.sum((routes.reshape(-1)[:, None] == experts[None, :]).astype(jnp.int32), axis=0)
    tiles = (jnp.maximum(count, 1) + TILE - 1) // TILE
    extra = tiles * TILE - count
    filler = jnp.where(
        jnp.arange(TILE, dtype=jnp.int32)[None, :] < extra[:, None], (experts * 4096)[:, None] + DUMMY, EXPERTS * 4096 + DUMMY
    ).reshape(-1)
    ordered = lax.sort(jnp.concatenate([keys, filler])) & 4095
    ordered = jnp.concatenate([ordered, jnp.full((TILE,), DUMMY, jnp.int32)])
    ends = jnp.sum(jnp.where(experts[None, :] <= experts[:, None], tiles[None, :], 0), axis=1)
    steps = jnp.arange(max_tiles(), dtype=jnp.int32)
    owner = jnp.minimum(jnp.sum((ends[None, :] <= steps[:, None]).astype(jnp.int32), axis=1), EXPERTS - 1)
    return ordered, jnp.concatenate([owner, jnp.sum(tiles)[None]])


HEADS = 12
HEAD_DIM = 64
PART_ROWS = 8704


def pick_mask(pick):
    return (lane_iota((1, ADAPT)) // RANK) == pick


def norm_stats(values):
    centre = jnp.sum(values, axis=1, keepdims=True) * (1.0 / D)
    shifted = values - centre
    spread = jnp.sum(shifted * shifted, axis=1, keepdims=True) * (1.0 / D)
    inverse = lax.rsqrt(spread + 1e-06)
    return shifted * inverse, inverse


def norm_back(grad, gain, unit, inverse):
    scaled = grad * gain
    total = jnp.sum(scaled, axis=1, keepdims=True) * (1.0 / D)
    along = jnp.sum(scaled * unit, axis=1, keepdims=True) * (1.0 / D)
    return inverse * (scaled - total - unit * along)


def load_weights(place_ref, blocks, scratch, sem):
    qkv, low_a, low_b, out_w, out_a = blocks
    w_qkv, a_qkv, b_qkv, w_out, a_out = scratch
    row, col = place_ref[0], place_ref[1]
    copies = []

    def copy(source, target):
        copies.append(pltpu.make_async_copy(source, target, sem.at[len(copies)]))

    for t in range(2):
        rows_at = pl.multiple_of((row ^ t) * 384, 128)
        for s in range(4):
            at = pl.multiple_of((col ^ s) * 192, 64)
            copy(qkv[4 * t + s], w_qkv.at[:, pl.ds(at, 192), pl.ds(rows_at, 384)])
        copy(low_b[t], b_qkv.at[:, :, pl.ds(rows_at, 384)])
        copy(out_w[t], w_out.at[pl.ds(rows_at, 384), :])
        copy(out_a[t], a_out.at[pl.ds(rows_at, 384), :])
    for s in range(4):
        at = pl.multiple_of((col ^ s) * 192, 64)
        copy(low_a[s], a_qkv.at[:, pl.ds(at, 192), :])
    for one in copies:
        one.start()
    for one in copies:
        one.wait()


N_COPIES = 18
WEIGHT_SCRATCH = [
    pltpu.VMEM((3, D, D), bf16),
    pltpu.VMEM((3, D, ADAPT), bf16),
    pltpu.VMEM((3, ADAPT, D), bf16),
    pltpu.VMEM((D, D), bf16),
    pltpu.VMEM((D, ADAPT), bf16),
    pltpu.SemaphoreType.DMA((N_COPIES,)),
]


def split_blocks(refs):
    qkv, refs = refs[:8], refs[8:]
    low_a, refs = refs[:4], refs[4:]
    low_b, refs = refs[:2], refs[2:]
    out_w, refs = refs[:2], refs[2:]
    out_a, refs = refs[:2], refs[2:]
    return (qkv, low_a, low_b, out_w, out_a), refs


def attend_kernel(picks_ref, place_ref, *refs):
    blocks, refs = split_blocks(refs)
    (
        x_ref, gain_one, gain_two, b_out,
        two_out, resid_out, normed_out, qkv_out, mixed_out, probs_out, lows_out,
        w_qkv, a_qkv, b_qkv, w_out, a_out, sem,
    ) = refs
    image = pl.program_id(0)

    @pl.when(image == 0)
    def start():
        load_weights(place_ref, blocks, (w_qkv, a_qkv, b_qkv, w_out, a_out), sem)

    mask = pick_mask(picks_ref[image])
    x = x_ref[...].astype(f32)
    unit, unused = norm_stats(x)
    normed = (unit * gain_one[...]).astype(bf16)
    normed_out[...] = normed
    for p in range(3):
        low = jnp.where(mask, dot(normed, a_qkv[p]), 0.0).astype(bf16)
        lows_out[:, 128 * p : 128 * p + 128] = low
        qkv_out[p] = (dot(normed, w_qkv[p]) + dot(low, b_qkv[p])).astype(bf16)
    lane = lane_iota((1, 128))
    key_lane = lane_iota((1, SEQP))
    for pair in range(HEADS // 2):
        at = slice(128 * pair, 128 * pair + 128)
        q = qkv_out[0, :, at]
        k = qkv_out[1, :, at]
        v = qkv_out[2, :, at]
        parts = []
        for side in range(2):
            own = (lane // HEAD_DIM) == side
            scores = dot_nt(jnp.where(own, q, jnp.zeros_like(q)), k) * (HEAD_DIM**-0.5)
            scores = jnp.where(key_lane < SEQ, scores, -1e30)
            power = jnp.exp(scores - jnp.max(scores, axis=1, keepdims=True))
            probs = (power / jnp.sum(power, axis=1, keepdims=True)).astype(bf16)
            probs_out[0, 2 * pair + side] = probs
            parts.append(dot(probs, v))
        mixed_out[:, at] = jnp.where(lane < HEAD_DIM, parts[0], parts[1]).astype(bf16)
    mixed = mixed_out[...]
    low = jnp.where(mask, dot(mixed, a_out[...]), 0.0).astype(bf16)
    lows_out[:, 384:512] = low
    resid = x + dot(mixed, w_out[...]) + dot(low, b_out[...])
    resid_out[...] = resid
    unit, unused = norm_stats(resid)
    real = lax.broadcasted_iota(jnp.int32, (SEQP, 1), 0) < SEQ
    two_out[...] = jnp.where(real, unit * gain_two[...], 0.0).astype(bf16)


def image_rows(lanes):
    return pl.BlockSpec((SEQP, lanes), lambda i, *_: (i, 0))


def kept(*shape):
    return pl.BlockSpec(shape, lambda i, *_: (0,) * len(shape))


QKV_SPEC = pl.BlockSpec((3, SEQP, D), lambda i, *_: (0, i, 0))
PROBS_SPEC = pl.BlockSpec((1, HEADS, SEQP, SEQP), lambda i, *_: (i, 0, 0, 0))
ANYWHERE = pl.BlockSpec(memory_space=pl.ANY)


def attend_call(picks, place, blocks, x, gain_one, gain_two, b_out):
    rows = x.shape[0]
    return pl.pallas_call(
        attend_kernel,
        grid_spec=pltpu.PrefetchScalarGridSpec(
            num_scalar_prefetch=2,
            grid=(2,),
            in_specs=[ANYWHERE] * len(blocks)
            + [image_rows(D), kept(1, D), kept(1, D), kept(ADAPT, D)],
            out_specs=[
                image_rows(D), image_rows(D), image_rows(D), QKV_SPEC,
                image_rows(D), PROBS_SPEC, image_rows(512),
            ],
            scratch_shapes=WEIGHT_SCRATCH,
        ),
        out_shape=[
            jax.ShapeDtypeStruct((rows, D), bf16),
            jax.ShapeDtypeStruct((rows, D), f32),
            jax.ShapeDtypeStruct((rows, D), bf16),
            jax.ShapeDtypeStruct((3, rows, D), bf16),
            jax.ShapeDtypeStruct((rows, D), bf16),
            jax.ShapeDtypeStruct((2, HEADS, SEQP, SEQP), bf16),
            jax.ShapeDtypeStruct((rows, 512), bf16),
        ],
        compiler_params=pltpu.CompilerParams(vmem_limit_bytes=48 * 1024 * 1024),
        cost_estimate=pl.CostEstimate(flops=4_000_000_000, bytes_accessed=15_000_000, transcendentals=2_000_000),
    )(picks, place, *blocks, x, gain_one, gain_two, b_out)


def attend_back_kernel(picks_ref, place_ref, *refs):
    blocks, refs = split_blocks(refs)
    (
        x_ref, gain_one, gain_two, b_out,
        two_ref, resid_ref, normed_ref, qkv_ref, mixed_ref, probs_ref, lows_ref,
        cot_ref, grad_a, grad_b, w_router, a_router, b_router, a_up, b_down,
        tokens_out, parts_out, base_out,
        w_qkv, a_qkv, b_qkv, w_out, a_out, sem, parts, grads, grad_mixed,
    ) = refs
    image = pl.program_id(0)

    @pl.when(image == 0)
    def start():
        parts[...] = jnp.zeros_like(parts)
        load_weights(place_ref, blocks, (w_qkv, a_qkv, b_qkv, w_out, a_out), sem)

    mask = pick_mask(picks_ref[image])
    lane = lane_iota((1, 128))

    def add_part(row, value):
        at = slice(row, row + value.shape[0])
        parts[at, :] += value

    two = two_ref[...]
    received = grad_a[...].astype(f32) + grad_b[...].astype(f32)
    low_r = jnp.where(mask, dot(two, a_router[...]), 0.0).astype(bf16)
    logits = dot(two, w_router[...]) + dot(low_r, b_router[...])
    logits = jnp.where(lane < EXPERTS, logits, -1e30)
    power = jnp.exp(logits - jnp.max(logits, axis=1, keepdims=True))
    probs = power / jnp.sum(power, axis=1, keepdims=True)
    last = received[:, D:]
    grad_probs = jnp.where(lane < EXPERTS, last, 0.0)
    low_in = jnp.where(mask, repeat_lanes(jnp.where((lane >= 32) & (lane < 48), last, 0.0)), 0.0).astype(bf16)
    low_out = jnp.where(mask, repeat_lanes(jnp.where((lane >= 48) & (lane < 64), last, 0.0)), 0.0).astype(bf16)
    cot = cot_ref[...]
    resid = resid_ref[...]
    base_out[...] = resid + dot(low_out, b_down[...])
    add_part(6944, dot_tn(two, low_in))
    add_part(7712, dot_tn(cot, low_out))
    grad_logits = probs * (grad_probs - jnp.sum(probs * grad_probs, axis=1, keepdims=True))
    grad_logits = grad_logits.astype(bf16)
    grad_low = jnp.where(mask, dot_nt(grad_logits, b_router[...]), 0.0).astype(bf16)
    grad_two = received[:, :D] + dot_nt(low_in, a_up[...])
    grad_two = grad_two + dot_nt(grad_logits, w_router[...]) + dot_nt(grad_low, a_router[...])
    add_part(6144, dot_tn(two, grad_low))
    add_part(6912, dot_tn(grad_logits, low_r))
    unit, inverse = norm_stats(resid)
    grad_resid = cot.astype(f32) + norm_back(grad_two, gain_two[...], unit, inverse)
    grad_attn = grad_resid.astype(bf16)
    mixed = mixed_ref[...]
    grad_low = jnp.where(mask, dot_nt(grad_attn, b_out[...]), 0.0).astype(bf16)
    grad_mixed[...] = (dot_nt(grad_attn, w_out[...]) + dot_nt(grad_low, a_out[...])).astype(bf16)
    add_part(4608, dot_tn(mixed, grad_low))
    add_part(5376, dot_tn(grad_attn, lows_ref[:, 384:512]))
    for pair in range(HEADS // 2):
        at = slice(128 * pair, 128 * pair + 128)
        q = qkv_ref[0, :, at]
        k = qkv_ref[1, :, at]
        v = qkv_ref[2, :, at]
        gm = grad_mixed[:, at]
        found = []
        for side in range(2):
            own = (lane // HEAD_DIM) == side
            weights = probs_ref[0, 2 * pair + side]
            weights_f = weights.astype(f32)
            grad_w = dot_nt(jnp.where(own, gm, jnp.zeros_like(gm)), v)
            inner = jnp.sum(weights_f * grad_w, axis=1, keepdims=True)
            grad_s = (weights_f * (grad_w - inner)).astype(bf16)
            found.append(
                (
                    dot(grad_s, k) * (HEAD_DIM**-0.5),
                    dot_tn(grad_s, q) * (HEAD_DIM**-0.5),
                    dot_tn(weights, gm),
                )
            )
        for p in range(3):
            grads[p, :, at] = jnp.where(lane < HEAD_DIM, found[0][p], found[1][p]).astype(bf16)
    normed = normed_ref[...]
    grad_normed = jnp.zeros((SEQP, D), f32)
    for p in range(3):
        piece = grads[p]
        grad_low = jnp.where(mask, dot_nt(piece, b_qkv[p]), 0.0).astype(bf16)
        grad_normed = grad_normed + dot_nt(piece, w_qkv[p]) + dot_nt(grad_low, a_qkv[p])
        add_part(768 * p, dot_tn(normed, grad_low))
        add_part(2304 + 768 * p, dot_tn(piece, lows_ref[:, 128 * p : 128 * p + 128]))
    unit, inverse = norm_stats(x_ref[...].astype(f32))
    tokens_out[...] = (grad_resid + norm_back(grad_normed, gain_one[...], unit, inverse)).astype(bf16)

    @pl.when(image == 1)
    def finish():
        parts_out[...] = parts[...].astype(bf16)


def attend_back_call(picks, place, blocks, x, gain_one, gain_two, b_out, saved, cot, grad_a, grad_b, w_router, a_router, b_router, a_up, b_down):
    rows = x.shape[0]
    return pl.pallas_call(
        attend_back_kernel,
        grid_spec=pltpu.PrefetchScalarGridSpec(
            num_scalar_prefetch=2,
            grid=(2,),
            in_specs=[ANYWHERE] * len(blocks)
            + [image_rows(D), kept(1, D), kept(1, D), kept(ADAPT, D)]
            + [
                image_rows(D), image_rows(D), image_rows(D), QKV_SPEC,
                image_rows(D), PROBS_SPEC, image_rows(512),
            ]
            + [image_rows(D), image_rows(D + 128), image_rows(D + 128)]
            + [kept(D, 128), kept(D, ADAPT), kept(ADAPT, 128), kept(D, ADAPT), kept(ADAPT, D)],
            out_specs=[image_rows(D), kept(PART_ROWS, 128), image_rows(D)],
            scratch_shapes=WEIGHT_SCRATCH
            + [
                pltpu.VMEM((PART_ROWS, 128), f32),
                pltpu.VMEM((3, SEQP, D), bf16),
                pltpu.VMEM((SEQP, D), bf16),
            ],
        ),
        out_shape=[
            jax.ShapeDtypeStruct((rows, D), bf16),
            jax.ShapeDtypeStruct((PART_ROWS, 128), bf16),
            jax.ShapeDtypeStruct((rows, D), f32),
        ],
        compiler_params=pltpu.CompilerParams(vmem_limit_bytes=56 * 1024 * 1024),
        cost_estimate=pl.CostEstimate(flops=9_000_000_000, bytes_accessed=20_000_000, transcendentals=100_000),
    )(picks, place, *blocks, x, gain_one, gain_two, b_out, *saved, cot, grad_a, grad_b, w_router, a_router, b_router, a_up, b_down)


TABLES = ((0, 4), (1, 2, 5, 6), (3, 7))


def across_row(value):
    return lax.ppermute(value, "row", [(0, 1), (1, 0)])


def across_col(value, step):
    return lax.ppermute(value, "col", [(i, i ^ step) for i in range(4)])


def by_place(blocks, col):
    found = []
    for place in range(4):
        value = blocks[place]
        for other in range(1, 4):
            value = jnp.where(col == other, blocks[place ^ other], value)
        found.append(value)
    return found


def gather_col(value, axis=0):
    middle = value.shape[axis] // 2
    from_x = across_col(value, 1)
    from_y = across_col(value, 2)
    head = across_col(lax.slice_in_dim(from_y, 0, middle, axis=axis), 1)
    tail = across_col(lax.slice_in_dim(from_x, middle, 2 * middle, axis=axis), 2)
    return [value, from_x, from_y, head, tail]


def joined(blocks, axis=0):
    return blocks[:3] + [jnp.concatenate(blocks[3:], axis=axis)]


def gather_group(value):
    own = joined(gather_col(value))
    return own + [across_row(block) for block in own]


def added(*values):
    total = values[0].astype(f32)
    for value in values[1:]:
        total = total + value.astype(f32)
    return total


def scatter_group(value):
    lanes = value.shape[1]
    both = added(value[: TOK // 2], across_row(value[TOK // 2 :])).astype(bf16)
    both = both.reshape(4, 2, SEQP, lanes)
    from_x = across_col(jnp.stack([both[1, 0], both[3, 0]]), 1)
    from_y = across_col(jnp.stack([both[2, 1], both[3, 1]]), 2)
    last_y = across_col(added(both[2, 0], from_x[1]).astype(bf16), 2)
    last_x = across_col(added(both[1, 1], from_y[1]).astype(bf16), 1)
    mine = jnp.concatenate([added(both[0, 0], from_x[0]), added(both[0, 1], from_y[0])])
    return mine.astype(bf16), jnp.concatenate([last_y, last_x])


def reduce_parts(value, row, col):
    n = value.shape[0] // 8
    view = value.reshape(2, 4, n, 128)
    theirs = lax.dynamic_index_in_dim(view, 1 - row, 0, keepdims=False)
    ours = lax.dynamic_index_in_dim(view, row, 0, keepdims=False)
    both = added(ours, across_row(theirs)).astype(bf16)
    found = [lax.dynamic_index_in_dim(both, col, 0, keepdims=False)]
    for s in range(1, 4):
        found.append(across_col(lax.dynamic_index_in_dim(both, col ^ s, 0, keepdims=False), s))
    return added(*found).astype(bf16)


def reduce_dp(value):
    n_dp = lax.axis_size("dp")
    if n_dp != 4:
        return lax.psum(value, "dp")
    place = lax.axis_index("dp")

    def across(part, step):
        return lax.ppermute(part, "dp", [(i, i ^ step) for i in range(4)])

    view = value.reshape(4, -1, 128)
    found = [lax.dynamic_index_in_dim(view, place, 0, keepdims=False)]
    for s in range(1, 4):
        found.append(across(lax.dynamic_index_in_dim(view, place ^ s, 0, keepdims=False), s))
    total = added(*found).astype(bf16)
    blocks = [total] + [across(total, s) for s in range(1, 4)]
    return jnp.concatenate(by_place(blocks, place))


def spread_parts(value, row, col):
    blocks = [value] + [across_col(value, s) for s in range(1, 4)]
    half = jnp.concatenate(by_place(blocks, col))
    other = across_row(half)
    return jnp.where(row == 0, jnp.concatenate([half, other]), jnp.concatenate([other, half]))


def token_blocks(value):
    images = value.reshape(8, SEQ, value.shape[1])
    return jnp.pad(images, ((0, 0), (0, SEQP - SEQ), (0, 0))).reshape(4, BLK, value.shape[1])


def to_features(value, col):
    width = D // 4
    chunks = by_place([value[:, width * p : width * p + width] for p in range(4)], col)
    sent = [jnp.concatenate([chunk[:SEQP], chunk[SEQP:]], axis=1) for chunk in chunks]
    got = [sent[0]] + [across_col(sent[s], s) for s in range(1, 4)]
    rows = []
    for block in by_place(got, col):
        rows += [block[:SEQ, :width], block[:SEQ, width:]]
    return jnp.concatenate(rows, axis=0)


def on_device(
    tokens, cotangent, routes, adapter_pick, gain_attn, gain_moe, w_qkv, w_out, w_router, w_up, w_down,
    a_qkv, b_qkv, a_out, b_out, a_router, b_router, a_up, b_up, a_down, b_down,
):
    row = lax.axis_index("row")
    col = lax.axis_index("col")
    me = row * 4 + col
    place = jnp.stack([row, col]).astype(jnp.int32)

    both = jnp.concatenate([token_blocks(tokens), token_blocks(cotangent)], axis=2)
    pairs = [lax.dynamic_index_in_dim(both, col, 0, keepdims=False)]
    for s in range(1, 4):
        pairs.append(across_col(lax.dynamic_index_in_dim(both, col ^ s, 0, keepdims=False), s))
    pairs = by_place(pairs, col)
    width = D // 4
    x = jnp.concatenate([pair[:, :width] for pair in pairs], axis=1)
    cot = jnp.concatenate([pair[:, width:] for pair in pairs], axis=1)

    own_qkv = joined(gather_col(w_qkv, axis=1), axis=1)
    qkv_blocks = own_qkv + [across_row(block) for block in own_qkv]
    low_a = joined(gather_col(a_qkv, axis=1), axis=1)
    low_b = [b_qkv, across_row(b_qkv)]
    gains = []
    for gain in (gain_attn, gain_moe):
        left = gain
        for unused in range(3):
            lead = lax.reduce_precision(left, 8, 7)
            gains.append(lead.astype(bf16))
            left = left - lead
    small = jnp.concatenate([w_out, b_out, jnp.stack(gains), jnp.zeros((10, width), bf16)], axis=0)
    small = jnp.concatenate([small[:264], small[264:]], axis=1)
    small = by_place([small] + [across_col(small, s) for s in range(1, 4)], col)
    small = jnp.concatenate(
        [jnp.concatenate([block[:, :width] for block in small], axis=1),
         jnp.concatenate([block[:, width:] for block in small], axis=1)], axis=0
    )
    out_w = [small[:384], across_row(small[:384])]
    full_b_out = small[384:512]
    gain_rows = small[512:518].astype(f32)
    gain_one = jnp.sum(gain_rows[:3], axis=0, keepdims=True)
    gain_two = jnp.sum(gain_rows[3:], axis=0, keepdims=True)
    out_a = [a_out, across_row(a_out)]
    blocks = qkv_blocks + low_a + low_b + out_w + out_a

    picks_group = lax.dynamic_slice_in_dim(adapter_pick, lax.axis_index("dp") * IMG_GRP, IMG_GRP)
    order = jnp.arange(IMG_GRP, dtype=jnp.int32)
    picks = jnp.take(picks_group, ((order // 2) ^ me) * 2 + order % 2)
    token_list, tile_experts = routing(routes, me)
    wide_router = jnp.concatenate([w_router, w_router, jnp.zeros((D, 64), bf16)], axis=1)
    wide_b_router = jnp.concatenate([b_router, b_router, jnp.zeros((ADAPT, 64), bf16)], axis=1)
    slim_router = jnp.concatenate([w_router, jnp.zeros((D, 96), bf16)], axis=1)
    slim_b_router = jnp.concatenate([b_router, jnp.zeros((ADAPT, 96), bf16)], axis=1)

    saved = attend_call(picks, place, blocks, x, gain_one, gain_two, full_b_out)
    cot_blocks = gather_group(cot)
    two_blocks = gather_group(saved[0])
    tables = []
    for spots in TABLES:
        tables.append(
            table_call(
                jnp.stack([picks[2 * spot + side] for spot in spots for side in range(2)]),
                [two_blocks[spot] for spot in spots], [cot_blocks[spot] for spot in spots],
                a_up, b_down, wide_router, a_router, wide_b_router,
            )
        )
    sums, grads, part_b_up, part_a_down = moe_call(token_list, tile_experts, picks, tables, TABLES, w_up, w_down, b_up, a_down)
    grad_a, grad_b = scatter_group(grads)
    grad_a, grad_b, sums, part_b_up, part_a_down = lax.optimization_barrier(
        (grad_a, grad_b, sums, part_b_up, part_a_down)
    )
    sum_a, sum_b = scatter_group(sums)
    early = reduce_dp(jnp.concatenate([part_b_up.astype(bf16), part_a_down.astype(bf16)]))
    grad_tokens, parts, base = attend_back_call(
        picks, place, blocks, x, gain_one, gain_two, full_b_out, saved, cot, grad_a, grad_b,
        slim_router, a_router, slim_b_router, a_up, b_down,
    )
    block_out = to_features((base + added(sum_a, sum_b)).astype(bf16), col)
    grad_tokens = to_features(grad_tokens, col).astype(f32)
    grad_b_up = early[:384].astype(f32).T
    grad_a_down = early[384:].astype(f32)

    late = spread_parts(reduce_dp(reduce_parts(parts, row, col)), row, col)
    half = D // 2
    grad_a_qkv = lax.dynamic_slice_in_dim(late[:2304].reshape(3, D, ADAPT), col * width, width, axis=1)
    grad_b_qkv = lax.dynamic_slice_in_dim(late[2304:4608].reshape(3, D, ADAPT), row * half, half, axis=1)
    grad_a_out = lax.dynamic_slice_in_dim(late[4608:5376], row * half, half, axis=0)
    grad_b_out = lax.dynamic_slice_in_dim(late[5376:6144], col * width, width, axis=0)
    return (
        block_out,
        grad_tokens,
        grad_a_qkv.astype(f32),
        jnp.swapaxes(grad_b_qkv.astype(f32), 1, 2),
        grad_a_out.astype(f32),
        grad_b_out.astype(f32).T,
        late[6144:6912].astype(f32),
        late[6912:6944].astype(f32).T,
        late[6944:7712].astype(f32),
        grad_b_up,
        grad_a_down,
        late[7712:8480].astype(f32).T,
    )


def solution(mesh):
    return jax.shard_map(
        on_device,
        mesh=mesh,
        in_specs=(
            P(("dp", "row"), "col"),
            P(("dp", "row"), "col"),
            P("dp", None),
            P(),
            P("col"),
            P("col"),
            P(None, "col", "row"),
            P("row", "col"),
            P(),
            P(None, None, ("row", "col")),
            P(None, ("row", "col"), None),
            P(None, "col", None),
            P(None, None, "row"),
            P("row", None),
            P(None, "col"),
            P(),
            P(),
            P(),
            P(None, ("row", "col")),
            P(("row", "col"), None),
            P(),
        ),
        out_specs=(
            P(("dp", "row"), "col"),
            P(("dp", "row"), "col"),
            P(None, "col", None),
            P(None, None, "row"),
            P("row", None),
            P(None, "col"),
            P(),
            P(),
            P(),
            P(None, ("row", "col")),
            P(("row", "col"), None),
            P(),
        ),
        check_vma=False,
    )
```

```python
import jax
import jax.numpy as jnp
from jax import lax
from jax.experimental import pallas as pl
from jax.experimental.pallas import tpu as pltpu
from jax.sharding import PartitionSpec as P

D = 768
EXPERTS = 32
SEQ = 197
SEQP = 208
RANK = 16
ADAPT = 128
IMG_GRP = 16
TOK = IMG_GRP * SEQP
BLK = 2 * SEQP
DUMMY = SEQ
TILE = 192
f32 = jnp.float32
bf16 = jnp.bfloat16


def max_tiles():
    return (2 * IMG_GRP * SEQ) // TILE + EXPERTS + 1


def dot(left, right):
    return jnp.dot(left, right, preferred_element_type=f32)


def dot_nt(left, right):
    return lax.dot_general(left, right, (((1,), (1,)), ((), ())), preferred_element_type=f32)


def dot_tn(left, right):
    return lax.dot_general(left, right, (((0,), (0,)), ((), ())), preferred_element_type=f32)


def lane_iota(shape):
    return lax.broadcasted_iota(jnp.int32, shape, len(shape) - 1)


def repeat_lanes(value):
    for shift in (16, 32, 64):
        value = value + pltpu.roll(value, shift, 1)
    return value


def table_kernel(n_blocks, picks_ref, *refs):
    x_blocks = refs[:n_blocks]
    c_blocks = refs[n_blocks : 2 * n_blocks]
    a_up, b_down, w_router, a_router, b_router, table_out, xin, cin, rows_x, rows_c, sem = refs[2 * n_blocks :]
    image = pl.program_id(0)
    lane = lane_iota((1, 128))

    @pl.when(image == 0)
    def start():
        copies = []
        for blocks, place in ((x_blocks, xin), (c_blocks, cin)):
            for b, block in enumerate(blocks):
                copies.append(pltpu.make_async_copy(block, place.at[pl.ds(b * BLK, BLK)], sem.at[len(copies)]))
        for copy in copies:
            copy.start()
        for copy in copies:
            copy.wait()

    row = pl.multiple_of(image * SEQP, 16)
    mask = (lane // RANK) == picks_ref[image]
    x = xin[pl.ds(row, SEQP), :]
    c = cin[pl.ds(row, SEQP), :]
    flat_x = rows_x.reshape(SEQP * 8, 128)
    flat_c = rows_c.reshape(SEQP * 8, 128)
    low_x = jnp.where(mask, dot(x, a_up[...]), 0.0)
    low_c = jnp.where(mask, dot_nt(c, b_down[...]), 0.0)
    low_r = jnp.where(mask, dot(x, a_router[...]), 0.0).astype(bf16)
    logits = dot(x, w_router[...]) + dot(low_r, b_router[...])
    logits = jnp.where(lane < 2 * EXPERTS, logits, -1e30)
    power = jnp.exp(logits - jnp.max(logits, axis=1, keepdims=True))
    total = jnp.sum(jnp.where(lane < EXPERTS, power, 0.0), axis=1, keepdims=True)
    probs = power / total
    lead = probs.astype(bf16).astype(f32)
    probs = jnp.where(lane < EXPERTS, lead, probs - lead)
    for j in range(6):
        flat_x[pl.ds(j, SEQP, 8), :] = x[:, 128 * j : 128 * j + 128].astype(f32)
        flat_c[pl.ds(j, SEQP, 8), :] = c[:, 128 * j : 128 * j + 128].astype(f32)
    flat_x[pl.ds(6, SEQP, 8), :] = low_x
    flat_x[pl.ds(7, SEQP, 8), :] = probs
    flat_c[pl.ds(6, SEQP, 8), :] = low_c
    flat_c[pl.ds(7, SEQP, 8), :] = jnp.zeros((SEQP, 128), f32)
    table_out[...] = jnp.concatenate([rows_x[...], rows_c[...]], axis=1).astype(bf16)


def table_call(picks, x_blocks, c_blocks, a_up, b_down, w_router, a_router, b_router):
    n = len(x_blocks)

    def whole(*shape):
        return pl.BlockSpec(shape, lambda e, *_: (0,) * len(shape))

    anywhere = pl.BlockSpec(memory_space=pl.ANY)
    return pl.pallas_call(
        lambda *refs: table_kernel(n, *refs),
        grid_spec=pltpu.PrefetchScalarGridSpec(
            num_scalar_prefetch=1,
            grid=(2 * n,),
            in_specs=[anywhere] * (2 * n)
            + [whole(D, ADAPT), whole(ADAPT, D), whole(D, 128), whole(D, ADAPT), whole(ADAPT, 128)],
            out_specs=pl.BlockSpec((SEQP, 16, 128), lambda i, *_: (i, 0, 0)),
            scratch_shapes=[
                pltpu.VMEM((n * BLK, D), bf16),
                pltpu.VMEM((n * BLK, D), bf16),
                pltpu.VMEM((SEQP, 8, 128), f32),
                pltpu.VMEM((SEQP, 8, 128), f32),
                pltpu.SemaphoreType.DMA((2 * n,)),
            ],
        ),
        out_shape=jax.ShapeDtypeStruct((n * BLK, 16, 128), bf16),
        compiler_params=pltpu.CompilerParams(vmem_limit_bytes=32 * 1024 * 1024),
        cost_estimate=pl.CostEstimate(flops=n * 3_000_000_000, bytes_accessed=n * 3_000_000, transcendentals=n * 60_000),
    )(picks, *x_blocks, *c_blocks, a_up, b_down, w_router, a_router, b_router)


def moe_kernel(places, list_ref, expert_ref, picks_ref, *refs):
    n = len(places)
    tables = refs[:n]
    (
        w_up_hbm, w_down_hbm, b_up, a_down,
        ep_near, ep_far, tg_near, tg_far, gbu_out, gad_out,
        table, acc_e, acc_t, in_x, in_c, out_e, out_t, xb, cb, w_up, w_down, stage_ep, stage_tg,
        in_sem, up_sem, down_sem, ep_sem, tg_sem,
    ) = refs[n:]
    acc_e_flat = acc_e.reshape(TOK * 8, 128)
    acc_t_flat = acc_t.reshape(TOK * 8, 128)
    in_x_flat = in_x.reshape(TILE * 8, 128)
    in_c_flat = in_c.reshape(TILE * 8, 128)
    out_e_flat = out_e.reshape(TILE * 8, 128)
    out_t_flat = out_t.reshape(TILE * 8, 128)
    lane = lane_iota((1, 128))
    n_tiles = expert_ref[max_tiles()]

    copies = []
    for piece, spots in zip(tables, places):
        for b, spot in enumerate(spots):
            copies.append(
                pltpu.make_async_copy(
                    piece.at[pl.ds(b * BLK, BLK)], table.at[pl.ds(spot * BLK, BLK)], in_sem.at[len(copies)]
                )
            )
    for copy in copies:
        copy.start()

    def weights(expert):
        slot = expert % 2
        return (
            pltpu.make_async_copy(w_up_hbm.at[expert], w_up.at[slot], up_sem.at[slot]),
            pltpu.make_async_copy(w_down_hbm.at[expert], w_down.at[slot], down_sem.at[slot]),
        )

    for copy in weights(0):
        copy.start()
    out_e[...] = jnp.zeros_like(out_e)
    out_t[...] = jnp.zeros_like(out_t)
    gbu_out[...] = jnp.zeros_like(gbu_out)
    gad_out[...] = jnp.zeros_like(gad_out)

    def clear(i, carry):
        acc_e[pl.ds(i * 64, 64)] = jnp.zeros((64, 8, 128), f32)
        acc_t[pl.ds(i * 64, 64)] = jnp.zeros((64, 8, 128), f32)
        return carry

    lax.fori_loop(0, TOK // 64, clear, 0)
    for copy in copies:
        copy.wait()

    def fetch(t):
        for i in range(TILE):
            both = table[list_ref[t * TILE + i]].astype(f32)
            in_x[i] = both[:8]
            in_c[i] = both[8:]

    def give(t):
        for b in range(TILE // 8):
            tokens = [list_ref[t * TILE + 8 * b + k] for k in range(8)]
            sums_e = [acc_e[tokens[k]] + out_e[8 * b + k] for k in range(8)]
            sums_t = [acc_t[tokens[k]] + out_t[8 * b + k] for k in range(8)]
            for k in range(8):
                acc_e[tokens[k]] = sums_e[k]
                acc_t[tokens[k]] = sums_t[k]

    fetch(0)

    def tile(t, carry):
        expert = expert_ref[t]
        slot = expert % 2

        @pl.when((t == 0) | (expert_ref[jnp.maximum(t - 1, 0)] != expert))
        def arrive():
            for copy in weights(expert):
                copy.wait()

            @pl.when(expert + 1 < EXPERTS)
            def ahead():
                for copy in weights(expert + 1):
                    copy.start()

        for j in range(7):
            xb[:, 128 * j : 128 * j + 128] = in_x_flat[pl.ds(j, TILE, 8), :].astype(bf16)
            cb[:, 128 * j : 128 * j + 128] = in_c_flat[pl.ds(j, TILE, 8), :].astype(bf16)
        spread = in_x_flat[pl.ds(7, TILE, 8), :]
        mine = (lane == expert) | (lane == expert + EXPERTS)
        gate = jnp.sum(jnp.where(mine, spread, 0.0), axis=1, keepdims=True)
        fetch(t + 1)
        give(jnp.maximum(t - 1, 0))
        hidden = dot(xb[:, :D], w_up[slot]) + dot(xb[:, D:], b_up[...])
        back = dot_nt(cb[:, :D], w_down[slot]) + dot_nt(cb[:, D:], a_down[...])
        cdf = 0.5 + 0.5 * lax.erf(hidden * 0.7071067811865476)
        slope = cdf + hidden * jnp.exp(hidden * hidden * -0.5) * 0.3989422804014327
        act = (hidden * cdf).astype(bf16)
        act_f = act.astype(f32)
        gate_grad = jnp.sum(act_f * back, axis=1, keepdims=True)
        grad_hidden = (gate * back * slope).astype(bf16)
        act_gate = (gate * act_f).astype(bf16)
        out_main = dot(act_gate, w_down[slot])
        out_low = dot(act_gate, a_down[...])
        in_main = dot_nt(grad_hidden, w_up[slot])
        in_low = dot_nt(grad_hidden, b_up[...])
        gbu_out[...] += dot_tn(grad_hidden, xb[:, D:])
        gad_out[...] += dot_tn(act_gate, cb[:, D:])
        for j in range(6):
            out_e_flat[pl.ds(j, TILE, 8), :] = out_main[:, 128 * j : 128 * j + 128]
            out_t_flat[pl.ds(j, TILE, 8), :] = in_main[:, 128 * j : 128 * j + 128]
        out_e_flat[pl.ds(6, TILE, 8), :] = out_low
        out_t_flat[pl.ds(6, TILE, 8), :] = in_low
        out_t_flat[pl.ds(7, TILE, 8), :] = jnp.where(lane == expert, gate_grad, 0.0)
        return carry

    lax.fori_loop(0, n_tiles, tile, 0)
    give(n_tiles - 1)

    half_images = IMG_GRP // 2
    for side, (ep_out, tg_out) in enumerate(((ep_near, tg_near), (ep_far, tg_far))):

        def image(i, carry):
            slot = i % 2
            base = pl.multiple_of((i + side * half_images) * SEQP, 16) * 8
            mask = (lane // RANK) == picks_ref[i + side * half_images]
            rows = pl.ds(pl.multiple_of(i * SEQP, 16), SEQP)
            put_tg = pltpu.make_async_copy(stage_tg.at[slot], tg_out.at[rows], tg_sem.at[slot])
            put_ep = pltpu.make_async_copy(stage_ep.at[slot], ep_out.at[rows], ep_sem.at[slot])

            @pl.when(i >= 2)
            def drain():
                put_tg.wait()
                put_ep.wait()

            def chunk(j):
                flat = acc_e_flat if j < 8 else acc_t_flat
                return flat[pl.ds(base + j % 8, SEQP, 8), :]

            for j in range(6):
                at = slice(128 * j, 128 * j + 128)
                stage_tg[slot, :, at] = chunk(8 + j).astype(bf16)
                stage_ep[slot, :, at] = chunk(j).astype(bf16)
            low_in = repeat_lanes(jnp.where(mask, chunk(14), 0.0))
            low_out = repeat_lanes(jnp.where(mask, chunk(6), 0.0))
            last = jnp.where(lane < 48, low_in, jnp.where(lane < 64, low_out, 0.0))
            stage_tg[slot, :, D:] = jnp.where(lane < 32, chunk(15), last).astype(bf16)
            put_tg.start()
            put_ep.start()
            return carry

        lax.fori_loop(0, half_images, image, 0)
        for i in range(half_images - 2, half_images):
            rows = pl.ds(i * SEQP, SEQP)
            pltpu.make_async_copy(stage_tg.at[i % 2], tg_out.at[rows], tg_sem.at[i % 2]).wait()
            pltpu.make_async_copy(stage_ep.at[i % 2], ep_out.at[rows], ep_sem.at[i % 2]).wait()


def moe_call(token_list, tile_experts, picks, tables, places, w_up, w_down, b_up, a_down):
    half = w_up.shape[2]
    n = len(tables)
    n_copies = sum(len(spots) for spots in places)
    anywhere = pl.BlockSpec(memory_space=pl.ANY)
    inside = pl.BlockSpec(memory_space=pltpu.VMEM)
    return pl.pallas_call(
        lambda *refs: moe_kernel(places, *refs),
        grid_spec=pltpu.PrefetchScalarGridSpec(
            num_scalar_prefetch=3,
            grid=(1,),
            in_specs=[anywhere] * (n + 2) + [inside, inside],
            out_specs=[anywhere, anywhere, anywhere, anywhere, inside, inside],
            scratch_shapes=[
                pltpu.VMEM((TOK, 16, 128), bf16),
                pltpu.VMEM((TOK, 8, 128), f32),
                pltpu.VMEM((TOK, 8, 128), f32),
                pltpu.VMEM((TILE, 8, 128), f32),
                pltpu.VMEM((TILE, 8, 128), f32),
                pltpu.VMEM((TILE, 8, 128), f32),
                pltpu.VMEM((TILE, 8, 128), f32),
                pltpu.VMEM((TILE, D + 128), bf16),
                pltpu.VMEM((TILE, D + 128), bf16),
                pltpu.VMEM((2, D, half), bf16),
                pltpu.VMEM((2, half, D), bf16),
                pltpu.VMEM((2, SEQP, D), bf16),
                pltpu.VMEM((2, SEQP, D + 128), bf16),
                pltpu.SemaphoreType.DMA((n_copies,)),
                pltpu.SemaphoreType.DMA((2,)),
                pltpu.SemaphoreType.DMA((2,)),
                pltpu.SemaphoreType.DMA((2,)),
                pltpu.SemaphoreType.DMA((2,)),
            ],
        ),
        out_shape=[
            jax.ShapeDtypeStruct((TOK // 2, D), bf16),
            jax.ShapeDtypeStruct((TOK // 2, D), bf16),
            jax.ShapeDtypeStruct((TOK // 2, D + 128), bf16),
            jax.ShapeDtypeStruct((TOK // 2, D + 128), bf16),
            jax.ShapeDtypeStruct((half, ADAPT), f32),
            jax.ShapeDtypeStruct((half, ADAPT), f32),
        ],
        compiler_params=pltpu.CompilerParams(vmem_limit_bytes=58 * 1024 * 1024),
        cost_estimate=pl.CostEstimate(flops=20_000_000_000, bytes_accessed=60_000_000, transcendentals=10_000_000),
    )(token_list, tile_experts, picks, *tables, w_up, w_down, b_up, a_down)


def routing(routes, me):
    token = jnp.arange(IMG_GRP * SEQ, dtype=jnp.int32)
    image = token // SEQ
    spot = ((image // 2) ^ me) * BLK + (image % 2) * SEQP + token % SEQ
    keys = (routes * 4096 + spot[:, None]).reshape(-1)
    experts = jnp.arange(EXPERTS, dtype=jnp.int32)
    count = jnp.sum((routes.reshape(-1)[:, None] == experts[None, :]).astype(jnp.int32), axis=0)
    tiles = (jnp.maximum(count, 1) + TILE - 1) // TILE
    extra = tiles * TILE - count
    filler = jnp.where(
        jnp.arange(TILE, dtype=jnp.int32)[None, :] < extra[:, None], (experts * 4096)[:, None] + DUMMY, EXPERTS * 4096 + DUMMY
    ).reshape(-1)
    ordered = lax.sort(jnp.concatenate([keys, filler])) & 4095
    ordered = jnp.concatenate([ordered, jnp.full((TILE,), DUMMY, jnp.int32)])
    ends = jnp.sum(jnp.where(experts[None, :] <= experts[:, None], tiles[None, :], 0), axis=1)
    steps = jnp.arange(max_tiles(), dtype=jnp.int32)
    owner = jnp.minimum(jnp.sum((ends[None, :] <= steps[:, None]).astype(jnp.int32), axis=1), EXPERTS - 1)
    return ordered, jnp.concatenate([owner, jnp.sum(tiles)[None]])


HEADS = 12
HEAD_DIM = 64


def pick_mask(pick):
    return (lane_iota((1, ADAPT)) // RANK) == pick


def norm_stats(values):
    centre = jnp.sum(values, axis=1, keepdims=True) * (1.0 / D)
    shifted = values - centre
    spread = jnp.sum(shifted * shifted, axis=1, keepdims=True) * (1.0 / D)
    inverse = lax.rsqrt(spread + 1e-06)
    return shifted * inverse, inverse


def norm_back(grad, gain, unit, inverse):
    scaled = grad * gain
    total = jnp.sum(scaled, axis=1, keepdims=True) * (1.0 / D)
    along = jnp.sum(scaled * unit, axis=1, keepdims=True) * (1.0 / D)
    return inverse * (scaled - total - unit * along)


def qkv_copies(place_ref, blocks, own_b, scratch, sem):
    w_qkv, a_qkv, b_qkv = scratch
    row, col = place_ref[0], place_ref[1]
    copies = []

    def copy(source, target):
        copies.append(pltpu.make_async_copy(source, target, sem.at[len(copies)]))

    for t in range(2):
        half_at = pl.multiple_of((row ^ t) * 384, 128)
        for s in range(4):
            block = blocks[4 * t + s]
            at = pl.multiple_of((col ^ s) * 192, 64)
            low_at = pl.multiple_of((col ^ s) * 192 + (row ^ t) * 96, 32)
            for p in range(3):
                copy(block.at[pl.ds(192 * p, 192)], w_qkv.at[p, pl.ds(at, 192), pl.ds(half_at, 384)])
                copy(block.at[pl.ds(576, 96), pl.ds(128 * p, 128)], a_qkv.at[p, pl.ds(low_at, 96), :])
        for p in range(3):
            source = own_b.at[p] if t == 0 else blocks[4].at[pl.ds(W_ROWS + 128 * p, 128)]
            copy(source, b_qkv.at[p, :, pl.ds(half_at, 384)])
    return copies


def out_copies(place_ref, far_block, own_a, out_w, scratch, sem):
    w_out, a_out = scratch
    row = place_ref[0]
    copies = []

    def copy(source, target):
        copies.append(pltpu.make_async_copy(source, target, sem.at[len(copies)]))

    for t in range(2):
        half_at = pl.multiple_of((row ^ t) * 384, 128)
        copy(out_w[t].at[pl.ds(0, 384)], w_out.at[pl.ds(half_at, 384), :])
        for j in range(3):
            if t == 0:
                source = own_a.at[pl.ds(128 * j, 128)]
            else:
                source = far_block.at[pl.ds(W_ROWS + 384, 128), pl.ds(128 * j, 128)]
            copy(source, a_out.at[pl.ds(half_at + 128 * j, 128), :])
    return copies


W_ROWS = 944
QKV_SCRATCH = [
    pltpu.VMEM((3, D, D), bf16),
    pltpu.VMEM((3, D, ADAPT), bf16),
    pltpu.VMEM((3, ADAPT, D), bf16),
    pltpu.SemaphoreType.DMA((54,)),
]
OUT_SCRATCH = [
    pltpu.VMEM((D, D), bf16),
    pltpu.VMEM((D, ADAPT), bf16),
    pltpu.SemaphoreType.DMA((8,)),
]


def attend_kernel(picks_ref, place_ref, *refs):
    blocks, refs = refs[:8], refs[8:]
    (
        own_b, own_a, out_near, out_far, x_ref, gain_one, gain_two, b_out,
        two_out, resid_out, normed_out, qkv_out, mixed_out, probs_out, lows_out,
        w_qkv, a_qkv, b_qkv, qkv_sem, w_out, a_out, out_sem,
    ) = refs
    image = pl.program_id(0)

    @pl.when(image == 0)
    def start():
        copies = qkv_copies(place_ref, blocks, own_b, (w_qkv, a_qkv, b_qkv), qkv_sem)
        copies += out_copies(place_ref, blocks[4], own_a, (out_near, out_far), (w_out, a_out), out_sem)
        for copy in copies:
            copy.start()
        for copy in copies:
            copy.wait()

    mask = pick_mask(picks_ref[image])
    x = x_ref[...].astype(f32)
    unit, unused = norm_stats(x)
    normed = (unit * gain_one[...]).astype(bf16)
    normed_out[...] = normed
    for p in range(3):
        low = jnp.where(mask, dot(normed, a_qkv[p]), 0.0).astype(bf16)
        lows_out[:, 128 * p : 128 * p + 128] = low
        qkv_out[p] = (dot(normed, w_qkv[p]) + dot(low, b_qkv[p])).astype(bf16)
    lane = lane_iota((1, 128))
    key_lane = lane_iota((1, SEQP))
    for pair in range(HEADS // 2):
        at = slice(128 * pair, 128 * pair + 128)
        q = qkv_out[0, :, at]
        k = qkv_out[1, :, at]
        v = qkv_out[2, :, at]
        parts = []
        for side in range(2):
            own = (lane // HEAD_DIM) == side
            scores = dot_nt(jnp.where(own, q, jnp.zeros_like(q)), k) * (HEAD_DIM**-0.5)
            scores = jnp.where(key_lane < SEQ, scores, -1e30)
            power = jnp.exp(scores - jnp.max(scores, axis=1, keepdims=True))
            probs = (power / jnp.sum(power, axis=1, keepdims=True)).astype(bf16)
            probs_out[0, 2 * pair + side] = probs
            parts.append(dot(probs, v))
        mixed_out[:, at] = jnp.where(lane < HEAD_DIM, parts[0], parts[1]).astype(bf16)
    mixed = mixed_out[...]
    low = jnp.where(mask, dot(mixed, a_out[...]), 0.0).astype(bf16)
    lows_out[:, 384:512] = low
    resid = x + dot(mixed, w_out[...]) + dot(low, b_out[...])
    resid_out[...] = resid
    unit, unused = norm_stats(resid)
    real = lax.broadcasted_iota(jnp.int32, (SEQP, 1), 0) < SEQ
    two_out[...] = jnp.where(real, unit * gain_two[...], 0.0).astype(bf16)


def image_rows(lanes):
    return pl.BlockSpec((SEQP, lanes), lambda i, *_: (i, 0))


def kept(*shape):
    return pl.BlockSpec(shape, lambda i, *_: (0,) * len(shape))


QKV_SPEC = pl.BlockSpec((3, SEQP, D), lambda i, *_: (0, i, 0))
PROBS_SPEC = pl.BlockSpec((1, HEADS, SEQP, SEQP), lambda i, *_: (i, 0, 0, 0))
ANYWHERE = pl.BlockSpec(memory_space=pl.ANY)


def attend_call(picks, place, blocks, own_b, own_a, out_w, x, gain_one, gain_two, b_out):
    rows = x.shape[0]
    return pl.pallas_call(
        attend_kernel,
        grid_spec=pltpu.PrefetchScalarGridSpec(
            num_scalar_prefetch=2,
            grid=(2,),
            in_specs=[ANYWHERE] * (len(blocks) + 4)
            + [image_rows(D), kept(1, D), kept(1, D), kept(ADAPT, D)],
            out_specs=[
                image_rows(D), image_rows(D), image_rows(D), QKV_SPEC,
                image_rows(D), PROBS_SPEC, image_rows(512),
            ],
            scratch_shapes=QKV_SCRATCH + OUT_SCRATCH,
        ),
        out_shape=[
            jax.ShapeDtypeStruct((rows, D), bf16),
            jax.ShapeDtypeStruct((rows, D), f32),
            jax.ShapeDtypeStruct((rows, D), bf16),
            jax.ShapeDtypeStruct((3, rows, D), bf16),
            jax.ShapeDtypeStruct((rows, D), bf16),
            jax.ShapeDtypeStruct((2, HEADS, SEQP, SEQP), bf16),
            jax.ShapeDtypeStruct((rows, 512), bf16),
        ],
        compiler_params=pltpu.CompilerParams(vmem_limit_bytes=48 * 1024 * 1024),
        cost_estimate=pl.CostEstimate(flops=4_000_000_000, bytes_accessed=15_000_000, transcendentals=2_000_000),
    )(picks, place, *blocks, own_b, own_a, *out_w, x, gain_one, gain_two, b_out)


def out_back_kernel(picks_ref, place_ref, *refs):
    (
        far_block, own_a, out_near, out_far, gain_two, b_out, two_ref, resid_ref, mixed_ref, lows_ref,
        cot_ref, grad_a, grad_b, w_router, a_router, b_router, a_up, b_down,
        resid_grad_out, mixed_grad_out, base_out, both_out, a_part_out, b_part_out,
        w_out, a_out, sem, both, a_part, b_part,
    ) = refs
    image = pl.program_id(0)

    @pl.when(image == 0)
    def start():
        copies = out_copies(place_ref, far_block, own_a, (out_near, out_far), (w_out, a_out), sem)
        for copy in copies:
            copy.start()
        for part in (both, a_part, b_part):
            part[...] = jnp.zeros_like(part)
        for copy in copies:
            copy.wait()

    mask = pick_mask(picks_ref[image])
    lane = lane_iota((1, 128))

    def add_part(row, value):
        at = slice(row, row + value.shape[0])
        both[at, :] += value

    two = two_ref[...]
    received = grad_a[...].astype(f32) + grad_b[...].astype(f32)
    low_r = jnp.where(mask, dot(two, a_router[...]), 0.0).astype(bf16)
    logits = dot(two, w_router[...]) + dot(low_r, b_router[...])
    logits = jnp.where(lane < EXPERTS, logits, -1e30)
    power = jnp.exp(logits - jnp.max(logits, axis=1, keepdims=True))
    probs = power / jnp.sum(power, axis=1, keepdims=True)
    last = received[:, D:]
    grad_probs = jnp.where(lane < EXPERTS, last, 0.0)
    low_in = jnp.where(mask, repeat_lanes(jnp.where((lane >= 32) & (lane < 48), last, 0.0)), 0.0).astype(bf16)
    low_out = jnp.where(mask, repeat_lanes(jnp.where((lane >= 48) & (lane < 64), last, 0.0)), 0.0).astype(bf16)
    cot = cot_ref[...]
    resid = resid_ref[...]
    base_out[...] = resid + dot(low_out, b_down[...])
    add_part(768, dot_tn(two, low_in))
    add_part(1536, dot_tn(cot, low_out))
    grad_logits = probs * (grad_probs - jnp.sum(probs * grad_probs, axis=1, keepdims=True))
    grad_logits = grad_logits.astype(bf16)
    grad_low = jnp.where(mask, dot_nt(grad_logits, b_router[...]), 0.0).astype(bf16)
    grad_two = received[:, :D] + dot_nt(low_in, a_up[...])
    grad_two = grad_two + dot_nt(grad_logits, w_router[...]) + dot_nt(grad_low, a_router[...])
    add_part(0, dot_tn(two, grad_low))
    add_part(2304, dot_tn(grad_logits, low_r))
    unit, inverse = norm_stats(resid)
    grad_resid = cot.astype(f32) + norm_back(grad_two, gain_two[...], unit, inverse)
    resid_grad_out[...] = grad_resid
    grad_attn = grad_resid.astype(bf16)
    grad_low = jnp.where(mask, dot_nt(grad_attn, b_out[...]), 0.0).astype(bf16)
    mixed_grad_out[...] = (dot_nt(grad_attn, w_out[...]) + dot_nt(grad_low, a_out[...])).astype(bf16)
    a_part[...] += dot_tn(mixed_ref[...], grad_low)
    b_part[...] += dot_tn(grad_attn, lows_ref[:, 384:512])

    @pl.when(image == 1)
    def finish():
        both_out[...] = both[...].astype(bf16)
        a_part_out[...] = a_part[...].astype(bf16)
        b_part_out[...] = b_part[...].astype(bf16)


BOTH_ROWS = 2560


def out_back_call(picks, place, far_block, own_a, out_w, gain_two, b_out, two, resid, mixed, lows, cot, grad_a, grad_b,
                  w_router, a_router, b_router, a_up, b_down):
    rows = two.shape[0]
    return pl.pallas_call(
        out_back_kernel,
        grid_spec=pltpu.PrefetchScalarGridSpec(
            num_scalar_prefetch=2,
            grid=(2,),
            in_specs=[ANYWHERE] * 4
            + [kept(1, D), kept(ADAPT, D), image_rows(D), image_rows(D), image_rows(D), image_rows(512)]
            + [image_rows(D), image_rows(D + 128), image_rows(D + 128)]
            + [kept(D, 128), kept(D, ADAPT), kept(ADAPT, 128), kept(D, ADAPT), kept(ADAPT, D)],
            out_specs=[image_rows(D), image_rows(D), image_rows(D), kept(BOTH_ROWS, 128), kept(D, 128), kept(D, 128)],
            scratch_shapes=OUT_SCRATCH
            + [pltpu.VMEM((BOTH_ROWS, 128), f32), pltpu.VMEM((D, 128), f32), pltpu.VMEM((D, 128), f32)],
        ),
        out_shape=[
            jax.ShapeDtypeStruct((rows, D), f32),
            jax.ShapeDtypeStruct((rows, D), bf16),
            jax.ShapeDtypeStruct((rows, D), f32),
            jax.ShapeDtypeStruct((BOTH_ROWS, 128), bf16),
            jax.ShapeDtypeStruct((D, 128), bf16),
            jax.ShapeDtypeStruct((D, 128), bf16),
        ],
        compiler_params=pltpu.CompilerParams(vmem_limit_bytes=48 * 1024 * 1024),
        cost_estimate=pl.CostEstimate(flops=6_000_000_000, bytes_accessed=15_000_000, transcendentals=100_000),
    )(picks, place, far_block, own_a, *out_w, gain_two, b_out, two, resid, mixed, lows, cot, grad_a, grad_b,
      w_router, a_router, b_router, a_up, b_down)


def qkv_back_kernel(picks_ref, place_ref, *refs):
    blocks, refs = refs[:8], refs[8:]
    (
        own_b, x_ref, gain_one, normed_ref, qkv_ref, probs_ref, lows_ref, resid_grad, grad_mixed,
        tokens_out, a_part_out, b_part_out,
        w_qkv, a_qkv, b_qkv, sem, a_part, b_part, grads,
    ) = refs
    image = pl.program_id(0)
    copies = qkv_copies(place_ref, blocks, own_b, (w_qkv, a_qkv, b_qkv), sem)

    @pl.when(image == 0)
    def start():
        for copy in copies:
            copy.start()
        a_part[...] = jnp.zeros_like(a_part)
        b_part[...] = jnp.zeros_like(b_part)

    mask = pick_mask(picks_ref[image])
    lane = lane_iota((1, 128))
    for pair in range(HEADS // 2):
        at = slice(128 * pair, 128 * pair + 128)
        q = qkv_ref[0, :, at]
        k = qkv_ref[1, :, at]
        v = qkv_ref[2, :, at]
        gm = grad_mixed[:, at]
        found = []
        for side in range(2):
            own = (lane // HEAD_DIM) == side
            weights = probs_ref[0, 2 * pair + side]
            weights_f = weights.astype(f32)
            grad_w = dot_nt(jnp.where(own, gm, jnp.zeros_like(gm)), v)
            inner = jnp.sum(weights_f * grad_w, axis=1, keepdims=True)
            grad_s = (weights_f * (grad_w - inner)).astype(bf16)
            found.append(
                (
                    dot(grad_s, k) * (HEAD_DIM**-0.5),
                    dot_tn(grad_s, q) * (HEAD_DIM**-0.5),
                    dot_tn(weights, gm),
                )
            )
        for p in range(3):
            grads[p, :, at] = jnp.where(lane < HEAD_DIM, found[0][p], found[1][p]).astype(bf16)

    @pl.when(image == 0)
    def arrived():
        for copy in copies:
            copy.wait()

    normed = normed_ref[...]
    grad_normed = jnp.zeros((SEQP, D), f32)
    for p in range(3):
        piece = grads[p]
        grad_low = jnp.where(mask, dot_nt(piece, b_qkv[p]), 0.0).astype(bf16)
        grad_normed = grad_normed + dot_nt(piece, w_qkv[p]) + dot_nt(grad_low, a_qkv[p])
        a_part[D * p : D * p + D, :] += dot_tn(normed, grad_low)
        b_part[D * p : D * p + D, :] += dot_tn(piece, lows_ref[:, 128 * p : 128 * p + 128])
    unit, inverse = norm_stats(x_ref[...].astype(f32))
    tokens_out[...] = (resid_grad[...] + norm_back(grad_normed, gain_one[...], unit, inverse)).astype(bf16)

    @pl.when(image == 1)
    def finish():
        a_part_out[...] = a_part[...].astype(bf16)
        b_part_out[...] = b_part[...].astype(bf16)


def qkv_back_call(picks, place, blocks, own_b, x, gain_one, normed, qkv, probs, lows, resid_grad, grad_mixed):
    rows = x.shape[0]
    return pl.pallas_call(
        qkv_back_kernel,
        grid_spec=pltpu.PrefetchScalarGridSpec(
            num_scalar_prefetch=2,
            grid=(2,),
            in_specs=[ANYWHERE] * (len(blocks) + 1)
            + [image_rows(D), kept(1, D), image_rows(D), QKV_SPEC, PROBS_SPEC, image_rows(512)]
            + [image_rows(D), image_rows(D)],
            out_specs=[image_rows(D), kept(3 * D, 128), kept(3 * D, 128)],
            scratch_shapes=QKV_SCRATCH
            + [
                pltpu.VMEM((3 * D, 128), f32),
                pltpu.VMEM((3 * D, 128), f32),
                pltpu.VMEM((3, SEQP, D), bf16),
            ],
        ),
        out_shape=[
            jax.ShapeDtypeStruct((rows, D), bf16),
            jax.ShapeDtypeStruct((3 * D, 128), bf16),
            jax.ShapeDtypeStruct((3 * D, 128), bf16),
        ],
        compiler_params=pltpu.CompilerParams(vmem_limit_bytes=48 * 1024 * 1024),
        cost_estimate=pl.CostEstimate(flops=9_000_000_000, bytes_accessed=15_000_000, transcendentals=1000),
    )(picks, place, *blocks, own_b, x, gain_one, normed, qkv, probs, lows, resid_grad, grad_mixed)


TABLES = ((0, 4), (1, 2, 5, 6), (3, 7))


def across_row(value):
    return lax.ppermute(value, "row", [(0, 1), (1, 0)])


def across_col(value, step):
    return lax.ppermute(value, "col", [(i, i ^ step) for i in range(4)])


def by_place(blocks, col):
    found = []
    for place in range(4):
        value = blocks[place]
        for other in range(1, 4):
            value = jnp.where(col == other, blocks[place ^ other], value)
        found.append(value)
    return found


def gather_col(value, middle):
    from_x = across_col(value, 1)
    from_y = across_col(value, 2)
    head = across_col(from_y[:middle], 1)
    tail = across_col(from_x[middle:], 2)
    return [value, from_x, from_y, jnp.concatenate([head, tail])]


def gather_group(value):
    own = gather_col(value, SEQP)
    return own + [across_row(block) for block in own]


def added(*values):
    total = values[0].astype(f32)
    for value in values[1:]:
        total = total + value.astype(f32)
    return total


def row_sum(near, far):
    both = added(near, across_row(far)).astype(bf16)
    return both.reshape(4, 2, SEQP, both.shape[1])


def first_exchange(both):
    from_x = across_col(jnp.stack([both[1, 0], both[3, 0]]), 1)
    from_y = across_col(jnp.stack([both[2, 1], both[3, 1]]), 2)
    return from_x, from_y


def last_exchange(both, from_x, from_y):
    last_y = across_col(added(both[2, 0], from_x[1]).astype(bf16), 2)
    last_x = across_col(added(both[1, 1], from_y[1]).astype(bf16), 1)
    mine = jnp.concatenate([added(both[0, 0], from_x[0]), added(both[0, 1], from_y[0])])
    return mine.astype(bf16), jnp.concatenate([last_y, last_x])


def at_place(value, axis, place):
    return lax.dynamic_index_in_dim(value, place, axis, keepdims=False)


def reduce_dp(value):
    n_dp = lax.axis_size("dp")
    if n_dp != 4:
        return lax.psum(value, "dp")
    place = lax.axis_index("dp")

    def across(part, step):
        return lax.ppermute(part, "dp", [(i, i ^ step) for i in range(4)])

    view = value.reshape(4, -1, 128)
    found = [at_place(view, 0, place)]
    for s in range(1, 4):
        found.append(across(at_place(view, 0, place ^ s), s))
    total = added(*found).astype(bf16)
    blocks = [total] + [across(total, s) for s in range(1, 4)]
    return jnp.concatenate(by_place(blocks, place))


def reduce_parts(col_parts, row_parts, both_parts, dp_parts, row, col):
    col_parts = col_parts.reshape(4, 4, 2, 96, 128)
    row_parts = row_parts.reshape(4, 2, 4, 96, 128)
    both_parts = both_parts.reshape(2, 4, BOTH_ROWS // 8, 128)

    def share(place):
        one = at_place(col_parts, 2, place).swapaxes(0, 1).reshape(4, 384, 128)
        two = at_place(row_parts, 1, place).swapaxes(0, 1).reshape(4, 384, 128)
        return jnp.concatenate([one, two, at_place(both_parts, 0, place)], axis=1)

    both = added(share(row), across_row(share(1 - row))).astype(bf16)
    found = [at_place(both, 0, col)]
    for s in range(1, 4):
        found.append(across_col(at_place(both, 0, col ^ s), s))
    mine = added(*found).astype(bf16)
    rows = mine.shape[0]
    mine = reduce_dp(jnp.concatenate([mine, dp_parts]))
    dp_sums = mine[rows:]
    mine = mine[:rows]
    spread = mine[384:]
    spread = by_place([spread] + [across_col(spread, s) for s in range(1, 4)], col)
    row_sums = jnp.stack([one[:384].reshape(4, 96, 128) for one in spread], axis=1).reshape(4, 384, 128)
    near = jnp.concatenate([mine[:384]] + [one[384:] for one in spread])
    far = across_row(near)
    first = jnp.where(row == 0, near, far)
    second = jnp.where(row == 0, far, near)
    col_sums = jnp.stack([first[:384].reshape(4, 96, 128), second[:384].reshape(4, 96, 128)], axis=1).reshape(4, 192, 128)
    both_sums = jnp.concatenate([first[384:], second[384:]])
    return col_sums, row_sums, both_sums, dp_sums


def token_blocks(value):
    images = value.reshape(4, 2, SEQ, value.shape[1])
    images = jnp.pad(images, ((0, 0), (0, 0), (0, SEQP - SEQ), (0, 0)))
    return jnp.concatenate([images[:, 0], images[:, 1]], axis=2)


def to_tokens(value, col):
    blocks = token_blocks(value)
    width = value.shape[1]
    got = [at_place(blocks, 0, col)]
    for s in range(1, 4):
        got.append(across_col(at_place(blocks, 0, col ^ s), s))
    got = by_place(got, col)
    return jnp.concatenate(
        [jnp.concatenate([one[:, :width] for one in got], axis=1), jnp.concatenate([one[:, width:] for one in got], axis=1)]
    )


def to_features(value, col):
    width = D // 4
    chunks = by_place([value[:, width * p : width * p + width] for p in range(4)], col)
    sent = [jnp.concatenate([chunk[:SEQP], chunk[SEQP:]], axis=1) for chunk in chunks]
    got = [sent[0]] + [across_col(sent[s], s) for s in range(1, 4)]
    rows = []
    for block in by_place(got, col):
        rows += [block[:SEQ, :width], block[:SEQ, width:]]
    return jnp.concatenate(rows, axis=0)


def on_device(
    tokens, cotangent, routes, adapter_pick, gain_attn, gain_moe, w_qkv, w_out, w_router, w_up, w_down,
    a_qkv, b_qkv, a_out, b_out, a_router, b_router, a_up, b_up, a_down, b_down,
):
    row = lax.axis_index("row")
    col = lax.axis_index("col")
    me = row * 4 + col
    place = jnp.stack([row, col]).astype(jnp.int32)

    x = to_tokens(tokens, col)
    width = D // 4
    half = D // 2
    gains = []
    for gain in (gain_attn, gain_moe):
        left = gain
        for unused in range(3):
            lead = lax.reduce_precision(left, 8, 7)
            gains.append(lead.astype(bf16))
            left = left - lead
    small = jnp.concatenate([w_out, b_out, jnp.stack(gains), jnp.zeros((26, width), bf16)], axis=0)
    low = at_place(a_qkv.reshape(3, 2, 96, ADAPT), 1, row)
    packed = jnp.concatenate(
        [w_qkv.reshape(576, half), jnp.concatenate([low[0], low[1], low[2]], axis=1),
         jnp.concatenate([small[:272], small[272:]], axis=1)]
    )
    for_row = jnp.concatenate(
        [packed, b_qkv.reshape(half, half), jnp.concatenate([a_out[:128], a_out[128:256], a_out[256:]], axis=1)]
    )
    near = gather_col(packed, 480)
    far = [across_row(for_row)] + [across_row(block) for block in near[1:]]
    blocks = near + far

    def assembled(group):
        parts = by_place([block[672:944] for block in group], col)
        return jnp.concatenate(
            [jnp.concatenate([part[:, :width] for part in parts], axis=1),
             jnp.concatenate([part[:, width:] for part in parts], axis=1)], axis=0
        )

    out_w = [assembled(near), assembled(far)]
    full_b_out = out_w[0][384:512]
    gain_rows = out_w[0][512:518].astype(f32)
    gain_one = jnp.sum(gain_rows[:3], axis=0, keepdims=True)
    gain_two = jnp.sum(gain_rows[3:], axis=0, keepdims=True)

    picks_group = lax.dynamic_slice_in_dim(adapter_pick, lax.axis_index("dp") * IMG_GRP, IMG_GRP)
    order = jnp.arange(IMG_GRP, dtype=jnp.int32)
    picks = jnp.take(picks_group, ((order // 2) ^ me) * 2 + order % 2)
    token_list, tile_experts = routing(routes, me)
    wide_router = jnp.concatenate([w_router, w_router, jnp.zeros((D, 64), bf16)], axis=1)
    wide_b_router = jnp.concatenate([b_router, b_router, jnp.zeros((ADAPT, 64), bf16)], axis=1)
    slim_router = jnp.concatenate([w_router, jnp.zeros((D, 96), bf16)], axis=1)
    slim_b_router = jnp.concatenate([b_router, jnp.zeros((ADAPT, 96), bf16)], axis=1)

    two, resid, normed, qkv, mixed, probs, lows = attend_call(
        picks, place, blocks, b_qkv, a_out, out_w, x, gain_one, gain_two, full_b_out
    )
    cotangent, unused, unused = lax.optimization_barrier((cotangent, near[1], near[2]))
    cot = to_tokens(cotangent, col)
    cot_blocks = gather_group(cot)
    two_blocks = gather_group(two)
    tables = []
    for spots in TABLES:
        tables.append(
            table_call(
                jnp.stack([picks[2 * spot + side] for spot in spots for side in range(2)]),
                [two_blocks[spot] for spot in spots], [cot_blocks[spot] for spot in spots],
                a_up, b_down, wide_router, a_router, wide_b_router,
            )
        )
    sum_near, sum_far, grad_near, grad_far, part_b_up, part_a_down = moe_call(
        token_list, tile_experts, picks, tables, TABLES, w_up, w_down, b_up, a_down
    )
    grads = row_sum(grad_near, grad_far)
    grads, sum_near, sum_far = lax.optimization_barrier((grads, sum_near, sum_far))
    grads_x, grads_y = first_exchange(grads)
    sums = row_sum(sum_near, sum_far)
    grads_x, grads_y, sums = lax.optimization_barrier((grads_x, grads_y, sums))
    grad_a, grad_b = last_exchange(grads, grads_x, grads_y)
    sums_x, sums_y = first_exchange(sums)
    resid_grad, mixed_grad, base, both_parts, part_a_out, part_b_out = out_back_call(
        picks, place, blocks[4], a_out, out_w, gain_two, full_b_out, two, resid, mixed, lows, cot, grad_a, grad_b,
        slim_router, a_router, slim_b_router, a_up, b_down,
    )
    resid_grad, mixed_grad, sums_x, sums_y = lax.optimization_barrier((resid_grad, mixed_grad, sums_x, sums_y))
    grad_tokens, part_a_qkv, part_b_qkv = qkv_back_call(
        picks, place, blocks, b_qkv, x, gain_one, normed, qkv, probs, lows, resid_grad, mixed_grad
    )
    sum_a, sum_b = last_exchange(sums, sums_x, sums_y)
    block_out = to_features((base + added(sum_a, sum_b)).astype(bf16), col)
    grad_tokens = to_features(grad_tokens, col).astype(f32)
    col_sums, row_sums, both_sums, dp_sums = reduce_parts(
        jnp.concatenate([part_a_qkv, part_b_out]),
        jnp.concatenate([part_b_qkv, part_a_out]),
        both_parts,
        jnp.concatenate([part_b_up.astype(bf16), part_a_down.astype(bf16)]),
        row,
        col,
    )
    col_sums = col_sums.astype(f32)
    row_sums = row_sums.astype(f32)
    both_sums = both_sums.astype(f32)
    dp_sums = dp_sums.astype(f32)
    return (
        block_out,
        grad_tokens,
        col_sums[:3],
        jnp.swapaxes(row_sums[:3], 1, 2),
        row_sums[3],
        col_sums[3].T,
        both_sums[:768],
        both_sums[2304:2336].T,
        both_sums[768:1536],
        dp_sums[:384].T,
        dp_sums[384:],
        both_sums[1536:2304].T,
    )


def solution(mesh):
    return jax.shard_map(
        on_device,
        mesh=mesh,
        in_specs=(
            P(("dp", "row"), "col"),
            P(("dp", "row"), "col"),
            P("dp", None),
            P(),
            P("col"),
            P("col"),
            P(None, "col", "row"),
            P("row", "col"),
            P(),
            P(None, None, ("row", "col")),
            P(None, ("row", "col"), None),
            P(None, "col", None),
            P(None, None, "row"),
            P("row", None),
            P(None, "col"),
            P(),
            P(),
            P(),
            P(None, ("row", "col")),
            P(("row", "col"), None),
            P(),
        ),
        out_specs=(
            P(("dp", "row"), "col"),
            P(("dp", "row"), "col"),
            P(None, "col", None),
            P(None, None, "row"),
            P("row", None),
            P(None, "col"),
            P(),
            P(),
            P(),
            P(None, ("row", "col")),
            P(("row", "col"), None),
            P(),
        ),
        check_vma=False,
    )
```

```python
import jax
import jax.numpy as jnp
from jax import lax
from jax.experimental import pallas as pl
from jax.experimental.pallas import tpu as pltpu
from jax.sharding import PartitionSpec as P

D = 768
EXPERTS = 32
SEQ = 197
SEQP = 208
RANK = 16
ADAPT = 128
IMG_GRP = 16
TOK = IMG_GRP * SEQP
BLK = 2 * SEQP
DUMMY = SEQ
TILE = 192
f32 = jnp.float32
bf16 = jnp.bfloat16


def max_tiles():
    return (2 * IMG_GRP * SEQ) // TILE + EXPERTS + 1


def dot(left, right):
    return jnp.dot(left, right, preferred_element_type=f32)


def dot_nt(left, right):
    return lax.dot_general(left, right, (((1,), (1,)), ((), ())), preferred_element_type=f32)


def dot_tn(left, right):
    return lax.dot_general(left, right, (((0,), (0,)), ((), ())), preferred_element_type=f32)


def lane_iota(shape):
    return lax.broadcasted_iota(jnp.int32, shape, len(shape) - 1)


def repeat_lanes(value):
    for shift in (16, 32, 64):
        value = value + pltpu.roll(value, shift, 1)
    return value


def table_kernel(n_blocks, picks_ref, *refs):
    x_blocks = refs[:n_blocks]
    c_blocks = refs[n_blocks : 2 * n_blocks]
    a_up, b_down, w_router, a_router, b_router, table_out, xin, cin, rows_x, rows_c, sem = refs[2 * n_blocks :]
    image = pl.program_id(0)
    lane = lane_iota((1, 128))

    @pl.when(image == 0)
    def start():
        copies = []
        for blocks, place in ((x_blocks, xin), (c_blocks, cin)):
            for b, block in enumerate(blocks):
                copies.append(pltpu.make_async_copy(block, place.at[pl.ds(b * BLK, BLK)], sem.at[len(copies)]))
        for copy in copies:
            copy.start()
        for copy in copies:
            copy.wait()

    row = pl.multiple_of(image * SEQP, 16)
    mask = (lane // RANK) == picks_ref[image]
    x = xin[pl.ds(row, SEQP), :]
    c = cin[pl.ds(row, SEQP), :]
    flat_x = rows_x.reshape(SEQP * 8, 128)
    flat_c = rows_c.reshape(SEQP * 8, 128)
    low_x = jnp.where(mask, dot(x, a_up[...]), 0.0)
    low_c = jnp.where(mask, dot_nt(c, b_down[...]), 0.0)
    low_r = jnp.where(mask, dot(x, a_router[...]), 0.0).astype(bf16)
    logits = dot(x, w_router[...]) + dot(low_r, b_router[...])
    logits = jnp.where(lane < 2 * EXPERTS, logits, -1e30)
    power = jnp.exp(logits - jnp.max(logits, axis=1, keepdims=True))
    total = jnp.sum(jnp.where(lane < EXPERTS, power, 0.0), axis=1, keepdims=True)
    probs = power / total
    lead = probs.astype(bf16).astype(f32)
    probs = jnp.where(lane < EXPERTS, lead, probs - lead)
    for j in range(6):
        flat_x[pl.ds(j, SEQP, 8), :] = x[:, 128 * j : 128 * j + 128].astype(f32)
        flat_c[pl.ds(j, SEQP, 8), :] = c[:, 128 * j : 128 * j + 128].astype(f32)
    flat_x[pl.ds(6, SEQP, 8), :] = low_x
    flat_x[pl.ds(7, SEQP, 8), :] = probs
    flat_c[pl.ds(6, SEQP, 8), :] = low_c
    flat_c[pl.ds(7, SEQP, 8), :] = jnp.zeros((SEQP, 128), f32)
    table_out[...] = jnp.concatenate([rows_x[...], rows_c[...]], axis=1).astype(bf16)


def table_call(picks, x_blocks, c_blocks, a_up, b_down, w_router, a_router, b_router):
    n = len(x_blocks)

    def whole(*shape):
        return pl.BlockSpec(shape, lambda e, *_: (0,) * len(shape))

    anywhere = pl.BlockSpec(memory_space=pl.ANY)
    return pl.pallas_call(
        lambda *refs: table_kernel(n, *refs),
        grid_spec=pltpu.PrefetchScalarGridSpec(
            num_scalar_prefetch=1,
            grid=(2 * n,),
            in_specs=[anywhere] * (2 * n)
            + [whole(D, ADAPT), whole(ADAPT, D), whole(D, 128), whole(D, ADAPT), whole(ADAPT, 128)],
            out_specs=pl.BlockSpec((SEQP, 16, 128), lambda i, *_: (i, 0, 0)),
            scratch_shapes=[
                pltpu.VMEM((n * BLK, D), bf16),
                pltpu.VMEM((n * BLK, D), bf16),
                pltpu.VMEM((SEQP, 8, 128), f32),
                pltpu.VMEM((SEQP, 8, 128), f32),
                pltpu.SemaphoreType.DMA((2 * n,)),
            ],
        ),
        out_shape=jax.ShapeDtypeStruct((n * BLK, 16, 128), bf16),
        compiler_params=pltpu.CompilerParams(vmem_limit_bytes=32 * 1024 * 1024),
        cost_estimate=pl.CostEstimate(flops=n * 3_000_000_000, bytes_accessed=n * 3_000_000, transcendentals=n * 60_000),
    )(picks, *x_blocks, *c_blocks, a_up, b_down, w_router, a_router, b_router)


def moe_kernel(places, list_ref, expert_ref, picks_ref, place_ref, *refs):
    n = len(places)
    tables = refs[:n]
    (
        w_up_hbm, w_down_hbm, b_up, a_down,
        ep_near, ep_far, tg_near, tg_far, gbu_out, gad_out,
        table, acc_e, acc_t, in_x, in_c, out_e, out_t, xb, cb, w_up, w_down, stage_ep, stage_tg,
        in_sem, up_sem, down_sem, ep_sem, tg_sem,
    ) = refs[n:]
    acc_e_flat = acc_e.reshape(TOK * 8, 128)
    acc_t_flat = acc_t.reshape(TOK * 8, 128)
    in_x_flat = in_x.reshape(TILE * 8, 128)
    in_c_flat = in_c.reshape(TILE * 8, 128)
    out_e_flat = out_e.reshape(TILE * 8, 128)
    out_t_flat = out_t.reshape(TILE * 8, 128)
    lane = lane_iota((1, 128))
    n_tiles = expert_ref[max_tiles()]

    copies = []
    for piece, spots in zip(tables, places):
        for b, (t, s) in enumerate(spots):
            spot = 4 * t + jnp.where(place_ref[0] == t, swapped(s), s)
            copies.append(
                pltpu.make_async_copy(
                    piece.at[pl.ds(b * BLK, BLK)], table.at[pl.ds(pl.multiple_of(spot * BLK, 32), BLK)], in_sem.at[len(copies)]
                )
            )
    for copy in copies:
        copy.start()

    def weights(expert):
        slot = expert % 2
        return (
            pltpu.make_async_copy(w_up_hbm.at[expert], w_up.at[slot], up_sem.at[slot]),
            pltpu.make_async_copy(w_down_hbm.at[expert], w_down.at[slot], down_sem.at[slot]),
        )

    for copy in weights(0):
        copy.start()
    out_e[...] = jnp.zeros_like(out_e)
    out_t[...] = jnp.zeros_like(out_t)
    gbu_out[...] = jnp.zeros_like(gbu_out)
    gad_out[...] = jnp.zeros_like(gad_out)

    def clear(i, carry):
        acc_e[pl.ds(i * 64, 64)] = jnp.zeros((64, 8, 128), f32)
        acc_t[pl.ds(i * 64, 64)] = jnp.zeros((64, 8, 128), f32)
        return carry

    lax.fori_loop(0, TOK // 64, clear, 0)
    for copy in copies:
        copy.wait()

    def fetch(t):
        for i in range(TILE):
            both = table[list_ref[t * TILE + i]].astype(f32)
            in_x[i] = both[:8]
            in_c[i] = both[8:]

    def give(t):
        for b in range(TILE // 8):
            tokens = [list_ref[t * TILE + 8 * b + k] for k in range(8)]
            sums_e = [acc_e[tokens[k]] + out_e[8 * b + k] for k in range(8)]
            sums_t = [acc_t[tokens[k]] + out_t[8 * b + k] for k in range(8)]
            for k in range(8):
                acc_e[tokens[k]] = sums_e[k]
                acc_t[tokens[k]] = sums_t[k]

    fetch(0)

    def tile(t, carry):
        expert = expert_ref[t]
        slot = expert % 2

        @pl.when((t == 0) | (expert_ref[jnp.maximum(t - 1, 0)] != expert))
        def arrive():
            for copy in weights(expert):
                copy.wait()

            @pl.when(expert + 1 < EXPERTS)
            def ahead():
                for copy in weights(expert + 1):
                    copy.start()

        for j in range(7):
            xb[:, 128 * j : 128 * j + 128] = in_x_flat[pl.ds(j, TILE, 8), :].astype(bf16)
            cb[:, 128 * j : 128 * j + 128] = in_c_flat[pl.ds(j, TILE, 8), :].astype(bf16)
        spread = in_x_flat[pl.ds(7, TILE, 8), :]
        mine = (lane == expert) | (lane == expert + EXPERTS)
        gate = jnp.sum(jnp.where(mine, spread, 0.0), axis=1, keepdims=True)
        fetch(t + 1)
        give(jnp.maximum(t - 1, 0))
        hidden = dot(xb[:, :D], w_up[slot]) + dot(xb[:, D:], b_up[...])
        back = dot_nt(cb[:, :D], w_down[slot]) + dot_nt(cb[:, D:], a_down[...])
        cdf = 0.5 + 0.5 * lax.erf(hidden * 0.7071067811865476)
        slope = cdf + hidden * jnp.exp(hidden * hidden * -0.5) * 0.3989422804014327
        act = (hidden * cdf).astype(bf16)
        act_f = act.astype(f32)
        gate_grad = jnp.sum(act_f * back, axis=1, keepdims=True)
        grad_hidden = (gate * back * slope).astype(bf16)
        act_gate = (gate * act_f).astype(bf16)
        out_main = dot(act_gate, w_down[slot])
        out_low = dot(act_gate, a_down[...])
        in_main = dot_nt(grad_hidden, w_up[slot])
        in_low = dot_nt(grad_hidden, b_up[...])
        gbu_out[...] += dot_tn(grad_hidden, xb[:, D:])
        gad_out[...] += dot_tn(act_gate, cb[:, D:])
        for j in range(6):
            out_e_flat[pl.ds(j, TILE, 8), :] = out_main[:, 128 * j : 128 * j + 128]
            out_t_flat[pl.ds(j, TILE, 8), :] = in_main[:, 128 * j : 128 * j + 128]
        out_e_flat[pl.ds(6, TILE, 8), :] = out_low
        out_t_flat[pl.ds(6, TILE, 8), :] = in_low
        out_t_flat[pl.ds(7, TILE, 8), :] = jnp.where(lane == expert, gate_grad, 0.0)
        return carry

    lax.fori_loop(0, n_tiles, tile, 0)
    give(n_tiles - 1)

    half_images = IMG_GRP // 2
    for side, (ep_out, tg_out) in enumerate(((ep_near, tg_near), (ep_far, tg_far))):

        def image(i, carry):
            slot = i % 2
            base = pl.multiple_of((i + side * half_images) * SEQP, 16) * 8
            mask = (lane // RANK) == picks_ref[i + side * half_images]
            rows = pl.ds(pl.multiple_of(i * SEQP, 16), SEQP)
            put_tg = pltpu.make_async_copy(stage_tg.at[slot], tg_out.at[rows], tg_sem.at[slot])
            put_ep = pltpu.make_async_copy(stage_ep.at[slot], ep_out.at[rows], ep_sem.at[slot])

            @pl.when(i >= 2)
            def drain():
                put_tg.wait()
                put_ep.wait()

            def chunk(j):
                flat = acc_e_flat if j < 8 else acc_t_flat
                return flat[pl.ds(base + j % 8, SEQP, 8), :]

            for j in range(6):
                at = slice(128 * j, 128 * j + 128)
                stage_tg[slot, :, at] = chunk(8 + j).astype(bf16)
                stage_ep[slot, :, at] = chunk(j).astype(bf16)
            low_in = repeat_lanes(jnp.where(mask, chunk(14), 0.0))
            low_out = repeat_lanes(jnp.where(mask, chunk(6), 0.0))
            last = jnp.where(lane < 48, low_in, jnp.where(lane < 64, low_out, 0.0))
            stage_tg[slot, :, D:] = jnp.where(lane < 32, chunk(15), last).astype(bf16)
            put_tg.start()
            put_ep.start()
            return carry

        lax.fori_loop(0, half_images, image, 0)
        for i in range(half_images - 2, half_images):
            rows = pl.ds(i * SEQP, SEQP)
            pltpu.make_async_copy(stage_tg.at[i % 2], tg_out.at[rows], tg_sem.at[i % 2]).wait()
            pltpu.make_async_copy(stage_ep.at[i % 2], ep_out.at[rows], ep_sem.at[i % 2]).wait()


def moe_call(token_list, tile_experts, picks, place, tables, places, w_up, w_down, b_up, a_down):
    half = w_up.shape[2]
    n = len(tables)
    n_copies = sum(len(spots) for spots in places)
    anywhere = pl.BlockSpec(memory_space=pl.ANY)
    inside = pl.BlockSpec(memory_space=pltpu.VMEM)
    return pl.pallas_call(
        lambda *refs: moe_kernel(places, *refs),
        grid_spec=pltpu.PrefetchScalarGridSpec(
            num_scalar_prefetch=4,
            grid=(1,),
            in_specs=[anywhere] * (n + 2) + [inside, inside],
            out_specs=[anywhere, anywhere, anywhere, anywhere, inside, inside],
            scratch_shapes=[
                pltpu.VMEM((TOK, 16, 128), bf16),
                pltpu.VMEM((TOK, 8, 128), f32),
                pltpu.VMEM((TOK, 8, 128), f32),
                pltpu.VMEM((TILE, 8, 128), f32),
                pltpu.VMEM((TILE, 8, 128), f32),
                pltpu.VMEM((TILE, 8, 128), f32),
                pltpu.VMEM((TILE, 8, 128), f32),
                pltpu.VMEM((TILE, D + 128), bf16),
                pltpu.VMEM((TILE, D + 128), bf16),
                pltpu.VMEM((2, D, half), bf16),
                pltpu.VMEM((2, half, D), bf16),
                pltpu.VMEM((2, SEQP, D), bf16),
                pltpu.VMEM((2, SEQP, D + 128), bf16),
                pltpu.SemaphoreType.DMA((n_copies,)),
                pltpu.SemaphoreType.DMA((2,)),
                pltpu.SemaphoreType.DMA((2,)),
                pltpu.SemaphoreType.DMA((2,)),
                pltpu.SemaphoreType.DMA((2,)),
            ],
        ),
        out_shape=[
            jax.ShapeDtypeStruct((TOK // 2, D), bf16),
            jax.ShapeDtypeStruct((TOK // 2, D), bf16),
            jax.ShapeDtypeStruct((TOK // 2, D + 128), bf16),
            jax.ShapeDtypeStruct((TOK // 2, D + 128), bf16),
            jax.ShapeDtypeStruct((half, ADAPT), f32),
            jax.ShapeDtypeStruct((half, ADAPT), f32),
        ],
        compiler_params=pltpu.CompilerParams(vmem_limit_bytes=58 * 1024 * 1024),
        cost_estimate=pl.CostEstimate(flops=20_000_000_000, bytes_accessed=60_000_000, transcendentals=10_000_000),
    )(token_list, tile_experts, picks, place, *tables, w_up, w_down, b_up, a_down)


def swapped(s):
    return ((s & 1) << 1) | (s >> 1)


def block_spot(block, row, col):
    from_row = block // 4
    s = (block % 4) ^ col
    return 4 * (from_row ^ row) + jnp.where(from_row == 0, swapped(s), s)


def routing(routes, row, col):
    token = jnp.arange(25 * 128, dtype=jnp.int32)[None, :]
    image = token // SEQ
    spot = block_spot(image // 2, row, col) * BLK + (image % 2) * SEQP + token % SEQ
    real = token < IMG_GRP * SEQ
    picked = jnp.pad(routes.T, ((0, 0), (0, 25 * 128 - IMG_GRP * SEQ)), constant_values=EXPERTS)
    beyond = EXPERTS * 4096 + DUMMY
    keys = jnp.where(real, picked * 4096 + spot, beyond).reshape(-1)
    experts = jnp.arange(EXPERTS, dtype=jnp.int32)
    count = jnp.sum((picked[None] == experts[:, None, None]).astype(jnp.int32), axis=(1, 2))
    tiles = (jnp.maximum(count, 1) + TILE - 1) // TILE
    extra = tiles * TILE - count
    filler = jnp.where(
        jnp.arange(256, dtype=jnp.int32)[None, :] < extra[:, None], (experts * 4096)[:, None] + DUMMY, beyond
    ).reshape(-1)
    ordered = lax.sort(jnp.concatenate([keys, filler])) & 4095
    ends = jnp.sum(jnp.where(experts[None, :] <= experts[:, None], tiles[None, :], 0), axis=1)
    steps = jnp.arange(max_tiles(), dtype=jnp.int32)
    owner = jnp.minimum(jnp.sum((ends[None, :] <= steps[:, None]).astype(jnp.int32), axis=1), EXPERTS - 1)
    return ordered, jnp.concatenate([owner, jnp.sum(tiles)[None]])


HEADS = 12
HEAD_DIM = 64


def pick_mask(pick):
    return (lane_iota((1, ADAPT)) // RANK) == pick


def norm_stats(values):
    centre = jnp.sum(values, axis=1, keepdims=True) * (1.0 / D)
    shifted = values - centre
    spread = jnp.sum(shifted * shifted, axis=1, keepdims=True) * (1.0 / D)
    inverse = lax.rsqrt(spread + 1e-06)
    return shifted * inverse, inverse


def norm_back(grad, gain, unit, inverse):
    scaled = grad * gain
    total = jnp.sum(scaled, axis=1, keepdims=True) * (1.0 / D)
    along = jnp.sum(scaled * unit, axis=1, keepdims=True) * (1.0 / D)
    return inverse * (scaled - total - unit * along)


def qkv_copies(place_ref, blocks, own_b, scratch, sem):
    w_qkv, a_qkv, b_qkv = scratch
    row, col = place_ref[0], place_ref[1]
    copies = []

    def copy(source, target):
        copies.append(pltpu.make_async_copy(source, target, sem.at[len(copies)]))

    for t in range(2):
        half_at = pl.multiple_of((row ^ t) * 384, 128)
        for s in range(4):
            block = blocks[4 * t + s]
            at = pl.multiple_of((col ^ s) * 192, 64)
            low_at = pl.multiple_of((col ^ s) * 192 + (row ^ t) * 96, 32)
            for p in range(3):
                copy(block.at[pl.ds(192 * p, 192)], w_qkv.at[p, pl.ds(at, 192), pl.ds(half_at, 384)])
                copy(block.at[pl.ds(576, 96), pl.ds(128 * p, 128)], a_qkv.at[p, pl.ds(low_at, 96), :])
        for p in range(3):
            source = own_b.at[p] if t == 0 else blocks[4].at[pl.ds(W_ROWS + 128 * p, 128)]
            copy(source, b_qkv.at[p, :, pl.ds(half_at, 384)])
    return copies


def out_copies(place_ref, far_block, own_a, out_w, scratch, sem):
    w_out, a_out = scratch
    row = place_ref[0]
    copies = []

    def copy(source, target):
        copies.append(pltpu.make_async_copy(source, target, sem.at[len(copies)]))

    for t in range(2):
        half_at = pl.multiple_of((row ^ t) * 384, 128)
        copy(out_w[t].at[pl.ds(0, 384)], w_out.at[pl.ds(half_at, 384), :])
        for j in range(3):
            if t == 0:
                source = own_a.at[pl.ds(128 * j, 128)]
            else:
                source = far_block.at[pl.ds(W_ROWS + 384, 128), pl.ds(128 * j, 128)]
            copy(source, a_out.at[pl.ds(half_at + 128 * j, 128), :])
    return copies


W_ROWS = 944
QKV_SCRATCH = [
    pltpu.VMEM((3, D, D), bf16),
    pltpu.VMEM((3, D, ADAPT), bf16),
    pltpu.VMEM((3, ADAPT, D), bf16),
    pltpu.SemaphoreType.DMA((54,)),
]
OUT_SCRATCH = [
    pltpu.VMEM((D, D), bf16),
    pltpu.VMEM((D, ADAPT), bf16),
    pltpu.SemaphoreType.DMA((8,)),
]


def attend_kernel(picks_ref, place_ref, *refs):
    blocks, refs = refs[:8], refs[8:]
    (
        own_b, own_a, out_near, out_far, x_ref, gain_one, gain_two, b_out,
        two_out, resid_out, normed_out, qkv_out, mixed_out, probs_out, lows_out,
        w_qkv, a_qkv, b_qkv, qkv_sem, w_out, a_out, out_sem,
    ) = refs
    image = pl.program_id(0)

    @pl.when(image == 0)
    def start():
        copies = qkv_copies(place_ref, blocks, own_b, (w_qkv, a_qkv, b_qkv), qkv_sem)
        copies += out_copies(place_ref, blocks[4], own_a, (out_near, out_far), (w_out, a_out), out_sem)
        for copy in copies:
            copy.start()
        for copy in copies:
            copy.wait()

    mask = pick_mask(picks_ref[image])
    x = x_ref[...].astype(f32)
    unit, unused = norm_stats(x)
    normed = (unit * gain_one[...]).astype(bf16)
    normed_out[...] = normed
    for p in range(3):
        low = jnp.where(mask, dot(normed, a_qkv[p]), 0.0).astype(bf16)
        lows_out[:, 128 * p : 128 * p + 128] = low
        qkv_out[p] = (dot(normed, w_qkv[p]) + dot(low, b_qkv[p])).astype(bf16)
    lane = lane_iota((1, 128))
    key_lane = lane_iota((1, SEQP))
    for pair in range(HEADS // 2):
        at = slice(128 * pair, 128 * pair + 128)
        q = qkv_out[0, :, at]
        k = qkv_out[1, :, at]
        v = qkv_out[2, :, at]
        parts = []
        for side in range(2):
            own = (lane // HEAD_DIM) == side
            scores = dot_nt(jnp.where(own, q, jnp.zeros_like(q)), k) * (HEAD_DIM**-0.5)
            scores = jnp.where(key_lane < SEQ, scores, -1e30)
            power = jnp.exp(scores - jnp.max(scores, axis=1, keepdims=True))
            probs = (power / jnp.sum(power, axis=1, keepdims=True)).astype(bf16)
            probs_out[0, 2 * pair + side] = probs
            parts.append(dot(probs, v))
        mixed_out[:, at] = jnp.where(lane < HEAD_DIM, parts[0], parts[1]).astype(bf16)
    mixed = mixed_out[...]
    low = jnp.where(mask, dot(mixed, a_out[...]), 0.0).astype(bf16)
    lows_out[:, 384:512] = low
    resid = x + dot(mixed, w_out[...]) + dot(low, b_out[...])
    resid_out[...] = resid
    unit, unused = norm_stats(resid)
    real = lax.broadcasted_iota(jnp.int32, (SEQP, 1), 0) < SEQ
    two_out[...] = jnp.where(real, unit * gain_two[...], 0.0).astype(bf16)


def image_rows(lanes):
    return pl.BlockSpec((SEQP, lanes), lambda i, *_: (i, 0))


def kept(*shape):
    return pl.BlockSpec(shape, lambda i, *_: (0,) * len(shape))


QKV_SPEC = pl.BlockSpec((3, SEQP, D), lambda i, *_: (0, i, 0))
PROBS_SPEC = pl.BlockSpec((1, HEADS, SEQP, SEQP), lambda i, *_: (i, 0, 0, 0))
ANYWHERE = pl.BlockSpec(memory_space=pl.ANY)


def attend_call(picks, place, blocks, own_b, own_a, out_w, x, gain_one, gain_two, b_out):
    rows = x.shape[0]
    return pl.pallas_call(
        attend_kernel,
        grid_spec=pltpu.PrefetchScalarGridSpec(
            num_scalar_prefetch=2,
            grid=(2,),
            in_specs=[ANYWHERE] * (len(blocks) + 4)
            + [image_rows(D), kept(1, D), kept(1, D), kept(ADAPT, D)],
            out_specs=[
                image_rows(D), image_rows(D), image_rows(D), QKV_SPEC,
                image_rows(D), PROBS_SPEC, image_rows(512),
            ],
            scratch_shapes=QKV_SCRATCH + OUT_SCRATCH,
        ),
        out_shape=[
            jax.ShapeDtypeStruct((rows, D), bf16),
            jax.ShapeDtypeStruct((rows, D), f32),
            jax.ShapeDtypeStruct((rows, D), bf16),
            jax.ShapeDtypeStruct((3, rows, D), bf16),
            jax.ShapeDtypeStruct((rows, D), bf16),
            jax.ShapeDtypeStruct((2, HEADS, SEQP, SEQP), bf16),
            jax.ShapeDtypeStruct((rows, 512), bf16),
        ],
        compiler_params=pltpu.CompilerParams(vmem_limit_bytes=48 * 1024 * 1024),
        cost_estimate=pl.CostEstimate(flops=4_000_000_000, bytes_accessed=15_000_000, transcendentals=2_000_000),
    )(picks, place, *blocks, own_b, own_a, *out_w, x, gain_one, gain_two, b_out)


def out_back_kernel(picks_ref, place_ref, *refs):
    (
        far_block, own_a, out_near, out_far, gain_two, b_out, two_ref, resid_ref, mixed_ref, lows_ref,
        cot_ref, grad_a, grad_b, w_router, a_router, b_router, a_up, b_down,
        resid_grad_out, mixed_grad_out, base_out, both_out, a_part_out, b_part_out,
        w_out, a_out, sem, both, a_part, b_part,
    ) = refs
    image = pl.program_id(0)

    @pl.when(image == 0)
    def start():
        copies = out_copies(place_ref, far_block, own_a, (out_near, out_far), (w_out, a_out), sem)
        for copy in copies:
            copy.start()
        for part in (both, a_part, b_part):
            part[...] = jnp.zeros_like(part)
        for copy in copies:
            copy.wait()

    mask = pick_mask(picks_ref[image])
    lane = lane_iota((1, 128))

    def add_part(row, value):
        at = slice(row, row + value.shape[0])
        both[at, :] += value

    two = two_ref[...]
    received = grad_a[...].astype(f32) + grad_b[...].astype(f32)
    low_r = jnp.where(mask, dot(two, a_router[...]), 0.0).astype(bf16)
    logits = dot(two, w_router[...]) + dot(low_r, b_router[...])
    logits = jnp.where(lane < EXPERTS, logits, -1e30)
    power = jnp.exp(logits - jnp.max(logits, axis=1, keepdims=True))
    probs = power / jnp.sum(power, axis=1, keepdims=True)
    last = received[:, D:]
    grad_probs = jnp.where(lane < EXPERTS, last, 0.0)
    low_in = jnp.where(mask, repeat_lanes(jnp.where((lane >= 32) & (lane < 48), last, 0.0)), 0.0).astype(bf16)
    low_out = jnp.where(mask, repeat_lanes(jnp.where((lane >= 48) & (lane < 64), last, 0.0)), 0.0).astype(bf16)
    cot = cot_ref[...]
    resid = resid_ref[...]
    base_out[...] = resid + dot(low_out, b_down[...])
    add_part(768, dot_tn(two, low_in))
    add_part(1536, dot_tn(cot, low_out))
    grad_logits = probs * (grad_probs - jnp.sum(probs * grad_probs, axis=1, keepdims=True))
    grad_logits = grad_logits.astype(bf16)
    grad_low = jnp.where(mask, dot_nt(grad_logits, b_router[...]), 0.0).astype(bf16)
    grad_two = received[:, :D] + dot_nt(low_in, a_up[...])
    grad_two = grad_two + dot_nt(grad_logits, w_router[...]) + dot_nt(grad_low, a_router[...])
    add_part(0, dot_tn(two, grad_low))
    add_part(2304, dot_tn(grad_logits, low_r))
    unit, inverse = norm_stats(resid)
    grad_resid = cot.astype(f32) + norm_back(grad_two, gain_two[...], unit, inverse)
    resid_grad_out[...] = grad_resid
    grad_attn = grad_resid.astype(bf16)
    grad_low = jnp.where(mask, dot_nt(grad_attn, b_out[...]), 0.0).astype(bf16)
    mixed_grad_out[...] = (dot_nt(grad_attn, w_out[...]) + dot_nt(grad_low, a_out[...])).astype(bf16)
    a_part[...] += dot_tn(mixed_ref[...], grad_low)
    b_part[...] += dot_tn(grad_attn, lows_ref[:, 384:512])

    @pl.when(image == 1)
    def finish():
        both_out[...] = both[...].astype(bf16)
        a_part_out[...] = a_part[...].astype(bf16)
        b_part_out[...] = b_part[...].astype(bf16)


BOTH_ROWS = 2560


def out_back_call(picks, place, far_block, own_a, out_w, gain_two, b_out, two, resid, mixed, lows, cot, grad_a, grad_b,
                  w_router, a_router, b_router, a_up, b_down):
    rows = two.shape[0]
    return pl.pallas_call(
        out_back_kernel,
        grid_spec=pltpu.PrefetchScalarGridSpec(
            num_scalar_prefetch=2,
            grid=(2,),
            in_specs=[ANYWHERE] * 4
            + [kept(1, D), kept(ADAPT, D), image_rows(D), image_rows(D), image_rows(D), image_rows(512)]
            + [image_rows(D), image_rows(D + 128), image_rows(D + 128)]
            + [kept(D, 128), kept(D, ADAPT), kept(ADAPT, 128), kept(D, ADAPT), kept(ADAPT, D)],
            out_specs=[image_rows(D), image_rows(D), image_rows(D), kept(BOTH_ROWS, 128), kept(D, 128), kept(D, 128)],
            scratch_shapes=OUT_SCRATCH
            + [pltpu.VMEM((BOTH_ROWS, 128), f32), pltpu.VMEM((D, 128), f32), pltpu.VMEM((D, 128), f32)],
        ),
        out_shape=[
            jax.ShapeDtypeStruct((rows, D), f32),
            jax.ShapeDtypeStruct((rows, D), bf16),
            jax.ShapeDtypeStruct((rows, D), f32),
            jax.ShapeDtypeStruct((BOTH_ROWS, 128), bf16),
            jax.ShapeDtypeStruct((D, 128), bf16),
            jax.ShapeDtypeStruct((D, 128), bf16),
        ],
        compiler_params=pltpu.CompilerParams(vmem_limit_bytes=48 * 1024 * 1024),
        cost_estimate=pl.CostEstimate(flops=6_000_000_000, bytes_accessed=15_000_000, transcendentals=100_000),
    )(picks, place, far_block, own_a, *out_w, gain_two, b_out, two, resid, mixed, lows, cot, grad_a, grad_b,
      w_router, a_router, b_router, a_up, b_down)


def qkv_back_kernel(picks_ref, place_ref, *refs):
    blocks, refs = refs[:8], refs[8:]
    (
        own_b, x_ref, gain_one, normed_ref, qkv_ref, probs_ref, lows_ref, resid_grad, grad_mixed,
        tokens_out, a_part_out, b_part_out,
        w_qkv, a_qkv, b_qkv, sem, a_part, b_part, grads,
    ) = refs
    image = pl.program_id(0)
    copies = qkv_copies(place_ref, blocks, own_b, (w_qkv, a_qkv, b_qkv), sem)

    @pl.when(image == 0)
    def start():
        for copy in copies:
            copy.start()
        a_part[...] = jnp.zeros_like(a_part)
        b_part[...] = jnp.zeros_like(b_part)

    mask = pick_mask(picks_ref[image])
    lane = lane_iota((1, 128))
    for pair in range(HEADS // 2):
        at = slice(128 * pair, 128 * pair + 128)
        q = qkv_ref[0, :, at]
        k = qkv_ref[1, :, at]
        v = qkv_ref[2, :, at]
        gm = grad_mixed[:, at]
        found = []
        for side in range(2):
            own = (lane // HEAD_DIM) == side
            weights = probs_ref[0, 2 * pair + side]
            weights_f = weights.astype(f32)
            grad_w = dot_nt(jnp.where(own, gm, jnp.zeros_like(gm)), v)
            inner = jnp.sum(weights_f * grad_w, axis=1, keepdims=True)
            grad_s = (weights_f * (grad_w - inner)).astype(bf16)
            found.append(
                (
                    dot(grad_s, k) * (HEAD_DIM**-0.5),
                    dot_tn(grad_s, q) * (HEAD_DIM**-0.5),
                    dot_tn(weights, gm),
                )
            )
        for p in range(3):
            grads[p, :, at] = jnp.where(lane < HEAD_DIM, found[0][p], found[1][p]).astype(bf16)

    @pl.when(image == 0)
    def arrived():
        for copy in copies:
            copy.wait()

    normed = normed_ref[...]
    grad_normed = jnp.zeros((SEQP, D), f32)
    for p in range(3):
        piece = grads[p]
        grad_low = jnp.where(mask, dot_nt(piece, b_qkv[p]), 0.0).astype(bf16)
        grad_normed = grad_normed + dot_nt(piece, w_qkv[p]) + dot_nt(grad_low, a_qkv[p])
        a_part[D * p : D * p + D, :] += dot_tn(normed, grad_low)
        b_part[D * p : D * p + D, :] += dot_tn(piece, lows_ref[:, 128 * p : 128 * p + 128])
    unit, inverse = norm_stats(x_ref[...].astype(f32))
    tokens_out[...] = (resid_grad[...] + norm_back(grad_normed, gain_one[...], unit, inverse)).astype(bf16)

    @pl.when(image == 1)
    def finish():
        a_part_out[...] = a_part[...].astype(bf16)
        b_part_out[...] = b_part[...].astype(bf16)


def qkv_back_call(picks, place, blocks, own_b, x, gain_one, normed, qkv, probs, lows, resid_grad, grad_mixed):
    rows = x.shape[0]
    return pl.pallas_call(
        qkv_back_kernel,
        grid_spec=pltpu.PrefetchScalarGridSpec(
            num_scalar_prefetch=2,
            grid=(2,),
            in_specs=[ANYWHERE] * (len(blocks) + 1)
            + [image_rows(D), kept(1, D), image_rows(D), QKV_SPEC, PROBS_SPEC, image_rows(512)]
            + [image_rows(D), image_rows(D)],
            out_specs=[image_rows(D), kept(3 * D, 128), kept(3 * D, 128)],
            scratch_shapes=QKV_SCRATCH
            + [
                pltpu.VMEM((3 * D, 128), f32),
                pltpu.VMEM((3 * D, 128), f32),
                pltpu.VMEM((3, SEQP, D), bf16),
            ],
        ),
        out_shape=[
            jax.ShapeDtypeStruct((rows, D), bf16),
            jax.ShapeDtypeStruct((3 * D, 128), bf16),
            jax.ShapeDtypeStruct((3 * D, 128), bf16),
        ],
        compiler_params=pltpu.CompilerParams(vmem_limit_bytes=48 * 1024 * 1024),
        cost_estimate=pl.CostEstimate(flops=9_000_000_000, bytes_accessed=15_000_000, transcendentals=1000),
    )(picks, place, *blocks, own_b, x, gain_one, normed, qkv, probs, lows, resid_grad, grad_mixed)


TABLES = (((0, 0), (1, 0)), ((0, 1), (0, 2), (1, 1), (1, 2)), ((0, 3), (1, 3)))


def across_row(value):
    return lax.ppermute(value, "row", [(0, 1), (1, 0)])


def across_col(value, step):
    return lax.ppermute(value, "col", [(i, i ^ step) for i in range(4)])


def by_place(blocks, col):
    found = []
    for place in range(4):
        value = blocks[place]
        for other in range(1, 4):
            value = jnp.where(col == other, blocks[place ^ other], value)
        found.append(value)
    return found


def across_chip(value, first, second):
    pairs = [(i, i ^ first) for i in range(4)] + [(4 + i, 4 + (i ^ second)) for i in range(4)]
    return lax.ppermute(value, ("row", "col"), pairs)


def gather_col(value, row):
    from_x = across_col(value, 1)
    from_y = across_col(value, 2)
    return [value, from_x, from_y, across_chip(jnp.where(row == 0, from_x, from_y), 2, 1)]


def across_pair(first, second):
    both = across_row(jnp.stack([first, second]))
    return both[0], both[1]


def added(*values):
    total = values[0].astype(f32)
    for value in values[1:]:
        total = total + value.astype(f32)
    return total


def row_sum(near, far):
    got = across_row(far)
    return added(near[BLK * 2 :], got[BLK * 2 :]).astype(bf16), added(near[: BLK * 2], got[: BLK * 2]).astype(bf16)


def last_exchange(kept_rows, got):
    sent = added(kept_rows[BLK:], got[BLK:]).astype(bf16)
    return added(kept_rows[:BLK], got[:BLK]).astype(bf16), across_chip(sent, 2, 1)


def at_place(value, axis, place):
    return lax.dynamic_index_in_dim(value, place, axis, keepdims=False)


def reduce_dp(value):
    n_dp = lax.axis_size("dp")
    if n_dp != 4:
        return lax.psum(value, "dp")
    place = lax.axis_index("dp")

    def across(part, step):
        return lax.ppermute(part, "dp", [(i, i ^ step) for i in range(4)])

    view = value.reshape(4, -1, 128)
    found = [at_place(view, 0, place)]
    for s in range(1, 4):
        found.append(across(at_place(view, 0, place ^ s), s))
    total = added(*found).astype(bf16)
    blocks = [total] + [across(total, s) for s in range(1, 4)]
    return jnp.concatenate(by_place(blocks, place))


def part_share(col_parts, row_parts, both_parts, place):
    col_parts = at_place(col_parts.reshape(4, 4, 2, 96, 128), 2, place)
    row_parts = at_place(row_parts.reshape(4, 2, 4, 96, 128), 1, place)
    both_parts = at_place(both_parts.reshape(2, 4, BOTH_ROWS // 8, 128), 0, place)
    col_parts = col_parts.swapaxes(0, 1).reshape(4, 384, 128)
    row_parts = row_parts.swapaxes(0, 1).reshape(4, 384, 128)
    return jnp.concatenate([col_parts, row_parts, both_parts], axis=1)


def reduce_col(value, col):
    found = [at_place(value, 0, col)]
    for s in range(1, 4):
        found.append(across_col(at_place(value, 0, col ^ s), s))
    return added(*found).astype(bf16)


def spread_parts(mine, row, col):
    spread = mine[384:]
    spread = by_place([spread] + [across_col(spread, s) for s in range(1, 4)], col)
    row_sums = jnp.stack([one[:384].reshape(4, 96, 128) for one in spread], axis=1).reshape(4, 384, 128)
    near = jnp.concatenate([mine[:384]] + [one[384:] for one in spread])
    far = across_row(near)
    first = jnp.where(row == 0, near, far)
    second = jnp.where(row == 0, far, near)
    col_sums = jnp.stack([first[:384].reshape(4, 96, 128), second[:384].reshape(4, 96, 128)], axis=1).reshape(4, 192, 128)
    both_sums = jnp.concatenate([first[384:], second[384:]])
    return col_sums, row_sums, both_sums


def token_blocks(value):
    images = value.reshape(8, SEQ, value.shape[1])
    return jnp.pad(images, ((0, 0), (0, SEQP - SEQ), (0, 0))).reshape(4, BLK, value.shape[1])


def to_features(value, col):
    width = D // 4
    chunks = by_place([value[:, width * p : width * p + width] for p in range(4)], col)
    sent = [jnp.concatenate([chunk[:SEQP], chunk[SEQP:]], axis=1) for chunk in chunks]
    got = [sent[0]] + [across_col(sent[s], s) for s in range(1, 4)]
    rows = []
    for block in by_place(got, col):
        rows += [block[:SEQ, :width], block[:SEQ, width:]]
    return jnp.concatenate(rows, axis=0)


def on_device(
    tokens, cotangent, routes, adapter_pick, gain_attn, gain_moe, w_qkv, w_out, w_router, w_up, w_down,
    a_qkv, b_qkv, a_out, b_out, a_router, b_router, a_up, b_up, a_down, b_down,
):
    row = lax.axis_index("row")
    col = lax.axis_index("col")
    me = row * 4 + col
    place = jnp.stack([row, col]).astype(jnp.int32)

    width = D // 4
    mixed_blocks = jnp.concatenate([token_blocks(tokens), token_blocks(cotangent)], axis=2)
    pairs = [at_place(mixed_blocks, 0, col)]
    for s in range(1, 4):
        pairs.append(across_col(at_place(mixed_blocks, 0, col ^ s), s))
    pairs = by_place(pairs, col)
    x = jnp.concatenate([pair[:, :width] for pair in pairs], axis=1)
    cot = jnp.concatenate([pair[:, width:] for pair in pairs], axis=1)
    half = D // 2
    gains = []
    for gain in (gain_attn, gain_moe):
        left = gain
        for unused in range(3):
            lead = lax.reduce_precision(left, 8, 7)
            gains.append(lead.astype(bf16))
            left = left - lead
    small = jnp.concatenate([w_out, b_out, jnp.stack(gains), jnp.zeros((26, width), bf16)], axis=0)
    low = at_place(a_qkv.reshape(3, 2, 96, ADAPT), 1, row)
    packed = jnp.concatenate(
        [w_qkv.reshape(576, half), jnp.concatenate([low[0], low[1], low[2]], axis=1),
         jnp.concatenate([small[:272], small[272:]], axis=1)]
    )
    for_row = jnp.concatenate(
        [packed, b_qkv.reshape(half, half), jnp.concatenate([a_out[:128], a_out[128:256], a_out[256:]], axis=1)]
    )
    near = gather_col(packed, row)
    far = [across_row(for_row), *across_pair(near[1], near[2]), across_row(near[3])]
    blocks = near + far

    def assembled(group):
        parts = by_place([block[672:944] for block in group], col)
        return jnp.concatenate(
            [jnp.concatenate([part[:, :width] for part in parts], axis=1),
             jnp.concatenate([part[:, width:] for part in parts], axis=1)], axis=0
        )

    out_w = [assembled(near), assembled(far)]
    full_b_out = out_w[0][384:512]
    gain_rows = out_w[0][512:518].astype(f32)
    gain_one = jnp.sum(gain_rows[:3], axis=0, keepdims=True)
    gain_two = jnp.sum(gain_rows[3:], axis=0, keepdims=True)

    picks_group = lax.dynamic_slice_in_dim(adapter_pick, lax.axis_index("dp") * IMG_GRP, IMG_GRP)
    order = jnp.arange(IMG_GRP, dtype=jnp.int32)
    picks = jnp.take(picks_group, ((order // 2) ^ me) * 2 + order % 2)
    spot_picks = jnp.sum(
        jnp.where(block_spot(order // 2, row, col)[None, :] * 2 + order[None, :] % 2 == order[:, None], picks_group[None, :], 0), axis=1
    )
    token_list, tile_experts = routing(routes, row, col)
    wide_router = jnp.concatenate([w_router, w_router, jnp.zeros((D, 64), bf16)], axis=1)
    wide_b_router = jnp.concatenate([b_router, b_router, jnp.zeros((ADAPT, 64), bf16)], axis=1)
    slim_router = jnp.concatenate([w_router, jnp.zeros((D, 96), bf16)], axis=1)
    slim_b_router = jnp.concatenate([b_router, jnp.zeros((ADAPT, 96), bf16)], axis=1)

    two, resid, normed, qkv, mixed, probs, lows = attend_call(
        picks, place, blocks, b_qkv, a_out, out_w, x, gain_one, gain_two, full_b_out
    )
    cot_near = gather_col(cot, row)
    two_near = gather_col(two, row)

    def table(spots, twos, cots):
        return table_call(
            jnp.stack([picks[8 * t + 2 * s + side] for t, s in spots for side in range(2)]),
            twos, cots, a_up, b_down, wide_router, a_router, wide_b_router,
        )

    cot_far = [across_row(cot), *across_pair(cot_near[1], cot_near[2]), across_row(cot_near[3])]
    tables = [table(TABLES[0], [two, across_row(two)], [cot, cot_far[0]])]
    two_x, two_y = across_pair(two_near[1], two_near[2])
    tables.append(table(TABLES[1], [two_near[1], two_near[2], two_x, two_y], [cot_near[1], cot_near[2], cot_far[1], cot_far[2]]))
    diag, *tables = lax.optimization_barrier((two_near[3], *tables))
    tables.append(table(TABLES[2], [diag, across_row(diag)], [cot_near[3], cot_far[3]]))
    sum_near, sum_far, grad_near, grad_far, part_b_up, part_a_down = moe_call(
        token_list, tile_experts, spot_picks, place, tables, TABLES, w_up, w_down, b_up, a_down
    )
    grad_sent, grad_kept = row_sum(grad_near, grad_far)
    grad_sent, grad_kept, sum_near, sum_far, part_b_up, part_a_down = lax.optimization_barrier(
        (grad_sent, grad_kept, sum_near, sum_far, part_b_up, part_a_down)
    )
    grad_got = across_chip(grad_sent, 1, 2)
    sum_sent, sum_kept = row_sum(sum_near, sum_far)
    grad_got, sum_sent, sum_kept = lax.optimization_barrier((grad_got, sum_sent, sum_kept))
    grad_a, grad_b = last_exchange(grad_kept, grad_got)
    sum_got = across_chip(sum_sent, 1, 2)
    resid_grad, mixed_grad, base, both_parts, part_a_out, part_b_out = out_back_call(
        picks, place, blocks[4], a_out, out_w, gain_two, full_b_out, two, resid, mixed, lows, cot, grad_a, grad_b,
        slim_router, a_router, slim_b_router, a_up, b_down,
    )
    resid_grad, mixed_grad, sum_got = lax.optimization_barrier((resid_grad, mixed_grad, sum_got))
    grad_tokens, part_a_qkv, part_b_qkv = qkv_back_call(
        picks, place, blocks, b_qkv, x, gain_one, normed, qkv, probs, lows, resid_grad, mixed_grad
    )
    sum_a, sum_b = last_exchange(sum_kept, sum_got)
    col_parts = jnp.concatenate([part_a_qkv, part_b_out])
    row_parts = jnp.concatenate([part_b_qkv, part_a_out])
    theirs = across_row(part_share(col_parts, row_parts, both_parts, 1 - row))
    shared = added(part_share(col_parts, row_parts, both_parts, row), theirs).astype(bf16)
    shared, grad_tokens, sum_b = lax.optimization_barrier((shared, grad_tokens, sum_b))
    grad_tokens = to_features(grad_tokens, col).astype(f32)
    mine = reduce_col(shared, col)
    mine, sum_b = lax.optimization_barrier((mine, sum_b))
    block_out = to_features((base + added(sum_a, sum_b)).astype(bf16), col)
    part_rows = mine.shape[0]
    mine = reduce_dp(jnp.concatenate([mine, part_b_up.astype(bf16), part_a_down.astype(bf16)]))
    dp_sums = mine[part_rows:]
    col_sums, row_sums, both_sums = spread_parts(mine[:part_rows], row, col)
    col_sums = col_sums.astype(f32)
    row_sums = row_sums.astype(f32)
    both_sums = both_sums.astype(f32)
    dp_sums = dp_sums.astype(f32)
    return (
        block_out,
        grad_tokens,
        col_sums[:3],
        jnp.swapaxes(row_sums[:3], 1, 2),
        row_sums[3],
        col_sums[3].T,
        both_sums[:768],
        both_sums[2304:2336].T,
        both_sums[768:1536],
        dp_sums[:384].T,
        dp_sums[384:],
        both_sums[1536:2304].T,
    )


def solution(mesh):
    return jax.shard_map(
        on_device,
        mesh=mesh,
        in_specs=(
            P(("dp", "row"), "col"),
            P(("dp", "row"), "col"),
            P("dp", None),
            P(),
            P("col"),
            P("col"),
            P(None, "col", "row"),
            P("row", "col"),
            P(),
            P(None, None, ("row", "col")),
            P(None, ("row", "col"), None),
            P(None, "col", None),
            P(None, None, "row"),
            P("row", None),
            P(None, "col"),
            P(),
            P(),
            P(),
            P(None, ("row", "col")),
            P(("row", "col"), None),
            P(),
        ),
        out_specs=(
            P(("dp", "row"), "col"),
            P(("dp", "row"), "col"),
            P(None, "col", None),
            P(None, None, "row"),
            P("row", None),
            P(None, "col"),
            P(),
            P(),
            P(),
            P(None, ("row", "col")),
            P(("row", "col"), None),
            P(),
        ),
        check_vma=False,
    )
```

```python
import jax
import jax.numpy as jnp
from jax import lax
from jax.experimental import pallas as pl
from jax.experimental.pallas import tpu as pltpu
from jax.sharding import PartitionSpec as P

D = 768
EXPERTS = 32
SEQ = 197
SEQP = 208
RANK = 16
ADAPT = 128
IMG_GRP = 16
TOK = IMG_GRP * SEQP
BLK = 2 * SEQP
DUMMY = SEQ
TILE = 192
f32 = jnp.float32
bf16 = jnp.bfloat16


def max_tiles():
    return (2 * IMG_GRP * SEQ) // TILE + EXPERTS + 1


def dot(left, right):
    return jnp.dot(left, right, preferred_element_type=f32)


def dot_nt(left, right):
    return lax.dot_general(left, right, (((1,), (1,)), ((), ())), preferred_element_type=f32)


def dot_tn(left, right):
    return lax.dot_general(left, right, (((0,), (0,)), ((), ())), preferred_element_type=f32)


def lane_iota(shape):
    return lax.broadcasted_iota(jnp.int32, shape, len(shape) - 1)


def repeat_lanes(value):
    for shift in (16, 32, 64):
        value = value + pltpu.roll(value, shift, 1)
    return value


def table_kernel(n_blocks, picks_ref, *refs):
    x_blocks = refs[:n_blocks]
    c_blocks = refs[n_blocks : 2 * n_blocks]
    a_up, b_down, w_router, a_router, b_router, table_out, xin, cin, rows_x, rows_c, sem = refs[2 * n_blocks :]
    image = pl.program_id(0)
    lane = lane_iota((1, 128))

    @pl.when(image == 0)
    def start():
        copies = []
        for blocks, place in ((x_blocks, xin), (c_blocks, cin)):
            for b, block in enumerate(blocks):
                copies.append(pltpu.make_async_copy(block, place.at[pl.ds(b * BLK, BLK)], sem.at[len(copies)]))
        for copy in copies:
            copy.start()
        for copy in copies:
            copy.wait()

    row = pl.multiple_of(image * SEQP, 16)
    mask = (lane // RANK) == picks_ref[image]
    x = xin[pl.ds(row, SEQP), :]
    c = cin[pl.ds(row, SEQP), :]
    flat_x = rows_x.reshape(SEQP * 8, 128)
    flat_c = rows_c.reshape(SEQP * 8, 128)
    low_x = jnp.where(mask, dot(x, a_up[...]), 0.0)
    low_c = jnp.where(mask, dot_nt(c, b_down[...]), 0.0)
    low_r = jnp.where(mask, dot(x, a_router[...]), 0.0).astype(bf16)
    logits = dot(x, w_router[...]) + dot(low_r, b_router[...])
    logits = jnp.where(lane < 2 * EXPERTS, logits, -1e30)
    power = jnp.exp(logits - jnp.max(logits, axis=1, keepdims=True))
    total = jnp.sum(jnp.where(lane < EXPERTS, power, 0.0), axis=1, keepdims=True)
    probs = power / total
    lead = probs.astype(bf16).astype(f32)
    probs = jnp.where(lane < EXPERTS, lead, probs - lead)
    for j in range(6):
        flat_x[pl.ds(j, SEQP, 8), :] = x[:, 128 * j : 128 * j + 128].astype(f32)
        flat_c[pl.ds(j, SEQP, 8), :] = c[:, 128 * j : 128 * j + 128].astype(f32)
    flat_x[pl.ds(6, SEQP, 8), :] = low_x
    flat_x[pl.ds(7, SEQP, 8), :] = probs
    flat_c[pl.ds(6, SEQP, 8), :] = low_c
    flat_c[pl.ds(7, SEQP, 8), :] = jnp.zeros((SEQP, 128), f32)
    table_out[...] = jnp.concatenate([rows_x[...], rows_c[...]], axis=1).astype(bf16)


def table_call(picks, x_blocks, c_blocks, a_up, b_down, w_router, a_router, b_router):
    n = len(x_blocks)

    def whole(*shape):
        return pl.BlockSpec(shape, lambda e, *_: (0,) * len(shape))

    anywhere = pl.BlockSpec(memory_space=pl.ANY)
    return pl.pallas_call(
        lambda *refs: table_kernel(n, *refs),
        grid_spec=pltpu.PrefetchScalarGridSpec(
            num_scalar_prefetch=1,
            grid=(2 * n,),
            in_specs=[anywhere] * (2 * n)
            + [whole(D, ADAPT), whole(ADAPT, D), whole(D, 128), whole(D, ADAPT), whole(ADAPT, 128)],
            out_specs=pl.BlockSpec((SEQP, 16, 128), lambda i, *_: (i, 0, 0)),
            scratch_shapes=[
                pltpu.VMEM((n * BLK, D), bf16),
                pltpu.VMEM((n * BLK, D), bf16),
                pltpu.VMEM((SEQP, 8, 128), f32),
                pltpu.VMEM((SEQP, 8, 128), f32),
                pltpu.SemaphoreType.DMA((2 * n,)),
            ],
        ),
        out_shape=jax.ShapeDtypeStruct((n * BLK, 16, 128), bf16),
        compiler_params=pltpu.CompilerParams(vmem_limit_bytes=60 * 1024 * 1024),
        cost_estimate=pl.CostEstimate(flops=n * 3_000_000_000, bytes_accessed=n * 3_000_000, transcendentals=n * 60_000),
    )(picks, *x_blocks, *c_blocks, a_up, b_down, w_router, a_router, b_router)


def moe_kernel(places, list_ref, expert_ref, picks_ref, place_ref, *refs):
    n = len(places)
    tables = refs[:n]
    (
        w_up_hbm, w_down_hbm, b_up, a_down,
        ep_near, ep_far, tg_near, tg_far, gbu_out, gad_out,
        table, acc_e, acc_t, in_x, in_c, out_e, out_t, xb, cb, w_up, w_down, stage_ep, stage_tg,
        in_sem, up_sem, down_sem, ep_sem, tg_sem,
    ) = refs[n:]
    acc_e_flat = acc_e.reshape(TOK * 8, 128)
    acc_t_flat = acc_t.reshape(TOK * 8, 128)
    in_x_flat = in_x.reshape(TILE * 8, 128)
    in_c_flat = in_c.reshape(TILE * 8, 128)
    out_e_flat = out_e.reshape(TILE * 8, 128)
    out_t_flat = out_t.reshape(TILE * 8, 128)
    lane = lane_iota((1, 128))
    n_tiles = expert_ref[max_tiles()]

    copies = []
    for piece, spots in zip(tables, places):
        for b, (t, s) in enumerate(spots):
            spot = 4 * t + jnp.where(place_ref[0] == t, swapped(s), s)
            copies.append(
                pltpu.make_async_copy(
                    piece.at[pl.ds(b * BLK, BLK)], table.at[pl.ds(pl.multiple_of(spot * BLK, 32), BLK)], in_sem.at[len(copies)]
                )
            )
    for copy in copies:
        copy.start()

    def weights(expert):
        slot = expert % 2
        return (
            pltpu.make_async_copy(w_up_hbm.at[expert], w_up.at[slot], up_sem.at[slot]),
            pltpu.make_async_copy(w_down_hbm.at[expert], w_down.at[slot], down_sem.at[slot]),
        )

    for copy in weights(0):
        copy.start()
    out_e[...] = jnp.zeros_like(out_e)
    out_t[...] = jnp.zeros_like(out_t)
    gbu_out[...] = jnp.zeros_like(gbu_out)
    gad_out[...] = jnp.zeros_like(gad_out)

    def clear(i, carry):
        acc_e[pl.ds(i * 64, 64)] = jnp.zeros((64, 8, 128), f32)
        acc_t[pl.ds(i * 64, 64)] = jnp.zeros((64, 8, 128), f32)
        return carry

    lax.fori_loop(0, TOK // 64, clear, 0)
    for copy in copies:
        copy.wait()

    def fetch(t):
        for i in range(TILE):
            both = table[list_ref[t * TILE + i]].astype(f32)
            in_x[i] = both[:8]
            in_c[i] = both[8:]

    def give(t):
        for b in range(TILE // 8):
            tokens = [list_ref[t * TILE + 8 * b + k] for k in range(8)]
            sums_e = [acc_e[tokens[k]] + out_e[8 * b + k] for k in range(8)]
            sums_t = [acc_t[tokens[k]] + out_t[8 * b + k] for k in range(8)]
            for k in range(8):
                acc_e[tokens[k]] = sums_e[k]
                acc_t[tokens[k]] = sums_t[k]

    fetch(0)

    def tile(t, carry):
        expert = expert_ref[t]
        slot = expert % 2

        @pl.when((t == 0) | (expert_ref[jnp.maximum(t - 1, 0)] != expert))
        def arrive():
            for copy in weights(expert):
                copy.wait()

            @pl.when(expert + 1 < EXPERTS)
            def ahead():
                for copy in weights(expert + 1):
                    copy.start()

        for j in range(7):
            xb[:, 128 * j : 128 * j + 128] = in_x_flat[pl.ds(j, TILE, 8), :].astype(bf16)
            cb[:, 128 * j : 128 * j + 128] = in_c_flat[pl.ds(j, TILE, 8), :].astype(bf16)
        spread = in_x_flat[pl.ds(7, TILE, 8), :]
        mine = (lane == expert) | (lane == expert + EXPERTS)
        gate = jnp.sum(jnp.where(mine, spread, 0.0), axis=1, keepdims=True)
        fetch(t + 1)
        give(jnp.maximum(t - 1, 0))
        hidden = dot(xb[:, :D], w_up[slot]) + dot(xb[:, D:], b_up[...])
        back = dot_nt(cb[:, :D], w_down[slot]) + dot_nt(cb[:, D:], a_down[...])
        cdf = 0.5 + 0.5 * lax.erf(hidden * 0.7071067811865476)
        slope = cdf + hidden * jnp.exp(hidden * hidden * -0.5) * 0.3989422804014327
        act = (hidden * cdf).astype(bf16)
        act_f = act.astype(f32)
        gate_grad = jnp.sum(act_f * back, axis=1, keepdims=True)
        grad_hidden = (gate * back * slope).astype(bf16)
        act_gate = (gate * act_f).astype(bf16)
        out_main = dot(act_gate, w_down[slot])
        out_low = dot(act_gate, a_down[...])
        in_main = dot_nt(grad_hidden, w_up[slot])
        in_low = dot_nt(grad_hidden, b_up[...])
        gbu_out[...] += dot_tn(grad_hidden, xb[:, D:])
        gad_out[...] += dot_tn(act_gate, cb[:, D:])
        for j in range(6):
            out_e_flat[pl.ds(j, TILE, 8), :] = out_main[:, 128 * j : 128 * j + 128]
            out_t_flat[pl.ds(j, TILE, 8), :] = in_main[:, 128 * j : 128 * j + 128]
        out_e_flat[pl.ds(6, TILE, 8), :] = out_low
        out_t_flat[pl.ds(6, TILE, 8), :] = in_low
        out_t_flat[pl.ds(7, TILE, 8), :] = jnp.where(lane == expert, gate_grad, 0.0)
        return carry

    lax.fori_loop(0, n_tiles, tile, 0)
    give(n_tiles - 1)

    half_images = IMG_GRP // 2
    for side, (ep_out, tg_out) in enumerate(((ep_near, tg_near), (ep_far, tg_far))):

        def image(i, carry):
            slot = i % 2
            base = pl.multiple_of((i + side * half_images) * SEQP, 16) * 8
            mask = (lane // RANK) == picks_ref[i + side * half_images]
            rows = pl.ds(pl.multiple_of(i * SEQP, 16), SEQP)
            put_tg = pltpu.make_async_copy(stage_tg.at[slot], tg_out.at[rows], tg_sem.at[slot])
            put_ep = pltpu.make_async_copy(stage_ep.at[slot], ep_out.at[rows], ep_sem.at[slot])

            @pl.when(i >= 2)
            def drain():
                put_tg.wait()
                put_ep.wait()

            def chunk(j):
                flat = acc_e_flat if j < 8 else acc_t_flat
                return flat[pl.ds(base + j % 8, SEQP, 8), :]

            for j in range(6):
                at = slice(128 * j, 128 * j + 128)
                stage_tg[slot, :, at] = chunk(8 + j).astype(bf16)
                stage_ep[slot, :, at] = chunk(j).astype(bf16)
            low_in = repeat_lanes(jnp.where(mask, chunk(14), 0.0))
            low_out = repeat_lanes(jnp.where(mask, chunk(6), 0.0))
            last = jnp.where(lane < 48, low_in, jnp.where(lane < 64, low_out, 0.0))
            stage_tg[slot, :, D:] = jnp.where(lane < 32, chunk(15), last).astype(bf16)
            put_tg.start()
            put_ep.start()
            return carry

        lax.fori_loop(0, half_images, image, 0)
        for i in range(half_images - 2, half_images):
            rows = pl.ds(i * SEQP, SEQP)
            pltpu.make_async_copy(stage_tg.at[i % 2], tg_out.at[rows], tg_sem.at[i % 2]).wait()
            pltpu.make_async_copy(stage_ep.at[i % 2], ep_out.at[rows], ep_sem.at[i % 2]).wait()


def moe_call(token_list, tile_experts, picks, place, tables, places, w_up, w_down, b_up, a_down):
    half = w_up.shape[2]
    n = len(tables)
    n_copies = sum(len(spots) for spots in places)
    anywhere = pl.BlockSpec(memory_space=pl.ANY)
    inside = pl.BlockSpec(memory_space=pltpu.VMEM)
    return pl.pallas_call(
        lambda *refs: moe_kernel(places, *refs),
        grid_spec=pltpu.PrefetchScalarGridSpec(
            num_scalar_prefetch=4,
            grid=(1,),
            in_specs=[anywhere] * (n + 2) + [inside, inside],
            out_specs=[anywhere, anywhere, anywhere, anywhere, inside, inside],
            scratch_shapes=[
                pltpu.VMEM((TOK, 16, 128), bf16),
                pltpu.VMEM((TOK, 8, 128), f32),
                pltpu.VMEM((TOK, 8, 128), f32),
                pltpu.VMEM((TILE, 8, 128), f32),
                pltpu.VMEM((TILE, 8, 128), f32),
                pltpu.VMEM((TILE, 8, 128), f32),
                pltpu.VMEM((TILE, 8, 128), f32),
                pltpu.VMEM((TILE, D + 128), bf16),
                pltpu.VMEM((TILE, D + 128), bf16),
                pltpu.VMEM((2, D, half), bf16),
                pltpu.VMEM((2, half, D), bf16),
                pltpu.VMEM((2, SEQP, D), bf16),
                pltpu.VMEM((2, SEQP, D + 128), bf16),
                pltpu.SemaphoreType.DMA((n_copies,)),
                pltpu.SemaphoreType.DMA((2,)),
                pltpu.SemaphoreType.DMA((2,)),
                pltpu.SemaphoreType.DMA((2,)),
                pltpu.SemaphoreType.DMA((2,)),
            ],
        ),
        out_shape=[
            jax.ShapeDtypeStruct((TOK // 2, D), bf16),
            jax.ShapeDtypeStruct((TOK // 2, D), bf16),
            jax.ShapeDtypeStruct((TOK // 2, D + 128), bf16),
            jax.ShapeDtypeStruct((TOK // 2, D + 128), bf16),
            jax.ShapeDtypeStruct((half, ADAPT), f32),
            jax.ShapeDtypeStruct((half, ADAPT), f32),
        ],
        compiler_params=pltpu.CompilerParams(vmem_limit_bytes=58 * 1024 * 1024),
        cost_estimate=pl.CostEstimate(flops=20_000_000_000, bytes_accessed=60_000_000, transcendentals=10_000_000),
    )(token_list, tile_experts, picks, place, *tables, w_up, w_down, b_up, a_down)


def swapped(s):
    return ((s & 1) << 1) | (s >> 1)


def block_spot(block, row, col):
    from_row = block // 4
    s = (block % 4) ^ col
    return 4 * (from_row ^ row) + jnp.where(from_row == 0, swapped(s), s)


def routing(routes, row, col):
    token = jnp.arange(25 * 128, dtype=jnp.int32)[None, :]
    image = token // SEQ
    spot = block_spot(image // 2, row, col) * BLK + (image % 2) * SEQP + token % SEQ
    real = token < IMG_GRP * SEQ
    picked = jnp.pad(routes.T, ((0, 0), (0, 25 * 128 - IMG_GRP * SEQ)), constant_values=EXPERTS)
    beyond = EXPERTS * 4096 + DUMMY
    keys = jnp.where(real, picked * 4096 + spot, beyond).reshape(-1)
    experts = jnp.arange(EXPERTS, dtype=jnp.int32)
    count = jnp.sum((picked[None] == experts[:, None, None]).astype(jnp.int32), axis=(1, 2))
    tiles = (jnp.maximum(count, 1) + TILE - 1) // TILE
    extra = tiles * TILE - count
    filler = jnp.where(
        jnp.arange(256, dtype=jnp.int32)[None, :] < extra[:, None], (experts * 4096)[:, None] + DUMMY, beyond
    ).reshape(-1)
    ordered = lax.sort(jnp.concatenate([keys, filler])) & 4095
    ends = jnp.sum(jnp.where(experts[None, :] <= experts[:, None], tiles[None, :], 0), axis=1)
    steps = jnp.arange(max_tiles(), dtype=jnp.int32)
    owner = jnp.minimum(jnp.sum((ends[None, :] <= steps[:, None]).astype(jnp.int32), axis=1), EXPERTS - 1)
    return ordered, jnp.concatenate([owner, jnp.sum(tiles)[None]])


HEADS = 12
HEAD_DIM = 64


def pick_mask(pick):
    return (lane_iota((1, ADAPT)) // RANK) == pick


def norm_stats(values):
    centre = jnp.sum(values, axis=1, keepdims=True) * (1.0 / D)
    shifted = values - centre
    spread = jnp.sum(shifted * shifted, axis=1, keepdims=True) * (1.0 / D)
    inverse = lax.rsqrt(spread + 1e-06)
    return shifted * inverse, inverse


def norm_back(grad, gain, unit, inverse):
    scaled = grad * gain
    total = jnp.sum(scaled, axis=1, keepdims=True) * (1.0 / D)
    along = jnp.sum(scaled * unit, axis=1, keepdims=True) * (1.0 / D)
    return inverse * (scaled - total - unit * along)


def qkv_copies(place_ref, blocks, own_b, scratch, sem):
    w_qkv, a_qkv, b_qkv = scratch
    row, col = place_ref[0], place_ref[1]
    copies = []

    def copy(source, target):
        copies.append(pltpu.make_async_copy(source, target, sem.at[len(copies)]))

    for t in range(2):
        half_at = pl.multiple_of((row ^ t) * 384, 128)
        for s in range(4):
            block = blocks[4 * t + s]
            at = pl.multiple_of((col ^ s) * 192, 64)
            low_at = pl.multiple_of((col ^ s) * 192 + (row ^ t) * 96, 32)
            for p in range(3):
                copy(block.at[pl.ds(192 * p, 192)], w_qkv.at[p, pl.ds(at, 192), pl.ds(half_at, 384)])
                copy(block.at[pl.ds(576, 96), pl.ds(128 * p, 128)], a_qkv.at[p, pl.ds(low_at, 96), :])
        for p in range(3):
            source = own_b.at[p] if t == 0 else blocks[4].at[pl.ds(W_ROWS + 128 * p, 128)]
            copy(source, b_qkv.at[p, :, pl.ds(half_at, 384)])
    return copies


def out_copies(place_ref, far_block, own_a, out_w, scratch, sem):
    w_out, a_out = scratch
    row = place_ref[0]
    copies = []

    def copy(source, target):
        copies.append(pltpu.make_async_copy(source, target, sem.at[len(copies)]))

    for t in range(2):
        half_at = pl.multiple_of((row ^ t) * 384, 128)
        copy(out_w[t].at[pl.ds(0, 384)], w_out.at[pl.ds(half_at, 384), :])
        for j in range(3):
            if t == 0:
                source = own_a.at[pl.ds(128 * j, 128)]
            else:
                source = far_block.at[pl.ds(W_ROWS + 384, 128), pl.ds(128 * j, 128)]
            copy(source, a_out.at[pl.ds(half_at + 128 * j, 128), :])
    return copies


W_ROWS = 944
QKV_SCRATCH = [
    pltpu.VMEM((3, D, D), bf16),
    pltpu.VMEM((3, D, ADAPT), bf16),
    pltpu.VMEM((3, ADAPT, D), bf16),
    pltpu.SemaphoreType.DMA((54,)),
]
OUT_SCRATCH = [
    pltpu.VMEM((D, D), bf16),
    pltpu.VMEM((D, ADAPT), bf16),
    pltpu.SemaphoreType.DMA((8,)),
]


def split_kernel(place_ref, tokens_ref, cot_ref, own_out, one_out, two_out, three_out, left, right, stage, sem):
    rows = tokens_ref.shape[0]
    width = D // 4
    left[0:rows, 0:width] = tokens_ref[...].astype(f32)
    right[0:rows, 0:width] = cot_ref[...].astype(f32)
    lane = lane_iota((1, 128))
    real = lax.broadcasted_iota(jnp.int32, (SEQP, 1), 0) < SEQ
    for i in range(8):
        at = slice(SEQ * i, SEQ * i + SEQP)
        spot = slice(SEQP * (i % 2), SEQP * (i % 2) + SEQP)
        moved = pltpu.roll(right[at, :], 64, 1)
        middle = jnp.where(lane < 64, left[at, 128:256], moved[:, 0:128])
        stage[i // 2, spot, 0:128] = jnp.where(real, left[at, 0:128], 0.0).astype(bf16)
        stage[i // 2, spot, 128:256] = jnp.where(real, middle, 0.0).astype(bf16)
        stage[i // 2, spot, 256:384] = jnp.where(real, moved[:, 128:256], 0.0).astype(bf16)
    copies = [
        pltpu.make_async_copy(stage.at[place_ref[1] ^ s], out, sem.at[s])
        for s, out in enumerate((own_out, one_out, two_out, three_out))
    ]
    for copy in copies:
        copy.start()
    for copy in copies:
        copy.wait()


def split_call(place, tokens, cotangent):
    rows = tokens.shape[0]
    tall = -(-(SEQ * 7 + SEQP) // 8) * 8
    inside = pl.BlockSpec(memory_space=pltpu.VMEM)
    return pl.pallas_call(
        split_kernel,
        grid_spec=pltpu.PrefetchScalarGridSpec(
            num_scalar_prefetch=1,
            grid=(1,),
            in_specs=[inside, inside],
            out_specs=[ANYWHERE] * 4,
            scratch_shapes=[
                pltpu.VMEM((tall, 256), f32),
                pltpu.VMEM((tall, 256), f32),
                pltpu.VMEM((4, BLK, 384), bf16),
                pltpu.SemaphoreType.DMA((4,)),
            ],
        ),
        out_shape=[jax.ShapeDtypeStruct((BLK, 384), bf16)] * 4,
        compiler_params=pltpu.CompilerParams(vmem_limit_bytes=32 * 1024 * 1024),
        cost_estimate=pl.CostEstimate(flops=1_000_000_000, bytes_accessed=3_000_000, transcendentals=0),
    )(place, tokens, cotangent)


def attend_kernel(picks_ref, place_ref, *refs):
    blocks, refs = refs[:8], refs[8:]
    (
        own_b, own_a, out_near, out_far, x_ref, gain_one, gain_two, b_out,
        two_out, resid_out, normed_out, qkv_out, mixed_out, probs_out, lows_out,
        w_qkv, a_qkv, b_qkv, qkv_sem, w_out, a_out, out_sem,
    ) = refs
    image = pl.program_id(0)

    @pl.when(image == 0)
    def start():
        copies = qkv_copies(place_ref, blocks, own_b, (w_qkv, a_qkv, b_qkv), qkv_sem)
        copies += out_copies(place_ref, blocks[4], own_a, (out_near, out_far), (w_out, a_out), out_sem)
        for copy in copies:
            copy.start()
        for copy in copies:
            copy.wait()

    mask = pick_mask(picks_ref[image])
    x = x_ref[...].astype(f32)
    unit, unused = norm_stats(x)
    normed = (unit * gain_one[...]).astype(bf16)
    normed_out[...] = normed
    for p in range(3):
        low = jnp.where(mask, dot(normed, a_qkv[p]), 0.0).astype(bf16)
        lows_out[:, 128 * p : 128 * p + 128] = low
        qkv_out[p] = (dot(normed, w_qkv[p]) + dot(low, b_qkv[p])).astype(bf16)
    lane = lane_iota((1, 128))
    key_lane = lane_iota((1, SEQP))
    for pair in range(HEADS // 2):
        at = slice(128 * pair, 128 * pair + 128)
        q = qkv_out[0, :, at]
        k = qkv_out[1, :, at]
        v = qkv_out[2, :, at]
        parts = []
        for side in range(2):
            own = (lane // HEAD_DIM) == side
            scores = dot_nt(jnp.where(own, q, jnp.zeros_like(q)), k) * (HEAD_DIM**-0.5)
            scores = jnp.where(key_lane < SEQ, scores, -1e30)
            power = jnp.exp(scores - jnp.max(scores, axis=1, keepdims=True))
            probs = (power / jnp.sum(power, axis=1, keepdims=True)).astype(bf16)
            probs_out[0, 2 * pair + side] = probs
            parts.append(dot(probs, v))
        mixed_out[:, at] = jnp.where(lane < HEAD_DIM, parts[0], parts[1]).astype(bf16)
    mixed = mixed_out[...]
    low = jnp.where(mask, dot(mixed, a_out[...]), 0.0).astype(bf16)
    lows_out[:, 384:512] = low
    resid = x + dot(mixed, w_out[...]) + dot(low, b_out[...])
    resid_out[...] = resid
    unit, unused = norm_stats(resid)
    real = lax.broadcasted_iota(jnp.int32, (SEQP, 1), 0) < SEQ
    two_out[...] = jnp.where(real, unit * gain_two[...], 0.0).astype(bf16)


def image_rows(lanes):
    return pl.BlockSpec((SEQP, lanes), lambda i, *_: (i, 0))


def kept(*shape):
    return pl.BlockSpec(shape, lambda i, *_: (0,) * len(shape))


QKV_SPEC = pl.BlockSpec((3, SEQP, D), lambda i, *_: (0, i, 0))
PROBS_SPEC = pl.BlockSpec((1, HEADS, SEQP, SEQP), lambda i, *_: (i, 0, 0, 0))
ANYWHERE = pl.BlockSpec(memory_space=pl.ANY)


def attend_call(picks, place, blocks, own_b, own_a, out_w, x, gain_one, gain_two, b_out):
    rows = x.shape[0]
    return pl.pallas_call(
        attend_kernel,
        grid_spec=pltpu.PrefetchScalarGridSpec(
            num_scalar_prefetch=2,
            grid=(2,),
            in_specs=[ANYWHERE] * (len(blocks) + 4)
            + [image_rows(D), kept(1, D), kept(1, D), kept(ADAPT, D)],
            out_specs=[
                image_rows(D), image_rows(D), image_rows(D), QKV_SPEC,
                image_rows(D), PROBS_SPEC, image_rows(512),
            ],
            scratch_shapes=QKV_SCRATCH + OUT_SCRATCH,
        ),
        out_shape=[
            jax.ShapeDtypeStruct((rows, D), bf16),
            jax.ShapeDtypeStruct((rows, D), f32),
            jax.ShapeDtypeStruct((rows, D), bf16),
            jax.ShapeDtypeStruct((3, rows, D), bf16),
            jax.ShapeDtypeStruct((rows, D), bf16),
            jax.ShapeDtypeStruct((2, HEADS, SEQP, SEQP), bf16),
            jax.ShapeDtypeStruct((rows, 512), bf16),
        ],
        compiler_params=pltpu.CompilerParams(vmem_limit_bytes=48 * 1024 * 1024),
        cost_estimate=pl.CostEstimate(flops=4_000_000_000, bytes_accessed=15_000_000, transcendentals=2_000_000),
    )(picks, place, *blocks, own_b, own_a, *out_w, x, gain_one, gain_two, b_out)


def out_back_kernel(picks_ref, place_ref, *refs):
    (
        far_block, own_a, out_near, out_far, gain_two, b_out, two_ref, resid_ref, mixed_ref, lows_ref,
        cot_ref, grad_a, grad_b, w_router, a_router, b_router, a_up, b_down,
        resid_grad_out, mixed_grad_out, base_out, both_out, a_part_out, b_part_out,
        w_out, a_out, sem, both, a_part, b_part,
    ) = refs
    image = pl.program_id(0)

    @pl.when(image == 0)
    def start():
        copies = out_copies(place_ref, far_block, own_a, (out_near, out_far), (w_out, a_out), sem)
        for copy in copies:
            copy.start()
        for part in (both, a_part, b_part):
            part[...] = jnp.zeros_like(part)
        for copy in copies:
            copy.wait()

    mask = pick_mask(picks_ref[image])
    lane = lane_iota((1, 128))

    def add_part(row, value):
        at = slice(row, row + value.shape[0])
        both[at, :] += value

    two = two_ref[...]
    received = grad_a[...].astype(f32) + grad_b[...].astype(f32)
    low_r = jnp.where(mask, dot(two, a_router[...]), 0.0).astype(bf16)
    logits = dot(two, w_router[...]) + dot(low_r, b_router[...])
    logits = jnp.where(lane < EXPERTS, logits, -1e30)
    power = jnp.exp(logits - jnp.max(logits, axis=1, keepdims=True))
    probs = power / jnp.sum(power, axis=1, keepdims=True)
    last = received[:, D:]
    grad_probs = jnp.where(lane < EXPERTS, last, 0.0)
    low_in = jnp.where(mask, repeat_lanes(jnp.where((lane >= 32) & (lane < 48), last, 0.0)), 0.0).astype(bf16)
    low_out = jnp.where(mask, repeat_lanes(jnp.where((lane >= 48) & (lane < 64), last, 0.0)), 0.0).astype(bf16)
    cot = cot_ref[...]
    resid = resid_ref[...]
    base_out[...] = resid + dot(low_out, b_down[...])
    add_part(768, dot_tn(two, low_in))
    add_part(1536, dot_tn(cot, low_out))
    grad_logits = probs * (grad_probs - jnp.sum(probs * grad_probs, axis=1, keepdims=True))
    grad_logits = grad_logits.astype(bf16)
    grad_low = jnp.where(mask, dot_nt(grad_logits, b_router[...]), 0.0).astype(bf16)
    grad_two = received[:, :D] + dot_nt(low_in, a_up[...])
    grad_two = grad_two + dot_nt(grad_logits, w_router[...]) + dot_nt(grad_low, a_router[...])
    add_part(0, dot_tn(two, grad_low))
    add_part(2304, dot_tn(grad_logits, low_r))
    unit, inverse = norm_stats(resid)
    grad_resid = cot.astype(f32) + norm_back(grad_two, gain_two[...], unit, inverse)
    resid_grad_out[...] = grad_resid
    grad_attn = grad_resid.astype(bf16)
    grad_low = jnp.where(mask, dot_nt(grad_attn, b_out[...]), 0.0).astype(bf16)
    mixed_grad_out[...] = (dot_nt(grad_attn, w_out[...]) + dot_nt(grad_low, a_out[...])).astype(bf16)
    a_part[...] += dot_tn(mixed_ref[...], grad_low)
    b_part[...] += dot_tn(grad_attn, lows_ref[:, 384:512])

    @pl.when(image == 1)
    def finish():
        both_out[...] = both[...].astype(bf16)
        a_part_out[...] = a_part[...].astype(bf16)
        b_part_out[...] = b_part[...].astype(bf16)


BOTH_ROWS = 2560


def out_back_call(picks, place, far_block, own_a, out_w, gain_two, b_out, two, resid, mixed, lows, cot, grad_a, grad_b,
                  w_router, a_router, b_router, a_up, b_down):
    rows = two.shape[0]
    return pl.pallas_call(
        out_back_kernel,
        grid_spec=pltpu.PrefetchScalarGridSpec(
            num_scalar_prefetch=2,
            grid=(2,),
            in_specs=[ANYWHERE] * 4
            + [kept(1, D), kept(ADAPT, D), image_rows(D), image_rows(D), image_rows(D), image_rows(512)]
            + [image_rows(D), image_rows(D + 128), image_rows(D + 128)]
            + [kept(D, 128), kept(D, ADAPT), kept(ADAPT, 128), kept(D, ADAPT), kept(ADAPT, D)],
            out_specs=[image_rows(D), image_rows(D), image_rows(D), kept(BOTH_ROWS, 128), kept(D, 128), kept(D, 128)],
            scratch_shapes=OUT_SCRATCH
            + [pltpu.VMEM((BOTH_ROWS, 128), f32), pltpu.VMEM((D, 128), f32), pltpu.VMEM((D, 128), f32)],
        ),
        out_shape=[
            jax.ShapeDtypeStruct((rows, D), f32),
            jax.ShapeDtypeStruct((rows, D), bf16),
            jax.ShapeDtypeStruct((rows, D), f32),
            jax.ShapeDtypeStruct((BOTH_ROWS, 128), bf16),
            jax.ShapeDtypeStruct((D, 128), bf16),
            jax.ShapeDtypeStruct((D, 128), bf16),
        ],
        compiler_params=pltpu.CompilerParams(vmem_limit_bytes=48 * 1024 * 1024),
        cost_estimate=pl.CostEstimate(flops=6_000_000_000, bytes_accessed=15_000_000, transcendentals=100_000),
    )(picks, place, far_block, own_a, *out_w, gain_two, b_out, two, resid, mixed, lows, cot, grad_a, grad_b,
      w_router, a_router, b_router, a_up, b_down)


def qkv_back_kernel(picks_ref, place_ref, *refs):
    blocks, refs = refs[:8], refs[8:]
    (
        own_b, x_ref, gain_one, normed_ref, qkv_ref, probs_ref, lows_ref, resid_grad, grad_mixed,
        tokens_out, a_part_out, b_part_out,
        w_qkv, a_qkv, b_qkv, sem, a_part, b_part, grads,
    ) = refs
    image = pl.program_id(0)
    copies = qkv_copies(place_ref, blocks, own_b, (w_qkv, a_qkv, b_qkv), sem)

    @pl.when(image == 0)
    def start():
        for copy in copies:
            copy.start()
        a_part[...] = jnp.zeros_like(a_part)
        b_part[...] = jnp.zeros_like(b_part)

    mask = pick_mask(picks_ref[image])
    lane = lane_iota((1, 128))
    for pair in range(HEADS // 2):
        at = slice(128 * pair, 128 * pair + 128)
        q = qkv_ref[0, :, at]
        k = qkv_ref[1, :, at]
        v = qkv_ref[2, :, at]
        gm = grad_mixed[:, at]
        found = []
        for side in range(2):
            own = (lane // HEAD_DIM) == side
            weights = probs_ref[0, 2 * pair + side]
            weights_f = weights.astype(f32)
            grad_w = dot_nt(jnp.where(own, gm, jnp.zeros_like(gm)), v)
            inner = jnp.sum(weights_f * grad_w, axis=1, keepdims=True)
            grad_s = (weights_f * (grad_w - inner)).astype(bf16)
            found.append(
                (
                    dot(grad_s, k) * (HEAD_DIM**-0.5),
                    dot_tn(grad_s, q) * (HEAD_DIM**-0.5),
                    dot_tn(weights, gm),
                )
            )
        for p in range(3):
            grads[p, :, at] = jnp.where(lane < HEAD_DIM, found[0][p], found[1][p]).astype(bf16)

    @pl.when(image == 0)
    def arrived():
        for copy in copies:
            copy.wait()

    normed = normed_ref[...]
    grad_normed = jnp.zeros((SEQP, D), f32)
    for p in range(3):
        piece = grads[p]
        grad_low = jnp.where(mask, dot_nt(piece, b_qkv[p]), 0.0).astype(bf16)
        grad_normed = grad_normed + dot_nt(piece, w_qkv[p]) + dot_nt(grad_low, a_qkv[p])
        a_part[D * p : D * p + D, :] += dot_tn(normed, grad_low)
        b_part[D * p : D * p + D, :] += dot_tn(piece, lows_ref[:, 128 * p : 128 * p + 128])
    unit, inverse = norm_stats(x_ref[...].astype(f32))
    tokens_out[...] = (resid_grad[...] + norm_back(grad_normed, gain_one[...], unit, inverse)).astype(bf16)

    @pl.when(image == 1)
    def finish():
        a_part_out[...] = a_part[...].astype(bf16)
        b_part_out[...] = b_part[...].astype(bf16)


def qkv_back_call(picks, place, blocks, own_b, x, gain_one, normed, qkv, probs, lows, resid_grad, grad_mixed):
    rows = x.shape[0]
    return pl.pallas_call(
        qkv_back_kernel,
        grid_spec=pltpu.PrefetchScalarGridSpec(
            num_scalar_prefetch=2,
            grid=(2,),
            in_specs=[ANYWHERE] * (len(blocks) + 1)
            + [image_rows(D), kept(1, D), image_rows(D), QKV_SPEC, PROBS_SPEC, image_rows(512)]
            + [image_rows(D), image_rows(D)],
            out_specs=[image_rows(D), kept(3 * D, 128), kept(3 * D, 128)],
            scratch_shapes=QKV_SCRATCH
            + [
                pltpu.VMEM((3 * D, 128), f32),
                pltpu.VMEM((3 * D, 128), f32),
                pltpu.VMEM((3, SEQP, D), bf16),
            ],
        ),
        out_shape=[
            jax.ShapeDtypeStruct((rows, D), bf16),
            jax.ShapeDtypeStruct((3 * D, 128), bf16),
            jax.ShapeDtypeStruct((3 * D, 128), bf16),
        ],
        compiler_params=pltpu.CompilerParams(vmem_limit_bytes=48 * 1024 * 1024),
        cost_estimate=pl.CostEstimate(flops=9_000_000_000, bytes_accessed=15_000_000, transcendentals=1000),
    )(picks, place, *blocks, own_b, x, gain_one, normed, qkv, probs, lows, resid_grad, grad_mixed)


TABLES = (((0, 0), (1, 0)), ((0, 1), (0, 2), (1, 1), (1, 2)), ((0, 3), (1, 3)))


def across_row(value):
    return lax.ppermute(value, "row", [(0, 1), (1, 0)])


def across_col(value, step):
    return lax.ppermute(value, "col", [(i, i ^ step) for i in range(4)])


def by_place(blocks, col):
    found = []
    for place in range(4):
        value = blocks[place]
        for other in range(1, 4):
            value = jnp.where(col == other, blocks[place ^ other], value)
        found.append(value)
    return found


def across_chip(value, first, second):
    pairs = [(i, i ^ first) for i in range(4)] + [(4 + i, 4 + (i ^ second)) for i in range(4)]
    return lax.ppermute(value, ("row", "col"), pairs)


def gather_col(value, row):
    from_x = across_col(value, 1)
    from_y = across_col(value, 2)
    return [value, from_x, from_y, across_chip(jnp.where(row == 0, from_x, from_y), 2, 1)]


def across_pair(first, second):
    both = across_row(jnp.stack([first, second]))
    return both[0], both[1]


def added(*values):
    total = values[0].astype(f32)
    for value in values[1:]:
        total = total + value.astype(f32)
    return total


def row_sum(near, far):
    cut = 2 * BLK
    sent = across_row(far[cut:])
    kept_rows = across_row(far[:cut])
    return added(near[cut:], sent).astype(bf16), added(near[:cut], kept_rows).astype(bf16)


def last_exchange(kept_rows, got):
    sent = added(kept_rows[BLK:], got[BLK:]).astype(bf16)
    return added(kept_rows[:BLK], got[:BLK]).astype(bf16), across_chip(sent, 2, 1)


def at_place(value, axis, place):
    return lax.dynamic_index_in_dim(value, place, axis, keepdims=False)


def reduce_dp(value):
    n_dp = lax.axis_size("dp")
    if n_dp != 4:
        return lax.psum(value, "dp")
    place = lax.axis_index("dp")

    def across(part, step):
        return lax.ppermute(part, "dp", [(i, i ^ step) for i in range(4)])

    view = value.reshape(4, -1, 128)
    found = [at_place(view, 0, place)]
    for s in range(1, 4):
        found.append(across(at_place(view, 0, place ^ s), s))
    total = added(*found).astype(bf16)
    blocks = [total] + [across(total, s) for s in range(1, 4)]
    return jnp.concatenate(by_place(blocks, place))


def part_share(col_parts, row_parts, both_parts, place):
    col_parts = at_place(col_parts.reshape(4, 4, 2, 96, 128), 2, place)
    row_parts = at_place(row_parts.reshape(4, 2, 4, 96, 128), 1, place)
    both_parts = at_place(both_parts.reshape(2, 4, BOTH_ROWS // 8, 128), 0, place)
    col_parts = col_parts.swapaxes(0, 1).reshape(4, 384, 128)
    row_parts = row_parts.swapaxes(0, 1).reshape(4, 384, 128)
    return jnp.concatenate([col_parts, row_parts, both_parts], axis=1)


def reduce_col(value, col):
    found = [at_place(value, 0, col)]
    for s in range(1, 4):
        found.append(across_col(at_place(value, 0, col ^ s), s))
    return added(*found).astype(bf16)


def spread_parts(mine, row, col):
    spread = mine[384:]
    spread = by_place([spread] + [across_col(spread, s) for s in range(1, 4)], col)
    row_sums = jnp.stack([one[:384].reshape(4, 96, 128) for one in spread], axis=1).reshape(4, 384, 128)
    near = jnp.concatenate([mine[:384]] + [one[384:] for one in spread])
    far = across_row(near)
    first = jnp.where(row == 0, near, far)
    second = jnp.where(row == 0, far, near)
    col_sums = jnp.stack([first[:384].reshape(4, 96, 128), second[:384].reshape(4, 96, 128)], axis=1).reshape(4, 192, 128)
    both_sums = jnp.concatenate([first[384:], second[384:]])
    return col_sums, row_sums, both_sums


def to_features(value, col):
    width = D // 4
    chunks = by_place([value[:, width * p : width * p + width] for p in range(4)], col)
    sent = [jnp.concatenate([chunk[:SEQP], chunk[SEQP:]], axis=1) for chunk in chunks]
    got = [sent[0]] + [across_col(sent[s], s) for s in range(1, 4)]
    rows = []
    for block in by_place(got, col):
        rows += [block[:SEQ, :width], block[:SEQ, width:]]
    return jnp.concatenate(rows, axis=0)


def on_device(
    tokens, cotangent, routes, adapter_pick, gain_attn, gain_moe, w_qkv, w_out, w_router, w_up, w_down,
    a_qkv, b_qkv, a_out, b_out, a_router, b_router, a_up, b_up, a_down, b_down,
):
    row = lax.axis_index("row")
    col = lax.axis_index("col")
    me = row * 4 + col
    place = jnp.stack([row, col]).astype(jnp.int32)

    width = D // 4
    pairs = split_call(place, tokens, cotangent)
    pairs = by_place([pairs[0]] + [across_col(pairs[s], s) for s in range(1, 4)], col)
    x = jnp.concatenate([pair[:, :width] for pair in pairs], axis=1)
    cot = jnp.concatenate([pair[:, width:] for pair in pairs], axis=1)
    half = D // 2
    gains = []
    for gain in (gain_attn, gain_moe):
        left = gain
        for unused in range(3):
            lead = lax.reduce_precision(left, 8, 7)
            gains.append(lead.astype(bf16))
            left = left - lead
    small = jnp.concatenate([w_out, b_out, jnp.stack(gains), jnp.zeros((26, width), bf16)], axis=0)
    low = at_place(a_qkv.reshape(3, 2, 96, ADAPT), 1, row)
    packed = jnp.concatenate(
        [w_qkv.reshape(576, half), jnp.concatenate([low[0], low[1], low[2]], axis=1),
         jnp.concatenate([small[:272], small[272:]], axis=1)]
    )
    for_row = jnp.concatenate(
        [packed, b_qkv.reshape(half, half), jnp.concatenate([a_out[:128], a_out[128:256], a_out[256:]], axis=1)]
    )
    near = gather_col(packed, row)
    far = [across_row(for_row), *across_pair(near[1], near[2]), across_row(near[3])]
    blocks = near + far

    def assembled(group):
        parts = by_place([block[672:944] for block in group], col)
        return jnp.concatenate(
            [jnp.concatenate([part[:, :width] for part in parts], axis=1),
             jnp.concatenate([part[:, width:] for part in parts], axis=1)], axis=0
        )

    out_w = [assembled(near), assembled(far)]
    full_b_out = out_w[0][384:512]
    gain_rows = out_w[0][512:518].astype(f32)
    gain_one = jnp.sum(gain_rows[:3], axis=0, keepdims=True)
    gain_two = jnp.sum(gain_rows[3:], axis=0, keepdims=True)

    picks_group = lax.dynamic_slice_in_dim(adapter_pick, lax.axis_index("dp") * IMG_GRP, IMG_GRP)
    order = jnp.arange(IMG_GRP, dtype=jnp.int32)
    picks = jnp.take(picks_group, ((order // 2) ^ me) * 2 + order % 2)
    spot_picks = jnp.sum(
        jnp.where(block_spot(order // 2, row, col)[None, :] * 2 + order[None, :] % 2 == order[:, None], picks_group[None, :], 0), axis=1
    )
    token_list, tile_experts = routing(routes, row, col)
    wide_router = jnp.concatenate([w_router, w_router, jnp.zeros((D, 64), bf16)], axis=1)
    wide_b_router = jnp.concatenate([b_router, b_router, jnp.zeros((ADAPT, 64), bf16)], axis=1)
    slim_router = jnp.concatenate([w_router, jnp.zeros((D, 96), bf16)], axis=1)
    slim_b_router = jnp.concatenate([b_router, jnp.zeros((ADAPT, 96), bf16)], axis=1)

    x, token_list, tile_experts = lax.optimization_barrier((x, token_list, tile_experts))
    cot, unused = lax.optimization_barrier((cot, near[3]))
    two, resid, normed, qkv, mixed, probs, lows = attend_call(
        picks, place, blocks, b_qkv, a_out, out_w, x, gain_one, gain_two, full_b_out
    )
    cot_near = gather_col(cot, row)
    two_near = gather_col(two, row)

    def table(spots, twos, cots):
        return table_call(
            jnp.stack([picks[8 * t + 2 * s + side] for t, s in spots for side in range(2)]),
            twos, cots, a_up, b_down, wide_router, a_router, wide_b_router,
        )

    cot_far = [across_row(cot), *across_pair(cot_near[1], cot_near[2]), across_row(cot_near[3])]
    tables = [table(TABLES[0], [two, across_row(two)], [cot, cot_far[0]])]
    two_x, two_y = across_pair(two_near[1], two_near[2])
    tables.append(table(TABLES[1], [two_near[1], two_near[2], two_x, two_y], [cot_near[1], cot_near[2], cot_far[1], cot_far[2]]))
    diag, *tables = lax.optimization_barrier((two_near[3], *tables))
    tables.append(table(TABLES[2], [diag, across_row(diag)], [cot_near[3], cot_far[3]]))
    sum_near, sum_far, grad_near, grad_far, part_b_up, part_a_down = moe_call(
        token_list, tile_experts, spot_picks, place, tables, TABLES, w_up, w_down, b_up, a_down
    )
    grad_sent, grad_kept = row_sum(grad_near, grad_far)
    grad_sent, sum_near, sum_far, part_b_up, part_a_down = lax.optimization_barrier(
        (grad_sent, sum_near, sum_far, part_b_up, part_a_down)
    )
    grad_got = across_chip(grad_sent, 1, 2)
    sum_sent, sum_kept = row_sum(sum_near, sum_far)
    grad_got, sum_sent, sum_kept = lax.optimization_barrier((grad_got, sum_sent, sum_kept))
    grad_a, grad_b = last_exchange(grad_kept, grad_got)
    grad_b, sum_sent, sum_kept = lax.optimization_barrier((grad_b, sum_sent, sum_kept))
    sums = [
        sum_kept[:BLK],
        across_chip(sum_kept[BLK:], 2, 1),
        across_chip(sum_sent[:BLK], 1, 2),
        across_chip(sum_sent[BLK:], 3, 3),
    ]
    resid_grad, mixed_grad, base, both_parts, part_a_out, part_b_out = out_back_call(
        picks, place, blocks[4], a_out, out_w, gain_two, full_b_out, two, resid, mixed, lows, cot, grad_a, grad_b,
        slim_router, a_router, slim_b_router, a_up, b_down,
    )
    grad_tokens, part_a_qkv, part_b_qkv = qkv_back_call(
        picks, place, blocks, b_qkv, x, gain_one, normed, qkv, probs, lows, resid_grad, mixed_grad
    )
    part_a_qkv, part_b_qkv, *sums = lax.optimization_barrier((part_a_qkv, part_b_qkv, *sums))
    col_parts = jnp.concatenate([part_a_qkv, part_b_out])
    row_parts = jnp.concatenate([part_b_qkv, part_a_out])
    theirs = across_row(part_share(col_parts, row_parts, both_parts, 1 - row))
    shared = added(part_share(col_parts, row_parts, both_parts, row), theirs).astype(bf16)
    mine = reduce_col(shared, col)
    part_rows = mine.shape[0]
    mine, grad_tokens, base = lax.optimization_barrier((mine, grad_tokens, base))
    grad_tokens = to_features(grad_tokens, col).astype(f32)
    block_out = to_features((base + added(*sums)).astype(bf16), col)
    mine = reduce_dp(jnp.concatenate([mine, part_b_up.astype(bf16), part_a_down.astype(bf16)]))
    dp_sums = mine[part_rows:]
    col_sums, row_sums, both_sums = spread_parts(mine[:part_rows], row, col)
    col_sums = col_sums.astype(f32)
    row_sums = row_sums.astype(f32)
    both_sums = both_sums.astype(f32)
    dp_sums = dp_sums.astype(f32)
    return (
        block_out,
        grad_tokens,
        col_sums[:3],
        jnp.swapaxes(row_sums[:3], 1, 2),
        row_sums[3],
        col_sums[3].T,
        both_sums[:768],
        both_sums[2304:2336].T,
        both_sums[768:1536],
        dp_sums[:384].T,
        dp_sums[384:],
        both_sums[1536:2304].T,
    )


def solution(mesh):
    return jax.shard_map(
        on_device,
        mesh=mesh,
        in_specs=(
            P(("dp", "row"), "col"),
            P(("dp", "row"), "col"),
            P("dp", None),
            P(),
            P("col"),
            P("col"),
            P(None, "col", "row"),
            P("row", "col"),
            P(),
            P(None, None, ("row", "col")),
            P(None, ("row", "col"), None),
            P(None, "col", None),
            P(None, None, "row"),
            P("row", None),
            P(None, "col"),
            P(),
            P(),
            P(),
            P(None, ("row", "col")),
            P(("row", "col"), None),
            P(),
        ),
        out_specs=(
            P(("dp", "row"), "col"),
            P(("dp", "row"), "col"),
            P(None, "col", None),
            P(None, None, "row"),
            P("row", None),
            P(None, "col"),
            P(),
            P(),
            P(),
            P(None, ("row", "col")),
            P(("row", "col"), None),
            P(),
        ),
        check_vma=False,
    )
```

```python
import jax
import jax.numpy as jnp
from jax import lax
from jax.experimental import pallas as pl
from jax.experimental.pallas import tpu as pltpu
from jax.sharding import PartitionSpec as P

D = 768
EXPERTS = 32
SEQ = 197
SEQP = 208
RANK = 16
ADAPT = 128
IMG_GRP = 16
TOK = IMG_GRP * SEQP
BLK = 2 * SEQP
DUMMY = SEQ
TILE = 192
f32 = jnp.float32
bf16 = jnp.bfloat16


def max_tiles():
    return (2 * IMG_GRP * SEQ) // TILE + EXPERTS + 1


def dot(left, right):
    return jnp.dot(left, right, preferred_element_type=f32)


def dot_nt(left, right):
    return lax.dot_general(left, right, (((1,), (1,)), ((), ())), preferred_element_type=f32)


def dot_tn(left, right):
    return lax.dot_general(left, right, (((0,), (0,)), ((), ())), preferred_element_type=f32)


def lane_iota(shape):
    return lax.broadcasted_iota(jnp.int32, shape, len(shape) - 1)


def repeat_lanes(value):
    for shift in (16, 32, 64):
        value = value + pltpu.roll(value, shift, 1)
    return value


def table_kernel(n_blocks, picks_ref, *refs):
    x_blocks = refs[:n_blocks]
    c_blocks = refs[n_blocks : 2 * n_blocks]
    a_up, b_down, w_router, a_router, b_router, table_out, xin, cin, rows_x, rows_c, sem = refs[2 * n_blocks :]
    image = pl.program_id(0)
    lane = lane_iota((1, 128))

    @pl.when(image == 0)
    def start():
        copies = []
        for blocks, place in ((x_blocks, xin), (c_blocks, cin)):
            for b, block in enumerate(blocks):
                copies.append(pltpu.make_async_copy(block, place.at[pl.ds(b * BLK, BLK)], sem.at[len(copies)]))
        for copy in copies:
            copy.start()
        for copy in copies:
            copy.wait()

    row = pl.multiple_of(image * SEQP, 16)
    mask = (lane // RANK) == picks_ref[image]
    x = xin[pl.ds(row, SEQP), :]
    c = cin[pl.ds(row, SEQP), :]
    flat_x = rows_x.reshape(SEQP * 8, 128)
    flat_c = rows_c.reshape(SEQP * 8, 128)
    low_x = jnp.where(mask, dot(x, a_up[...]), 0.0)
    low_c = jnp.where(mask, dot_nt(c, b_down[...]), 0.0)
    low_r = jnp.where(mask, dot(x, a_router[...]), 0.0).astype(bf16)
    logits = dot(x, w_router[...]) + dot(low_r, b_router[...])
    logits = jnp.where(lane < 2 * EXPERTS, logits, -1e30)
    power = jnp.exp(logits - jnp.max(logits, axis=1, keepdims=True))
    total = jnp.sum(jnp.where(lane < EXPERTS, power, 0.0), axis=1, keepdims=True)
    probs = power / total
    lead = probs.astype(bf16).astype(f32)
    probs = jnp.where(lane < EXPERTS, lead, probs - lead)
    for j in range(6):
        flat_x[pl.ds(j, SEQP, 8), :] = x[:, 128 * j : 128 * j + 128].astype(f32)
        flat_c[pl.ds(j, SEQP, 8), :] = c[:, 128 * j : 128 * j + 128].astype(f32)
    flat_x[pl.ds(6, SEQP, 8), :] = low_x
    flat_x[pl.ds(7, SEQP, 8), :] = probs
    flat_c[pl.ds(6, SEQP, 8), :] = low_c
    flat_c[pl.ds(7, SEQP, 8), :] = jnp.zeros((SEQP, 128), f32)
    table_out[...] = jnp.concatenate([rows_x[...], rows_c[...]], axis=1).astype(bf16)


def table_call(picks, x_blocks, c_blocks, a_up, b_down, w_router, a_router, b_router):
    n = len(x_blocks)

    def whole(*shape):
        return pl.BlockSpec(shape, lambda e, *_: (0,) * len(shape))

    anywhere = pl.BlockSpec(memory_space=pl.ANY)
    return pl.pallas_call(
        lambda *refs: table_kernel(n, *refs),
        grid_spec=pltpu.PrefetchScalarGridSpec(
            num_scalar_prefetch=1,
            grid=(2 * n,),
            in_specs=[anywhere] * (2 * n)
            + [whole(D, ADAPT), whole(ADAPT, D), whole(D, 128), whole(D, ADAPT), whole(ADAPT, 128)],
            out_specs=pl.BlockSpec((SEQP, 16, 128), lambda i, *_: (i, 0, 0)),
            scratch_shapes=[
                pltpu.VMEM((n * BLK, D), bf16),
                pltpu.VMEM((n * BLK, D), bf16),
                pltpu.VMEM((SEQP, 8, 128), f32),
                pltpu.VMEM((SEQP, 8, 128), f32),
                pltpu.SemaphoreType.DMA((2 * n,)),
            ],
        ),
        out_shape=jax.ShapeDtypeStruct((n * BLK, 16, 128), bf16),
        compiler_params=pltpu.CompilerParams(vmem_limit_bytes=32 * 1024 * 1024),
        cost_estimate=pl.CostEstimate(flops=n * 3_000_000_000, bytes_accessed=n * 3_000_000, transcendentals=n * 60_000),
    )(picks, *x_blocks, *c_blocks, a_up, b_down, w_router, a_router, b_router)


def moe_kernel(places, list_ref, expert_ref, picks_ref, place_ref, *refs):
    n = len(places)
    tables = refs[:n]
    ep_outs, tg_outs = refs[n + 4 : n + 8], refs[n + 8 : n + 12]
    refs = refs[: n + 4] + refs[n + 12 :]
    (
        w_up_hbm, w_down_hbm, b_up, a_down,
        gbu_out, gad_out,
        table, acc_e, acc_t, in_x, in_c, out_e, out_t, xb, cb, w_up, w_down, stage_ep, stage_tg,
        in_sem, up_sem, down_sem, ep_sem, tg_sem,
    ) = refs[n:]
    acc_e_flat = acc_e.reshape(TOK * 8, 128)
    acc_t_flat = acc_t.reshape(TOK * 8, 128)
    in_x_flat = in_x.reshape(TILE * 8, 128)
    in_c_flat = in_c.reshape(TILE * 8, 128)
    out_e_flat = out_e.reshape(TILE * 8, 128)
    out_t_flat = out_t.reshape(TILE * 8, 128)
    lane = lane_iota((1, 128))
    n_tiles = expert_ref[max_tiles()]

    copies = []
    for piece, spots in zip(tables, places):
        for b, (t, s) in enumerate(spots):
            spot = 4 * t + jnp.where(place_ref[0] == t, swapped(s), s)
            copies.append(
                pltpu.make_async_copy(
                    piece.at[pl.ds(b * BLK, BLK)], table.at[pl.ds(pl.multiple_of(spot * BLK, 32), BLK)], in_sem.at[len(copies)]
                )
            )
    for copy in copies:
        copy.start()

    def weights(expert):
        slot = expert % 2
        return (
            pltpu.make_async_copy(w_up_hbm.at[expert], w_up.at[slot], up_sem.at[slot]),
            pltpu.make_async_copy(w_down_hbm.at[expert], w_down.at[slot], down_sem.at[slot]),
        )

    for copy in weights(0):
        copy.start()
    out_e[...] = jnp.zeros_like(out_e)
    out_t[...] = jnp.zeros_like(out_t)
    gbu_out[...] = jnp.zeros_like(gbu_out)
    gad_out[...] = jnp.zeros_like(gad_out)

    def clear(i, carry):
        acc_e[pl.ds(i * 64, 64)] = jnp.zeros((64, 8, 128), f32)
        acc_t[pl.ds(i * 64, 64)] = jnp.zeros((64, 8, 128), f32)
        return carry

    lax.fori_loop(0, TOK // 64, clear, 0)
    for copy in copies:
        copy.wait()

    def fetch(t):
        for i in range(TILE):
            both = table[list_ref[t * TILE + i]].astype(f32)
            in_x[i] = both[:8]
            in_c[i] = both[8:]

    def give(t):
        for b in range(TILE // 8):
            tokens = [list_ref[t * TILE + 8 * b + k] for k in range(8)]
            sums_e = [acc_e[tokens[k]] + out_e[8 * b + k] for k in range(8)]
            sums_t = [acc_t[tokens[k]] + out_t[8 * b + k] for k in range(8)]
            for k in range(8):
                acc_e[tokens[k]] = sums_e[k]
                acc_t[tokens[k]] = sums_t[k]

    fetch(0)

    def tile(t, carry):
        expert = expert_ref[t]
        slot = expert % 2

        @pl.when((t == 0) | (expert_ref[jnp.maximum(t - 1, 0)] != expert))
        def arrive():
            for copy in weights(expert):
                copy.wait()

            @pl.when(expert + 1 < EXPERTS)
            def ahead():
                for copy in weights(expert + 1):
                    copy.start()

        for j in range(7):
            xb[:, 128 * j : 128 * j + 128] = in_x_flat[pl.ds(j, TILE, 8), :].astype(bf16)
            cb[:, 128 * j : 128 * j + 128] = in_c_flat[pl.ds(j, TILE, 8), :].astype(bf16)
        spread = in_x_flat[pl.ds(7, TILE, 8), :]
        mine = (lane == expert) | (lane == expert + EXPERTS)
        gate = jnp.sum(jnp.where(mine, spread, 0.0), axis=1, keepdims=True)
        fetch(t + 1)
        give(jnp.maximum(t - 1, 0))
        hidden = dot(xb[:, :D], w_up[slot]) + dot(xb[:, D:], b_up[...])
        back = dot_nt(cb[:, :D], w_down[slot]) + dot_nt(cb[:, D:], a_down[...])
        cdf = 0.5 + 0.5 * lax.erf(hidden * 0.7071067811865476)
        slope = cdf + hidden * jnp.exp(hidden * hidden * -0.5) * 0.3989422804014327
        act = (hidden * cdf).astype(bf16)
        act_f = act.astype(f32)
        gate_grad = jnp.sum(act_f * back, axis=1, keepdims=True)
        grad_hidden = (gate * back * slope).astype(bf16)
        act_gate = (gate * act_f).astype(bf16)
        out_main = dot(act_gate, w_down[slot])
        out_low = dot(act_gate, a_down[...])
        in_main = dot_nt(grad_hidden, w_up[slot])
        in_low = dot_nt(grad_hidden, b_up[...])
        gbu_out[...] += dot_tn(grad_hidden, xb[:, D:])
        gad_out[...] += dot_tn(act_gate, cb[:, D:])
        for j in range(6):
            out_e_flat[pl.ds(j, TILE, 8), :] = out_main[:, 128 * j : 128 * j + 128]
            out_t_flat[pl.ds(j, TILE, 8), :] = in_main[:, 128 * j : 128 * j + 128]
        out_e_flat[pl.ds(6, TILE, 8), :] = out_low
        out_t_flat[pl.ds(6, TILE, 8), :] = in_low
        out_t_flat[pl.ds(7, TILE, 8), :] = jnp.where(lane == expert, gate_grad, 0.0)
        return carry

    lax.fori_loop(0, n_tiles, tile, 0)
    give(n_tiles - 1)

    some = IMG_GRP // 4
    for side, (ep_out, tg_out) in enumerate(zip(ep_outs, tg_outs)):

        def image(i, carry):
            slot = i % 2
            base = pl.multiple_of((i + side * some) * SEQP, 16) * 8
            mask = (lane // RANK) == picks_ref[i + side * some]
            rows = pl.ds(pl.multiple_of(i * SEQP, 16), SEQP)
            put_tg = pltpu.make_async_copy(stage_tg.at[slot], tg_out.at[rows], tg_sem.at[slot])
            put_ep = pltpu.make_async_copy(stage_ep.at[slot], ep_out.at[rows], ep_sem.at[slot])

            @pl.when(i >= 2)
            def drain():
                put_tg.wait()
                put_ep.wait()

            def chunk(j):
                flat = acc_e_flat if j < 8 else acc_t_flat
                return flat[pl.ds(base + j % 8, SEQP, 8), :]

            for j in range(6):
                at = slice(128 * j, 128 * j + 128)
                stage_tg[slot, :, at] = chunk(8 + j).astype(bf16)
                stage_ep[slot, :, at] = chunk(j).astype(bf16)
            low_in = repeat_lanes(jnp.where(mask, chunk(14), 0.0))
            low_out = repeat_lanes(jnp.where(mask, chunk(6), 0.0))
            last = jnp.where(lane < 48, low_in, jnp.where(lane < 64, low_out, 0.0))
            stage_tg[slot, :, D:] = jnp.where(lane < 32, chunk(15), last).astype(bf16)
            put_tg.start()
            put_ep.start()
            return carry

        lax.fori_loop(0, some, image, 0)
        for i in range(some - 2, some):
            rows = pl.ds(i * SEQP, SEQP)
            pltpu.make_async_copy(stage_tg.at[i % 2], tg_out.at[rows], tg_sem.at[i % 2]).wait()
            pltpu.make_async_copy(stage_ep.at[i % 2], ep_out.at[rows], ep_sem.at[i % 2]).wait()


def moe_call(token_list, tile_experts, picks, place, tables, places, w_up, w_down, b_up, a_down):
    half = w_up.shape[2]
    n = len(tables)
    n_copies = sum(len(spots) for spots in places)
    anywhere = pl.BlockSpec(memory_space=pl.ANY)
    inside = pl.BlockSpec(memory_space=pltpu.VMEM)
    return pl.pallas_call(
        lambda *refs: moe_kernel(places, *refs),
        grid_spec=pltpu.PrefetchScalarGridSpec(
            num_scalar_prefetch=4,
            grid=(1,),
            in_specs=[anywhere] * (n + 2) + [inside, inside],
            out_specs=[anywhere] * 8 + [inside, inside],
            scratch_shapes=[
                pltpu.VMEM((TOK, 16, 128), bf16),
                pltpu.VMEM((TOK, 8, 128), f32),
                pltpu.VMEM((TOK, 8, 128), f32),
                pltpu.VMEM((TILE, 8, 128), f32),
                pltpu.VMEM((TILE, 8, 128), f32),
                pltpu.VMEM((TILE, 8, 128), f32),
                pltpu.VMEM((TILE, 8, 128), f32),
                pltpu.VMEM((TILE, D + 128), bf16),
                pltpu.VMEM((TILE, D + 128), bf16),
                pltpu.VMEM((2, D, half), bf16),
                pltpu.VMEM((2, half, D), bf16),
                pltpu.VMEM((2, SEQP, D), bf16),
                pltpu.VMEM((2, SEQP, D + 128), bf16),
                pltpu.SemaphoreType.DMA((n_copies,)),
                pltpu.SemaphoreType.DMA((2,)),
                pltpu.SemaphoreType.DMA((2,)),
                pltpu.SemaphoreType.DMA((2,)),
                pltpu.SemaphoreType.DMA((2,)),
            ],
        ),
        out_shape=[
            *[jax.ShapeDtypeStruct((TOK // 4, D), bf16)] * 4,
            *[jax.ShapeDtypeStruct((TOK // 4, D + 128), bf16)] * 4,
            jax.ShapeDtypeStruct((half, ADAPT), f32),
            jax.ShapeDtypeStruct((half, ADAPT), f32),
        ],
        compiler_params=pltpu.CompilerParams(vmem_limit_bytes=58 * 1024 * 1024),
        cost_estimate=pl.CostEstimate(flops=20_000_000_000, bytes_accessed=60_000_000, transcendentals=10_000_000),
    )(token_list, tile_experts, picks, place, *tables, w_up, w_down, b_up, a_down)


def swapped(s):
    return ((s & 1) << 1) | (s >> 1)


def block_spot(block, row, col):
    from_row = block // 4
    s = (block % 4) ^ col
    return 4 * (from_row ^ row) + jnp.where(from_row == 0, swapped(s), s)


def routing(routes, row, col):
    token = jnp.arange(25 * 128, dtype=jnp.int32)[None, :]
    image = token // SEQ
    spot = block_spot(image // 2, row, col) * BLK + (image % 2) * SEQP + token % SEQ
    real = token < IMG_GRP * SEQ
    picked = jnp.pad(routes.T, ((0, 0), (0, 25 * 128 - IMG_GRP * SEQ)), constant_values=EXPERTS)
    beyond = EXPERTS * 4096 + DUMMY
    keys = jnp.where(real, picked * 4096 + spot, beyond).reshape(-1)
    experts = jnp.arange(EXPERTS, dtype=jnp.int32)
    count = jnp.sum((picked[None] == experts[:, None, None]).astype(jnp.int32), axis=(1, 2))
    tiles = (jnp.maximum(count, 1) + TILE - 1) // TILE
    extra = tiles * TILE - count
    filler = jnp.where(
        jnp.arange(256, dtype=jnp.int32)[None, :] < extra[:, None], (experts * 4096)[:, None] + DUMMY, beyond
    ).reshape(-1)
    ordered = lax.sort(jnp.concatenate([keys, filler])) & 4095
    ends = jnp.sum(jnp.where(experts[None, :] <= experts[:, None], tiles[None, :], 0), axis=1)
    steps = jnp.arange(max_tiles(), dtype=jnp.int32)
    owner = jnp.minimum(jnp.sum((ends[None, :] <= steps[:, None]).astype(jnp.int32), axis=1), EXPERTS - 1)
    return ordered, jnp.concatenate([owner, jnp.sum(tiles)[None]])


HEADS = 12
HEAD_DIM = 64


def pick_mask(pick):
    return (lane_iota((1, ADAPT)) // RANK) == pick


def norm_stats(values):
    centre = jnp.sum(values, axis=1, keepdims=True) * (1.0 / D)
    shifted = values - centre
    spread = jnp.sum(shifted * shifted, axis=1, keepdims=True) * (1.0 / D)
    inverse = lax.rsqrt(spread + 1e-06)
    return shifted * inverse, inverse


def norm_back(grad, gain, unit, inverse):
    scaled = grad * gain
    total = jnp.sum(scaled, axis=1, keepdims=True) * (1.0 / D)
    along = jnp.sum(scaled * unit, axis=1, keepdims=True) * (1.0 / D)
    return inverse * (scaled - total - unit * along)


def qkv_copies(place_ref, blocks, own_b, scratch, sem):
    w_qkv, a_qkv, b_qkv = scratch
    row, col = place_ref[0], place_ref[1]
    copies = []

    def copy(source, target):
        copies.append(pltpu.make_async_copy(source, target, sem.at[len(copies)]))

    for t in range(2):
        half_at = pl.multiple_of((row ^ t) * 384, 128)
        for s in range(4):
            block = blocks[4 * t + s]
            at = pl.multiple_of((col ^ s) * 192, 64)
            low_at = pl.multiple_of((col ^ s) * 192 + (row ^ t) * 96, 32)
            for p in range(3):
                copy(block.at[pl.ds(192 * p, 192)], w_qkv.at[p, pl.ds(at, 192), pl.ds(half_at, 384)])
                copy(block.at[pl.ds(576, 96), pl.ds(128 * p, 128)], a_qkv.at[p, pl.ds(low_at, 96), :])
        for p in range(3):
            source = own_b.at[p] if t == 0 else blocks[4].at[pl.ds(W_ROWS + 128 * p, 128)]
            copy(source, b_qkv.at[p, :, pl.ds(half_at, 384)])
    return copies


def out_copies(place_ref, far_block, own_a, out_w, scratch, sem):
    w_out, a_out = scratch
    row = place_ref[0]
    copies = []

    def copy(source, target):
        copies.append(pltpu.make_async_copy(source, target, sem.at[len(copies)]))

    for t in range(2):
        half_at = pl.multiple_of((row ^ t) * 384, 128)
        copy(out_w[t].at[pl.ds(0, 384)], w_out.at[pl.ds(half_at, 384), :])
        for j in range(3):
            if t == 0:
                source = own_a.at[pl.ds(128 * j, 128)]
            else:
                source = far_block.at[pl.ds(W_ROWS + 384, 128), pl.ds(128 * j, 128)]
            copy(source, a_out.at[pl.ds(half_at + 128 * j, 128), :])
    return copies


W_ROWS = 944
QKV_SCRATCH = [
    pltpu.VMEM((3, D, D), bf16),
    pltpu.VMEM((3, D, ADAPT), bf16),
    pltpu.VMEM((3, ADAPT, D), bf16),
    pltpu.SemaphoreType.DMA((54,)),
]
OUT_SCRATCH = [
    pltpu.VMEM((D, D), bf16),
    pltpu.VMEM((D, ADAPT), bf16),
    pltpu.SemaphoreType.DMA((8,)),
]


def split_kernel(place_ref, tokens_ref, cot_ref, own_out, one_out, two_out, three_out, left, right, stage, sem):
    rows = tokens_ref.shape[0]
    width = D // 4
    left[0:rows, 0:width] = tokens_ref[...].astype(f32)
    right[0:rows, 0:width] = cot_ref[...].astype(f32)
    lane = lane_iota((1, 128))
    real = lax.broadcasted_iota(jnp.int32, (SEQP, 1), 0) < SEQ
    for i in range(8):
        at = slice(SEQ * i, SEQ * i + SEQP)
        spot = slice(SEQP * (i % 2), SEQP * (i % 2) + SEQP)
        moved = pltpu.roll(right[at, :], 64, 1)
        middle = jnp.where(lane < 64, left[at, 128:256], moved[:, 0:128])
        stage[i // 2, spot, 0:128] = jnp.where(real, left[at, 0:128], 0.0).astype(bf16)
        stage[i // 2, spot, 128:256] = jnp.where(real, middle, 0.0).astype(bf16)
        stage[i // 2, spot, 256:384] = jnp.where(real, moved[:, 128:256], 0.0).astype(bf16)
    copies = [
        pltpu.make_async_copy(stage.at[place_ref[1] ^ s], out, sem.at[s])
        for s, out in enumerate((own_out, one_out, two_out, three_out))
    ]
    for copy in copies:
        copy.start()
    for copy in copies:
        copy.wait()


def split_call(place, tokens, cotangent):
    rows = tokens.shape[0]
    tall = -(-(SEQ * 7 + SEQP) // 8) * 8
    inside = pl.BlockSpec(memory_space=pltpu.VMEM)
    return pl.pallas_call(
        split_kernel,
        grid_spec=pltpu.PrefetchScalarGridSpec(
            num_scalar_prefetch=1,
            grid=(1,),
            in_specs=[inside, inside],
            out_specs=[ANYWHERE] * 4,
            scratch_shapes=[
                pltpu.VMEM((tall, 256), f32),
                pltpu.VMEM((tall, 256), f32),
                pltpu.VMEM((4, BLK, 384), bf16),
                pltpu.SemaphoreType.DMA((4,)),
            ],
        ),
        out_shape=[jax.ShapeDtypeStruct((BLK, 384), bf16)] * 4,
        compiler_params=pltpu.CompilerParams(vmem_limit_bytes=32 * 1024 * 1024),
        cost_estimate=pl.CostEstimate(flops=1_000_000_000, bytes_accessed=3_000_000, transcendentals=0),
    )(place, tokens, cotangent)


def place_weights(place_ref, blocks, own_b, own_a, out_w, w_qkv, a_qkv, b_qkv, w_out, a_out):
    row, col = place_ref[0], place_ref[1]
    for t in range(2):
        half_at = pl.multiple_of((row ^ t) * 384, 128)
        across = pl.ds(half_at, 384)
        for s in range(4):
            block = blocks[4 * t + s]
            at = pl.multiple_of((col ^ s) * 192, 64)
            low_at = pl.multiple_of((col ^ s) * 192 + (row ^ t) * 96, 32)
            for p in range(3):
                w_qkv[p, pl.ds(at, 192), across] = block[192 * p : 192 * p + 192, :]
                a_qkv[p, pl.ds(low_at, 96), :] = block[576:672, 128 * p : 128 * p + 128]
        w_out[across, :] = out_w[t][0:384, :]
        for p in range(3):
            down = pl.ds(pl.multiple_of(half_at + 128 * p, 128), 128)
            if t == 0:
                b_qkv[p, :, across] = own_b[p]
                a_out[down, :] = own_a[128 * p : 128 * p + 128, :]
            else:
                b_qkv[p, :, across] = blocks[4][W_ROWS + 128 * p : W_ROWS + 128 * p + 128, :]
                a_out[down, :] = blocks[4][W_ROWS + 384 : W_ROWS + 512, 128 * p : 128 * p + 128]


def attend_kernel(picks_ref, place_ref, *refs):
    blocks, refs = refs[:8], refs[8:]
    (
        own_b, own_a, out_near, out_far, x_ref, gain_one, gain_two, b_out,
        two_out, resid_out, normed_out, qkv_out, mixed_out, probs_out, lows_out,
        w_qkv, a_qkv, b_qkv, w_out, a_out,
    ) = refs
    image = pl.program_id(0)

    @pl.when(image == 0)
    def start():
        place_weights(place_ref, blocks, own_b, own_a, (out_near, out_far), w_qkv, a_qkv, b_qkv, w_out, a_out)

    mask = pick_mask(picks_ref[image])
    x = x_ref[...].astype(f32)
    unit, unused = norm_stats(x)
    normed = (unit * gain_one[...]).astype(bf16)
    normed_out[...] = normed
    for p in range(3):
        low = jnp.where(mask, dot(normed, a_qkv[p]), 0.0).astype(bf16)
        lows_out[:, 128 * p : 128 * p + 128] = low
        qkv_out[p] = (dot(normed, w_qkv[p]) + dot(low, b_qkv[p])).astype(bf16)
    lane = lane_iota((1, 128))
    key_lane = lane_iota((1, SEQP))
    for pair in range(HEADS // 2):
        at = slice(128 * pair, 128 * pair + 128)
        q = qkv_out[0, :, at]
        k = qkv_out[1, :, at]
        v = qkv_out[2, :, at]
        parts = []
        for side in range(2):
            own = (lane // HEAD_DIM) == side
            scores = dot_nt(jnp.where(own, q, jnp.zeros_like(q)), k) * (HEAD_DIM**-0.5)
            scores = jnp.where(key_lane < SEQ, scores, -1e30)
            power = jnp.exp(scores - jnp.max(scores, axis=1, keepdims=True))
            probs = (power / jnp.sum(power, axis=1, keepdims=True)).astype(bf16)
            probs_out[0, 2 * pair + side] = probs
            parts.append(dot(probs, v))
        mixed_out[:, at] = jnp.where(lane < HEAD_DIM, parts[0], parts[1]).astype(bf16)
    mixed = mixed_out[...]
    low = jnp.where(mask, dot(mixed, a_out[...]), 0.0).astype(bf16)
    lows_out[:, 384:512] = low
    resid = x + dot(mixed, w_out[...]) + dot(low, b_out[...])
    resid_out[...] = resid
    unit, unused = norm_stats(resid)
    real = lax.broadcasted_iota(jnp.int32, (SEQP, 1), 0) < SEQ
    two_out[...] = jnp.where(real, unit * gain_two[...], 0.0).astype(bf16)


def image_rows(lanes):
    return pl.BlockSpec((SEQP, lanes), lambda i, *_: (i, 0))


def kept(*shape):
    return pl.BlockSpec(shape, lambda i, *_: (0,) * len(shape))


QKV_SPEC = pl.BlockSpec((3, SEQP, D), lambda i, *_: (0, i, 0))
PROBS_SPEC = pl.BlockSpec((1, HEADS, SEQP, SEQP), lambda i, *_: (i, 0, 0, 0))
ANYWHERE = pl.BlockSpec(memory_space=pl.ANY)


def attend_call(picks, place, blocks, own_b, own_a, out_w, x, gain_one, gain_two, b_out):
    rows = x.shape[0]
    return pl.pallas_call(
        attend_kernel,
        grid_spec=pltpu.PrefetchScalarGridSpec(
            num_scalar_prefetch=2,
            grid=(2,),
            in_specs=[kept(*block.shape) for block in (*blocks, own_b, own_a, *out_w)]
            + [image_rows(D), kept(1, D), kept(1, D), kept(ADAPT, D)],
            out_specs=[
                image_rows(D), image_rows(D), image_rows(D), QKV_SPEC,
                image_rows(D), PROBS_SPEC, image_rows(512),
            ],
            scratch_shapes=QKV_SCRATCH[:-1] + OUT_SCRATCH[:-1],
        ),
        out_shape=[
            jax.ShapeDtypeStruct((rows, D), bf16),
            jax.ShapeDtypeStruct((rows, D), f32),
            jax.ShapeDtypeStruct((rows, D), bf16),
            jax.ShapeDtypeStruct((3, rows, D), bf16),
            jax.ShapeDtypeStruct((rows, D), bf16),
            jax.ShapeDtypeStruct((2, HEADS, SEQP, SEQP), bf16),
            jax.ShapeDtypeStruct((rows, 512), bf16),
        ],
        compiler_params=pltpu.CompilerParams(vmem_limit_bytes=48 * 1024 * 1024),
        cost_estimate=pl.CostEstimate(flops=4_000_000_000, bytes_accessed=15_000_000, transcendentals=2_000_000),
    )(picks, place, *blocks, own_b, own_a, *out_w, x, gain_one, gain_two, b_out)


def out_back_kernel(picks_ref, place_ref, *refs):
    (
        far_block, own_a, out_near, out_far, gain_two, b_out, two_ref, resid_ref, mixed_ref, lows_ref,
        cot_ref, grad_a, grad_b, w_router, a_router, b_router, a_up, b_down,
        resid_grad_out, mixed_grad_out, base_out, both_out, a_part_out, b_part_out,
        w_out, a_out, sem, both, a_part, b_part,
    ) = refs
    image = pl.program_id(0)

    @pl.when(image == 0)
    def start():
        copies = out_copies(place_ref, far_block, own_a, (out_near, out_far), (w_out, a_out), sem)
        for copy in copies:
            copy.start()
        for part in (both, a_part, b_part):
            part[...] = jnp.zeros_like(part)
        for copy in copies:
            copy.wait()

    mask = pick_mask(picks_ref[image])
    lane = lane_iota((1, 128))

    def add_part(row, value):
        at = slice(row, row + value.shape[0])
        both[at, :] += value

    two = two_ref[...]
    received = grad_a[...].astype(f32) + grad_b[...].astype(f32)
    low_r = jnp.where(mask, dot(two, a_router[...]), 0.0).astype(bf16)
    logits = dot(two, w_router[...]) + dot(low_r, b_router[...])
    logits = jnp.where(lane < EXPERTS, logits, -1e30)
    power = jnp.exp(logits - jnp.max(logits, axis=1, keepdims=True))
    probs = power / jnp.sum(power, axis=1, keepdims=True)
    last = received[:, D:]
    grad_probs = jnp.where(lane < EXPERTS, last, 0.0)
    low_in = jnp.where(mask, repeat_lanes(jnp.where((lane >= 32) & (lane < 48), last, 0.0)), 0.0).astype(bf16)
    low_out = jnp.where(mask, repeat_lanes(jnp.where((lane >= 48) & (lane < 64), last, 0.0)), 0.0).astype(bf16)
    cot = cot_ref[...]
    resid = resid_ref[...]
    base_out[...] = resid + dot(low_out, b_down[...])
    add_part(768, dot_tn(two, low_in))
    add_part(1536, dot_tn(cot, low_out))
    grad_logits = probs * (grad_probs - jnp.sum(probs * grad_probs, axis=1, keepdims=True))
    grad_logits = grad_logits.astype(bf16)
    grad_low = jnp.where(mask, dot_nt(grad_logits, b_router[...]), 0.0).astype(bf16)
    grad_two = received[:, :D] + dot_nt(low_in, a_up[...])
    grad_two = grad_two + dot_nt(grad_logits, w_router[...]) + dot_nt(grad_low, a_router[...])
    add_part(0, dot_tn(two, grad_low))
    add_part(2304, dot_tn(grad_logits, low_r))
    unit, inverse = norm_stats(resid)
    grad_resid = cot.astype(f32) + norm_back(grad_two, gain_two[...], unit, inverse)
    resid_grad_out[...] = grad_resid
    grad_attn = grad_resid.astype(bf16)
    grad_low = jnp.where(mask, dot_nt(grad_attn, b_out[...]), 0.0).astype(bf16)
    mixed_grad_out[...] = (dot_nt(grad_attn, w_out[...]) + dot_nt(grad_low, a_out[...])).astype(bf16)
    a_part[...] += dot_tn(mixed_ref[...], grad_low)
    b_part[...] += dot_tn(grad_attn, lows_ref[:, 384:512])

    @pl.when(image == 1)
    def finish():
        both_out[...] = both[...].astype(bf16)
        a_part_out[...] = a_part[...].astype(bf16)
        b_part_out[...] = b_part[...].astype(bf16)


BOTH_ROWS = 2560


def out_back_call(picks, place, far_block, own_a, out_w, gain_two, b_out, two, resid, mixed, lows, cot, grad_a, grad_b,
                  w_router, a_router, b_router, a_up, b_down):
    rows = two.shape[0]
    return pl.pallas_call(
        out_back_kernel,
        grid_spec=pltpu.PrefetchScalarGridSpec(
            num_scalar_prefetch=2,
            grid=(2,),
            in_specs=[ANYWHERE] * 4
            + [kept(1, D), kept(ADAPT, D), image_rows(D), image_rows(D), image_rows(D), image_rows(512)]
            + [image_rows(D), image_rows(D + 128), image_rows(D + 128)]
            + [kept(D, 128), kept(D, ADAPT), kept(ADAPT, 128), kept(D, ADAPT), kept(ADAPT, D)],
            out_specs=[image_rows(D), image_rows(D), image_rows(D), kept(BOTH_ROWS, 128), kept(D, 128), kept(D, 128)],
            scratch_shapes=OUT_SCRATCH
            + [pltpu.VMEM((BOTH_ROWS, 128), f32), pltpu.VMEM((D, 128), f32), pltpu.VMEM((D, 128), f32)],
        ),
        out_shape=[
            jax.ShapeDtypeStruct((rows, D), f32),
            jax.ShapeDtypeStruct((rows, D), bf16),
            jax.ShapeDtypeStruct((rows, D), f32),
            jax.ShapeDtypeStruct((BOTH_ROWS, 128), bf16),
            jax.ShapeDtypeStruct((D, 128), bf16),
            jax.ShapeDtypeStruct((D, 128), bf16),
        ],
        compiler_params=pltpu.CompilerParams(vmem_limit_bytes=48 * 1024 * 1024),
        cost_estimate=pl.CostEstimate(flops=6_000_000_000, bytes_accessed=15_000_000, transcendentals=100_000),
    )(picks, place, far_block, own_a, *out_w, gain_two, b_out, two, resid, mixed, lows, cot, grad_a, grad_b,
      w_router, a_router, b_router, a_up, b_down)


def qkv_back_kernel(picks_ref, place_ref, *refs):
    blocks, refs = refs[:8], refs[8:]
    (
        own_b, x_ref, gain_one, normed_ref, qkv_ref, probs_ref, lows_ref, resid_grad, grad_mixed,
        tokens_out, a_part_out, b_part_out,
        w_qkv, a_qkv, b_qkv, sem, a_part, b_part, grads,
    ) = refs
    image = pl.program_id(0)
    copies = qkv_copies(place_ref, blocks, own_b, (w_qkv, a_qkv, b_qkv), sem)

    @pl.when(image == 0)
    def start():
        for copy in copies:
            copy.start()
        a_part[...] = jnp.zeros_like(a_part)
        b_part[...] = jnp.zeros_like(b_part)

    mask = pick_mask(picks_ref[image])
    lane = lane_iota((1, 128))
    for pair in range(HEADS // 2):
        at = slice(128 * pair, 128 * pair + 128)
        q = qkv_ref[0, :, at]
        k = qkv_ref[1, :, at]
        v = qkv_ref[2, :, at]
        gm = grad_mixed[:, at]
        found = []
        for side in range(2):
            own = (lane // HEAD_DIM) == side
            weights = probs_ref[0, 2 * pair + side]
            weights_f = weights.astype(f32)
            grad_w = dot_nt(jnp.where(own, gm, jnp.zeros_like(gm)), v)
            inner = jnp.sum(weights_f * grad_w, axis=1, keepdims=True)
            grad_s = (weights_f * (grad_w - inner)).astype(bf16)
            found.append(
                (
                    dot(grad_s, k) * (HEAD_DIM**-0.5),
                    dot_tn(grad_s, q) * (HEAD_DIM**-0.5),
                    dot_tn(weights, gm),
                )
            )
        for p in range(3):
            grads[p, :, at] = jnp.where(lane < HEAD_DIM, found[0][p], found[1][p]).astype(bf16)

    @pl.when(image == 0)
    def arrived():
        for copy in copies:
            copy.wait()

    normed = normed_ref[...]
    grad_normed = jnp.zeros((SEQP, D), f32)
    for p in range(3):
        piece = grads[p]
        grad_low = jnp.where(mask, dot_nt(piece, b_qkv[p]), 0.0).astype(bf16)
        grad_normed = grad_normed + dot_nt(piece, w_qkv[p]) + dot_nt(grad_low, a_qkv[p])
        a_part[D * p : D * p + D, :] += dot_tn(normed, grad_low)
        b_part[D * p : D * p + D, :] += dot_tn(piece, lows_ref[:, 128 * p : 128 * p + 128])
    unit, inverse = norm_stats(x_ref[...].astype(f32))
    tokens_out[...] = (resid_grad[...] + norm_back(grad_normed, gain_one[...], unit, inverse)).astype(bf16)

    @pl.when(image == 1)
    def finish():
        a_part_out[...] = a_part[...].astype(bf16)
        b_part_out[...] = b_part[...].astype(bf16)


def qkv_back_call(picks, place, blocks, own_b, x, gain_one, normed, qkv, probs, lows, resid_grad, grad_mixed):
    rows = x.shape[0]
    return pl.pallas_call(
        qkv_back_kernel,
        grid_spec=pltpu.PrefetchScalarGridSpec(
            num_scalar_prefetch=2,
            grid=(2,),
            in_specs=[ANYWHERE] * (len(blocks) + 1)
            + [image_rows(D), kept(1, D), image_rows(D), QKV_SPEC, PROBS_SPEC, image_rows(512)]
            + [image_rows(D), image_rows(D)],
            out_specs=[image_rows(D), kept(3 * D, 128), kept(3 * D, 128)],
            scratch_shapes=QKV_SCRATCH
            + [
                pltpu.VMEM((3 * D, 128), f32),
                pltpu.VMEM((3 * D, 128), f32),
                pltpu.VMEM((3, SEQP, D), bf16),
            ],
        ),
        out_shape=[
            jax.ShapeDtypeStruct((rows, D), bf16),
            jax.ShapeDtypeStruct((3 * D, 128), bf16),
            jax.ShapeDtypeStruct((3 * D, 128), bf16),
        ],
        compiler_params=pltpu.CompilerParams(vmem_limit_bytes=48 * 1024 * 1024),
        cost_estimate=pl.CostEstimate(flops=9_000_000_000, bytes_accessed=15_000_000, transcendentals=1000),
    )(picks, place, *blocks, own_b, x, gain_one, normed, qkv, probs, lows, resid_grad, grad_mixed)


TABLES = (((0, 0), (1, 0)), ((0, 1), (0, 2), (1, 1), (1, 2)), ((0, 3), (1, 3)))


def across_row(value):
    return lax.ppermute(value, "row", [(0, 1), (1, 0)])


def across_col(value, step):
    return lax.ppermute(value, "col", [(i, i ^ step) for i in range(4)])


def by_place(blocks, col):
    found = []
    for place in range(4):
        value = blocks[place]
        for other in range(1, 4):
            value = jnp.where(col == other, blocks[place ^ other], value)
        found.append(value)
    return found


def across_chip(value, first, second):
    pairs = [(i, i ^ first) for i in range(4)] + [(4 + i, 4 + (i ^ second)) for i in range(4)]
    return lax.ppermute(value, ("row", "col"), pairs)


def gather_col(value, row):
    from_x = across_col(value, 1)
    from_y = across_col(value, 2)
    return [value, from_x, from_y, across_chip(jnp.where(row == 0, from_x, from_y), 2, 1)]


def added(*values):
    total = values[0].astype(f32)
    for value in values[1:]:
        total = total + value.astype(f32)
    return total


def last_exchange(kept_rows, got):
    sent = added(kept_rows[BLK:], got[BLK:]).astype(bf16)
    return added(kept_rows[:BLK], got[:BLK]).astype(bf16), across_chip(sent, 2, 1)


def at_place(value, axis, place):
    return lax.dynamic_index_in_dim(value, place, axis, keepdims=False)


def scatter_dp(value):
    place = lax.axis_index("dp")
    view = value.reshape(4, -1, 128)
    found = [at_place(view, 0, place)]
    for s in range(1, 4):
        found.append(across_dp(at_place(view, 0, place ^ s), s))
    return added(*found).astype(bf16)


def across_dp(value, step):
    return lax.ppermute(value, "dp", [(i, i ^ step) for i in range(4)])


def spread_dp(value):
    return jnp.concatenate(by_place([value] + [across_dp(value, s) for s in range(1, 4)], lax.axis_index("dp")))


def part_share(col_parts, row_parts, both_parts, place):
    col_parts = at_place(col_parts.reshape(4, 4, 2, 96, 128), 2, place)
    row_parts = at_place(row_parts.reshape(4, 2, 4, 96, 128), 1, place)
    both_parts = at_place(both_parts.reshape(2, 4, BOTH_ROWS // 8, 128), 0, place)
    col_parts = col_parts.swapaxes(0, 1).reshape(4, 384, 128)
    row_parts = row_parts.swapaxes(0, 1).reshape(4, 384, 128)
    return jnp.concatenate([col_parts, row_parts, both_parts], axis=1)


def reduce_col(value, col):
    found = [at_place(value, 0, col)]
    for s in range(1, 4):
        found.append(across_col(at_place(value, 0, col ^ s), s))
    return added(*found).astype(bf16)


def spread_parts(mine, row, col):
    spread = mine[384:]
    spread = by_place([spread] + [across_col(spread, s) for s in range(1, 4)], col)
    row_sums = jnp.stack([one[:384].reshape(4, 96, 128) for one in spread], axis=1).reshape(4, 384, 128)
    near = jnp.concatenate([mine[:384]] + [one[384:] for one in spread])
    far = across_row(near)
    first = jnp.where(row == 0, near, far)
    second = jnp.where(row == 0, far, near)
    col_sums = jnp.stack([first[:384].reshape(4, 96, 128), second[:384].reshape(4, 96, 128)], axis=1).reshape(4, 192, 128)
    both_sums = jnp.concatenate([first[384:], second[384:]])
    return col_sums, row_sums, both_sums


def to_features(value, col):
    width = D // 4
    chunks = by_place([value[:, width * p : width * p + width] for p in range(4)], col)
    sent = [jnp.concatenate([chunk[:SEQP], chunk[SEQP:]], axis=1) for chunk in chunks]
    got = [sent[0]] + [across_col(sent[s], s) for s in range(1, 4)]
    rows = []
    for block in by_place(got, col):
        rows += [block[:SEQ, :width], block[:SEQ, width:]]
    return jnp.concatenate(rows, axis=0)


def on_device(
    tokens, cotangent, routes, adapter_pick, gain_attn, gain_moe, w_qkv, w_out, w_router, w_up, w_down,
    a_qkv, b_qkv, a_out, b_out, a_router, b_router, a_up, b_up, a_down, b_down,
):
    row = lax.axis_index("row")
    col = lax.axis_index("col")
    me = row * 4 + col
    place = jnp.stack([row, col]).astype(jnp.int32)

    width = D // 4
    pairs = split_call(place, tokens, cotangent)
    pairs = by_place([pairs[0]] + [across_col(pairs[s], s) for s in range(1, 4)], col)
    x = jnp.concatenate([pair[:, :width] for pair in pairs], axis=1)
    cot = jnp.concatenate([pair[:, width:] for pair in pairs], axis=1)
    half = D // 2
    gains = []
    for gain in (gain_attn, gain_moe):
        left = gain
        for unused in range(3):
            lead = lax.reduce_precision(left, 8, 7)
            gains.append(lead.astype(bf16))
            left = left - lead
    small = jnp.concatenate([w_out, b_out, jnp.stack(gains), jnp.zeros((26, width), bf16)], axis=0)
    low = at_place(a_qkv.reshape(3, 2, 96, ADAPT), 1, row)
    packed = jnp.concatenate(
        [w_qkv.reshape(576, half), jnp.concatenate([low[0], low[1], low[2]], axis=1),
         jnp.concatenate([small[:272], small[272:]], axis=1)]
    )
    for_row = jnp.concatenate(
        [packed, b_qkv.reshape(half, half), jnp.concatenate([a_out[:128], a_out[128:256], a_out[256:]], axis=1)]
    )
    near = gather_col(packed, row)
    far = [across_row(for_row)] + [across_row(block) for block in near[1:]]
    blocks = near + far

    def assembled(group):
        parts = by_place([block[672:944] for block in group], col)
        return jnp.concatenate(
            [jnp.concatenate([part[:, :width] for part in parts], axis=1),
             jnp.concatenate([part[:, width:] for part in parts], axis=1)], axis=0
        )

    out_w = [assembled(near), assembled(far)]
    full_b_out = out_w[0][384:512]
    gain_rows = out_w[0][512:518].astype(f32)
    gain_one = jnp.sum(gain_rows[:3], axis=0, keepdims=True)
    gain_two = jnp.sum(gain_rows[3:], axis=0, keepdims=True)

    picks_group = lax.dynamic_slice_in_dim(adapter_pick, lax.axis_index("dp") * IMG_GRP, IMG_GRP)
    order = jnp.arange(IMG_GRP, dtype=jnp.int32)
    picks = jnp.take(picks_group, ((order // 2) ^ me) * 2 + order % 2)
    spot_picks = jnp.sum(
        jnp.where(block_spot(order // 2, row, col)[None, :] * 2 + order[None, :] % 2 == order[:, None], picks_group[None, :], 0), axis=1
    )
    token_list, tile_experts = routing(routes, row, col)
    wide_router = jnp.concatenate([w_router, w_router, jnp.zeros((D, 64), bf16)], axis=1)
    wide_b_router = jnp.concatenate([b_router, b_router, jnp.zeros((ADAPT, 64), bf16)], axis=1)
    slim_router = jnp.concatenate([w_router, jnp.zeros((D, 96), bf16)], axis=1)
    slim_b_router = jnp.concatenate([b_router, jnp.zeros((ADAPT, 96), bf16)], axis=1)

    x, token_list, tile_experts = lax.optimization_barrier((x, token_list, tile_experts))
    cot, unused = lax.optimization_barrier((cot, far[3]))
    two, resid, normed, qkv, mixed, probs, lows = attend_call(
        picks, place, blocks, b_qkv, a_out, out_w, x, gain_one, gain_two, full_b_out
    )
    cot_near = gather_col(cot, row)
    two_near = gather_col(two, row)

    def table(spots, twos, cots):
        return table_call(
            jnp.stack([picks[8 * t + 2 * s + side] for t, s in spots for side in range(2)]),
            twos, cots, a_up, b_down, wide_router, a_router, wide_b_router,
        )

    cot_far = [across_row(block) for block in cot_near]
    tables = [table(TABLES[0], [two, across_row(two)], [cot, cot_far[0]])]
    two_x, two_y = across_row(two_near[1]), across_row(two_near[2])
    tables.append(table(TABLES[1], [two_near[1], two_near[2], two_x, two_y], [cot_near[1], cot_near[2], cot_far[1], cot_far[2]]))
    diag, *tables = lax.optimization_barrier((two_near[3], *tables))
    tables.append(table(TABLES[2], [diag, across_row(diag)], [cot_near[3], cot_far[3]]))
    *moved, part_b_up, part_a_down = moe_call(
        token_list, tile_experts, spot_picks, place, tables, TABLES, w_up, w_down, b_up, a_down
    )
    sums, grads = moved[:4], moved[4:]
    dp_parts = jnp.concatenate([part_b_up.astype(bf16), part_a_down.astype(bf16)])
    grad_sent = added(grads[1], across_row(grads[3])).astype(bf16)
    grad_kept = added(grads[0], across_row(grads[2])).astype(bf16)
    grad_sent, dp_parts, *sums = lax.optimization_barrier((grad_sent, dp_parts, *sums))
    grad_got = across_chip(grad_sent, 1, 2)
    sum_kept, sum_sent = across_row(sums[2]), across_row(sums[3])
    sums = [
        added(near[at : at + BLK], far[at : at + BLK]).astype(bf16)
        for near, far in ((sums[0], sum_kept), (sums[1], sum_sent)) for at in (0, BLK)
    ]
    four_dp = lax.axis_size("dp") == 4
    dp_sums = scatter_dp(dp_parts) if four_dp else lax.psum(dp_parts, "dp")
    grad_got, dp_sums, *sums = lax.optimization_barrier((grad_got, dp_sums, *sums))
    grad_a, grad_b = last_exchange(grad_kept, grad_got)
    if four_dp:
        dp_sums = spread_dp(dp_sums)
    grad_a, grad_b, dp_sums, *sums = lax.optimization_barrier((grad_a, grad_b, dp_sums, *sums))
    sums = [sums[0], across_chip(sums[1], 2, 1), across_chip(sums[2], 1, 2), across_chip(sums[3], 3, 3)]
    resid_grad, mixed_grad, base, both_parts, part_a_out, part_b_out = out_back_call(
        picks, place, blocks[4], a_out, out_w, gain_two, full_b_out, two, resid, mixed, lows, cot, grad_a, grad_b,
        slim_router, a_router, slim_b_router, a_up, b_down,
    )
    grad_tokens, part_a_qkv, part_b_qkv = qkv_back_call(
        picks, place, blocks, b_qkv, x, gain_one, normed, qkv, probs, lows, resid_grad, mixed_grad
    )
    part_a_qkv, part_b_qkv, *sums = lax.optimization_barrier((part_a_qkv, part_b_qkv, *sums))
    col_parts = jnp.concatenate([part_a_qkv, part_b_out])
    row_parts = jnp.concatenate([part_b_qkv, part_a_out])
    theirs = across_row(part_share(col_parts, row_parts, both_parts, 1 - row))
    shared = added(part_share(col_parts, row_parts, both_parts, row), theirs).astype(bf16)
    mine = reduce_col(shared, col)
    mine, grad_tokens, base = lax.optimization_barrier((mine, grad_tokens, base))
    grad_tokens = to_features(grad_tokens, col).astype(f32)
    block_out = to_features((base + added(*sums)).astype(bf16), col)
    mine = spread_dp(scatter_dp(mine)) if four_dp else lax.psum(mine, "dp")
    col_sums, row_sums, both_sums = spread_parts(mine, row, col)
    col_sums = col_sums.astype(f32)
    row_sums = row_sums.astype(f32)
    both_sums = both_sums.astype(f32)
    dp_sums = dp_sums.astype(f32)
    return (
        block_out,
        grad_tokens,
        col_sums[:3],
        jnp.swapaxes(row_sums[:3], 1, 2),
        row_sums[3],
        col_sums[3].T,
        both_sums[:768],
        both_sums[2304:2336].T,
        both_sums[768:1536],
        dp_sums[:384].T,
        dp_sums[384:],
        both_sums[1536:2304].T,
    )


def solution(mesh):
    return jax.shard_map(
        on_device,
        mesh=mesh,
        in_specs=(
            P(("dp", "row"), "col"),
            P(("dp", "row"), "col"),
            P("dp", None),
            P(),
            P("col"),
            P("col"),
            P(None, "col", "row"),
            P("row", "col"),
            P(),
            P(None, None, ("row", "col")),
            P(None, ("row", "col"), None),
            P(None, "col", None),
            P(None, None, "row"),
            P("row", None),
            P(None, "col"),
            P(),
            P(),
            P(),
            P(None, ("row", "col")),
            P(("row", "col"), None),
            P(),
        ),
        out_specs=(
            P(("dp", "row"), "col"),
            P(("dp", "row"), "col"),
            P(None, "col", None),
            P(None, None, "row"),
            P("row", None),
            P(None, "col"),
            P(),
            P(),
            P(),
            P(None, ("row", "col")),
            P(("row", "col"), None),
            P(),
        ),
        check_vma=False,
    )
```

```python
import jax
import jax.numpy as jnp
from jax import lax
from jax.experimental import pallas as pl
from jax.experimental.pallas import tpu as pltpu
from jax.sharding import PartitionSpec as P

D = 768
EXPERTS = 32
SEQ = 197
SEQP = 208
RANK = 16
ADAPT = 128
IMG_GRP = 16
TOK = IMG_GRP * SEQP
BLK = 2 * SEQP
DUMMY = SEQ
TILE = 160
f32 = jnp.float32
bf16 = jnp.bfloat16


def max_tiles():
    return (2 * IMG_GRP * SEQ) // TILE + EXPERTS + 1


def dot(left, right):
    return jnp.dot(left, right, preferred_element_type=f32)


def dot_nt(left, right):
    return lax.dot_general(left, right, (((1,), (1,)), ((), ())), preferred_element_type=f32)


def dot_tn(left, right):
    return lax.dot_general(left, right, (((0,), (0,)), ((), ())), preferred_element_type=f32)


def lane_iota(shape):
    return lax.broadcasted_iota(jnp.int32, shape, len(shape) - 1)


def repeat_lanes(value):
    for shift in (16, 32, 64):
        value = value + pltpu.roll(value, shift, 1)
    return value


def table_kernel(n_blocks, picks_ref, *refs):
    x_blocks = refs[:n_blocks]
    c_blocks = refs[n_blocks : 2 * n_blocks]
    a_up, b_down, w_router, a_router, b_router, table_out, xin, cin, rows_x, rows_c, sem = refs[2 * n_blocks :]
    image = pl.program_id(0)
    lane = lane_iota((1, 128))

    @pl.when(image == 0)
    def start():
        copies = []
        for blocks, place in ((x_blocks, xin), (c_blocks, cin)):
            for b, block in enumerate(blocks):
                copies.append(pltpu.make_async_copy(block, place.at[pl.ds(b * BLK, BLK)], sem.at[len(copies)]))
        for copy in copies:
            copy.start()
        for copy in copies:
            copy.wait()

    row = pl.multiple_of(image * SEQP, 16)
    mask = (lane // RANK) == picks_ref[image]
    x = xin[pl.ds(row, SEQP), :]
    c = cin[pl.ds(row, SEQP), :]
    flat_x = rows_x.reshape(SEQP * 8, 128)
    flat_c = rows_c.reshape(SEQP * 8, 128)
    low_x = jnp.where(mask, dot(x, a_up[...]), 0.0)
    low_c = jnp.where(mask, dot_nt(c, b_down[...]), 0.0)
    low_r = jnp.where(mask, dot(x, a_router[...]), 0.0).astype(bf16)
    logits = dot(x, w_router[...]) + dot(low_r, b_router[...])
    logits = jnp.where(lane < 2 * EXPERTS, logits, -1e30)
    power = jnp.exp(logits - jnp.max(logits, axis=1, keepdims=True))
    total = jnp.sum(jnp.where(lane < EXPERTS, power, 0.0), axis=1, keepdims=True)
    probs = power / total
    lead = probs.astype(bf16).astype(f32)
    probs = jnp.where(lane < EXPERTS, lead, probs - lead)
    for j in range(6):
        flat_x[pl.ds(j, SEQP, 8), :] = x[:, 128 * j : 128 * j + 128].astype(f32)
        flat_c[pl.ds(j, SEQP, 8), :] = c[:, 128 * j : 128 * j + 128].astype(f32)
    flat_x[pl.ds(6, SEQP, 8), :] = low_x
    flat_x[pl.ds(7, SEQP, 8), :] = probs
    flat_c[pl.ds(6, SEQP, 8), :] = low_c
    flat_c[pl.ds(7, SEQP, 8), :] = jnp.zeros((SEQP, 128), f32)
    table_out[...] = jnp.concatenate([rows_x[...], rows_c[...]], axis=1).astype(bf16)


def table_call(picks, x_blocks, c_blocks, a_up, b_down, w_router, a_router, b_router):
    n = len(x_blocks)

    def whole(*shape):
        return pl.BlockSpec(shape, lambda e, *_: (0,) * len(shape))

    anywhere = pl.BlockSpec(memory_space=pl.ANY)
    return pl.pallas_call(
        lambda *refs: table_kernel(n, *refs),
        grid_spec=pltpu.PrefetchScalarGridSpec(
            num_scalar_prefetch=1,
            grid=(2 * n,),
            in_specs=[anywhere] * (2 * n)
            + [whole(D, ADAPT), whole(ADAPT, D), whole(D, 128), whole(D, ADAPT), whole(ADAPT, 128)],
            out_specs=pl.BlockSpec((SEQP, 16, 128), lambda i, *_: (i, 0, 0)),
            scratch_shapes=[
                pltpu.VMEM((n * BLK, D), bf16),
                pltpu.VMEM((n * BLK, D), bf16),
                pltpu.VMEM((SEQP, 8, 128), f32),
                pltpu.VMEM((SEQP, 8, 128), f32),
                pltpu.SemaphoreType.DMA((2 * n,)),
            ],
        ),
        out_shape=jax.ShapeDtypeStruct((n * BLK, 16, 128), bf16),
        compiler_params=pltpu.CompilerParams(vmem_limit_bytes=32 * 1024 * 1024),
        cost_estimate=pl.CostEstimate(flops=n * 3_000_000_000, bytes_accessed=n * 3_000_000, transcendentals=n * 60_000),
    )(picks, *x_blocks, *c_blocks, a_up, b_down, w_router, a_router, b_router)


def moe_kernel(places, list_ref, expert_ref, picks_ref, place_ref, *refs):
    n = len(places)
    tables = refs[:n]
    ep_outs, tg_outs = refs[n + 4 : n + 8], refs[n + 8 : n + 12]
    refs = refs[: n + 4] + refs[n + 12 :]
    (
        w_up_hbm, w_down_hbm, b_up, a_down,
        gbu_out, gad_out,
        table, acc_e, acc_t, in_x, in_c, out_e, out_t, xb, cb, w_up, w_down, stage_ep, stage_tg,
        in_sem, up_sem, down_sem, ep_sem, tg_sem,
    ) = refs[n:]
    acc_e_flat = acc_e.reshape(TOK * 8, 128)
    acc_t_flat = acc_t.reshape(TOK * 8, 128)
    in_x_flat = in_x.reshape(TILE * 8, 128)
    in_c_flat = in_c.reshape(TILE * 8, 128)
    out_e_flat = out_e.reshape(TILE * 8, 128)
    out_t_flat = out_t.reshape(TILE * 8, 128)
    lane = lane_iota((1, 128))
    n_tiles = expert_ref[max_tiles()]

    copies = []
    for piece, spots in zip(tables, places):
        for b, (t, s) in enumerate(spots):
            spot = 4 * t + jnp.where(place_ref[0] == t, swapped(s), s)
            copies.append(
                pltpu.make_async_copy(
                    piece.at[pl.ds(b * BLK, BLK)], table.at[pl.ds(pl.multiple_of(spot * BLK, 32), BLK)], in_sem.at[len(copies)]
                )
            )
    for copy in copies:
        copy.start()

    def weights(expert):
        slot = expert % 2
        return (
            pltpu.make_async_copy(w_up_hbm.at[expert], w_up.at[slot], up_sem.at[slot]),
            pltpu.make_async_copy(w_down_hbm.at[expert], w_down.at[slot], down_sem.at[slot]),
        )

    for copy in weights(0):
        copy.start()
    out_e[...] = jnp.zeros_like(out_e)
    out_t[...] = jnp.zeros_like(out_t)
    gbu_out[...] = jnp.zeros_like(gbu_out)
    gad_out[...] = jnp.zeros_like(gad_out)

    def clear(i, carry):
        acc_e[pl.ds(i * 64, 64)] = jnp.zeros((64, 8, 128), f32)
        acc_t[pl.ds(i * 64, 64)] = jnp.zeros((64, 8, 128), f32)
        return carry

    lax.fori_loop(0, TOK // 64, clear, 0)
    for copy in copies:
        copy.wait()

    def fetch(t):
        for i in range(TILE):
            both = table[list_ref[t * TILE + i]].astype(f32)
            in_x[i] = both[:8]
            in_c[i] = both[8:]

    def give(t):
        for b in range(TILE // 8):
            tokens = [list_ref[t * TILE + 8 * b + k] for k in range(8)]
            sums_e = [acc_e[tokens[k]] + out_e[8 * b + k] for k in range(8)]
            sums_t = [acc_t[tokens[k]] + out_t[8 * b + k] for k in range(8)]
            for k in range(8):
                acc_e[tokens[k]] = sums_e[k]
                acc_t[tokens[k]] = sums_t[k]

    fetch(0)

    def tile(t, carry):
        expert = expert_ref[t]
        slot = expert % 2

        @pl.when((t == 0) | (expert_ref[jnp.maximum(t - 1, 0)] != expert))
        def arrive():
            for copy in weights(expert):
                copy.wait()

            @pl.when(expert + 1 < EXPERTS)
            def ahead():
                for copy in weights(expert + 1):
                    copy.start()

        for j in range(7):
            xb[:, 128 * j : 128 * j + 128] = in_x_flat[pl.ds(j, TILE, 8), :].astype(bf16)
            cb[:, 128 * j : 128 * j + 128] = in_c_flat[pl.ds(j, TILE, 8), :].astype(bf16)
        spread = in_x_flat[pl.ds(7, TILE, 8), :]
        mine = (lane == expert) | (lane == expert + EXPERTS)
        gate = jnp.sum(jnp.where(mine, spread, 0.0), axis=1, keepdims=True)
        fetch(t + 1)
        give(jnp.maximum(t - 1, 0))
        hidden = dot(xb[:, :D], w_up[slot]) + dot(xb[:, D:], b_up[...])
        back = dot_nt(cb[:, :D], w_down[slot]) + dot_nt(cb[:, D:], a_down[...])
        cdf = 0.5 + 0.5 * lax.erf(hidden * 0.7071067811865476)
        slope = cdf + hidden * jnp.exp(hidden * hidden * -0.5) * 0.3989422804014327
        act = (hidden * cdf).astype(bf16)
        act_f = act.astype(f32)
        gate_grad = jnp.sum(act_f * back, axis=1, keepdims=True)
        grad_hidden = (gate * back * slope).astype(bf16)
        act_gate = (gate * act_f).astype(bf16)
        out_main = dot(act_gate, w_down[slot])
        out_low = dot(act_gate, a_down[...])
        in_main = dot_nt(grad_hidden, w_up[slot])
        in_low = dot_nt(grad_hidden, b_up[...])
        gbu_out[...] += dot_tn(grad_hidden, xb[:, D:])
        gad_out[...] += dot_tn(act_gate, cb[:, D:])
        for j in range(6):
            out_e_flat[pl.ds(j, TILE, 8), :] = out_main[:, 128 * j : 128 * j + 128]
            out_t_flat[pl.ds(j, TILE, 8), :] = in_main[:, 128 * j : 128 * j + 128]
        out_e_flat[pl.ds(6, TILE, 8), :] = out_low
        out_t_flat[pl.ds(6, TILE, 8), :] = in_low
        out_t_flat[pl.ds(7, TILE, 8), :] = jnp.where(lane == expert, gate_grad, 0.0)
        return carry

    lax.fori_loop(0, n_tiles, tile, 0)
    give(n_tiles - 1)

    some = IMG_GRP // 4
    for side, (ep_out, tg_out) in enumerate(zip(ep_outs, tg_outs)):

        def image(i, carry):
            slot = i % 2
            base = pl.multiple_of((i + side * some) * SEQP, 16) * 8
            mask = (lane // RANK) == picks_ref[i + side * some]
            rows = pl.ds(pl.multiple_of(i * SEQP, 16), SEQP)
            put_tg = pltpu.make_async_copy(stage_tg.at[slot], tg_out.at[rows], tg_sem.at[slot])
            put_ep = pltpu.make_async_copy(stage_ep.at[slot], ep_out.at[rows], ep_sem.at[slot])

            @pl.when(i >= 2)
            def drain():
                put_tg.wait()
                put_ep.wait()

            def chunk(j):
                flat = acc_e_flat if j < 8 else acc_t_flat
                return flat[pl.ds(base + j % 8, SEQP, 8), :]

            for j in range(6):
                at = slice(128 * j, 128 * j + 128)
                stage_tg[slot, :, at] = chunk(8 + j).astype(bf16)
                stage_ep[slot, :, at] = chunk(j).astype(bf16)
            low_in = repeat_lanes(jnp.where(mask, chunk(14), 0.0))
            low_out = repeat_lanes(jnp.where(mask, chunk(6), 0.0))
            last = jnp.where(lane < 48, low_in, jnp.where(lane < 64, low_out, 0.0))
            stage_tg[slot, :, D:] = jnp.where(lane < 32, chunk(15), last).astype(bf16)
            put_tg.start()
            put_ep.start()
            return carry

        lax.fori_loop(0, some, image, 0)
        for i in range(some - 2, some):
            rows = pl.ds(i * SEQP, SEQP)
            pltpu.make_async_copy(stage_tg.at[i % 2], tg_out.at[rows], tg_sem.at[i % 2]).wait()
            pltpu.make_async_copy(stage_ep.at[i % 2], ep_out.at[rows], ep_sem.at[i % 2]).wait()


def moe_call(token_list, tile_experts, picks, place, tables, places, w_up, w_down, b_up, a_down):
    half = w_up.shape[2]
    n = len(tables)
    n_copies = sum(len(spots) for spots in places)
    anywhere = pl.BlockSpec(memory_space=pl.ANY)
    inside = pl.BlockSpec(memory_space=pltpu.VMEM)
    return pl.pallas_call(
        lambda *refs: moe_kernel(places, *refs),
        grid_spec=pltpu.PrefetchScalarGridSpec(
            num_scalar_prefetch=4,
            grid=(1,),
            in_specs=[anywhere] * (n + 2) + [inside, inside],
            out_specs=[anywhere] * 8 + [inside, inside],
            scratch_shapes=[
                pltpu.VMEM((TOK, 16, 128), bf16),
                pltpu.VMEM((TOK, 8, 128), f32),
                pltpu.VMEM((TOK, 8, 128), f32),
                pltpu.VMEM((TILE, 8, 128), f32),
                pltpu.VMEM((TILE, 8, 128), f32),
                pltpu.VMEM((TILE, 8, 128), f32),
                pltpu.VMEM((TILE, 8, 128), f32),
                pltpu.VMEM((TILE, D + 128), bf16),
                pltpu.VMEM((TILE, D + 128), bf16),
                pltpu.VMEM((2, D, half), bf16),
                pltpu.VMEM((2, half, D), bf16),
                pltpu.VMEM((2, SEQP, D), bf16),
                pltpu.VMEM((2, SEQP, D + 128), bf16),
                pltpu.SemaphoreType.DMA((n_copies,)),
                pltpu.SemaphoreType.DMA((2,)),
                pltpu.SemaphoreType.DMA((2,)),
                pltpu.SemaphoreType.DMA((2,)),
                pltpu.SemaphoreType.DMA((2,)),
            ],
        ),
        out_shape=[
            *[jax.ShapeDtypeStruct((TOK // 4, D), bf16)] * 4,
            *[jax.ShapeDtypeStruct((TOK // 4, D + 128), bf16)] * 4,
            jax.ShapeDtypeStruct((half, ADAPT), f32),
            jax.ShapeDtypeStruct((half, ADAPT), f32),
        ],
        compiler_params=pltpu.CompilerParams(vmem_limit_bytes=58 * 1024 * 1024),
        cost_estimate=pl.CostEstimate(flops=20_000_000_000, bytes_accessed=60_000_000, transcendentals=10_000_000),
    )(token_list, tile_experts, picks, place, *tables, w_up, w_down, b_up, a_down)


def swapped(s):
    return ((s & 1) << 1) | (s >> 1)


def block_spot(block, row, col):
    from_row = block // 4
    s = (block % 4) ^ col
    return 4 * (from_row ^ row) + jnp.where(from_row == 0, swapped(s), s)


def routing(routes, row, col):
    token = jnp.arange(25 * 128, dtype=jnp.int32)[None, :]
    image = token // SEQ
    spot = block_spot(image // 2, row, col) * BLK + (image % 2) * SEQP + token % SEQ
    real = token < IMG_GRP * SEQ
    picked = jnp.pad(routes.T, ((0, 0), (0, 25 * 128 - IMG_GRP * SEQ)), constant_values=EXPERTS)
    beyond = EXPERTS * 4096 + DUMMY
    keys = jnp.where(real, picked * 4096 + spot, beyond).reshape(-1)
    experts = jnp.arange(EXPERTS, dtype=jnp.int32)
    count = jnp.sum((picked[None] == experts[:, None, None]).astype(jnp.int32), axis=(1, 2))
    tiles = (jnp.maximum(count, 1) + TILE - 1) // TILE
    extra = tiles * TILE - count
    filler = jnp.where(
        jnp.arange(256, dtype=jnp.int32)[None, :] < extra[:, None], (experts * 4096)[:, None] + DUMMY, beyond
    ).reshape(-1)
    ordered = lax.sort(jnp.concatenate([keys, filler])) & 4095
    ends = jnp.sum(jnp.where(experts[None, :] <= experts[:, None], tiles[None, :], 0), axis=1)
    steps = jnp.arange(max_tiles(), dtype=jnp.int32)
    owner = jnp.minimum(jnp.sum((ends[None, :] <= steps[:, None]).astype(jnp.int32), axis=1), EXPERTS - 1)
    return ordered, jnp.concatenate([owner, jnp.sum(tiles)[None]])


HEADS = 12
HEAD_DIM = 64


def pick_mask(pick):
    return (lane_iota((1, ADAPT)) // RANK) == pick


def norm_stats(values):
    centre = jnp.sum(values, axis=1, keepdims=True) * (1.0 / D)
    shifted = values - centre
    spread = jnp.sum(shifted * shifted, axis=1, keepdims=True) * (1.0 / D)
    inverse = lax.rsqrt(spread + 1e-06)
    return shifted * inverse, inverse


def norm_back(grad, gain, unit, inverse):
    scaled = grad * gain
    total = jnp.sum(scaled, axis=1, keepdims=True) * (1.0 / D)
    along = jnp.sum(scaled * unit, axis=1, keepdims=True) * (1.0 / D)
    return inverse * (scaled - total - unit * along)


def qkv_copies(place_ref, blocks, own_b, scratch, sem):
    w_qkv, a_qkv, b_qkv = scratch
    row, col = place_ref[0], place_ref[1]
    copies = []

    def copy(source, target):
        copies.append(pltpu.make_async_copy(source, target, sem.at[len(copies)]))

    for t in range(2):
        half_at = pl.multiple_of((row ^ t) * 384, 128)
        for s in range(4):
            block = blocks[4 * t + s]
            at = pl.multiple_of((col ^ s) * 192, 64)
            low_at = pl.multiple_of((col ^ s) * 192 + (row ^ t) * 96, 32)
            for p in range(3):
                copy(block.at[pl.ds(192 * p, 192)], w_qkv.at[p, pl.ds(at, 192), pl.ds(half_at, 384)])
                copy(block.at[pl.ds(576, 96), pl.ds(128 * p, 128)], a_qkv.at[p, pl.ds(low_at, 96), :])
        for p in range(3):
            source = own_b.at[p] if t == 0 else blocks[4].at[pl.ds(W_ROWS + 128 * p, 128)]
            copy(source, b_qkv.at[p, :, pl.ds(half_at, 384)])
    return copies


def out_copies(place_ref, far_block, own_a, out_w, scratch, sem):
    w_out, a_out = scratch
    row = place_ref[0]
    copies = []

    def copy(source, target):
        copies.append(pltpu.make_async_copy(source, target, sem.at[len(copies)]))

    for t in range(2):
        half_at = pl.multiple_of((row ^ t) * 384, 128)
        copy(out_w[t].at[pl.ds(0, 384)], w_out.at[pl.ds(half_at, 384), :])
        for j in range(3):
            if t == 0:
                source = own_a.at[pl.ds(128 * j, 128)]
            else:
                source = far_block.at[pl.ds(W_ROWS + 384, 128), pl.ds(128 * j, 128)]
            copy(source, a_out.at[pl.ds(half_at + 128 * j, 128), :])
    return copies


W_ROWS = 944
QKV_SCRATCH = [
    pltpu.VMEM((3, D, D), bf16),
    pltpu.VMEM((3, D, ADAPT), bf16),
    pltpu.VMEM((3, ADAPT, D), bf16),
    pltpu.SemaphoreType.DMA((54,)),
]
OUT_SCRATCH = [
    pltpu.VMEM((D, D), bf16),
    pltpu.VMEM((D, ADAPT), bf16),
    pltpu.SemaphoreType.DMA((8,)),
]


def split_kernel(place_ref, tokens_ref, cot_ref, own_out, one_out, two_out, three_out, left, right, stage, sem):
    rows = tokens_ref.shape[0]
    width = D // 4
    left[0:rows, 0:width] = tokens_ref[...].astype(f32)
    right[0:rows, 0:width] = cot_ref[...].astype(f32)
    lane = lane_iota((1, 128))
    real = lax.broadcasted_iota(jnp.int32, (SEQP, 1), 0) < SEQ
    for i in range(8):
        at = slice(SEQ * i, SEQ * i + SEQP)
        spot = slice(SEQP * (i % 2), SEQP * (i % 2) + SEQP)
        moved = pltpu.roll(right[at, :], 64, 1)
        middle = jnp.where(lane < 64, left[at, 128:256], moved[:, 0:128])
        stage[i // 2, spot, 0:128] = jnp.where(real, left[at, 0:128], 0.0).astype(bf16)
        stage[i // 2, spot, 128:256] = jnp.where(real, middle, 0.0).astype(bf16)
        stage[i // 2, spot, 256:384] = jnp.where(real, moved[:, 128:256], 0.0).astype(bf16)
    copies = [
        pltpu.make_async_copy(stage.at[place_ref[1] ^ s], out, sem.at[s])
        for s, out in enumerate((own_out, one_out, two_out, three_out))
    ]
    for copy in copies:
        copy.start()
    for copy in copies:
        copy.wait()


def split_call(place, tokens, cotangent):
    rows = tokens.shape[0]
    tall = -(-(SEQ * 7 + SEQP) // 8) * 8
    inside = pl.BlockSpec(memory_space=pltpu.VMEM)
    return pl.pallas_call(
        split_kernel,
        grid_spec=pltpu.PrefetchScalarGridSpec(
            num_scalar_prefetch=1,
            grid=(1,),
            in_specs=[inside, inside],
            out_specs=[ANYWHERE] * 4,
            scratch_shapes=[
                pltpu.VMEM((tall, 256), f32),
                pltpu.VMEM((tall, 256), f32),
                pltpu.VMEM((4, BLK, 384), bf16),
                pltpu.SemaphoreType.DMA((4,)),
            ],
        ),
        out_shape=[jax.ShapeDtypeStruct((BLK, 384), bf16)] * 4,
        compiler_params=pltpu.CompilerParams(vmem_limit_bytes=32 * 1024 * 1024),
        cost_estimate=pl.CostEstimate(flops=1_000_000_000, bytes_accessed=3_000_000, transcendentals=0),
    )(place, tokens, cotangent)


def merge_kernel(place_ref, *refs):
    blocks, refs = refs[:4], refs[4:]
    block_out, tokens_out, stage, tall, sem = refs
    copies = [
        pltpu.make_async_copy(block, stage.at[place_ref[1] ^ s], sem.at[s]) for s, block in enumerate(blocks)
    ]
    for copy in copies:
        copy.start()
    for copy in copies:
        copy.wait()
    width = D // 4
    rows = tokens_out.shape[0]
    for i in range(8):
        at = slice(SEQ * i, SEQ * i + SEQ)
        both = stage[i // 2, SEQP * (i % 2) : SEQP * (i % 2) + SEQP, :].astype(f32)[:SEQ]
        tokens_out[at, :] = both[:, :width]
        tall[at, :] = both[:, width:]
    block_out[...] = tall[0:rows, :].astype(bf16)


def merge_call(place, blocks, rows):
    width = D // 4
    inside = pl.BlockSpec(memory_space=pltpu.VMEM)
    return pl.pallas_call(
        merge_kernel,
        grid_spec=pltpu.PrefetchScalarGridSpec(
            num_scalar_prefetch=1,
            grid=(1,),
            in_specs=[ANYWHERE] * 4,
            out_specs=[inside, inside],
            scratch_shapes=[
                pltpu.VMEM((4, BLK, 2 * width), bf16),
                pltpu.VMEM((rows, width), f32),
                pltpu.SemaphoreType.DMA((4,)),
            ],
        ),
        out_shape=[jax.ShapeDtypeStruct((rows, width), bf16), jax.ShapeDtypeStruct((rows, width), f32)],
        compiler_params=pltpu.CompilerParams(vmem_limit_bytes=32 * 1024 * 1024),
        cost_estimate=pl.CostEstimate(flops=1_000_000_000, bytes_accessed=3_000_000, transcendentals=0),
    )(place, *blocks)


def place_weights(place_ref, blocks, own_b, own_a, out_w, w_qkv, a_qkv, b_qkv, w_out, a_out):
    row, col = place_ref[0], place_ref[1]
    for t in range(2):
        half_at = pl.multiple_of((row ^ t) * 384, 128)
        across = pl.ds(half_at, 384)
        for s in range(4):
            block = blocks[4 * t + s]
            at = pl.multiple_of((col ^ s) * 192, 64)
            low_at = pl.multiple_of((col ^ s) * 192 + (row ^ t) * 96, 32)
            for p in range(3):
                w_qkv[p, pl.ds(at, 192), across] = block[192 * p : 192 * p + 192, :]
                a_qkv[p, pl.ds(low_at, 96), :] = block[576:672, 128 * p : 128 * p + 128]
        w_out[across, :] = out_w[t][0:384, :]
        for p in range(3):
            down = pl.ds(pl.multiple_of(half_at + 128 * p, 128), 128)
            if t == 0:
                b_qkv[p, :, across] = own_b[p]
                a_out[down, :] = own_a[128 * p : 128 * p + 128, :]
            else:
                b_qkv[p, :, across] = blocks[4][W_ROWS + 128 * p : W_ROWS + 128 * p + 128, :]
                a_out[down, :] = blocks[4][W_ROWS + 384 : W_ROWS + 512, 128 * p : 128 * p + 128]


def attend_kernel(picks_ref, place_ref, *refs):
    blocks, refs = refs[:8], refs[8:]
    (
        own_b, own_a, out_near, out_far, x_ref, gain_one, gain_two, b_out,
        two_out, resid_out, normed_out, qkv_out, mixed_out, probs_out, lows_out,
        w_qkv, a_qkv, b_qkv, w_out, a_out,
    ) = refs
    image = pl.program_id(0)

    @pl.when(image == 0)
    def start():
        place_weights(place_ref, blocks, own_b, own_a, (out_near, out_far), w_qkv, a_qkv, b_qkv, w_out, a_out)

    mask = pick_mask(picks_ref[image])
    x = x_ref[...].astype(f32)
    unit, unused = norm_stats(x)
    normed = (unit * gain_one[...]).astype(bf16)
    normed_out[...] = normed
    for p in range(3):
        low = jnp.where(mask, dot(normed, a_qkv[p]), 0.0).astype(bf16)
        lows_out[:, 128 * p : 128 * p + 128] = low
        qkv_out[p] = (dot(normed, w_qkv[p]) + dot(low, b_qkv[p])).astype(bf16)
    lane = lane_iota((1, 128))
    key_lane = lane_iota((1, SEQP))
    for pair in range(HEADS // 2):
        at = slice(128 * pair, 128 * pair + 128)
        q = qkv_out[0, :, at]
        k = qkv_out[1, :, at]
        v = qkv_out[2, :, at]
        parts = []
        for side in range(2):
            own = (lane // HEAD_DIM) == side
            scores = dot_nt(jnp.where(own, q, jnp.zeros_like(q)), k) * (HEAD_DIM**-0.5)
            scores = jnp.where(key_lane < SEQ, scores, -1e30)
            power = jnp.exp(scores - jnp.max(scores, axis=1, keepdims=True))
            probs = (power / jnp.sum(power, axis=1, keepdims=True)).astype(bf16)
            probs_out[0, 2 * pair + side] = probs
            parts.append(dot(probs, v))
        mixed_out[:, at] = jnp.where(lane < HEAD_DIM, parts[0], parts[1]).astype(bf16)
    mixed = mixed_out[...]
    low = jnp.where(mask, dot(mixed, a_out[...]), 0.0).astype(bf16)
    lows_out[:, 384:512] = low
    resid = x + dot(mixed, w_out[...]) + dot(low, b_out[...])
    resid_out[...] = resid
    unit, unused = norm_stats(resid)
    real = lax.broadcasted_iota(jnp.int32, (SEQP, 1), 0) < SEQ
    two_out[...] = jnp.where(real, unit * gain_two[...], 0.0).astype(bf16)


def image_rows(lanes):
    return pl.BlockSpec((SEQP, lanes), lambda i, *_: (i, 0))


def kept(*shape):
    return pl.BlockSpec(shape, lambda i, *_: (0,) * len(shape))


QKV_SPEC = pl.BlockSpec((3, SEQP, D), lambda i, *_: (0, i, 0))
PROBS_SPEC = pl.BlockSpec((1, HEADS, SEQP, SEQP), lambda i, *_: (i, 0, 0, 0))
ANYWHERE = pl.BlockSpec(memory_space=pl.ANY)


def attend_call(picks, place, blocks, own_b, own_a, out_w, x, gain_one, gain_two, b_out):
    rows = x.shape[0]
    return pl.pallas_call(
        attend_kernel,
        grid_spec=pltpu.PrefetchScalarGridSpec(
            num_scalar_prefetch=2,
            grid=(2,),
            in_specs=[kept(*block.shape) for block in (*blocks, own_b, own_a, *out_w)]
            + [image_rows(D), kept(1, D), kept(1, D), kept(ADAPT, D)],
            out_specs=[
                image_rows(D), image_rows(D), image_rows(D), QKV_SPEC,
                image_rows(D), PROBS_SPEC, image_rows(512),
            ],
            scratch_shapes=QKV_SCRATCH[:-1] + OUT_SCRATCH[:-1],
        ),
        out_shape=[
            jax.ShapeDtypeStruct((rows, D), bf16),
            jax.ShapeDtypeStruct((rows, D), f32),
            jax.ShapeDtypeStruct((rows, D), bf16),
            jax.ShapeDtypeStruct((3, rows, D), bf16),
            jax.ShapeDtypeStruct((rows, D), bf16),
            jax.ShapeDtypeStruct((2, HEADS, SEQP, SEQP), bf16),
            jax.ShapeDtypeStruct((rows, 512), bf16),
        ],
        compiler_params=pltpu.CompilerParams(vmem_limit_bytes=60 * 1024 * 1024),
        cost_estimate=pl.CostEstimate(flops=4_000_000_000, bytes_accessed=15_000_000, transcendentals=2_000_000),
    )(picks, place, *blocks, own_b, own_a, *out_w, x, gain_one, gain_two, b_out)


def out_back_kernel(picks_ref, place_ref, *refs):
    (
        far_block, own_a, out_near, out_far, gain_two, b_out, two_ref, resid_ref, mixed_ref, lows_ref,
        cot_ref, grad_a, grad_b, w_router, a_router, b_router, a_up, b_down,
        resid_grad_out, mixed_grad_out, base_out, both_out, a_part_out, b_part_out,
        w_out, a_out, sem, both, a_part, b_part,
    ) = refs
    image = pl.program_id(0)

    @pl.when(image == 0)
    def start():
        copies = out_copies(place_ref, far_block, own_a, (out_near, out_far), (w_out, a_out), sem)
        for copy in copies:
            copy.start()
        for part in (both, a_part, b_part):
            part[...] = jnp.zeros_like(part)
        for copy in copies:
            copy.wait()

    mask = pick_mask(picks_ref[image])
    lane = lane_iota((1, 128))

    def add_part(row, value):
        at = slice(row, row + value.shape[0])
        both[at, :] += value

    two = two_ref[...]
    received = grad_a[...].astype(f32) + grad_b[...].astype(f32)
    low_r = jnp.where(mask, dot(two, a_router[...]), 0.0).astype(bf16)
    logits = dot(two, w_router[...]) + dot(low_r, b_router[...])
    logits = jnp.where(lane < EXPERTS, logits, -1e30)
    power = jnp.exp(logits - jnp.max(logits, axis=1, keepdims=True))
    probs = power / jnp.sum(power, axis=1, keepdims=True)
    last = received[:, D:]
    grad_probs = jnp.where(lane < EXPERTS, last, 0.0)
    low_in = jnp.where(mask, repeat_lanes(jnp.where((lane >= 32) & (lane < 48), last, 0.0)), 0.0).astype(bf16)
    low_out = jnp.where(mask, repeat_lanes(jnp.where((lane >= 48) & (lane < 64), last, 0.0)), 0.0).astype(bf16)
    cot = cot_ref[...]
    resid = resid_ref[...]
    base_out[...] = resid + dot(low_out, b_down[...])
    add_part(768, dot_tn(two, low_in))
    add_part(1536, dot_tn(cot, low_out))
    grad_logits = probs * (grad_probs - jnp.sum(probs * grad_probs, axis=1, keepdims=True))
    grad_logits = grad_logits.astype(bf16)
    grad_low = jnp.where(mask, dot_nt(grad_logits, b_router[...]), 0.0).astype(bf16)
    grad_two = received[:, :D] + dot_nt(low_in, a_up[...])
    grad_two = grad_two + dot_nt(grad_logits, w_router[...]) + dot_nt(grad_low, a_router[...])
    add_part(0, dot_tn(two, grad_low))
    add_part(2304, dot_tn(grad_logits, low_r))
    unit, inverse = norm_stats(resid)
    grad_resid = cot.astype(f32) + norm_back(grad_two, gain_two[...], unit, inverse)
    resid_grad_out[...] = grad_resid
    grad_attn = grad_resid.astype(bf16)
    grad_low = jnp.where(mask, dot_nt(grad_attn, b_out[...]), 0.0).astype(bf16)
    mixed_grad_out[...] = (dot_nt(grad_attn, w_out[...]) + dot_nt(grad_low, a_out[...])).astype(bf16)
    a_part[...] += dot_tn(mixed_ref[...], grad_low)
    b_part[...] += dot_tn(grad_attn, lows_ref[:, 384:512])

    @pl.when(image == 1)
    def finish():
        both_out[...] = both[...].astype(bf16)
        a_part_out[...] = a_part[...].astype(bf16)
        b_part_out[...] = b_part[...].astype(bf16)


BOTH_ROWS = 2560


def out_back_call(picks, place, far_block, own_a, out_w, gain_two, b_out, two, resid, mixed, lows, cot, grad_a, grad_b,
                  w_router, a_router, b_router, a_up, b_down):
    rows = two.shape[0]
    return pl.pallas_call(
        out_back_kernel,
        grid_spec=pltpu.PrefetchScalarGridSpec(
            num_scalar_prefetch=2,
            grid=(2,),
            in_specs=[ANYWHERE] * 4
            + [kept(1, D), kept(ADAPT, D), image_rows(D), image_rows(D), image_rows(D), image_rows(512)]
            + [image_rows(D), image_rows(D + 128), image_rows(D + 128)]
            + [kept(D, 128), kept(D, ADAPT), kept(ADAPT, 128), kept(D, ADAPT), kept(ADAPT, D)],
            out_specs=[image_rows(D), image_rows(D), image_rows(D), kept(BOTH_ROWS, 128), kept(D, 128), kept(D, 128)],
            scratch_shapes=OUT_SCRATCH
            + [pltpu.VMEM((BOTH_ROWS, 128), f32), pltpu.VMEM((D, 128), f32), pltpu.VMEM((D, 128), f32)],
        ),
        out_shape=[
            jax.ShapeDtypeStruct((rows, D), f32),
            jax.ShapeDtypeStruct((rows, D), bf16),
            jax.ShapeDtypeStruct((rows, D), f32),
            jax.ShapeDtypeStruct((BOTH_ROWS, 128), bf16),
            jax.ShapeDtypeStruct((D, 128), bf16),
            jax.ShapeDtypeStruct((D, 128), bf16),
        ],
        compiler_params=pltpu.CompilerParams(vmem_limit_bytes=60 * 1024 * 1024),
        cost_estimate=pl.CostEstimate(flops=6_000_000_000, bytes_accessed=15_000_000, transcendentals=100_000),
    )(picks, place, far_block, own_a, *out_w, gain_two, b_out, two, resid, mixed, lows, cot, grad_a, grad_b,
      w_router, a_router, b_router, a_up, b_down)


def qkv_back_kernel(picks_ref, place_ref, *refs):
    blocks, refs = refs[:8], refs[8:]
    (
        own_b, x_ref, gain_one, normed_ref, qkv_ref, probs_ref, lows_ref, resid_grad, grad_mixed,
        tokens_out, a_part_out, b_part_out,
        w_qkv, a_qkv, b_qkv, sem, a_part, b_part, grads,
    ) = refs
    image = pl.program_id(0)
    copies = qkv_copies(place_ref, blocks, own_b, (w_qkv, a_qkv, b_qkv), sem)

    @pl.when(image == 0)
    def start():
        for copy in copies:
            copy.start()
        a_part[...] = jnp.zeros_like(a_part)
        b_part[...] = jnp.zeros_like(b_part)

    mask = pick_mask(picks_ref[image])
    lane = lane_iota((1, 128))
    for pair in range(HEADS // 2):
        at = slice(128 * pair, 128 * pair + 128)
        q = qkv_ref[0, :, at]
        k = qkv_ref[1, :, at]
        v = qkv_ref[2, :, at]
        gm = grad_mixed[:, at]
        found = []
        for side in range(2):
            own = (lane // HEAD_DIM) == side
            weights = probs_ref[0, 2 * pair + side]
            weights_f = weights.astype(f32)
            grad_w = dot_nt(jnp.where(own, gm, jnp.zeros_like(gm)), v)
            inner = jnp.sum(weights_f * grad_w, axis=1, keepdims=True)
            grad_s = (weights_f * (grad_w - inner)).astype(bf16)
            found.append(
                (
                    dot(grad_s, k) * (HEAD_DIM**-0.5),
                    dot_tn(grad_s, q) * (HEAD_DIM**-0.5),
                    dot_tn(weights, gm),
                )
            )
        for p in range(3):
            grads[p, :, at] = jnp.where(lane < HEAD_DIM, found[0][p], found[1][p]).astype(bf16)

    @pl.when(image == 0)
    def arrived():
        for copy in copies:
            copy.wait()

    normed = normed_ref[...]
    grad_normed = jnp.zeros((SEQP, D), f32)
    for p in range(3):
        piece = grads[p]
        grad_low = jnp.where(mask, dot_nt(piece, b_qkv[p]), 0.0).astype(bf16)
        grad_normed = grad_normed + dot_nt(piece, w_qkv[p]) + dot_nt(grad_low, a_qkv[p])
        a_part[D * p : D * p + D, :] += dot_tn(normed, grad_low)
        b_part[D * p : D * p + D, :] += dot_tn(piece, lows_ref[:, 128 * p : 128 * p + 128])
    unit, inverse = norm_stats(x_ref[...].astype(f32))
    tokens_out[...] = (resid_grad[...] + norm_back(grad_normed, gain_one[...], unit, inverse)).astype(bf16)

    @pl.when(image == 1)
    def finish():
        a_part_out[...] = a_part[...].astype(bf16)
        b_part_out[...] = b_part[...].astype(bf16)


def qkv_back_call(picks, place, blocks, own_b, x, gain_one, normed, qkv, probs, lows, resid_grad, grad_mixed):
    rows = x.shape[0]
    return pl.pallas_call(
        qkv_back_kernel,
        grid_spec=pltpu.PrefetchScalarGridSpec(
            num_scalar_prefetch=2,
            grid=(2,),
            in_specs=[ANYWHERE] * (len(blocks) + 1)
            + [image_rows(D), kept(1, D), image_rows(D), QKV_SPEC, PROBS_SPEC, image_rows(512)]
            + [image_rows(D), image_rows(D)],
            out_specs=[image_rows(D), kept(3 * D, 128), kept(3 * D, 128)],
            scratch_shapes=QKV_SCRATCH
            + [
                pltpu.VMEM((3 * D, 128), f32),
                pltpu.VMEM((3 * D, 128), f32),
                pltpu.VMEM((3, SEQP, D), bf16),
            ],
        ),
        out_shape=[
            jax.ShapeDtypeStruct((rows, D), bf16),
            jax.ShapeDtypeStruct((3 * D, 128), bf16),
            jax.ShapeDtypeStruct((3 * D, 128), bf16),
        ],
        compiler_params=pltpu.CompilerParams(vmem_limit_bytes=60 * 1024 * 1024),
        cost_estimate=pl.CostEstimate(flops=9_000_000_000, bytes_accessed=15_000_000, transcendentals=1000),
    )(picks, place, *blocks, own_b, x, gain_one, normed, qkv, probs, lows, resid_grad, grad_mixed)


TABLES = (((0, 0), (1, 0)), ((0, 1), (0, 2), (1, 1), (1, 2)), ((0, 3), (1, 3)))


def across_row(value):
    return lax.ppermute(value, "row", [(0, 1), (1, 0)])


def across_col(value, step):
    return lax.ppermute(value, "col", [(i, i ^ step) for i in range(4)])


def by_place(blocks, col):
    found = []
    for place in range(4):
        value = blocks[place]
        for other in range(1, 4):
            value = jnp.where(col == other, blocks[place ^ other], value)
        found.append(value)
    return found


def across_chip(value, first, second):
    pairs = [(i, i ^ first) for i in range(4)] + [(4 + i, 4 + (i ^ second)) for i in range(4)]
    return lax.ppermute(value, ("row", "col"), pairs)


def gather_col(value, row):
    from_x = across_col(value, 1)
    from_y = across_col(value, 2)
    return [value, from_x, from_y, across_chip(jnp.where(row == 0, from_x, from_y), 2, 1)]


def added(*values):
    total = values[0].astype(f32)
    for value in values[1:]:
        total = total + value.astype(f32)
    return total


def last_exchange(kept_rows, got):
    sent = added(kept_rows[BLK:], got[BLK:]).astype(bf16)
    return added(kept_rows[:BLK], got[:BLK]).astype(bf16), across_chip(sent, 2, 1)


def at_place(value, axis, place):
    return lax.dynamic_index_in_dim(value, place, axis, keepdims=False)


def scatter_dp(value):
    place = lax.axis_index("dp")
    view = value.reshape(4, -1, 128)
    found = [at_place(view, 0, place)]
    for s in range(1, 4):
        found.append(across_dp(at_place(view, 0, place ^ s), s))
    return added(*found).astype(bf16)


def across_dp(value, step):
    return lax.ppermute(value, "dp", [(i, i ^ step) for i in range(4)])


def spread_dp(value):
    return jnp.concatenate(by_place([value] + [across_dp(value, s) for s in range(1, 4)], lax.axis_index("dp")))


def part_share(col_parts, row_parts, both_parts, place):
    col_parts = at_place(col_parts.reshape(4, 4, 2, 96, 128), 2, place)
    row_parts = at_place(row_parts.reshape(4, 2, 4, 96, 128), 1, place)
    both_parts = at_place(both_parts.reshape(2, 4, BOTH_ROWS // 8, 128), 0, place)
    col_parts = col_parts.swapaxes(0, 1).reshape(4, 384, 128)
    row_parts = row_parts.swapaxes(0, 1).reshape(4, 384, 128)
    return jnp.concatenate([col_parts, row_parts, both_parts], axis=1)


def reduce_col(value, col):
    found = [at_place(value, 0, col)]
    for s in range(1, 4):
        found.append(across_col(at_place(value, 0, col ^ s), s))
    return added(*found).astype(bf16)


def spread_parts(mine, row, col):
    spread = by_place([mine[384:]] + [across_col(mine[384:], s) for s in range(1, 4)], col)
    row_sums = jnp.stack([one[:384].reshape(4, 96, 128) for one in spread], axis=1).reshape(4, 384, 128)
    near = jnp.concatenate([mine[:384]] + [one[384:] for one in spread])
    far = across_row(near)
    first = jnp.where(row == 0, near, far)
    second = jnp.where(row == 0, far, near)
    col_sums = jnp.stack([first[:384].reshape(4, 96, 128), second[:384].reshape(4, 96, 128)], axis=1).reshape(4, 192, 128)
    both_sums = jnp.concatenate([first[384:], second[384:]])
    return col_sums, row_sums, both_sums


def to_features(first, second, col):
    width = D // 4
    pieces = []
    for p in range(4):
        at = slice(width * p, width * p + width)
        pieces.append(jnp.concatenate([first[:, at], second[:, at]], axis=1))
    sent = by_place(pieces, col)
    return [sent[0]] + [across_col(sent[s], s) for s in range(1, 4)]


def on_device(
    tokens, cotangent, routes, adapter_pick, gain_attn, gain_moe, w_qkv, w_out, w_router, w_up, w_down,
    a_qkv, b_qkv, a_out, b_out, a_router, b_router, a_up, b_up, a_down, b_down,
):
    row = lax.axis_index("row")
    col = lax.axis_index("col")
    me = row * 4 + col
    place = jnp.stack([row, col]).astype(jnp.int32)

    width = D // 4
    half = D // 2
    gains = []
    for gain in (gain_attn, gain_moe):
        left = gain
        for unused in range(3):
            lead = lax.reduce_precision(left, 8, 7)
            gains.append(lead.astype(bf16))
            left = left - lead
    small = jnp.concatenate([w_out, b_out, jnp.stack(gains), jnp.zeros((26, width), bf16)], axis=0)
    low = at_place(a_qkv.reshape(3, 2, 96, ADAPT), 1, row)
    packed = jnp.concatenate(
        [w_qkv.reshape(576, half), jnp.concatenate([low[0], low[1], low[2]], axis=1),
         jnp.concatenate([small[:272], small[272:]], axis=1)]
    )
    for_row = jnp.concatenate(
        [packed, b_qkv.reshape(half, half), jnp.concatenate([a_out[:128], a_out[128:256], a_out[256:]], axis=1)]
    )
    pairs = split_call(place, tokens, cotangent)
    from_x, from_y = across_col(packed, 1), across_col(packed, 2)
    from_x, from_y, *pairs = lax.optimization_barrier((from_x, from_y, *pairs))
    near = [packed, from_x, from_y, across_chip(jnp.where(row == 0, from_x, from_y), 2, 1)]
    pairs = by_place([pairs[0]] + [across_col(pairs[s], s) for s in range(1, 4)], col)
    x = jnp.concatenate([pair[:, :width] for pair in pairs], axis=1)
    cot = jnp.concatenate([pair[:, width:] for pair in pairs], axis=1)
    far = [across_row(for_row)] + [across_row(block) for block in near[1:]]
    blocks = near + far

    def assembled(group):
        parts = by_place([block[672:944] for block in group], col)
        return jnp.concatenate(
            [jnp.concatenate([part[:, :width] for part in parts], axis=1),
             jnp.concatenate([part[:, width:] for part in parts], axis=1)], axis=0
        )

    out_w = [assembled(near), assembled(far)]
    full_b_out = out_w[0][384:512]
    gain_rows = out_w[0][512:518].astype(f32)
    gain_one = jnp.sum(gain_rows[:3], axis=0, keepdims=True)
    gain_two = jnp.sum(gain_rows[3:], axis=0, keepdims=True)

    picks_group = lax.dynamic_slice_in_dim(adapter_pick, lax.axis_index("dp") * IMG_GRP, IMG_GRP)
    order = jnp.arange(IMG_GRP, dtype=jnp.int32)
    picks = jnp.take(picks_group, ((order // 2) ^ me) * 2 + order % 2)
    spot_picks = jnp.sum(
        jnp.where(block_spot(order // 2, row, col)[None, :] * 2 + order[None, :] % 2 == order[:, None], picks_group[None, :], 0), axis=1
    )
    token_list, tile_experts = routing(routes, row, col)
    wide_router = jnp.concatenate([w_router, w_router, jnp.zeros((D, 64), bf16)], axis=1)
    wide_b_router = jnp.concatenate([b_router, b_router, jnp.zeros((ADAPT, 64), bf16)], axis=1)
    slim_router = jnp.concatenate([w_router, jnp.zeros((D, 96), bf16)], axis=1)
    slim_b_router = jnp.concatenate([b_router, jnp.zeros((ADAPT, 96), bf16)], axis=1)

    x, token_list, tile_experts = lax.optimization_barrier((x, token_list, tile_experts))
    cot, unused = lax.optimization_barrier((cot, far[3]))
    two, resid, normed, qkv, mixed, probs, lows = attend_call(
        picks, place, blocks, b_qkv, a_out, out_w, x, gain_one, gain_two, full_b_out
    )
    cot_near = gather_col(cot, row)
    two_x, two_y = across_col(two, 1), across_col(two, 2)

    def table(spots, twos, cots):
        return table_call(
            jnp.stack([picks[8 * t + 2 * s + side] for t, s in spots for side in range(2)]),
            twos, cots, a_up, b_down, wide_router, a_router, wide_b_router,
        )

    cot_far = [across_row(block) for block in cot_near]
    tables = [table(TABLES[0], [two, across_row(two)], [cot, cot_far[0]])]
    two_x, two_y, tables[0] = lax.optimization_barrier((two_x, two_y, tables[0]))
    diag = across_chip(jnp.where(row == 0, two_x, two_y), 2, 1)
    tables.append(
        table(TABLES[1], [two_x, two_y, across_row(two_x), across_row(two_y)], [cot_near[1], cot_near[2], cot_far[1], cot_far[2]])
    )
    diag, *tables = lax.optimization_barrier((diag, *tables))
    tables.append(table(TABLES[2], [diag, across_row(diag)], [cot_near[3], cot_far[3]]))
    *moved, part_b_up, part_a_down = moe_call(
        token_list, tile_experts, spot_picks, place, tables, TABLES, w_up, w_down, b_up, a_down
    )
    sums, grads = moved[:4], moved[4:]
    dp_parts = jnp.concatenate([part_b_up.astype(bf16), part_a_down.astype(bf16)])
    grad_sent = added(grads[1], across_row(grads[3])).astype(bf16)
    grad_kept = added(grads[0], across_row(grads[2])).astype(bf16)
    grad_sent, dp_parts, *sums = lax.optimization_barrier((grad_sent, dp_parts, *sums))
    grad_got = across_chip(grad_sent, 1, 2)
    sum_kept, sum_sent = across_row(sums[2]), across_row(sums[3])
    sums = [
        added(near[at : at + BLK], far[at : at + BLK]).astype(bf16)
        for near, far in ((sums[0], sum_kept), (sums[1], sum_sent)) for at in (0, BLK)
    ]
    four_dp = lax.axis_size("dp") == 4
    dp_sums = scatter_dp(dp_parts) if four_dp else lax.psum(dp_parts, "dp")
    grad_got, dp_sums, *sums = lax.optimization_barrier((grad_got, dp_sums, *sums))
    grad_a, grad_b = last_exchange(grad_kept, grad_got)
    if four_dp:
        dp_sums = spread_dp(dp_sums)
    grad_a, grad_b, dp_sums, *sums = lax.optimization_barrier((grad_a, grad_b, dp_sums, *sums))
    sums = [sums[0], across_chip(sums[1], 2, 1), across_chip(sums[2], 1, 2), across_chip(sums[3], 3, 3)]
    resid_grad, mixed_grad, base, both_parts, part_a_out, part_b_out = out_back_call(
        picks, place, blocks[4], a_out, out_w, gain_two, full_b_out, two, resid, mixed, lows, cot, grad_a, grad_b,
        slim_router, a_router, slim_b_router, a_up, b_down,
    )
    grad_tokens, part_a_qkv, part_b_qkv = qkv_back_call(
        picks, place, blocks, b_qkv, x, gain_one, normed, qkv, probs, lows, resid_grad, mixed_grad
    )
    part_a_qkv, part_b_qkv, *sums = lax.optimization_barrier((part_a_qkv, part_b_qkv, *sums))
    col_parts = jnp.concatenate([part_a_qkv, part_b_out])
    row_parts = jnp.concatenate([part_b_qkv, part_a_out])
    theirs = across_row(part_share(col_parts, row_parts, both_parts, 1 - row))
    shared = added(part_share(col_parts, row_parts, both_parts, row), theirs).astype(bf16)
    mine = reduce_col(shared, col)
    mine, grad_tokens, base = lax.optimization_barrier((mine, grad_tokens, base))
    moves = to_features(grad_tokens, (base + added(*sums)).astype(bf16), col)
    mine = spread_dp(scatter_dp(mine)) if four_dp else lax.psum(mine, "dp")
    block_out, grad_tokens = merge_call(place, moves, tokens.shape[0])
    col_sums, row_sums, both_sums = spread_parts(mine, row, col)
    col_sums = col_sums.astype(f32)
    row_sums = row_sums.astype(f32)
    both_sums = both_sums.astype(f32)
    dp_sums = dp_sums.astype(f32)
    return (
        block_out,
        grad_tokens,
        col_sums[:3],
        jnp.swapaxes(row_sums[:3], 1, 2),
        row_sums[3],
        col_sums[3].T,
        both_sums[:768],
        both_sums[2304:2336].T,
        both_sums[768:1536],
        dp_sums[:384].T,
        dp_sums[384:],
        both_sums[1536:2304].T,
    )


def solution(mesh):
    return jax.shard_map(
        on_device,
        mesh=mesh,
        in_specs=(
            P(("dp", "row"), "col"),
            P(("dp", "row"), "col"),
            P("dp", None),
            P(),
            P("col"),
            P("col"),
            P(None, "col", "row"),
            P("row", "col"),
            P(),
            P(None, None, ("row", "col")),
            P(None, ("row", "col"), None),
            P(None, "col", None),
            P(None, None, "row"),
            P("row", None),
            P(None, "col"),
            P(),
            P(),
            P(),
            P(None, ("row", "col")),
            P(("row", "col"), None),
            P(),
        ),
        out_specs=(
            P(("dp", "row"), "col"),
            P(("dp", "row"), "col"),
            P(None, "col", None),
            P(None, None, "row"),
            P("row", None),
            P(None, "col"),
            P(),
            P(),
            P(),
            P(None, ("row", "col")),
            P(("row", "col"), None),
            P(),
        ),
        check_vma=False,
    )
```

```python
import jax
import jax.numpy as jnp
from jax import lax
from jax.experimental import pallas as pl
from jax.experimental.pallas import tpu as pltpu
from jax.sharding import PartitionSpec as P

D = 768
EXPERTS = 32
SEQ = 197
SEQP = 208
RANK = 16
ADAPT = 128
IMG_GRP = 16
TOK = IMG_GRP * SEQP
BLK = 2 * SEQP
DUMMY = SEQ
TILE = 160
f32 = jnp.float32
bf16 = jnp.bfloat16


def max_tiles():
    return (2 * IMG_GRP * SEQ) // TILE + EXPERTS + 1


def dot(left, right):
    return jnp.dot(left, right, preferred_element_type=f32)


def dot_nt(left, right):
    return lax.dot_general(left, right, (((1,), (1,)), ((), ())), preferred_element_type=f32)


def dot_tn(left, right):
    return lax.dot_general(left, right, (((0,), (0,)), ((), ())), preferred_element_type=f32)


def lane_iota(shape):
    return lax.broadcasted_iota(jnp.int32, shape, len(shape) - 1)


def repeat_lanes(value):
    for shift in (16, 32, 64):
        value = value + pltpu.roll(value, shift, 1)
    return value


def table_kernel(n_blocks, picks_ref, *refs):
    x_blocks = refs[:n_blocks]
    c_blocks = refs[n_blocks : 2 * n_blocks]
    a_up, b_down, w_router, a_router, b_router, table_out, xin, cin, rows_x, rows_c, sem = refs[2 * n_blocks :]
    image = pl.program_id(0)
    lane = lane_iota((1, 128))

    @pl.when(image == 0)
    def start():
        copies = []
        for blocks, place in ((x_blocks, xin), (c_blocks, cin)):
            for b, block in enumerate(blocks):
                copies.append(pltpu.make_async_copy(block, place.at[pl.ds(b * BLK, BLK)], sem.at[len(copies)]))
        for copy in copies:
            copy.start()
        for copy in copies:
            copy.wait()

    row = pl.multiple_of(image * SEQP, 16)
    mask = (lane // RANK) == picks_ref[image]
    x = xin[pl.ds(row, SEQP), :]
    c = cin[pl.ds(row, SEQP), :]
    flat_x = rows_x.reshape(SEQP * 8, 128)
    flat_c = rows_c.reshape(SEQP * 8, 128)
    low_x = jnp.where(mask, dot(x, a_up[...]), 0.0)
    low_c = jnp.where(mask, dot_nt(c, b_down[...]), 0.0)
    low_r = jnp.where(mask, dot(x, a_router[...]), 0.0).astype(bf16)
    logits = dot(x, w_router[...]) + dot(low_r, b_router[...])
    logits = jnp.where(lane < 2 * EXPERTS, logits, -1e30)
    power = jnp.exp(logits - jnp.max(logits, axis=1, keepdims=True))
    total = jnp.sum(jnp.where(lane < EXPERTS, power, 0.0), axis=1, keepdims=True)
    probs = power / total
    lead = probs.astype(bf16).astype(f32)
    probs = jnp.where(lane < EXPERTS, lead, probs - lead)
    for j in range(6):
        flat_x[pl.ds(j, SEQP, 8), :] = x[:, 128 * j : 128 * j + 128].astype(f32)
        flat_c[pl.ds(j, SEQP, 8), :] = c[:, 128 * j : 128 * j + 128].astype(f32)
    flat_x[pl.ds(6, SEQP, 8), :] = low_x
    flat_x[pl.ds(7, SEQP, 8), :] = probs
    flat_c[pl.ds(6, SEQP, 8), :] = low_c
    flat_c[pl.ds(7, SEQP, 8), :] = jnp.zeros((SEQP, 128), f32)
    table_out[...] = jnp.concatenate([rows_x[...], rows_c[...]], axis=1).astype(bf16)


def table_call(picks, x_blocks, c_blocks, a_up, b_down, w_router, a_router, b_router):
    n = len(x_blocks)

    def whole(*shape):
        return pl.BlockSpec(shape, lambda e, *_: (0,) * len(shape))

    anywhere = pl.BlockSpec(memory_space=pl.ANY)
    return pl.pallas_call(
        lambda *refs: table_kernel(n, *refs),
        grid_spec=pltpu.PrefetchScalarGridSpec(
            num_scalar_prefetch=1,
            grid=(2 * n,),
            in_specs=[anywhere] * (2 * n)
            + [whole(D, ADAPT), whole(ADAPT, D), whole(D, 128), whole(D, ADAPT), whole(ADAPT, 128)],
            out_specs=pl.BlockSpec((SEQP, 16, 128), lambda i, *_: (i, 0, 0)),
            scratch_shapes=[
                pltpu.VMEM((n * BLK, D), bf16),
                pltpu.VMEM((n * BLK, D), bf16),
                pltpu.VMEM((SEQP, 8, 128), f32),
                pltpu.VMEM((SEQP, 8, 128), f32),
                pltpu.SemaphoreType.DMA((2 * n,)),
            ],
        ),
        out_shape=jax.ShapeDtypeStruct((n * BLK, 16, 128), bf16),
        compiler_params=pltpu.CompilerParams(vmem_limit_bytes=32 * 1024 * 1024),
        cost_estimate=pl.CostEstimate(flops=n * 3_000_000_000, bytes_accessed=n * 3_000_000, transcendentals=n * 60_000),
    )(picks, *x_blocks, *c_blocks, a_up, b_down, w_router, a_router, b_router)


def moe_kernel(places, list_ref, expert_ref, picks_ref, place_ref, *refs):
    n = len(places)
    tables = refs[:n]
    ep_outs, tg_outs = refs[n + 4 : n + 8], refs[n + 8 : n + 12]
    refs = refs[: n + 4] + refs[n + 12 :]
    (
        w_up_hbm, w_down_hbm, b_up, a_down,
        gbu_out, gad_out,
        table, acc_e, acc_t, in_x, in_c, out_e, out_t, xb, cb, w_up, w_down, stage_ep, stage_tg,
        in_sem, up_sem, down_sem, ep_sem, tg_sem,
    ) = refs[n:]
    acc_e_flat = acc_e.reshape(TOK * 8, 128)
    acc_t_flat = acc_t.reshape(TOK * 8, 128)
    in_x_flat = in_x.reshape(TILE * 8, 128)
    in_c_flat = in_c.reshape(TILE * 8, 128)
    out_e_flat = out_e.reshape(TILE * 8, 128)
    out_t_flat = out_t.reshape(TILE * 8, 128)
    lane = lane_iota((1, 128))
    n_tiles = expert_ref[max_tiles()]

    copies = []
    for piece, spots in zip(tables, places):
        for b, (t, s) in enumerate(spots):
            spot = 4 * t + jnp.where(place_ref[0] == t, swapped(s), s)
            copies.append(
                pltpu.make_async_copy(
                    piece.at[pl.ds(b * BLK, BLK)], table.at[pl.ds(pl.multiple_of(spot * BLK, 32), BLK)], in_sem.at[len(copies)]
                )
            )
    for copy in copies:
        copy.start()

    def weights(expert):
        slot = expert % 2
        return (
            pltpu.make_async_copy(w_up_hbm.at[expert], w_up.at[slot], up_sem.at[slot]),
            pltpu.make_async_copy(w_down_hbm.at[expert], w_down.at[slot], down_sem.at[slot]),
        )

    for copy in weights(0):
        copy.start()
    out_e[...] = jnp.zeros_like(out_e)
    out_t[...] = jnp.zeros_like(out_t)
    gbu_out[...] = jnp.zeros_like(gbu_out)
    gad_out[...] = jnp.zeros_like(gad_out)

    def clear(i, carry):
        acc_e[pl.ds(i * 64, 64)] = jnp.zeros((64, 8, 128), f32)
        acc_t[pl.ds(i * 64, 64)] = jnp.zeros((64, 8, 128), f32)
        return carry

    lax.fori_loop(0, TOK // 64, clear, 0)
    for copy in copies:
        copy.wait()

    def fetch(t):
        for i in range(TILE):
            both = table[list_ref[t * TILE + i]].astype(f32)
            in_x[i] = both[:8]
            in_c[i] = both[8:]

    def give(t):
        for b in range(TILE // 8):
            tokens = [list_ref[t * TILE + 8 * b + k] for k in range(8)]
            sums_e = [acc_e[tokens[k]] + out_e[8 * b + k] for k in range(8)]
            sums_t = [acc_t[tokens[k]] + out_t[8 * b + k] for k in range(8)]
            for k in range(8):
                acc_e[tokens[k]] = sums_e[k]
                acc_t[tokens[k]] = sums_t[k]

    fetch(0)

    def tile(t, carry):
        expert = expert_ref[t]
        slot = expert % 2

        @pl.when((t == 0) | (expert_ref[jnp.maximum(t - 1, 0)] != expert))
        def arrive():
            for copy in weights(expert):
                copy.wait()

            @pl.when(expert + 1 < EXPERTS)
            def ahead():
                for copy in weights(expert + 1):
                    copy.start()

        for j in range(7):
            xb[:, 128 * j : 128 * j + 128] = in_x_flat[pl.ds(j, TILE, 8), :].astype(bf16)
            cb[:, 128 * j : 128 * j + 128] = in_c_flat[pl.ds(j, TILE, 8), :].astype(bf16)
        spread = in_x_flat[pl.ds(7, TILE, 8), :]
        mine = (lane == expert) | (lane == expert + EXPERTS)
        gate = jnp.sum(jnp.where(mine, spread, 0.0), axis=1, keepdims=True)
        fetch(t + 1)
        give(jnp.maximum(t - 1, 0))
        hidden = dot(xb[:, :D], w_up[slot]) + dot(xb[:, D:], b_up[...])
        back = dot_nt(cb[:, :D], w_down[slot]) + dot_nt(cb[:, D:], a_down[...])
        cdf = 0.5 + 0.5 * lax.erf(hidden * 0.7071067811865476)
        slope = cdf + hidden * jnp.exp(hidden * hidden * -0.5) * 0.3989422804014327
        act = (hidden * cdf).astype(bf16)
        act_f = act.astype(f32)
        gate_grad = jnp.sum(act_f * back, axis=1, keepdims=True)
        grad_hidden = (gate * back * slope).astype(bf16)
        act_gate = (gate * act_f).astype(bf16)
        out_main = dot(act_gate, w_down[slot])
        out_low = dot(act_gate, a_down[...])
        in_main = dot_nt(grad_hidden, w_up[slot])
        in_low = dot_nt(grad_hidden, b_up[...])
        gbu_out[...] += dot_tn(grad_hidden, xb[:, D:])
        gad_out[...] += dot_tn(act_gate, cb[:, D:])
        for j in range(6):
            out_e_flat[pl.ds(j, TILE, 8), :] = out_main[:, 128 * j : 128 * j + 128]
            out_t_flat[pl.ds(j, TILE, 8), :] = in_main[:, 128 * j : 128 * j + 128]
        out_e_flat[pl.ds(6, TILE, 8), :] = out_low
        out_t_flat[pl.ds(6, TILE, 8), :] = in_low
        out_t_flat[pl.ds(7, TILE, 8), :] = jnp.where(lane == expert, gate_grad, 0.0)
        return carry

    lax.fori_loop(0, n_tiles, tile, 0)
    give(n_tiles - 1)

    some = IMG_GRP // 4
    for side, (ep_out, tg_out) in enumerate(zip(ep_outs, tg_outs)):

        def image(i, carry):
            slot = i % 2
            base = pl.multiple_of((i + side * some) * SEQP, 16) * 8
            mask = (lane // RANK) == picks_ref[i + side * some]
            rows = pl.ds(pl.multiple_of(i * SEQP, 16), SEQP)
            put_tg = pltpu.make_async_copy(stage_tg.at[slot], tg_out.at[rows], tg_sem.at[slot])
            put_ep = pltpu.make_async_copy(stage_ep.at[slot], ep_out.at[rows], ep_sem.at[slot])

            @pl.when(i >= 2)
            def drain():
                put_tg.wait()
                put_ep.wait()

            def chunk(j):
                flat = acc_e_flat if j < 8 else acc_t_flat
                return flat[pl.ds(base + j % 8, SEQP, 8), :]

            for j in range(6):
                at = slice(128 * j, 128 * j + 128)
                stage_tg[slot, :, at] = chunk(8 + j).astype(bf16)
                stage_ep[slot, :, at] = chunk(j).astype(bf16)
            low_in = repeat_lanes(jnp.where(mask, chunk(14), 0.0))
            low_out = repeat_lanes(jnp.where(mask, chunk(6), 0.0))
            last = jnp.where(lane < 48, low_in, jnp.where(lane < 64, low_out, 0.0))
            stage_tg[slot, :, D:] = jnp.where(lane < 32, chunk(15), last).astype(bf16)
            put_tg.start()
            put_ep.start()
            return carry

        lax.fori_loop(0, some, image, 0)
        for i in range(some - 2, some):
            rows = pl.ds(i * SEQP, SEQP)
            pltpu.make_async_copy(stage_tg.at[i % 2], tg_out.at[rows], tg_sem.at[i % 2]).wait()
            pltpu.make_async_copy(stage_ep.at[i % 2], ep_out.at[rows], ep_sem.at[i % 2]).wait()


def moe_call(token_list, tile_experts, picks, place, tables, places, w_up, w_down, b_up, a_down):
    half = w_up.shape[2]
    n = len(tables)
    n_copies = sum(len(spots) for spots in places)
    anywhere = pl.BlockSpec(memory_space=pl.ANY)
    inside = pl.BlockSpec(memory_space=pltpu.VMEM)
    return pl.pallas_call(
        lambda *refs: moe_kernel(places, *refs),
        grid_spec=pltpu.PrefetchScalarGridSpec(
            num_scalar_prefetch=4,
            grid=(1,),
            in_specs=[anywhere] * (n + 2) + [inside, inside],
            out_specs=[anywhere] * 8 + [inside, inside],
            scratch_shapes=[
                pltpu.VMEM((TOK, 16, 128), bf16),
                pltpu.VMEM((TOK, 8, 128), f32),
                pltpu.VMEM((TOK, 8, 128), f32),
                pltpu.VMEM((TILE, 8, 128), f32),
                pltpu.VMEM((TILE, 8, 128), f32),
                pltpu.VMEM((TILE, 8, 128), f32),
                pltpu.VMEM((TILE, 8, 128), f32),
                pltpu.VMEM((TILE, D + 128), bf16),
                pltpu.VMEM((TILE, D + 128), bf16),
                pltpu.VMEM((2, D, half), bf16),
                pltpu.VMEM((2, half, D), bf16),
                pltpu.VMEM((2, SEQP, D), bf16),
                pltpu.VMEM((2, SEQP, D + 128), bf16),
                pltpu.SemaphoreType.DMA((n_copies,)),
                pltpu.SemaphoreType.DMA((2,)),
                pltpu.SemaphoreType.DMA((2,)),
                pltpu.SemaphoreType.DMA((2,)),
                pltpu.SemaphoreType.DMA((2,)),
            ],
        ),
        out_shape=[
            *[jax.ShapeDtypeStruct((TOK // 4, D), bf16)] * 4,
            *[jax.ShapeDtypeStruct((TOK // 4, D + 128), bf16)] * 4,
            jax.ShapeDtypeStruct((half, ADAPT), f32),
            jax.ShapeDtypeStruct((half, ADAPT), f32),
        ],
        compiler_params=pltpu.CompilerParams(vmem_limit_bytes=58 * 1024 * 1024),
        cost_estimate=pl.CostEstimate(flops=20_000_000_000, bytes_accessed=60_000_000, transcendentals=10_000_000),
    )(token_list, tile_experts, picks, place, *tables, w_up, w_down, b_up, a_down)


def swapped(s):
    return ((s & 1) << 1) | (s >> 1)


def block_spot(block, row, col):
    from_row = block // 4
    s = (block % 4) ^ col
    return 4 * (from_row ^ row) + jnp.where(from_row == 0, swapped(s), s)


def routing(routes, row, col):
    token = jnp.arange(25 * 128, dtype=jnp.int32)[None, :]
    image = token // SEQ
    spot = block_spot(image // 2, row, col) * BLK + (image % 2) * SEQP + token % SEQ
    real = token < IMG_GRP * SEQ
    picked = jnp.pad(routes.T, ((0, 0), (0, 25 * 128 - IMG_GRP * SEQ)), constant_values=EXPERTS)
    beyond = EXPERTS * 4096 + DUMMY
    keys = jnp.where(real, picked * 4096 + spot, beyond).reshape(-1)
    experts = jnp.arange(EXPERTS, dtype=jnp.int32)
    count = jnp.sum((picked[None] == experts[:, None, None]).astype(jnp.int32), axis=(1, 2))
    tiles = (jnp.maximum(count, 1) + TILE - 1) // TILE
    extra = tiles * TILE - count
    filler = jnp.where(
        jnp.arange(256, dtype=jnp.int32)[None, :] < extra[:, None], (experts * 4096)[:, None] + DUMMY, beyond
    ).reshape(-1)
    ordered = lax.sort(jnp.concatenate([keys, filler])) & 4095
    ends = jnp.sum(jnp.where(experts[None, :] <= experts[:, None], tiles[None, :], 0), axis=1)
    steps = jnp.arange(max_tiles(), dtype=jnp.int32)
    owner = jnp.minimum(jnp.sum((ends[None, :] <= steps[:, None]).astype(jnp.int32), axis=1), EXPERTS - 1)
    return ordered, jnp.concatenate([owner, jnp.sum(tiles)[None]])


HEADS = 12
HEAD_DIM = 64


def pick_mask(pick):
    return (lane_iota((1, ADAPT)) // RANK) == pick


def norm_stats(values):
    centre = jnp.sum(values, axis=1, keepdims=True) * (1.0 / D)
    shifted = values - centre
    spread = jnp.sum(shifted * shifted, axis=1, keepdims=True) * (1.0 / D)
    inverse = lax.rsqrt(spread + 1e-06)
    return shifted * inverse, inverse


def norm_back(grad, gain, unit, inverse):
    scaled = grad * gain
    total = jnp.sum(scaled, axis=1, keepdims=True) * (1.0 / D)
    along = jnp.sum(scaled * unit, axis=1, keepdims=True) * (1.0 / D)
    return inverse * (scaled - total - unit * along)


def qkv_copies(place_ref, blocks, own_b, scratch, sem):
    w_qkv, a_qkv, b_qkv = scratch
    row, col = place_ref[0], place_ref[1]
    copies = []

    def copy(source, target):
        copies.append(pltpu.make_async_copy(source, target, sem.at[len(copies)]))

    for t in range(2):
        half_at = pl.multiple_of((row ^ t) * 384, 128)
        for s in range(4):
            block = blocks[4 * t + s]
            at = pl.multiple_of((col ^ s) * 192, 64)
            low_at = pl.multiple_of((col ^ s) * 192 + (row ^ t) * 96, 32)
            for p in range(3):
                copy(block.at[pl.ds(192 * p, 192)], w_qkv.at[p, pl.ds(at, 192), pl.ds(half_at, 384)])
                copy(block.at[pl.ds(576, 96), pl.ds(128 * p, 128)], a_qkv.at[p, pl.ds(low_at, 96), :])
        for p in range(3):
            source = own_b.at[p] if t == 0 else blocks[4].at[pl.ds(W_ROWS + 128 * p, 128)]
            copy(source, b_qkv.at[p, :, pl.ds(half_at, 384)])
    return copies


def out_copies(place_ref, far_block, own_a, out_w, scratch, sem):
    w_out, a_out = scratch
    row = place_ref[0]
    copies = []

    def copy(source, target):
        copies.append(pltpu.make_async_copy(source, target, sem.at[len(copies)]))

    for t in range(2):
        half_at = pl.multiple_of((row ^ t) * 384, 128)
        copy(out_w[t].at[pl.ds(0, 384)], w_out.at[pl.ds(half_at, 384), :])
        for j in range(3):
            if t == 0:
                source = own_a.at[pl.ds(128 * j, 128)]
            else:
                source = far_block.at[pl.ds(W_ROWS + 384, 128), pl.ds(128 * j, 128)]
            copy(source, a_out.at[pl.ds(half_at + 128 * j, 128), :])
    return copies


W_ROWS = 944
QKV_SCRATCH = [
    pltpu.VMEM((3, D, D), bf16),
    pltpu.VMEM((3, D, ADAPT), bf16),
    pltpu.VMEM((3, ADAPT, D), bf16),
    pltpu.SemaphoreType.DMA((54,)),
]
OUT_SCRATCH = [
    pltpu.VMEM((D, D), bf16),
    pltpu.VMEM((D, ADAPT), bf16),
    pltpu.SemaphoreType.DMA((8,)),
]


def split_kernel(place_ref, tokens_ref, cot_ref, own_out, one_out, two_out, three_out, left, right, stage, sem):
    rows = tokens_ref.shape[0]
    width = D // 4
    left[0:rows, 0:width] = tokens_ref[...].astype(f32)
    right[0:rows, 0:width] = cot_ref[...].astype(f32)
    lane = lane_iota((1, 128))
    real = lax.broadcasted_iota(jnp.int32, (SEQP, 1), 0) < SEQ
    for i in range(8):
        at = slice(SEQ * i, SEQ * i + SEQP)
        spot = slice(SEQP * (i % 2), SEQP * (i % 2) + SEQP)
        moved = pltpu.roll(right[at, :], 64, 1)
        middle = jnp.where(lane < 64, left[at, 128:256], moved[:, 0:128])
        stage[i // 2, spot, 0:128] = jnp.where(real, left[at, 0:128], 0.0).astype(bf16)
        stage[i // 2, spot, 128:256] = jnp.where(real, middle, 0.0).astype(bf16)
        stage[i // 2, spot, 256:384] = jnp.where(real, moved[:, 128:256], 0.0).astype(bf16)
    copies = [
        pltpu.make_async_copy(stage.at[place_ref[1] ^ s], out, sem.at[s])
        for s, out in enumerate((own_out, one_out, two_out, three_out))
    ]
    for copy in copies:
        copy.start()
    for copy in copies:
        copy.wait()


def split_call(place, tokens, cotangent):
    rows = tokens.shape[0]
    tall = -(-(SEQ * 7 + SEQP) // 8) * 8
    inside = pl.BlockSpec(memory_space=pltpu.VMEM)
    return pl.pallas_call(
        split_kernel,
        grid_spec=pltpu.PrefetchScalarGridSpec(
            num_scalar_prefetch=1,
            grid=(1,),
            in_specs=[inside, inside],
            out_specs=[ANYWHERE] * 4,
            scratch_shapes=[
                pltpu.VMEM((tall, 256), f32),
                pltpu.VMEM((tall, 256), f32),
                pltpu.VMEM((4, BLK, 384), bf16),
                pltpu.SemaphoreType.DMA((4,)),
            ],
        ),
        out_shape=[jax.ShapeDtypeStruct((BLK, 384), bf16)] * 4,
        compiler_params=pltpu.CompilerParams(vmem_limit_bytes=32 * 1024 * 1024),
        cost_estimate=pl.CostEstimate(flops=1_000_000_000, bytes_accessed=3_000_000, transcendentals=0),
    )(place, tokens, cotangent)


def finish_kernel(place_ref, mine, one, two, three, far, dp_sums, *refs):
    (
        a_qkv, b_qkv, a_out, b_out, a_router, b_router, a_up, b_up, a_down, b_down, wide, tall, every,
    ) = refs
    row, col = place_ref[0], place_ref[1]
    near_at = pl.multiple_of(row * 96, 32)
    far_at = pl.multiple_of((1 - row) * 96, 32)
    for p in range(4):
        ours = mine[96 * p : 96 * p + 96, :].astype(f32)
        theirs = far[96 * p : 96 * p + 96, :].astype(f32)
        if p < 3:
            a_qkv[p, pl.ds(near_at, 96), :] = ours
            a_qkv[p, pl.ds(far_at, 96), :] = theirs
        else:
            wide[pl.ds(near_at, 96), :] = ours
            wide[pl.ds(far_at, 96), :] = theirs
    b_out[...] = wide[...].T[:, : D // 4]
    share = BOTH_ROWS // 8
    for s, got in enumerate((mine, one, two, three)):
        base = 384 if s == 0 else 0
        at = pl.multiple_of((col ^ s) * 96, 32)
        for p in range(4):
            piece = got[base + 96 * p : base + 96 * p + 96, :].astype(f32)
            if p < 3:
                tall[p, pl.ds(at, 96), :] = piece
            else:
                a_out[pl.ds(at, 96), :] = piece
        ours = got[base + 384 : base + 384 + share, :].astype(f32)
        theirs = far[384 + share * s : 384 + share * s + share, :].astype(f32)
        every[pl.ds(pl.multiple_of((row * 4 + (col ^ s)) * share, 64), share), :] = ours
        every[pl.ds(pl.multiple_of(((1 - row) * 4 + (col ^ s)) * share, 64), share), :] = theirs
    for p in range(3):
        b_qkv[p] = tall[p].T
    a_router[...] = every[0:768, :]
    a_up[...] = every[768:1536, :]
    b_down[...] = every[1536:2304, :].T
    b_router[...] = every[2304:2432, :].T[:, :EXPERTS]
    b_up[...] = dp_sums[0:384, :].astype(f32).T
    a_down[...] = dp_sums[384:768, :].astype(f32)


def finish_call(place, mine, got, far, dp_sums):
    inside = pl.BlockSpec(memory_space=pltpu.VMEM)
    half = D // 2
    shapes = [
        (3, D // 4, ADAPT), (3, ADAPT, half), (half, ADAPT), (ADAPT, D // 4), (D, ADAPT), (ADAPT, EXPERTS),
        (D, ADAPT), (ADAPT, half), (half, ADAPT), (ADAPT, D),
    ]
    return pl.pallas_call(
        finish_kernel,
        grid_spec=pltpu.PrefetchScalarGridSpec(
            num_scalar_prefetch=1,
            grid=(1,),
            in_specs=[inside] * 6,
            out_specs=[inside] * 10,
            scratch_shapes=[
                pltpu.VMEM((256, 128), f32),
                pltpu.VMEM((3, half, 128), f32),
                pltpu.VMEM((BOTH_ROWS, 128), f32),
            ],
        ),
        out_shape=[jax.ShapeDtypeStruct(shape, f32) for shape in shapes],
        compiler_params=pltpu.CompilerParams(vmem_limit_bytes=32 * 1024 * 1024),
        cost_estimate=pl.CostEstimate(flops=1_000_000_000, bytes_accessed=4_000_000, transcendentals=0),
    )(place, mine, *got, far, dp_sums)


def merge_kernel(place_ref, *refs):
    blocks, refs = refs[:4], refs[4:]
    block_out, tokens_out, stage, tall, sem = refs
    copies = [
        pltpu.make_async_copy(block, stage.at[place_ref[1] ^ s], sem.at[s]) for s, block in enumerate(blocks)
    ]
    for copy in copies:
        copy.start()
    for copy in copies:
        copy.wait()
    width = D // 4
    rows = tokens_out.shape[0]
    for i in range(8):
        at = slice(SEQ * i, SEQ * i + SEQ)
        both = stage[i // 2, SEQP * (i % 2) : SEQP * (i % 2) + SEQP, :].astype(f32)[:SEQ]
        tokens_out[at, :] = both[:, :width]
        tall[at, :] = both[:, width:]
    block_out[...] = tall[0:rows, :].astype(bf16)


def merge_call(place, blocks, rows):
    width = D // 4
    inside = pl.BlockSpec(memory_space=pltpu.VMEM)
    return pl.pallas_call(
        merge_kernel,
        grid_spec=pltpu.PrefetchScalarGridSpec(
            num_scalar_prefetch=1,
            grid=(1,),
            in_specs=[ANYWHERE] * 4,
            out_specs=[inside, inside],
            scratch_shapes=[
                pltpu.VMEM((4, BLK, 2 * width), bf16),
                pltpu.VMEM((rows, width), f32),
                pltpu.SemaphoreType.DMA((4,)),
            ],
        ),
        out_shape=[jax.ShapeDtypeStruct((rows, width), bf16), jax.ShapeDtypeStruct((rows, width), f32)],
        compiler_params=pltpu.CompilerParams(vmem_limit_bytes=32 * 1024 * 1024),
        cost_estimate=pl.CostEstimate(flops=8_000_000_000, bytes_accessed=3_000_000, transcendentals=0),
    )(place, *blocks)


def place_weights(place_ref, blocks, own_b, own_a, out_w, w_qkv, a_qkv, b_qkv, w_out, a_out):
    row, col = place_ref[0], place_ref[1]
    for t in range(2):
        half_at = pl.multiple_of((row ^ t) * 384, 128)
        across = pl.ds(half_at, 384)
        for s in range(4):
            block = blocks[4 * t + s]
            at = pl.multiple_of((col ^ s) * 192, 64)
            low_at = pl.multiple_of((col ^ s) * 192 + (row ^ t) * 96, 32)
            for p in range(3):
                w_qkv[p, pl.ds(at, 192), across] = block[192 * p : 192 * p + 192, :]
                a_qkv[p, pl.ds(low_at, 96), :] = block[576:672, 128 * p : 128 * p + 128]
        w_out[across, :] = out_w[t][0:384, :]
        for p in range(3):
            down = pl.ds(pl.multiple_of(half_at + 128 * p, 128), 128)
            if t == 0:
                b_qkv[p, :, across] = own_b[p]
                a_out[down, :] = own_a[128 * p : 128 * p + 128, :]
            else:
                b_qkv[p, :, across] = blocks[4][W_ROWS + 128 * p : W_ROWS + 128 * p + 128, :]
                a_out[down, :] = blocks[4][W_ROWS + 384 : W_ROWS + 512, 128 * p : 128 * p + 128]


def attend_kernel(picks_ref, place_ref, *refs):
    blocks, refs = refs[:8], refs[8:]
    (
        own_b, own_a, out_near, out_far, x_ref, gain_one, gain_two, b_out,
        two_out, resid_out, normed_out, qkv_out, mixed_out, probs_out, lows_out,
        w_qkv, a_qkv, b_qkv, w_out, a_out,
    ) = refs
    image = pl.program_id(0)

    @pl.when(image == 0)
    def start():
        place_weights(place_ref, blocks, own_b, own_a, (out_near, out_far), w_qkv, a_qkv, b_qkv, w_out, a_out)

    mask = pick_mask(picks_ref[image])
    x = x_ref[...].astype(f32)
    unit, unused = norm_stats(x)
    normed = (unit * gain_one[...]).astype(bf16)
    normed_out[...] = normed
    for p in range(3):
        low = jnp.where(mask, dot(normed, a_qkv[p]), 0.0).astype(bf16)
        lows_out[:, 128 * p : 128 * p + 128] = low
        qkv_out[p] = (dot(normed, w_qkv[p]) + dot(low, b_qkv[p])).astype(bf16)
    lane = lane_iota((1, 128))
    key_lane = lane_iota((1, SEQP))
    for pair in range(HEADS // 2):
        at = slice(128 * pair, 128 * pair + 128)
        q = qkv_out[0, :, at]
        k = qkv_out[1, :, at]
        v = qkv_out[2, :, at]
        parts = []
        for side in range(2):
            own = (lane // HEAD_DIM) == side
            scores = dot_nt(jnp.where(own, q, jnp.zeros_like(q)), k) * (HEAD_DIM**-0.5)
            scores = jnp.where(key_lane < SEQ, scores, -1e30)
            power = jnp.exp(scores - jnp.max(scores, axis=1, keepdims=True))
            probs = (power / jnp.sum(power, axis=1, keepdims=True)).astype(bf16)
            probs_out[0, 2 * pair + side] = probs
            parts.append(dot(probs, v))
        mixed_out[:, at] = jnp.where(lane < HEAD_DIM, parts[0], parts[1]).astype(bf16)
    mixed = mixed_out[...]
    low = jnp.where(mask, dot(mixed, a_out[...]), 0.0).astype(bf16)
    lows_out[:, 384:512] = low
    resid = x + dot(mixed, w_out[...]) + dot(low, b_out[...])
    resid_out[...] = resid
    unit, unused = norm_stats(resid)
    real = lax.broadcasted_iota(jnp.int32, (SEQP, 1), 0) < SEQ
    two_out[...] = jnp.where(real, unit * gain_two[...], 0.0).astype(bf16)


def image_rows(lanes):
    return pl.BlockSpec((SEQP, lanes), lambda i, *_: (i, 0))


def kept(*shape):
    return pl.BlockSpec(shape, lambda i, *_: (0,) * len(shape))


QKV_SPEC = pl.BlockSpec((3, SEQP, D), lambda i, *_: (0, i, 0))
PROBS_SPEC = pl.BlockSpec((1, HEADS, SEQP, SEQP), lambda i, *_: (i, 0, 0, 0))
ANYWHERE = pl.BlockSpec(memory_space=pl.ANY)


def attend_call(picks, place, blocks, own_b, own_a, out_w, x, gain_one, gain_two, b_out):
    rows = x.shape[0]
    return pl.pallas_call(
        attend_kernel,
        grid_spec=pltpu.PrefetchScalarGridSpec(
            num_scalar_prefetch=2,
            grid=(2,),
            in_specs=[kept(*block.shape) for block in (*blocks, own_b, own_a, *out_w)]
            + [image_rows(D), kept(1, D), kept(1, D), kept(ADAPT, D)],
            out_specs=[
                image_rows(D), image_rows(D), image_rows(D), QKV_SPEC,
                image_rows(D), PROBS_SPEC, image_rows(512),
            ],
            scratch_shapes=QKV_SCRATCH[:-1] + OUT_SCRATCH[:-1],
        ),
        out_shape=[
            jax.ShapeDtypeStruct((rows, D), bf16),
            jax.ShapeDtypeStruct((rows, D), f32),
            jax.ShapeDtypeStruct((rows, D), bf16),
            jax.ShapeDtypeStruct((3, rows, D), bf16),
            jax.ShapeDtypeStruct((rows, D), bf16),
            jax.ShapeDtypeStruct((2, HEADS, SEQP, SEQP), bf16),
            jax.ShapeDtypeStruct((rows, 512), bf16),
        ],
        compiler_params=pltpu.CompilerParams(vmem_limit_bytes=60 * 1024 * 1024),
        cost_estimate=pl.CostEstimate(flops=4_000_000_000, bytes_accessed=15_000_000, transcendentals=2_000_000),
    )(picks, place, *blocks, own_b, own_a, *out_w, x, gain_one, gain_two, b_out)


def out_back_kernel(picks_ref, place_ref, *refs):
    (
        far_block, own_a, out_near, out_far, gain_two, b_out, two_ref, resid_ref, mixed_ref, lows_ref,
        cot_ref, grad_a, grad_b, w_router, a_router, b_router, a_up, b_down,
        resid_grad_out, mixed_grad_out, base_out, both_out, a_part_out, b_part_out,
        w_out, a_out, sem, both, a_part, b_part,
    ) = refs
    image = pl.program_id(0)

    @pl.when(image == 0)
    def start():
        copies = out_copies(place_ref, far_block, own_a, (out_near, out_far), (w_out, a_out), sem)
        for copy in copies:
            copy.start()
        for part in (both, a_part, b_part):
            part[...] = jnp.zeros_like(part)
        for copy in copies:
            copy.wait()

    mask = pick_mask(picks_ref[image])
    lane = lane_iota((1, 128))

    def add_part(row, value):
        at = slice(row, row + value.shape[0])
        both[at, :] += value

    two = two_ref[...]
    received = grad_a[...].astype(f32) + grad_b[...].astype(f32)
    low_r = jnp.where(mask, dot(two, a_router[...]), 0.0).astype(bf16)
    logits = dot(two, w_router[...]) + dot(low_r, b_router[...])
    logits = jnp.where(lane < EXPERTS, logits, -1e30)
    power = jnp.exp(logits - jnp.max(logits, axis=1, keepdims=True))
    probs = power / jnp.sum(power, axis=1, keepdims=True)
    last = received[:, D:]
    grad_probs = jnp.where(lane < EXPERTS, last, 0.0)
    low_in = jnp.where(mask, repeat_lanes(jnp.where((lane >= 32) & (lane < 48), last, 0.0)), 0.0).astype(bf16)
    low_out = jnp.where(mask, repeat_lanes(jnp.where((lane >= 48) & (lane < 64), last, 0.0)), 0.0).astype(bf16)
    cot = cot_ref[...]
    resid = resid_ref[...]
    base_out[...] = resid + dot(low_out, b_down[...])
    add_part(768, dot_tn(two, low_in))
    add_part(1536, dot_tn(cot, low_out))
    grad_logits = probs * (grad_probs - jnp.sum(probs * grad_probs, axis=1, keepdims=True))
    grad_logits = grad_logits.astype(bf16)
    grad_low = jnp.where(mask, dot_nt(grad_logits, b_router[...]), 0.0).astype(bf16)
    grad_two = received[:, :D] + dot_nt(low_in, a_up[...])
    grad_two = grad_two + dot_nt(grad_logits, w_router[...]) + dot_nt(grad_low, a_router[...])
    add_part(0, dot_tn(two, grad_low))
    add_part(2304, dot_tn(grad_logits, low_r))
    unit, inverse = norm_stats(resid)
    grad_resid = cot.astype(f32) + norm_back(grad_two, gain_two[...], unit, inverse)
    resid_grad_out[...] = grad_resid
    grad_attn = grad_resid.astype(bf16)
    grad_low = jnp.where(mask, dot_nt(grad_attn, b_out[...]), 0.0).astype(bf16)
    mixed_grad_out[...] = (dot_nt(grad_attn, w_out[...]) + dot_nt(grad_low, a_out[...])).astype(bf16)
    a_part[...] += dot_tn(mixed_ref[...], grad_low)
    b_part[...] += dot_tn(grad_attn, lows_ref[:, 384:512])

    @pl.when(image == 1)
    def finish():
        both_out[...] = both[...].astype(bf16)
        a_part_out[...] = a_part[...].astype(bf16)
        b_part_out[...] = b_part[...].astype(bf16)


BOTH_ROWS = 2560


def out_back_call(picks, place, far_block, own_a, out_w, gain_two, b_out, two, resid, mixed, lows, cot, grad_a, grad_b,
                  w_router, a_router, b_router, a_up, b_down):
    rows = two.shape[0]
    return pl.pallas_call(
        out_back_kernel,
        grid_spec=pltpu.PrefetchScalarGridSpec(
            num_scalar_prefetch=2,
            grid=(2,),
            in_specs=[ANYWHERE] * 4
            + [kept(1, D), kept(ADAPT, D), image_rows(D), image_rows(D), image_rows(D), image_rows(512)]
            + [image_rows(D), image_rows(D + 128), image_rows(D + 128)]
            + [kept(D, 128), kept(D, ADAPT), kept(ADAPT, 128), kept(D, ADAPT), kept(ADAPT, D)],
            out_specs=[image_rows(D), image_rows(D), image_rows(D), kept(BOTH_ROWS, 128), kept(D, 128), kept(D, 128)],
            scratch_shapes=OUT_SCRATCH
            + [pltpu.VMEM((BOTH_ROWS, 128), f32), pltpu.VMEM((D, 128), f32), pltpu.VMEM((D, 128), f32)],
        ),
        out_shape=[
            jax.ShapeDtypeStruct((rows, D), f32),
            jax.ShapeDtypeStruct((rows, D), bf16),
            jax.ShapeDtypeStruct((rows, D), f32),
            jax.ShapeDtypeStruct((BOTH_ROWS, 128), bf16),
            jax.ShapeDtypeStruct((D, 128), bf16),
            jax.ShapeDtypeStruct((D, 128), bf16),
        ],
        compiler_params=pltpu.CompilerParams(vmem_limit_bytes=60 * 1024 * 1024),
        cost_estimate=pl.CostEstimate(flops=6_000_000_000, bytes_accessed=15_000_000, transcendentals=100_000),
    )(picks, place, far_block, own_a, *out_w, gain_two, b_out, two, resid, mixed, lows, cot, grad_a, grad_b,
      w_router, a_router, b_router, a_up, b_down)


def qkv_back_kernel(picks_ref, place_ref, *refs):
    blocks, refs = refs[:8], refs[8:]
    (
        own_b, x_ref, gain_one, normed_ref, qkv_ref, probs_ref, lows_ref, resid_grad, grad_mixed,
        tokens_out, a_part_out, b_part_out,
        w_qkv, a_qkv, b_qkv, sem, a_part, b_part, grads,
    ) = refs
    image = pl.program_id(0)
    copies = qkv_copies(place_ref, blocks, own_b, (w_qkv, a_qkv, b_qkv), sem)

    @pl.when(image == 0)
    def start():
        for copy in copies:
            copy.start()
        a_part[...] = jnp.zeros_like(a_part)
        b_part[...] = jnp.zeros_like(b_part)

    mask = pick_mask(picks_ref[image])
    lane = lane_iota((1, 128))
    for pair in range(HEADS // 2):
        at = slice(128 * pair, 128 * pair + 128)
        q = qkv_ref[0, :, at]
        k = qkv_ref[1, :, at]
        v = qkv_ref[2, :, at]
        gm = grad_mixed[:, at]
        found = []
        for side in range(2):
            own = (lane // HEAD_DIM) == side
            weights = probs_ref[0, 2 * pair + side]
            weights_f = weights.astype(f32)
            grad_w = dot_nt(jnp.where(own, gm, jnp.zeros_like(gm)), v)
            inner = jnp.sum(weights_f * grad_w, axis=1, keepdims=True)
            grad_s = (weights_f * (grad_w - inner)).astype(bf16)
            found.append(
                (
                    dot(grad_s, k) * (HEAD_DIM**-0.5),
                    dot_tn(grad_s, q) * (HEAD_DIM**-0.5),
                    dot_tn(weights, gm),
                )
            )
        for p in range(3):
            grads[p, :, at] = jnp.where(lane < HEAD_DIM, found[0][p], found[1][p]).astype(bf16)

    @pl.when(image == 0)
    def arrived():
        for copy in copies:
            copy.wait()

    normed = normed_ref[...]
    grad_normed = jnp.zeros((SEQP, D), f32)
    for p in range(3):
        piece = grads[p]
        grad_low = jnp.where(mask, dot_nt(piece, b_qkv[p]), 0.0).astype(bf16)
        grad_normed = grad_normed + dot_nt(piece, w_qkv[p]) + dot_nt(grad_low, a_qkv[p])
        a_part[D * p : D * p + D, :] += dot_tn(normed, grad_low)
        b_part[D * p : D * p + D, :] += dot_tn(piece, lows_ref[:, 128 * p : 128 * p + 128])
    unit, inverse = norm_stats(x_ref[...].astype(f32))
    tokens_out[...] = (resid_grad[...] + norm_back(grad_normed, gain_one[...], unit, inverse)).astype(bf16)

    @pl.when(image == 1)
    def finish():
        a_part_out[...] = a_part[...].astype(bf16)
        b_part_out[...] = b_part[...].astype(bf16)


def qkv_back_call(picks, place, blocks, own_b, x, gain_one, normed, qkv, probs, lows, resid_grad, grad_mixed):
    rows = x.shape[0]
    return pl.pallas_call(
        qkv_back_kernel,
        grid_spec=pltpu.PrefetchScalarGridSpec(
            num_scalar_prefetch=2,
            grid=(2,),
            in_specs=[ANYWHERE] * (len(blocks) + 1)
            + [image_rows(D), kept(1, D), image_rows(D), QKV_SPEC, PROBS_SPEC, image_rows(512)]
            + [image_rows(D), image_rows(D)],
            out_specs=[image_rows(D), kept(3 * D, 128), kept(3 * D, 128)],
            scratch_shapes=QKV_SCRATCH
            + [
                pltpu.VMEM((3 * D, 128), f32),
                pltpu.VMEM((3 * D, 128), f32),
                pltpu.VMEM((3, SEQP, D), bf16),
            ],
        ),
        out_shape=[
            jax.ShapeDtypeStruct((rows, D), bf16),
            jax.ShapeDtypeStruct((3 * D, 128), bf16),
            jax.ShapeDtypeStruct((3 * D, 128), bf16),
        ],
        compiler_params=pltpu.CompilerParams(vmem_limit_bytes=60 * 1024 * 1024),
        cost_estimate=pl.CostEstimate(flops=9_000_000_000, bytes_accessed=15_000_000, transcendentals=1000),
    )(picks, place, *blocks, own_b, x, gain_one, normed, qkv, probs, lows, resid_grad, grad_mixed)


TABLES = (((0, 0), (1, 0)), ((0, 1), (0, 2), (1, 1), (1, 2)), ((0, 3), (1, 3)))


def across_row(value):
    return lax.ppermute(value, "row", [(0, 1), (1, 0)])


def across_col(value, step):
    return lax.ppermute(value, "col", [(i, i ^ step) for i in range(4)])


def by_place(blocks, col):
    found = []
    for place in range(4):
        value = blocks[place]
        for other in range(1, 4):
            value = jnp.where(col == other, blocks[place ^ other], value)
        found.append(value)
    return found


def across_chip(value, first, second):
    pairs = [(i, i ^ first) for i in range(4)] + [(4 + i, 4 + (i ^ second)) for i in range(4)]
    return lax.ppermute(value, ("row", "col"), pairs)


def gather_col(value, row):
    from_x = across_col(value, 1)
    from_y = across_col(value, 2)
    return [value, from_x, from_y, across_chip(jnp.where(row == 0, from_x, from_y), 2, 1)]


def added(*values):
    total = values[0].astype(f32)
    for value in values[1:]:
        total = total + value.astype(f32)
    return total


def last_exchange(kept_rows, got):
    sent = added(kept_rows[BLK:], got[BLK:]).astype(bf16)
    return added(kept_rows[:BLK], got[:BLK]).astype(bf16), across_chip(sent, 2, 1)


def at_place(value, axis, place):
    return lax.dynamic_index_in_dim(value, place, axis, keepdims=False)


def scatter_dp(value):
    place = lax.axis_index("dp")
    view = value.reshape(4, -1, 128)
    found = [at_place(view, 0, place)]
    for s in range(1, 4):
        found.append(across_dp(at_place(view, 0, place ^ s), s))
    return added(*found).astype(bf16)


def across_dp(value, step):
    return lax.ppermute(value, "dp", [(i, i ^ step) for i in range(4)])


def spread_dp(value):
    return jnp.concatenate(by_place([value] + [across_dp(value, s) for s in range(1, 4)], lax.axis_index("dp")))


def part_share(col_parts, row_parts, both_parts, place):
    col_parts = at_place(col_parts.reshape(4, 4, 2, 96, 128), 2, place)
    row_parts = at_place(row_parts.reshape(4, 2, 4, 96, 128), 1, place)
    both_parts = at_place(both_parts.reshape(2, 4, BOTH_ROWS // 8, 128), 0, place)
    col_parts = col_parts.swapaxes(0, 1).reshape(4, 384, 128)
    row_parts = row_parts.swapaxes(0, 1).reshape(4, 384, 128)
    return jnp.concatenate([col_parts, row_parts, both_parts], axis=1)


def exchange_col(value, col):
    return [at_place(value, 0, col)] + [across_col(at_place(value, 0, col ^ s), s) for s in range(1, 4)]


def to_features(first, second, col):
    width = D // 4
    pieces = []
    for p in range(4):
        at = slice(width * p, width * p + width)
        pieces.append(jnp.concatenate([first[:, at], second[:, at]], axis=1))
    sent = by_place(pieces, col)
    return [sent[0]] + [across_col(sent[s], s) for s in range(1, 4)]


def on_device(
    tokens, cotangent, routes, adapter_pick, gain_attn, gain_moe, w_qkv, w_out, w_router, w_up, w_down,
    a_qkv, b_qkv, a_out, b_out, a_router, b_router, a_up, b_up, a_down, b_down,
):
    row = lax.axis_index("row")
    col = lax.axis_index("col")
    me = row * 4 + col
    place = jnp.stack([row, col]).astype(jnp.int32)

    width = D // 4
    half = D // 2
    gains = []
    for gain in (gain_attn, gain_moe):
        left = gain
        for unused in range(3):
            lead = lax.reduce_precision(left, 8, 7)
            gains.append(lead.astype(bf16))
            left = left - lead
    small = jnp.concatenate([w_out, b_out, jnp.stack(gains), jnp.zeros((26, width), bf16)], axis=0)
    low = at_place(a_qkv.reshape(3, 2, 96, ADAPT), 1, row)
    packed = jnp.concatenate(
        [w_qkv.reshape(576, half), jnp.concatenate([low[0], low[1], low[2]], axis=1),
         jnp.concatenate([small[:272], small[272:]], axis=1)]
    )
    for_row = jnp.concatenate(
        [packed, b_qkv.reshape(half, half), jnp.concatenate([a_out[:128], a_out[128:256], a_out[256:]], axis=1)]
    )
    pairs = split_call(place, tokens, cotangent)
    from_x, from_y = across_col(packed, 1), across_col(packed, 2)
    from_x, from_y, *pairs = lax.optimization_barrier((from_x, from_y, *pairs))
    near = [packed, from_x, from_y, across_chip(jnp.where(row == 0, from_x, from_y), 2, 1)]
    pairs = by_place([pairs[0]] + [across_col(pairs[s], s) for s in range(1, 4)], col)
    x = jnp.concatenate([pair[:, :width] for pair in pairs], axis=1)
    cot = jnp.concatenate([pair[:, width:] for pair in pairs], axis=1)
    far = [across_row(for_row)] + [across_row(block) for block in near[1:]]
    blocks = near + far

    def assembled(group):
        parts = by_place([block[672:944] for block in group], col)
        return jnp.concatenate(
            [jnp.concatenate([part[:, :width] for part in parts], axis=1),
             jnp.concatenate([part[:, width:] for part in parts], axis=1)], axis=0
        )

    out_w = [assembled(near), assembled(far)]
    full_b_out = out_w[0][384:512]
    gain_rows = out_w[0][512:518].astype(f32)
    gain_one = jnp.sum(gain_rows[:3], axis=0, keepdims=True)
    gain_two = jnp.sum(gain_rows[3:], axis=0, keepdims=True)

    picks_group = lax.dynamic_slice_in_dim(adapter_pick, lax.axis_index("dp") * IMG_GRP, IMG_GRP)
    order = jnp.arange(IMG_GRP, dtype=jnp.int32)
    picks = jnp.take(picks_group, ((order // 2) ^ me) * 2 + order % 2)
    spot_picks = jnp.sum(
        jnp.where(block_spot(order // 2, row, col)[None, :] * 2 + order[None, :] % 2 == order[:, None], picks_group[None, :], 0), axis=1
    )
    token_list, tile_experts = routing(routes, row, col)
    wide_router = jnp.concatenate([w_router, w_router, jnp.zeros((D, 64), bf16)], axis=1)
    wide_b_router = jnp.concatenate([b_router, b_router, jnp.zeros((ADAPT, 64), bf16)], axis=1)
    slim_router = jnp.concatenate([w_router, jnp.zeros((D, 96), bf16)], axis=1)
    slim_b_router = jnp.concatenate([b_router, jnp.zeros((ADAPT, 96), bf16)], axis=1)

    x, token_list, tile_experts, wide_router, wide_b_router, slim_router, slim_b_router = lax.optimization_barrier(
        (x, token_list, tile_experts, wide_router, wide_b_router, slim_router, slim_b_router)
    )
    cot, unused = lax.optimization_barrier((cot, near[3]))
    two, resid, normed, qkv, mixed, probs, lows = attend_call(
        picks, place, blocks, b_qkv, a_out, out_w, x, gain_one, gain_two, full_b_out
    )
    cot_near = gather_col(cot, row)
    two_x, two_y = across_col(two, 1), across_col(two, 2)

    def table(spots, twos, cots):
        return table_call(
            jnp.stack([picks[8 * t + 2 * s + side] for t, s in spots for side in range(2)]),
            twos, cots, a_up, b_down, wide_router, a_router, wide_b_router,
        )

    cot_far = [across_row(block) for block in cot_near]
    tables = [table(TABLES[0], [two, across_row(two)], [cot, cot_far[0]])]
    two_x, two_y, tables[0] = lax.optimization_barrier((two_x, two_y, tables[0]))
    diag = across_chip(jnp.where(row == 0, two_x, two_y), 2, 1)
    tables.append(
        table(TABLES[1], [two_x, two_y, across_row(two_x), across_row(two_y)], [cot_near[1], cot_near[2], cot_far[1], cot_far[2]])
    )
    diag, *tables = lax.optimization_barrier((diag, *tables))
    tables.append(table(TABLES[2], [diag, across_row(diag)], [cot_near[3], cot_far[3]]))
    *moved, part_b_up, part_a_down = moe_call(
        token_list, tile_experts, spot_picks, place, tables, TABLES, w_up, w_down, b_up, a_down
    )
    sums, grads = moved[:4], moved[4:]
    dp_parts = jnp.concatenate([part_b_up.astype(bf16), part_a_down.astype(bf16)])
    grad_sent = added(grads[1], across_row(grads[3])).astype(bf16)
    grad_kept = added(grads[0], across_row(grads[2])).astype(bf16)
    grad_sent, dp_parts, *sums = lax.optimization_barrier((grad_sent, dp_parts, *sums))
    grad_got = across_chip(grad_sent, 1, 2)
    sum_kept, sum_sent = across_row(sums[2]), across_row(sums[3])
    sums = [
        added(near[at : at + BLK], far[at : at + BLK]).astype(bf16)
        for near, far in ((sums[0], sum_kept), (sums[1], sum_sent)) for at in (0, BLK)
    ]
    four_dp = lax.axis_size("dp") == 4
    dp_sums = scatter_dp(dp_parts) if four_dp else lax.psum(dp_parts, "dp")
    grad_got, dp_sums, *sums = lax.optimization_barrier((grad_got, dp_sums, *sums))
    grad_a, grad_b = last_exchange(grad_kept, grad_got)
    if four_dp:
        dp_sums = spread_dp(dp_sums)
    grad_a, grad_b, dp_sums, *sums = lax.optimization_barrier((grad_a, grad_b, dp_sums, *sums))
    sums = [sums[0], across_chip(sums[1], 2, 1), across_chip(sums[2], 1, 2), across_chip(sums[3], 3, 3)]
    resid_grad, mixed_grad, base, both_parts, part_a_out, part_b_out = out_back_call(
        picks, place, blocks[4], a_out, out_w, gain_two, full_b_out, two, resid, mixed, lows, cot, grad_a, grad_b,
        slim_router, a_router, slim_b_router, a_up, b_down,
    )
    grad_tokens, part_a_qkv, part_b_qkv = qkv_back_call(
        picks, place, blocks, b_qkv, x, gain_one, normed, qkv, probs, lows, resid_grad, mixed_grad
    )
    part_a_qkv, part_b_qkv, *sums = lax.optimization_barrier((part_a_qkv, part_b_qkv, *sums))
    col_parts = jnp.concatenate([part_a_qkv, part_b_out])
    row_parts = jnp.concatenate([part_b_qkv, part_a_out])
    theirs = across_row(part_share(col_parts, row_parts, both_parts, 1 - row))
    shared = added(part_share(col_parts, row_parts, both_parts, row), theirs).astype(bf16)
    found = exchange_col(shared, col)
    mine = added(*found).astype(bf16)
    mine, grad_tokens, base = lax.optimization_barrier((mine, grad_tokens, base))
    moves = to_features(grad_tokens, (base + added(*sums)).astype(bf16), col)
    mine = spread_dp(scatter_dp(mine)) if four_dp else lax.psum(mine, "dp")
    got = [across_col(mine[384:], s) for s in range(1, 4)]
    far = across_row(jnp.concatenate([mine[:384], mine[768:]] + [one[384:] for one in got]))
    block_out, grad_tokens = merge_call(place, moves, tokens.shape[0])
    far, block_out, grad_tokens = lax.optimization_barrier((far, block_out, grad_tokens))
    return (block_out, grad_tokens, *finish_call(place, mine, got, far, dp_sums))


def solution(mesh):
    return jax.shard_map(
        on_device,
        mesh=mesh,
        in_specs=(
            P(("dp", "row"), "col"),
            P(("dp", "row"), "col"),
            P("dp", None),
            P(),
            P("col"),
            P("col"),
            P(None, "col", "row"),
            P("row", "col"),
            P(),
            P(None, None, ("row", "col")),
            P(None, ("row", "col"), None),
            P(None, "col", None),
            P(None, None, "row"),
            P("row", None),
            P(None, "col"),
            P(),
            P(),
            P(),
            P(None, ("row", "col")),
            P(("row", "col"), None),
            P(),
        ),
        out_specs=(
            P(("dp", "row"), "col"),
            P(("dp", "row"), "col"),
            P(None, "col", None),
            P(None, None, "row"),
            P("row", None),
            P(None, "col"),
            P(),
            P(),
            P(),
            P(None, ("row", "col")),
            P(("row", "col"), None),
            P(),
        ),
        check_vma=False,
    )
```

```python
import jax
import jax.numpy as jnp
from jax import lax
from jax.experimental import pallas as pl
from jax.experimental.pallas import tpu as pltpu
from jax.sharding import PartitionSpec as P

D = 768
EXPERTS = 32
SEQ = 197
SEQP = 208
RANK = 16
ADAPT = 128
IMG_GRP = 16
TOK = IMG_GRP * SEQP
BLK = 2 * SEQP
DUMMY = SEQ
TILE = 160
f32 = jnp.float32
bf16 = jnp.bfloat16


def max_tiles():
    return (2 * IMG_GRP * SEQ) // TILE + EXPERTS + 1


def dot(left, right):
    return jnp.dot(left, right, preferred_element_type=f32)


def dot_nt(left, right):
    return lax.dot_general(left, right, (((1,), (1,)), ((), ())), preferred_element_type=f32)


def dot_tn(left, right):
    return lax.dot_general(left, right, (((0,), (0,)), ((), ())), preferred_element_type=f32)


def lane_iota(shape):
    return lax.broadcasted_iota(jnp.int32, shape, len(shape) - 1)


def repeat_lanes(value):
    for shift in (16, 32, 64):
        value = value + pltpu.roll(value, shift, 1)
    return value


def table_kernel(n_blocks, picks_ref, *refs):
    x_blocks = refs[:n_blocks]
    c_blocks = refs[n_blocks : 2 * n_blocks]
    a_up, b_down, w_router, a_router, b_router, table_out, xin, cin, rows_x, rows_c, sem = refs[2 * n_blocks :]
    image = pl.program_id(0)
    lane = lane_iota((1, 128))

    @pl.when(image == 0)
    def start():
        copies = []
        for blocks, place in ((x_blocks, xin), (c_blocks, cin)):
            for b, block in enumerate(blocks):
                copies.append(pltpu.make_async_copy(block, place.at[pl.ds(b * BLK, BLK)], sem.at[len(copies)]))
        for copy in copies:
            copy.start()
        for copy in copies:
            copy.wait()

    row = pl.multiple_of(image * SEQP, 16)
    mask = (lane // RANK) == picks_ref[image]
    x = xin[pl.ds(row, SEQP), :]
    c = cin[pl.ds(row, SEQP), :]
    flat_x = rows_x.reshape(SEQP * 8, 128)
    flat_c = rows_c.reshape(SEQP * 8, 128)
    low_x = jnp.where(mask, dot(x, a_up[...]), 0.0)
    low_c = jnp.where(mask, dot_nt(c, b_down[...]), 0.0)
    low_r = jnp.where(mask, dot(x, a_router[...]), 0.0).astype(bf16)
    logits = dot(x, w_router[...]) + dot(low_r, b_router[...])
    logits = jnp.where(lane < 2 * EXPERTS, logits, -1e30)
    power = jnp.exp(logits - jnp.max(logits, axis=1, keepdims=True))
    total = jnp.sum(jnp.where(lane < EXPERTS, power, 0.0), axis=1, keepdims=True)
    probs = power / total
    lead = probs.astype(bf16).astype(f32)
    probs = jnp.where(lane < EXPERTS, lead, probs - lead)
    for j in range(6):
        flat_x[pl.ds(j, SEQP, 8), :] = x[:, 128 * j : 128 * j + 128].astype(f32)
        flat_c[pl.ds(j, SEQP, 8), :] = c[:, 128 * j : 128 * j + 128].astype(f32)
    flat_x[pl.ds(6, SEQP, 8), :] = low_x
    flat_x[pl.ds(7, SEQP, 8), :] = probs
    flat_c[pl.ds(6, SEQP, 8), :] = low_c
    flat_c[pl.ds(7, SEQP, 8), :] = jnp.zeros((SEQP, 128), f32)
    table_out[...] = jnp.concatenate([rows_x[...], rows_c[...]], axis=1).astype(bf16)


def table_call(picks, x_blocks, c_blocks, a_up, b_down, w_router, a_router, b_router):
    n = len(x_blocks)

    def whole(*shape):
        return pl.BlockSpec(shape, lambda e, *_: (0,) * len(shape))

    anywhere = pl.BlockSpec(memory_space=pl.ANY)
    return pl.pallas_call(
        lambda *refs: table_kernel(n, *refs),
        grid_spec=pltpu.PrefetchScalarGridSpec(
            num_scalar_prefetch=1,
            grid=(2 * n,),
            in_specs=[anywhere] * (2 * n)
            + [whole(D, ADAPT), whole(ADAPT, D), whole(D, 128), whole(D, ADAPT), whole(ADAPT, 128)],
            out_specs=pl.BlockSpec((SEQP, 16, 128), lambda i, *_: (i, 0, 0)),
            scratch_shapes=[
                pltpu.VMEM((n * BLK, D), bf16),
                pltpu.VMEM((n * BLK, D), bf16),
                pltpu.VMEM((SEQP, 8, 128), f32),
                pltpu.VMEM((SEQP, 8, 128), f32),
                pltpu.SemaphoreType.DMA((2 * n,)),
            ],
        ),
        out_shape=jax.ShapeDtypeStruct((n * BLK, 16, 128), bf16),
        compiler_params=pltpu.CompilerParams(vmem_limit_bytes=32 * 1024 * 1024),
        cost_estimate=pl.CostEstimate(flops=n * 3_000_000_000, bytes_accessed=n * 3_000_000, transcendentals=n * 60_000),
    )(picks, *x_blocks, *c_blocks, a_up, b_down, w_router, a_router, b_router)


def moe_kernel(places, list_ref, expert_ref, picks_ref, place_ref, *refs):
    n = len(places)
    tables = refs[:n]
    ep_outs, tg_outs = refs[n + 4 : n + 8], refs[n + 8 : n + 12]
    refs = refs[: n + 4] + refs[n + 12 :]
    (
        w_up_hbm, w_down_hbm, b_up, a_down,
        gbu_bf, gad_bf,
        table, acc_e, acc_t, in_x, in_c, out_e, out_t, xb, cb, w_up, w_down, stage_ep, stage_tg,
        gbu_out, gad_out, in_sem, up_sem, down_sem, ep_sem, tg_sem,
    ) = refs[n:]
    acc_e_flat = acc_e.reshape(TOK * 8, 128)
    acc_t_flat = acc_t.reshape(TOK * 8, 128)
    in_x_flat = in_x.reshape(TILE * 8, 128)
    in_c_flat = in_c.reshape(TILE * 8, 128)
    out_e_flat = out_e.reshape(TILE * 8, 128)
    out_t_flat = out_t.reshape(TILE * 8, 128)
    lane = lane_iota((1, 128))
    n_tiles = expert_ref[max_tiles()]

    copies = []
    for piece, spots in zip(tables, places):
        for b, (t, s) in enumerate(spots):
            spot = 4 * t + jnp.where(place_ref[0] == t, swapped(s), s)
            copies.append(
                pltpu.make_async_copy(
                    piece.at[pl.ds(b * BLK, BLK)], table.at[pl.ds(pl.multiple_of(spot * BLK, 32), BLK)], in_sem.at[len(copies)]
                )
            )
    for copy in copies:
        copy.start()

    def weights(expert):
        slot = expert % 2
        return (
            pltpu.make_async_copy(w_up_hbm.at[expert], w_up.at[slot], up_sem.at[slot]),
            pltpu.make_async_copy(w_down_hbm.at[expert], w_down.at[slot], down_sem.at[slot]),
        )

    for copy in weights(0):
        copy.start()
    out_e[...] = jnp.zeros_like(out_e)
    out_t[...] = jnp.zeros_like(out_t)
    gbu_out[...] = jnp.zeros_like(gbu_out)
    gad_out[...] = jnp.zeros_like(gad_out)

    def clear(i, carry):
        acc_e[pl.ds(i * 64, 64)] = jnp.zeros((64, 8, 128), f32)
        acc_t[pl.ds(i * 64, 64)] = jnp.zeros((64, 8, 128), f32)
        return carry

    lax.fori_loop(0, TOK // 64, clear, 0)
    for copy in copies:
        copy.wait()

    def fetch(t):
        for i in range(TILE):
            both = table[list_ref[t * TILE + i]].astype(f32)
            in_x[i] = both[:8]
            in_c[i] = both[8:]

    def give(t):
        for b in range(TILE // 8):
            tokens = [list_ref[t * TILE + 8 * b + k] for k in range(8)]
            sums_e = [acc_e[tokens[k]] + out_e[8 * b + k] for k in range(8)]
            sums_t = [acc_t[tokens[k]] + out_t[8 * b + k] for k in range(8)]
            for k in range(8):
                acc_e[tokens[k]] = sums_e[k]
                acc_t[tokens[k]] = sums_t[k]

    fetch(0)

    def tile(t, carry):
        expert = expert_ref[t]
        slot = expert % 2

        @pl.when((t == 0) | (expert_ref[jnp.maximum(t - 1, 0)] != expert))
        def arrive():
            for copy in weights(expert):
                copy.wait()

            @pl.when(expert + 1 < EXPERTS)
            def ahead():
                for copy in weights(expert + 1):
                    copy.start()

        for j in range(7):
            xb[:, 128 * j : 128 * j + 128] = in_x_flat[pl.ds(j, TILE, 8), :].astype(bf16)
            cb[:, 128 * j : 128 * j + 128] = in_c_flat[pl.ds(j, TILE, 8), :].astype(bf16)
        spread = in_x_flat[pl.ds(7, TILE, 8), :]
        mine = (lane == expert) | (lane == expert + EXPERTS)
        gate = jnp.sum(jnp.where(mine, spread, 0.0), axis=1, keepdims=True)
        fetch(t + 1)
        give(jnp.maximum(t - 1, 0))
        hidden = dot(xb[:, :D], w_up[slot]) + dot(xb[:, D:], b_up[...])
        back = dot_nt(cb[:, :D], w_down[slot]) + dot_nt(cb[:, D:], a_down[...])
        cdf = 0.5 + 0.5 * lax.erf(hidden * 0.7071067811865476)
        slope = cdf + hidden * jnp.exp(hidden * hidden * -0.5) * 0.3989422804014327
        act = (hidden * cdf).astype(bf16)
        act_f = act.astype(f32)
        gate_grad = jnp.sum(act_f * back, axis=1, keepdims=True)
        grad_hidden = (gate * back * slope).astype(bf16)
        act_gate = (gate * act_f).astype(bf16)
        out_main = dot(act_gate, w_down[slot])
        out_low = dot(act_gate, a_down[...])
        in_main = dot_nt(grad_hidden, w_up[slot])
        in_low = dot_nt(grad_hidden, b_up[...])
        gbu_out[...] += dot_tn(grad_hidden, xb[:, D:])
        gad_out[...] += dot_tn(act_gate, cb[:, D:])
        for j in range(6):
            out_e_flat[pl.ds(j, TILE, 8), :] = out_main[:, 128 * j : 128 * j + 128]
            out_t_flat[pl.ds(j, TILE, 8), :] = in_main[:, 128 * j : 128 * j + 128]
        out_e_flat[pl.ds(6, TILE, 8), :] = out_low
        out_t_flat[pl.ds(6, TILE, 8), :] = in_low
        out_t_flat[pl.ds(7, TILE, 8), :] = jnp.where(lane == expert, gate_grad, 0.0)
        return carry

    lax.fori_loop(0, n_tiles, tile, 0)
    give(n_tiles - 1)

    gbu_bf[...] = gbu_out[...].astype(bf16)
    gad_bf[...] = gad_out[...].astype(bf16)
    some = IMG_GRP // 4
    for side, (ep_out, tg_out) in enumerate(zip(ep_outs, tg_outs)):

        def image(i, carry):
            slot = i % 2
            base = pl.multiple_of((i + side * some) * SEQP, 16) * 8
            mask = (lane // RANK) == picks_ref[i + side * some]
            rows = pl.ds(pl.multiple_of(i * SEQP, 16), SEQP)
            put_tg = pltpu.make_async_copy(stage_tg.at[slot], tg_out.at[rows], tg_sem.at[slot])
            put_ep = pltpu.make_async_copy(stage_ep.at[slot], ep_out.at[rows], ep_sem.at[slot])

            @pl.when(i >= 2)
            def drain():
                put_tg.wait()
                put_ep.wait()

            def chunk(j):
                flat = acc_e_flat if j < 8 else acc_t_flat
                return flat[pl.ds(base + j % 8, SEQP, 8), :]

            for j in range(6):
                at = slice(128 * j, 128 * j + 128)
                stage_tg[slot, :, at] = chunk(8 + j).astype(bf16)
                stage_ep[slot, :, at] = chunk(j).astype(bf16)
            low_in = repeat_lanes(jnp.where(mask, chunk(14), 0.0))
            low_out = repeat_lanes(jnp.where(mask, chunk(6), 0.0))
            last = jnp.where(lane < 48, low_in, jnp.where(lane < 64, low_out, 0.0))
            stage_tg[slot, :, D:] = jnp.where(lane < 32, chunk(15), last).astype(bf16)
            put_tg.start()
            put_ep.start()
            return carry

        lax.fori_loop(0, some, image, 0)
        for i in range(some - 2, some):
            rows = pl.ds(i * SEQP, SEQP)
            pltpu.make_async_copy(stage_tg.at[i % 2], tg_out.at[rows], tg_sem.at[i % 2]).wait()
            pltpu.make_async_copy(stage_ep.at[i % 2], ep_out.at[rows], ep_sem.at[i % 2]).wait()


def moe_call(token_list, tile_experts, picks, place, tables, places, w_up, w_down, b_up, a_down):
    half = w_up.shape[2]
    n = len(tables)
    n_copies = sum(len(spots) for spots in places)
    anywhere = pl.BlockSpec(memory_space=pl.ANY)
    inside = pl.BlockSpec(memory_space=pltpu.VMEM)
    return pl.pallas_call(
        lambda *refs: moe_kernel(places, *refs),
        grid_spec=pltpu.PrefetchScalarGridSpec(
            num_scalar_prefetch=4,
            grid=(1,),
            in_specs=[anywhere] * (n + 2) + [inside, inside],
            out_specs=[anywhere] * 8 + [inside, inside],
            scratch_shapes=[
                pltpu.VMEM((TOK, 16, 128), bf16),
                pltpu.VMEM((TOK, 8, 128), f32),
                pltpu.VMEM((TOK, 8, 128), f32),
                pltpu.VMEM((TILE, 8, 128), f32),
                pltpu.VMEM((TILE, 8, 128), f32),
                pltpu.VMEM((TILE, 8, 128), f32),
                pltpu.VMEM((TILE, 8, 128), f32),
                pltpu.VMEM((TILE, D + 128), bf16),
                pltpu.VMEM((TILE, D + 128), bf16),
                pltpu.VMEM((2, D, half), bf16),
                pltpu.VMEM((2, half, D), bf16),
                pltpu.VMEM((2, SEQP, D), bf16),
                pltpu.VMEM((2, SEQP, D + 128), bf16),
                pltpu.VMEM((half, ADAPT), f32),
                pltpu.VMEM((half, ADAPT), f32),
                pltpu.SemaphoreType.DMA((n_copies,)),
                pltpu.SemaphoreType.DMA((2,)),
                pltpu.SemaphoreType.DMA((2,)),
                pltpu.SemaphoreType.DMA((2,)),
                pltpu.SemaphoreType.DMA((2,)),
            ],
        ),
        out_shape=[
            *[jax.ShapeDtypeStruct((TOK // 4, D), bf16)] * 4,
            *[jax.ShapeDtypeStruct((TOK // 4, D + 128), bf16)] * 4,
            jax.ShapeDtypeStruct((half, ADAPT), bf16),
            jax.ShapeDtypeStruct((half, ADAPT), bf16),
        ],
        compiler_params=pltpu.CompilerParams(vmem_limit_bytes=58 * 1024 * 1024),
        cost_estimate=pl.CostEstimate(flops=20_000_000_000, bytes_accessed=60_000_000, transcendentals=10_000_000),
    )(token_list, tile_experts, picks, place, *tables, w_up, w_down, b_up, a_down)


def swapped(s):
    return ((s & 1) << 1) | (s >> 1)


def block_spot(block, row, col):
    from_row = block // 4
    s = (block % 4) ^ col
    return 4 * (from_row ^ row) + jnp.where(from_row == 0, swapped(s), s)


def routing(routes, row, col):
    token = jnp.arange(25 * 128, dtype=jnp.int32)[None, :]
    image = token // SEQ
    spot = block_spot(image // 2, row, col) * BLK + (image % 2) * SEQP + token % SEQ
    real = token < IMG_GRP * SEQ
    picked = jnp.pad(routes.T, ((0, 0), (0, 25 * 128 - IMG_GRP * SEQ)), constant_values=EXPERTS)
    beyond = EXPERTS * 4096 + DUMMY
    keys = jnp.where(real, picked * 4096 + spot, beyond).reshape(-1)
    experts = jnp.arange(EXPERTS, dtype=jnp.int32)
    count = jnp.sum((picked[None] == experts[:, None, None]).astype(jnp.int32), axis=(1, 2))
    tiles = (jnp.maximum(count, 1) + TILE - 1) // TILE
    extra = tiles * TILE - count
    filler = jnp.where(
        jnp.arange(256, dtype=jnp.int32)[None, :] < extra[:, None], (experts * 4096)[:, None] + DUMMY, beyond
    ).reshape(-1)
    ordered = lax.sort(jnp.concatenate([keys, filler])) & 4095
    ends = jnp.sum(jnp.where(experts[None, :] <= experts[:, None], tiles[None, :], 0), axis=1)
    steps = jnp.arange(max_tiles(), dtype=jnp.int32)
    owner = jnp.minimum(jnp.sum((ends[None, :] <= steps[:, None]).astype(jnp.int32), axis=1), EXPERTS - 1)
    return ordered, jnp.concatenate([owner, jnp.sum(tiles)[None]])


HEADS = 12
HEAD_DIM = 64


def pick_mask(pick):
    return (lane_iota((1, ADAPT)) // RANK) == pick


def norm_stats(values):
    centre = jnp.sum(values, axis=1, keepdims=True) * (1.0 / D)
    shifted = values - centre
    spread = jnp.sum(shifted * shifted, axis=1, keepdims=True) * (1.0 / D)
    inverse = lax.rsqrt(spread + 1e-06)
    return shifted * inverse, inverse


def norm_back(grad, gain, unit, inverse):
    scaled = grad * gain
    total = jnp.sum(scaled, axis=1, keepdims=True) * (1.0 / D)
    along = jnp.sum(scaled * unit, axis=1, keepdims=True) * (1.0 / D)
    return inverse * (scaled - total - unit * along)


def qkv_copies(place_ref, blocks, own_b, scratch, sem):
    w_qkv, a_qkv, b_qkv = scratch
    row, col = place_ref[0], place_ref[1]
    copies = []

    def copy(source, target):
        copies.append(pltpu.make_async_copy(source, target, sem.at[len(copies)]))

    for t in range(2):
        half_at = pl.multiple_of((row ^ t) * 384, 128)
        for s in range(4):
            block = blocks[4 * t + s]
            at = pl.multiple_of((col ^ s) * 192, 64)
            low_at = pl.multiple_of((col ^ s) * 192 + (row ^ t) * 96, 32)
            for p in range(3):
                copy(block.at[pl.ds(192 * p, 192)], w_qkv.at[p, pl.ds(at, 192), pl.ds(half_at, 384)])
                copy(block.at[pl.ds(576, 96), pl.ds(128 * p, 128)], a_qkv.at[p, pl.ds(low_at, 96), :])
        for p in range(3):
            source = own_b.at[p] if t == 0 else blocks[4].at[pl.ds(W_ROWS + 128 * p, 128)]
            copy(source, b_qkv.at[p, :, pl.ds(half_at, 384)])
    return copies


def out_copies(place_ref, far_block, own_a, out_w, scratch, sem):
    w_out, a_out = scratch
    row = place_ref[0]
    copies = []

    def copy(source, target):
        copies.append(pltpu.make_async_copy(source, target, sem.at[len(copies)]))

    for t in range(2):
        half_at = pl.multiple_of((row ^ t) * 384, 128)
        copy(out_w[t].at[pl.ds(0, 384)], w_out.at[pl.ds(half_at, 384), :])
        for j in range(3):
            if t == 0:
                source = own_a.at[pl.ds(128 * j, 128)]
            else:
                source = far_block.at[pl.ds(W_ROWS + 384, 128), pl.ds(128 * j, 128)]
            copy(source, a_out.at[pl.ds(half_at + 128 * j, 128), :])
    return copies


W_ROWS = 944
QKV_SCRATCH = [
    pltpu.VMEM((3, D, D), bf16),
    pltpu.VMEM((3, D, ADAPT), bf16),
    pltpu.VMEM((3, ADAPT, D), bf16),
    pltpu.SemaphoreType.DMA((54,)),
]
OUT_SCRATCH = [
    pltpu.VMEM((D, D), bf16),
    pltpu.VMEM((D, ADAPT), bf16),
    pltpu.SemaphoreType.DMA((8,)),
]


def split_kernel(place_ref, tokens_ref, cot_ref, own_out, one_out, two_out, three_out, left, right, stage, sem):
    rows = tokens_ref.shape[0]
    width = D // 4
    left[0:rows, 0:width] = tokens_ref[...].astype(f32)
    right[0:rows, 0:width] = cot_ref[...].astype(f32)
    lane = lane_iota((1, 128))
    real = lax.broadcasted_iota(jnp.int32, (SEQP, 1), 0) < SEQ
    for i in range(8):
        at = slice(SEQ * i, SEQ * i + SEQP)
        spot = slice(SEQP * (i % 2), SEQP * (i % 2) + SEQP)
        moved = pltpu.roll(right[at, :], 64, 1)
        middle = jnp.where(lane < 64, left[at, 128:256], moved[:, 0:128])
        stage[i // 2, spot, 0:128] = jnp.where(real, left[at, 0:128], 0.0).astype(bf16)
        stage[i // 2, spot, 128:256] = jnp.where(real, middle, 0.0).astype(bf16)
        stage[i // 2, spot, 256:384] = jnp.where(real, moved[:, 128:256], 0.0).astype(bf16)
    copies = [
        pltpu.make_async_copy(stage.at[place_ref[1] ^ s], out, sem.at[s])
        for s, out in enumerate((own_out, one_out, two_out, three_out))
    ]
    for copy in copies:
        copy.start()
    for copy in copies:
        copy.wait()


def split_call(place, tokens, cotangent):
    rows = tokens.shape[0]
    tall = -(-(SEQ * 7 + SEQP) // 8) * 8
    inside = pl.BlockSpec(memory_space=pltpu.VMEM)
    return pl.pallas_call(
        split_kernel,
        grid_spec=pltpu.PrefetchScalarGridSpec(
            num_scalar_prefetch=1,
            grid=(1,),
            in_specs=[inside, inside],
            out_specs=[ANYWHERE] * 4,
            scratch_shapes=[
                pltpu.VMEM((tall, 256), f32),
                pltpu.VMEM((tall, 256), f32),
                pltpu.VMEM((4, BLK, 384), bf16),
                pltpu.SemaphoreType.DMA((4,)),
            ],
        ),
        out_shape=[jax.ShapeDtypeStruct((BLK, 384), bf16)] * 4,
        compiler_params=pltpu.CompilerParams(vmem_limit_bytes=32 * 1024 * 1024),
        cost_estimate=pl.CostEstimate(flops=1_000_000_000, bytes_accessed=3_000_000, transcendentals=0),
    )(place, tokens, cotangent)


def finish_kernel(place_ref, mine, one, two, three, far, dp_sums, *refs):
    (
        a_qkv, b_qkv, a_out, b_out, a_router, b_router, a_up, b_up, a_down, b_down, wide, tall, every,
    ) = refs
    row, col = place_ref[0], place_ref[1]
    near_at = pl.multiple_of(row * 96, 32)
    far_at = pl.multiple_of((1 - row) * 96, 32)
    for p in range(4):
        ours = mine[96 * p : 96 * p + 96, :].astype(f32)
        theirs = far[96 * p : 96 * p + 96, :].astype(f32)
        if p < 3:
            a_qkv[p, pl.ds(near_at, 96), :] = ours
            a_qkv[p, pl.ds(far_at, 96), :] = theirs
        else:
            wide[pl.ds(near_at, 96), :] = ours
            wide[pl.ds(far_at, 96), :] = theirs
    b_out[...] = wide[...].T[:, : D // 4]
    share = BOTH_ROWS // 8
    for s, got in enumerate((mine, one, two, three)):
        base = 384 if s == 0 else 0
        at = pl.multiple_of((col ^ s) * 96, 32)
        for p in range(4):
            piece = got[base + 96 * p : base + 96 * p + 96, :].astype(f32)
            if p < 3:
                tall[p, pl.ds(at, 96), :] = piece
            else:
                a_out[pl.ds(at, 96), :] = piece
        ours = got[base + 384 : base + 384 + share, :].astype(f32)
        theirs = far[384 + share * s : 384 + share * s + share, :].astype(f32)
        every[pl.ds(pl.multiple_of((row * 4 + (col ^ s)) * share, 64), share), :] = ours
        every[pl.ds(pl.multiple_of(((1 - row) * 4 + (col ^ s)) * share, 64), share), :] = theirs
    for p in range(3):
        b_qkv[p] = tall[p].T
    a_router[...] = every[0:768, :]
    a_up[...] = every[768:1536, :]
    b_down[...] = every[1536:2304, :].T
    b_router[...] = every[2304:2432, :].T[:, :EXPERTS]
    b_up[...] = dp_sums[0:384, :].astype(f32).T
    a_down[...] = dp_sums[384:768, :].astype(f32)


def finish_call(place, mine, got, far, dp_sums):
    inside = pl.BlockSpec(memory_space=pltpu.VMEM)
    half = D // 2
    shapes = [
        (3, D // 4, ADAPT), (3, ADAPT, half), (half, ADAPT), (ADAPT, D // 4), (D, ADAPT), (ADAPT, EXPERTS),
        (D, ADAPT), (ADAPT, half), (half, ADAPT), (ADAPT, D),
    ]
    return pl.pallas_call(
        finish_kernel,
        grid_spec=pltpu.PrefetchScalarGridSpec(
            num_scalar_prefetch=1,
            grid=(1,),
            in_specs=[inside] * 6,
            out_specs=[inside] * 10,
            scratch_shapes=[
                pltpu.VMEM((256, 128), f32),
                pltpu.VMEM((3, half, 128), f32),
                pltpu.VMEM((BOTH_ROWS, 128), f32),
            ],
        ),
        out_shape=[jax.ShapeDtypeStruct(shape, f32) for shape in shapes],
        compiler_params=pltpu.CompilerParams(vmem_limit_bytes=60 * 1024 * 1024),
        cost_estimate=pl.CostEstimate(flops=1_000_000_000, bytes_accessed=4_000_000, transcendentals=0),
    )(place, mine, *got, far, dp_sums)


def merge_kernel(place_ref, *refs):
    blocks, refs = refs[:4], refs[4:]
    block_out, tokens_out, stage, tall, sem = refs
    copies = [
        pltpu.make_async_copy(block, stage.at[place_ref[1] ^ s], sem.at[s]) for s, block in enumerate(blocks)
    ]
    for copy in copies:
        copy.start()
    for copy in copies:
        copy.wait()
    width = D // 4
    rows = tokens_out.shape[0]
    for i in range(8):
        at = slice(SEQ * i, SEQ * i + SEQ)
        both = stage[i // 2, SEQP * (i % 2) : SEQP * (i % 2) + SEQP, :].astype(f32)[:SEQ]
        tokens_out[at, :] = both[:, :width]
        tall[at, :] = both[:, width:]
    block_out[...] = tall[0:rows, :].astype(bf16)


def merge_call(place, blocks, rows):
    width = D // 4
    inside = pl.BlockSpec(memory_space=pltpu.VMEM)
    return pl.pallas_call(
        merge_kernel,
        grid_spec=pltpu.PrefetchScalarGridSpec(
            num_scalar_prefetch=1,
            grid=(1,),
            in_specs=[ANYWHERE] * 4,
            out_specs=[inside, inside],
            scratch_shapes=[
                pltpu.VMEM((4, BLK, 2 * width), bf16),
                pltpu.VMEM((rows, width), f32),
                pltpu.SemaphoreType.DMA((4,)),
            ],
        ),
        out_shape=[jax.ShapeDtypeStruct((rows, width), bf16), jax.ShapeDtypeStruct((rows, width), f32)],
        compiler_params=pltpu.CompilerParams(vmem_limit_bytes=60 * 1024 * 1024),
        cost_estimate=pl.CostEstimate(flops=8_000_000_000, bytes_accessed=3_000_000, transcendentals=0),
    )(place, *blocks)


def place_weights(place_ref, blocks, own_b, own_a, out_w, w_qkv, a_qkv, b_qkv, w_out, a_out):
    row, col = place_ref[0], place_ref[1]
    for t in range(2):
        half_at = pl.multiple_of((row ^ t) * 384, 128)
        across = pl.ds(half_at, 384)
        for s in range(4):
            block = blocks[4 * t + s]
            at = pl.multiple_of((col ^ s) * 192, 64)
            low_at = pl.multiple_of((col ^ s) * 192 + (row ^ t) * 96, 32)
            for p in range(3):
                w_qkv[p, pl.ds(at, 192), across] = block[192 * p : 192 * p + 192, :]
                a_qkv[p, pl.ds(low_at, 96), :] = block[576:672, 128 * p : 128 * p + 128]
        w_out[across, :] = out_w[t][0:384, :]
        for p in range(3):
            down = pl.ds(pl.multiple_of(half_at + 128 * p, 128), 128)
            if t == 0:
                b_qkv[p, :, across] = own_b[p]
                a_out[down, :] = own_a[128 * p : 128 * p + 128, :]
            else:
                b_qkv[p, :, across] = blocks[4][W_ROWS + 128 * p : W_ROWS + 128 * p + 128, :]
                a_out[down, :] = blocks[4][W_ROWS + 384 : W_ROWS + 512, 128 * p : 128 * p + 128]


def two_masks(picks_ref):
    row = lax.broadcasted_iota(jnp.int32, (BLK, 1), 0)
    pick = jnp.where(row < SEQP, picks_ref[0], picks_ref[1])
    return (lane_iota((1, ADAPT)) // RANK) == pick, (row < SEQ) | ((row >= SEQP) & (row < SEQP + SEQ))


def both_heads(value):
    lane = lane_iota((1, 128))
    nothing = jnp.zeros_like(value)
    return jnp.concatenate(
        [jnp.where(lane < HEAD_DIM, value, nothing), jnp.where(lane < HEAD_DIM, nothing, value)], axis=0
    )


def attend_kernel(picks_ref, place_ref, *refs):
    blocks, refs = refs[:8], refs[8:]
    (
        own_b, own_a, out_near, out_far, x_ref, gain_one, gain_two, b_out,
        two_out, resid_out, normed_out, qkv_out, mixed_out, probs_out, lows_out,
        w_qkv, a_qkv, b_qkv, w_out, a_out,
    ) = refs
    place_weights(place_ref, blocks, own_b, own_a, (out_near, out_far), w_qkv, a_qkv, b_qkv, w_out, a_out)
    mask, real = two_masks(picks_ref)
    x = x_ref[...].astype(f32)
    unit, unused = norm_stats(x)
    normed = (unit * gain_one[...]).astype(bf16)
    normed_out[...] = normed
    for p in range(3):
        low = jnp.where(mask, dot(normed, a_qkv[p]), 0.0).astype(bf16)
        lows_out[:, 128 * p : 128 * p + 128] = low
        qkv_out[p] = (dot(normed, w_qkv[p]) + dot(low, b_qkv[p])).astype(bf16)
    lane = lane_iota((1, 128))
    key_lane = lane_iota((1, SEQP))
    for pair in range(HEADS // 2):
        at = slice(128 * pair, 128 * pair + 128)
        for image in range(2):
            rows = slice(SEQP * image, SEQP * image + SEQP)
            scores = dot_nt(both_heads(qkv_out[0, rows, at]), qkv_out[1, rows, at]) * (HEAD_DIM**-0.5)
            scores = jnp.where(key_lane < SEQ, scores, -1e30)
            power = jnp.exp(scores - jnp.max(scores, axis=1, keepdims=True))
            probs = (power / jnp.sum(power, axis=1, keepdims=True)).astype(bf16)
            probs_out[image, pair] = probs
            found = dot(probs, qkv_out[2, rows, at])
            mixed_out[rows, at] = jnp.where(lane < HEAD_DIM, found[:SEQP], found[SEQP:]).astype(bf16)
    mixed = mixed_out[...]
    low = jnp.where(mask, dot(mixed, a_out[...]), 0.0).astype(bf16)
    lows_out[:, 384:512] = low
    resid = x + dot(mixed, w_out[...]) + dot(low, b_out[...])
    resid_out[...] = resid
    unit, unused = norm_stats(resid)
    two_out[...] = jnp.where(real, unit * gain_two[...], 0.0).astype(bf16)


INSIDE = pl.BlockSpec(memory_space=pltpu.VMEM)


ANYWHERE = pl.BlockSpec(memory_space=pl.ANY)


def attend_call(picks, place, blocks, own_b, own_a, out_w, x, gain_one, gain_two, b_out):
    rows = x.shape[0]
    return pl.pallas_call(
        attend_kernel,
        grid_spec=pltpu.PrefetchScalarGridSpec(
            num_scalar_prefetch=2,
            grid=(1,),
            in_specs=[INSIDE] * (len(blocks) + 8),
            out_specs=[INSIDE] * 7,
            scratch_shapes=QKV_SCRATCH[:-1] + OUT_SCRATCH[:-1],
        ),
        out_shape=[
            jax.ShapeDtypeStruct((rows, D), bf16),
            jax.ShapeDtypeStruct((rows, D), f32),
            jax.ShapeDtypeStruct((rows, D), bf16),
            jax.ShapeDtypeStruct((3, rows, D), bf16),
            jax.ShapeDtypeStruct((rows, D), bf16),
            jax.ShapeDtypeStruct((2, HEADS // 2, BLK, SEQP), bf16),
            jax.ShapeDtypeStruct((rows, 512), bf16),
        ],
        compiler_params=pltpu.CompilerParams(vmem_limit_bytes=48 * 1024 * 1024),
        cost_estimate=pl.CostEstimate(flops=4_000_000_000, bytes_accessed=15_000_000, transcendentals=2_000_000),
    )(picks, place, *blocks, own_b, own_a, *out_w, x, gain_one, gain_two, b_out)


def out_back_kernel(picks_ref, place_ref, *refs):
    (
        far_block, own_a, out_near, out_far, gain_two, b_out, two_ref, resid_ref, mixed_ref, lows_ref,
        cot_ref, grad_a, grad_b, w_router, a_router, b_router, a_up, b_down,
        resid_grad_out, mixed_grad_out, base_out, both_out, a_part_out, b_part_out,
        w_out, a_out, sem,
    ) = refs
    copies = out_copies(place_ref, far_block, own_a, (out_near, out_far), (w_out, a_out), sem)
    for copy in copies:
        copy.start()
    mask, unused = two_masks(picks_ref)
    lane = lane_iota((1, 128))

    def add_part(row, value):
        both_out[row : row + value.shape[0], :] = value.astype(bf16)

    two = two_ref[...]
    received = grad_a[...].astype(f32) + grad_b[...].astype(f32)
    low_r = jnp.where(mask, dot(two, a_router[...]), 0.0).astype(bf16)
    logits = dot(two, w_router[...]) + dot(low_r, b_router[...])
    logits = jnp.where(lane < EXPERTS, logits, -1e30)
    power = jnp.exp(logits - jnp.max(logits, axis=1, keepdims=True))
    probs = power / jnp.sum(power, axis=1, keepdims=True)
    last = received[:, D:]
    grad_probs = jnp.where(lane < EXPERTS, last, 0.0)
    low_in = jnp.where(mask, repeat_lanes(jnp.where((lane >= 32) & (lane < 48), last, 0.0)), 0.0).astype(bf16)
    low_out = jnp.where(mask, repeat_lanes(jnp.where((lane >= 48) & (lane < 64), last, 0.0)), 0.0).astype(bf16)
    cot = cot_ref[...]
    resid = resid_ref[...]
    base_out[...] = resid + dot(low_out, b_down[...])
    add_part(768, dot_tn(two, low_in))
    add_part(1536, dot_tn(cot, low_out))
    grad_logits = probs * (grad_probs - jnp.sum(probs * grad_probs, axis=1, keepdims=True))
    grad_logits = grad_logits.astype(bf16)
    grad_low = jnp.where(mask, dot_nt(grad_logits, b_router[...]), 0.0).astype(bf16)
    grad_two = received[:, :D] + dot_nt(low_in, a_up[...])
    grad_two = grad_two + dot_nt(grad_logits, w_router[...]) + dot_nt(grad_low, a_router[...])
    add_part(0, dot_tn(two, grad_low))
    add_part(2304, dot_tn(grad_logits, low_r))
    unit, inverse = norm_stats(resid)
    grad_resid = cot.astype(f32) + norm_back(grad_two, gain_two[...], unit, inverse)
    resid_grad_out[...] = grad_resid
    grad_attn = grad_resid.astype(bf16)
    grad_low = jnp.where(mask, dot_nt(grad_attn, b_out[...]), 0.0).astype(bf16)
    for copy in copies:
        copy.wait()
    mixed_grad_out[...] = (dot_nt(grad_attn, w_out[...]) + dot_nt(grad_low, a_out[...])).astype(bf16)
    a_part_out[...] = dot_tn(mixed_ref[...], grad_low).astype(bf16)
    b_part_out[...] = dot_tn(grad_attn, lows_ref[:, 384:512]).astype(bf16)
    both_out[2432:BOTH_ROWS, :] = jnp.zeros((BOTH_ROWS - 2432, 128), bf16)


BOTH_ROWS = 2560


def out_back_call(picks, place, far_block, own_a, out_w, gain_two, b_out, two, resid, mixed, lows, cot, grad_a, grad_b,
                  w_router, a_router, b_router, a_up, b_down):
    rows = two.shape[0]
    return pl.pallas_call(
        out_back_kernel,
        grid_spec=pltpu.PrefetchScalarGridSpec(
            num_scalar_prefetch=2,
            grid=(1,),
            in_specs=[ANYWHERE] * 4 + [INSIDE] * 14,
            out_specs=[INSIDE] * 6,
            scratch_shapes=OUT_SCRATCH,
        ),
        out_shape=[
            jax.ShapeDtypeStruct((rows, D), f32),
            jax.ShapeDtypeStruct((rows, D), bf16),
            jax.ShapeDtypeStruct((rows, D), f32),
            jax.ShapeDtypeStruct((BOTH_ROWS, 128), bf16),
            jax.ShapeDtypeStruct((D, 128), bf16),
            jax.ShapeDtypeStruct((D, 128), bf16),
        ],
        compiler_params=pltpu.CompilerParams(vmem_limit_bytes=60 * 1024 * 1024),
        cost_estimate=pl.CostEstimate(flops=6_000_000_000, bytes_accessed=15_000_000, transcendentals=100_000),
    )(picks, place, far_block, own_a, *out_w, gain_two, b_out, two, resid, mixed, lows, cot, grad_a, grad_b,
      w_router, a_router, b_router, a_up, b_down)


def qkv_back_kernel(picks_ref, place_ref, *refs):
    blocks, refs = refs[:8], refs[8:]
    (
        own_b, x_ref, gain_one, normed_ref, qkv_ref, probs_ref, lows_ref, resid_grad, grad_mixed,
        tokens_out, a_part_out, b_part_out,
        w_qkv, a_qkv, b_qkv, sem, grads,
    ) = refs
    copies = qkv_copies(place_ref, blocks, own_b, (w_qkv, a_qkv, b_qkv), sem)
    for copy in copies:
        copy.start()
    mask, unused = two_masks(picks_ref)
    lane = lane_iota((1, 128))
    for pair in range(HEADS // 2):
        at = slice(128 * pair, 128 * pair + 128)
        for image in range(2):
            rows = slice(SEQP * image, SEQP * image + SEQP)
            grad_out = both_heads(grad_mixed[rows, at])
            weights = probs_ref[image, pair]
            weights_f = weights.astype(f32)
            grad_w = dot_nt(grad_out, qkv_ref[2, rows, at])
            inner = jnp.sum(weights_f * grad_w, axis=1, keepdims=True)
            grad_s = (weights_f * (grad_w - inner) * (HEAD_DIM**-0.5)).astype(bf16)
            found = dot(grad_s, qkv_ref[1, rows, at])
            grads[0, rows, at] = jnp.where(lane < HEAD_DIM, found[:SEQP], found[SEQP:]).astype(bf16)
            grads[1, rows, at] = dot_tn(grad_s, both_heads(qkv_ref[0, rows, at])).astype(bf16)
            grads[2, rows, at] = dot_tn(weights, grad_out).astype(bf16)
    for copy in copies:
        copy.wait()
    normed = normed_ref[...]
    grad_normed = jnp.zeros((BLK, D), f32)
    for p in range(3):
        piece = grads[p]
        grad_low = jnp.where(mask, dot_nt(piece, b_qkv[p]), 0.0).astype(bf16)
        grad_normed = grad_normed + dot_nt(piece, w_qkv[p]) + dot_nt(grad_low, a_qkv[p])
        a_part_out[D * p : D * p + D, :] = dot_tn(normed, grad_low).astype(bf16)
        b_part_out[D * p : D * p + D, :] = dot_tn(piece, lows_ref[:, 128 * p : 128 * p + 128]).astype(bf16)
    unit, inverse = norm_stats(x_ref[...].astype(f32))
    tokens_out[...] = (resid_grad[...] + norm_back(grad_normed, gain_one[...], unit, inverse)).astype(bf16)


def qkv_back_call(picks, place, blocks, own_b, x, gain_one, normed, qkv, probs, lows, resid_grad, grad_mixed):
    rows = x.shape[0]
    return pl.pallas_call(
        qkv_back_kernel,
        grid_spec=pltpu.PrefetchScalarGridSpec(
            num_scalar_prefetch=2,
            grid=(1,),
            in_specs=[ANYWHERE] * (len(blocks) + 1) + [INSIDE] * 8,
            out_specs=[INSIDE] * 3,
            scratch_shapes=QKV_SCRATCH + [pltpu.VMEM((3, BLK, D), bf16)],
        ),
        out_shape=[
            jax.ShapeDtypeStruct((rows, D), bf16),
            jax.ShapeDtypeStruct((3 * D, 128), bf16),
            jax.ShapeDtypeStruct((3 * D, 128), bf16),
        ],
        compiler_params=pltpu.CompilerParams(vmem_limit_bytes=44 * 1024 * 1024),
        cost_estimate=pl.CostEstimate(flops=9_000_000_000, bytes_accessed=15_000_000, transcendentals=1000),
    )(picks, place, *blocks, own_b, x, gain_one, normed, qkv, probs, lows, resid_grad, grad_mixed)


TABLES = (((0, 0), (1, 0)), ((0, 1), (0, 2), (1, 1), (1, 2)), ((0, 3), (1, 3)))


def across_row(value):
    return lax.ppermute(value, "row", [(0, 1), (1, 0)])


def across_col(value, step):
    return lax.ppermute(value, "col", [(i, i ^ step) for i in range(4)])


def by_place(blocks, col):
    found = []
    for place in range(4):
        value = blocks[place]
        for other in range(1, 4):
            value = jnp.where(col == other, blocks[place ^ other], value)
        found.append(value)
    return found


def across_chip(value, first, second):
    pairs = [(i, i ^ first) for i in range(4)] + [(4 + i, 4 + (i ^ second)) for i in range(4)]
    return lax.ppermute(value, ("row", "col"), pairs)


def gather_col(value, row):
    from_x = across_col(value, 1)
    from_y = across_col(value, 2)
    return [value, from_x, from_y, across_chip(jnp.where(row == 0, from_x, from_y), 2, 1)]


def added(*values):
    total = values[0].astype(f32)
    for value in values[1:]:
        total = total + value.astype(f32)
    return total


def last_exchange(kept_rows, got):
    sent = added(kept_rows[BLK:], got[BLK:]).astype(bf16)
    return added(kept_rows[:BLK], got[:BLK]).astype(bf16), across_chip(sent, 2, 1)


def at_place(value, axis, place):
    return lax.dynamic_index_in_dim(value, place, axis, keepdims=False)


def scatter_dp(value):
    place = lax.axis_index("dp")
    view = value.reshape(4, -1, 128)
    found = [at_place(view, 0, place)]
    for s in range(1, 4):
        found.append(across_dp(at_place(view, 0, place ^ s), s))
    return added(*found).astype(bf16)


def across_dp(value, step):
    return lax.ppermute(value, "dp", [(i, i ^ step) for i in range(4)])


def spread_dp(value):
    return jnp.concatenate(by_place([value] + [across_dp(value, s) for s in range(1, 4)], lax.axis_index("dp")))


def part_share(col_parts, row_parts, both_parts, place):
    col_parts = at_place(col_parts.reshape(4, 4, 2, 96, 128), 2, place)
    row_parts = at_place(row_parts.reshape(4, 2, 4, 96, 128), 1, place)
    both_parts = at_place(both_parts.reshape(2, 4, BOTH_ROWS // 8, 128), 0, place)
    col_parts = col_parts.swapaxes(0, 1).reshape(4, 384, 128)
    row_parts = row_parts.swapaxes(0, 1).reshape(4, 384, 128)
    return jnp.concatenate([col_parts, row_parts, both_parts], axis=1)


def exchange_col(value, col):
    return [at_place(value, 0, col)] + [across_col(at_place(value, 0, col ^ s), s) for s in range(1, 4)]


def to_features(first, second, col):
    width = D // 4
    pieces = []
    for p in range(4):
        at = slice(width * p, width * p + width)
        pieces.append(jnp.concatenate([first[:, at], second[:, at]], axis=1))
    sent = by_place(pieces, col)
    return [sent[0]] + [across_col(sent[s], s) for s in range(1, 4)]


def on_device(
    tokens, cotangent, routes, adapter_pick, gain_attn, gain_moe, w_qkv, w_out, w_router, w_up, w_down,
    a_qkv, b_qkv, a_out, b_out, a_router, b_router, a_up, b_up, a_down, b_down,
):
    row = lax.axis_index("row")
    col = lax.axis_index("col")
    me = row * 4 + col
    place = jnp.stack([row, col]).astype(jnp.int32)

    width = D // 4
    half = D // 2
    gains = []
    for gain in (gain_attn, gain_moe):
        left = gain
        for unused in range(3):
            lead = lax.reduce_precision(left, 8, 7)
            gains.append(lead.astype(bf16))
            left = left - lead
    small = jnp.concatenate([w_out, b_out, jnp.stack(gains), jnp.zeros((26, width), bf16)], axis=0)
    low = at_place(a_qkv.reshape(3, 2, 96, ADAPT), 1, row)
    packed = jnp.concatenate(
        [w_qkv.reshape(576, half), jnp.concatenate([low[0], low[1], low[2]], axis=1),
         jnp.concatenate([small[:272], small[272:]], axis=1)]
    )
    for_row = jnp.concatenate(
        [packed, b_qkv.reshape(half, half), jnp.concatenate([a_out[:128], a_out[128:256], a_out[256:]], axis=1)]
    )
    pairs = split_call(place, tokens, cotangent)
    from_x, from_y = across_col(packed, 1), across_col(packed, 2)
    from_x, from_y, *pairs = lax.optimization_barrier((from_x, from_y, *pairs))
    near = [packed, from_x, from_y, across_chip(jnp.where(row == 0, from_x, from_y), 2, 1)]
    pairs = by_place([pairs[0]] + [across_col(pairs[s], s) for s in range(1, 4)], col)
    x = jnp.concatenate([pair[:, :width] for pair in pairs], axis=1)
    cot = jnp.concatenate([pair[:, width:] for pair in pairs], axis=1)
    far = [across_row(for_row)] + [across_row(block) for block in near[1:]]
    blocks = near + far

    def assembled(group):
        parts = by_place([block[672:944] for block in group], col)
        return jnp.concatenate(
            [jnp.concatenate([part[:, :width] for part in parts], axis=1),
             jnp.concatenate([part[:, width:] for part in parts], axis=1)], axis=0
        )

    out_w = [assembled(near), assembled(far)]
    full_b_out = out_w[0][384:512]
    gain_rows = out_w[0][512:518].astype(f32)
    gain_one = jnp.sum(gain_rows[:3], axis=0, keepdims=True)
    gain_two = jnp.sum(gain_rows[3:], axis=0, keepdims=True)

    picks_group = lax.dynamic_slice_in_dim(adapter_pick, lax.axis_index("dp") * IMG_GRP, IMG_GRP)
    order = jnp.arange(IMG_GRP, dtype=jnp.int32)
    picks = jnp.take(picks_group, ((order // 2) ^ me) * 2 + order % 2)
    spot_picks = jnp.sum(
        jnp.where(block_spot(order // 2, row, col)[None, :] * 2 + order[None, :] % 2 == order[:, None], picks_group[None, :], 0), axis=1
    )
    token_list, tile_experts = routing(routes, row, col)
    wide_router = jnp.concatenate([w_router, w_router, jnp.zeros((D, 64), bf16)], axis=1)
    wide_b_router = jnp.concatenate([b_router, b_router, jnp.zeros((ADAPT, 64), bf16)], axis=1)
    slim_router = jnp.concatenate([w_router, jnp.zeros((D, 96), bf16)], axis=1)
    slim_b_router = jnp.concatenate([b_router, jnp.zeros((ADAPT, 96), bf16)], axis=1)

    x, token_list, tile_experts, wide_router, wide_b_router, slim_router, slim_b_router = lax.optimization_barrier(
        (x, token_list, tile_experts, wide_router, wide_b_router, slim_router, slim_b_router)
    )
    cot, unused = lax.optimization_barrier((cot, near[3]))
    two, resid, normed, qkv, mixed, probs, lows = attend_call(
        picks, place, blocks, b_qkv, a_out, out_w, x, gain_one, gain_two, full_b_out
    )
    cot_near = gather_col(cot, row)
    two_x, two_y = across_col(two, 1), across_col(two, 2)

    def table(spots, twos, cots):
        return table_call(
            jnp.stack([picks[8 * t + 2 * s + side] for t, s in spots for side in range(2)]),
            twos, cots, a_up, b_down, wide_router, a_router, wide_b_router,
        )

    cot_far = [across_row(block) for block in cot_near]
    tables = [table(TABLES[0], [two, across_row(two)], [cot, cot_far[0]])]
    two_x, two_y, tables[0] = lax.optimization_barrier((two_x, two_y, tables[0]))
    diag = across_chip(jnp.where(row == 0, two_x, two_y), 2, 1)
    tables.append(
        table(TABLES[1], [two_x, two_y, across_row(two_x), across_row(two_y)], [cot_near[1], cot_near[2], cot_far[1], cot_far[2]])
    )
    diag, *tables = lax.optimization_barrier((diag, *tables))
    tables.append(table(TABLES[2], [diag, across_row(diag)], [cot_near[3], cot_far[3]]))
    *moved, part_b_up, part_a_down = moe_call(
        token_list, tile_experts, spot_picks, place, tables, TABLES, w_up, w_down, b_up, a_down
    )
    sums, grads = moved[:4], moved[4:]
    dp_parts = jnp.concatenate([part_b_up, part_a_down])
    grad_sent = added(grads[1], across_row(grads[3])).astype(bf16)
    grad_kept = added(grads[0], across_row(grads[2])).astype(bf16)
    grad_sent, dp_parts, *sums = lax.optimization_barrier((grad_sent, dp_parts, *sums))
    grad_got = across_chip(grad_sent, 1, 2)
    sum_kept, sum_sent = across_row(sums[2]), across_row(sums[3])
    sums = [
        added(near[at : at + BLK], far[at : at + BLK]).astype(bf16)
        for near, far in ((sums[0], sum_kept), (sums[1], sum_sent)) for at in (0, BLK)
    ]
    four_dp = lax.axis_size("dp") == 4
    dp_sums = scatter_dp(dp_parts) if four_dp else lax.psum(dp_parts, "dp")
    grad_got, dp_sums, *sums = lax.optimization_barrier((grad_got, dp_sums, *sums))
    grad_a, grad_b = last_exchange(grad_kept, grad_got)
    if four_dp:
        dp_sums = spread_dp(dp_sums)
    grad_a, grad_b, dp_sums, *sums = lax.optimization_barrier((grad_a, grad_b, dp_sums, *sums))
    sums = [sums[0], across_chip(sums[1], 2, 1), across_chip(sums[2], 1, 2), across_chip(sums[3], 3, 3)]
    resid_grad, mixed_grad, base, both_parts, part_a_out, part_b_out = out_back_call(
        picks, place, blocks[4], a_out, out_w, gain_two, full_b_out, two, resid, mixed, lows, cot, grad_a, grad_b,
        slim_router, a_router, slim_b_router, a_up, b_down,
    )
    grad_tokens, part_a_qkv, part_b_qkv = qkv_back_call(
        picks, place, blocks, b_qkv, x, gain_one, normed, qkv, probs, lows, resid_grad, mixed_grad
    )
    part_a_qkv, part_b_qkv, *sums = lax.optimization_barrier((part_a_qkv, part_b_qkv, *sums))
    col_parts = jnp.concatenate([part_a_qkv, part_b_out])
    row_parts = jnp.concatenate([part_b_qkv, part_a_out])
    theirs = across_row(part_share(col_parts, row_parts, both_parts, 1 - row))
    shared = added(part_share(col_parts, row_parts, both_parts, row), theirs).astype(bf16)
    found = exchange_col(shared, col)
    mine = added(*found).astype(bf16)
    mine, grad_tokens, base = lax.optimization_barrier((mine, grad_tokens, base))
    moves = to_features(grad_tokens, (base + added(*sums)).astype(bf16), col)
    mine = spread_dp(scatter_dp(mine)) if four_dp else lax.psum(mine, "dp")
    got = [across_col(mine[384:], s) for s in range(1, 4)]
    far = across_row(jnp.concatenate([mine[:384], mine[768:]] + [one[384:] for one in got]))
    block_out, grad_tokens = merge_call(place, moves, tokens.shape[0])
    far, block_out, grad_tokens = lax.optimization_barrier((far, block_out, grad_tokens))
    return (block_out, grad_tokens, *finish_call(place, mine, got, far, dp_sums))


def solution(mesh):
    return jax.shard_map(
        on_device,
        mesh=mesh,
        in_specs=(
            P(("dp", "row"), "col"),
            P(("dp", "row"), "col"),
            P("dp", None),
            P(),
            P("col"),
            P("col"),
            P(None, "col", "row"),
            P("row", "col"),
            P(),
            P(None, None, ("row", "col")),
            P(None, ("row", "col"), None),
            P(None, "col", None),
            P(None, None, "row"),
            P("row", None),
            P(None, "col"),
            P(),
            P(),
            P(),
            P(None, ("row", "col")),
            P(("row", "col"), None),
            P(),
        ),
        out_specs=(
            P(("dp", "row"), "col"),
            P(("dp", "row"), "col"),
            P(None, "col", None),
            P(None, None, "row"),
            P("row", None),
            P(None, "col"),
            P(),
            P(),
            P(),
            P(None, ("row", "col")),
            P(("row", "col"), None),
            P(),
        ),
        check_vma=False,
    )
```

```python
import jax
import jax.numpy as jnp
from jax import lax
from jax.experimental import pallas as pl
from jax.experimental.pallas import tpu as pltpu
from jax.sharding import PartitionSpec as P

D = 768
EXPERTS = 32
SEQ = 197
SEQP = 208
RANK = 16
ADAPT = 128
IMG_GRP = 16
TOK = IMG_GRP * SEQP
BLK = 2 * SEQP
DUMMY = SEQ
TILE = 160
f32 = jnp.float32
bf16 = jnp.bfloat16


def max_tiles():
    return (2 * IMG_GRP * SEQ) // TILE + EXPERTS + 1


def dot(left, right):
    return jnp.dot(left, right, preferred_element_type=f32)


def dot_nt(left, right):
    return lax.dot_general(left, right, (((1,), (1,)), ((), ())), preferred_element_type=f32)


def dot_tn(left, right):
    return lax.dot_general(left, right, (((0,), (0,)), ((), ())), preferred_element_type=f32)


def lane_iota(shape):
    return lax.broadcasted_iota(jnp.int32, shape, len(shape) - 1)


def repeat_lanes(value):
    for shift in (16, 32, 64):
        value = value + pltpu.roll(value, shift, 1)
    return value


def table_kernel(n_blocks, picks_ref, *refs):
    x_blocks = refs[:n_blocks]
    c_blocks = refs[n_blocks : 2 * n_blocks]
    a_up, b_down, w_router, a_router, b_router, table_out, xin, cin, rows_x, rows_c, sem = refs[2 * n_blocks :]
    image = pl.program_id(0)
    lane = lane_iota((1, 128))

    @pl.when(image == 0)
    def start():
        copies = []
        for blocks, place in ((x_blocks, xin), (c_blocks, cin)):
            for b, block in enumerate(blocks):
                copies.append(pltpu.make_async_copy(block, place.at[pl.ds(b * BLK, BLK)], sem.at[len(copies)]))
        for copy in copies:
            copy.start()
        for copy in copies:
            copy.wait()

    row = pl.multiple_of(image * SEQP, 16)
    mask = (lane // RANK) == picks_ref[image]
    x = xin[pl.ds(row, SEQP), :]
    c = cin[pl.ds(row, SEQP), :]
    flat_x = rows_x.reshape(SEQP * 8, 128)
    flat_c = rows_c.reshape(SEQP * 8, 128)
    low_x = jnp.where(mask, dot(x, a_up[...]), 0.0)
    low_c = jnp.where(mask, dot_nt(c, b_down[...]), 0.0)
    low_r = jnp.where(mask, dot(x, a_router[...]), 0.0).astype(bf16)
    logits = dot(x, w_router[...]) + dot(low_r, b_router[...])
    logits = jnp.where(lane < 2 * EXPERTS, logits, -1e30)
    power = jnp.exp(logits - jnp.max(logits, axis=1, keepdims=True))
    total = jnp.sum(jnp.where(lane < EXPERTS, power, 0.0), axis=1, keepdims=True)
    probs = power / total
    lead = probs.astype(bf16).astype(f32)
    probs = jnp.where(lane < EXPERTS, lead, probs - lead)
    for j in range(6):
        flat_x[pl.ds(j, SEQP, 8), :] = x[:, 128 * j : 128 * j + 128].astype(f32)
        flat_c[pl.ds(j, SEQP, 8), :] = c[:, 128 * j : 128 * j + 128].astype(f32)
    flat_x[pl.ds(6, SEQP, 8), :] = low_x
    flat_x[pl.ds(7, SEQP, 8), :] = probs
    flat_c[pl.ds(6, SEQP, 8), :] = low_c
    flat_c[pl.ds(7, SEQP, 8), :] = jnp.zeros((SEQP, 128), f32)
    table_out[...] = jnp.concatenate([rows_x[...], rows_c[...]], axis=1).astype(bf16)


def table_call(picks, x_blocks, c_blocks, a_up, b_down, w_router, a_router, b_router):
    n = len(x_blocks)

    def whole(*shape):
        return pl.BlockSpec(shape, lambda e, *_: (0,) * len(shape))

    anywhere = pl.BlockSpec(memory_space=pl.ANY)
    return pl.pallas_call(
        lambda *refs: table_kernel(n, *refs),
        grid_spec=pltpu.PrefetchScalarGridSpec(
            num_scalar_prefetch=1,
            grid=(2 * n,),
            in_specs=[anywhere] * (2 * n)
            + [whole(D, ADAPT), whole(ADAPT, D), whole(D, 128), whole(D, ADAPT), whole(ADAPT, 128)],
            out_specs=pl.BlockSpec((SEQP, 16, 128), lambda i, *_: (i, 0, 0)),
            scratch_shapes=[
                pltpu.VMEM((n * BLK, D), bf16),
                pltpu.VMEM((n * BLK, D), bf16),
                pltpu.VMEM((SEQP, 8, 128), f32),
                pltpu.VMEM((SEQP, 8, 128), f32),
                pltpu.SemaphoreType.DMA((2 * n,)),
            ],
        ),
        out_shape=jax.ShapeDtypeStruct((n * BLK, 16, 128), bf16),
        compiler_params=pltpu.CompilerParams(vmem_limit_bytes=32 * 1024 * 1024),
        cost_estimate=pl.CostEstimate(flops=n * 3_000_000_000, bytes_accessed=n * 3_000_000, transcendentals=n * 60_000),
    )(picks, *x_blocks, *c_blocks, a_up, b_down, w_router, a_router, b_router)


def moe_kernel(places, list_ref, expert_ref, picks_ref, place_ref, *refs):
    n = len(places)
    tables = refs[:n]
    ep_outs, tg_outs = refs[n + 4 : n + 8], refs[n + 8 : n + 12]
    refs = refs[: n + 4] + refs[n + 12 :]
    (
        w_up_hbm, w_down_hbm, b_up, a_down,
        gbu_bf, gad_bf,
        table, acc_e, acc_t, in_x, in_c, out_e, out_t, xb, cb, w_up, w_down, stage_ep, stage_tg,
        gbu_out, gad_out, in_sem, up_sem, down_sem, ep_sem, tg_sem,
    ) = refs[n:]
    acc_e_flat = acc_e.reshape(TOK * 8, 128)
    acc_t_flat = acc_t.reshape(TOK * 8, 128)
    in_x_flat = in_x.reshape(TILE * 8, 128)
    in_c_flat = in_c.reshape(TILE * 8, 128)
    out_e_flat = out_e.reshape(TILE * 8, 128)
    out_t_flat = out_t.reshape(TILE * 8, 128)
    lane = lane_iota((1, 128))
    n_tiles = expert_ref[max_tiles()]

    copies = []
    for piece, spots in zip(tables, places):
        for b, (t, s) in enumerate(spots):
            spot = 4 * t + jnp.where(place_ref[0] == t, swapped(s), s)
            copies.append(
                pltpu.make_async_copy(
                    piece.at[pl.ds(b * BLK, BLK)], table.at[pl.ds(pl.multiple_of(spot * BLK, 32), BLK)], in_sem.at[len(copies)]
                )
            )
    for copy in copies:
        copy.start()

    def weights(expert):
        slot = expert % 2
        return (
            pltpu.make_async_copy(w_up_hbm.at[expert], w_up.at[slot], up_sem.at[slot]),
            pltpu.make_async_copy(w_down_hbm.at[expert], w_down.at[slot], down_sem.at[slot]),
        )

    for copy in weights(0):
        copy.start()
    out_e[...] = jnp.zeros_like(out_e)
    out_t[...] = jnp.zeros_like(out_t)
    gbu_out[...] = jnp.zeros_like(gbu_out)
    gad_out[...] = jnp.zeros_like(gad_out)

    def clear(i, carry):
        acc_e[pl.ds(i * 64, 64)] = jnp.zeros((64, 8, 128), f32)
        acc_t[pl.ds(i * 64, 64)] = jnp.zeros((64, 8, 128), f32)
        return carry

    lax.fori_loop(0, TOK // 64, clear, 0)
    for copy in copies:
        copy.wait()

    def fetch(t):
        for i in range(TILE):
            both = table[list_ref[t * TILE + i]].astype(f32)
            in_x[i] = both[:8]
            in_c[i] = both[8:]

    def give(t):
        for b in range(TILE // 8):
            tokens = [list_ref[t * TILE + 8 * b + k] for k in range(8)]
            sums_e = [acc_e[tokens[k]] + out_e[8 * b + k] for k in range(8)]
            sums_t = [acc_t[tokens[k]] + out_t[8 * b + k] for k in range(8)]
            for k in range(8):
                acc_e[tokens[k]] = sums_e[k]
                acc_t[tokens[k]] = sums_t[k]

    fetch(0)

    def tile(t, carry):
        expert = expert_ref[t]
        slot = expert % 2

        @pl.when((t == 0) | (expert_ref[jnp.maximum(t - 1, 0)] != expert))
        def arrive():
            for copy in weights(expert):
                copy.wait()

            @pl.when(expert + 1 < EXPERTS)
            def ahead():
                for copy in weights(expert + 1):
                    copy.start()

        for j in range(7):
            xb[:, 128 * j : 128 * j + 128] = in_x_flat[pl.ds(j, TILE, 8), :].astype(bf16)
            cb[:, 128 * j : 128 * j + 128] = in_c_flat[pl.ds(j, TILE, 8), :].astype(bf16)
        spread = in_x_flat[pl.ds(7, TILE, 8), :]
        mine = (lane == expert) | (lane == expert + EXPERTS)
        gate = jnp.sum(jnp.where(mine, spread, 0.0), axis=1, keepdims=True)
        fetch(t + 1)
        give(jnp.maximum(t - 1, 0))
        hidden = dot(xb[:, :D], w_up[slot]) + dot(xb[:, D:], b_up[...])
        back = dot_nt(cb[:, :D], w_down[slot]) + dot_nt(cb[:, D:], a_down[...])
        cdf = 0.5 + 0.5 * lax.erf(hidden * 0.7071067811865476)
        slope = cdf + hidden * jnp.exp(hidden * hidden * -0.5) * 0.3989422804014327
        act = (hidden * cdf).astype(bf16)
        act_f = act.astype(f32)
        gate_grad = jnp.sum(act_f * back, axis=1, keepdims=True)
        grad_hidden = (gate * back * slope).astype(bf16)
        act_gate = (gate * act_f).astype(bf16)
        out_main = dot(act_gate, w_down[slot])
        out_low = dot(act_gate, a_down[...])
        in_main = dot_nt(grad_hidden, w_up[slot])
        in_low = dot_nt(grad_hidden, b_up[...])
        gbu_out[...] += dot_tn(grad_hidden, xb[:, D:])
        gad_out[...] += dot_tn(act_gate, cb[:, D:])
        for j in range(6):
            out_e_flat[pl.ds(j, TILE, 8), :] = out_main[:, 128 * j : 128 * j + 128]
            out_t_flat[pl.ds(j, TILE, 8), :] = in_main[:, 128 * j : 128 * j + 128]
        out_e_flat[pl.ds(6, TILE, 8), :] = out_low
        out_t_flat[pl.ds(6, TILE, 8), :] = in_low
        out_t_flat[pl.ds(7, TILE, 8), :] = jnp.where(lane == expert, gate_grad, 0.0)
        return carry

    lax.fori_loop(0, n_tiles, tile, 0)
    give(n_tiles - 1)

    gbu_bf[...] = gbu_out[...].astype(bf16)
    gad_bf[...] = gad_out[...].astype(bf16)
    some = IMG_GRP // 4
    for side, (ep_out, tg_out) in enumerate(zip(ep_outs, tg_outs)):

        def image(i, carry):
            slot = i % 2
            base = pl.multiple_of((i + side * some) * SEQP, 16) * 8
            mask = (lane // RANK) == picks_ref[i + side * some]
            rows = pl.ds(pl.multiple_of(i * SEQP, 16), SEQP)
            put_tg = pltpu.make_async_copy(stage_tg.at[slot], tg_out.at[rows], tg_sem.at[slot])
            put_ep = pltpu.make_async_copy(stage_ep.at[slot], ep_out.at[rows], ep_sem.at[slot])

            @pl.when(i >= 2)
            def drain():
                put_tg.wait()
                put_ep.wait()

            def chunk(j):
                flat = acc_e_flat if j < 8 else acc_t_flat
                return flat[pl.ds(base + j % 8, SEQP, 8), :]

            for j in range(6):
                at = slice(128 * j, 128 * j + 128)
                stage_tg[slot, :, at] = chunk(8 + j).astype(bf16)
                stage_ep[slot, :, at] = chunk(j).astype(bf16)
            low_in = repeat_lanes(jnp.where(mask, chunk(14), 0.0))
            low_out = repeat_lanes(jnp.where(mask, chunk(6), 0.0))
            last = jnp.where(lane < 48, low_in, jnp.where(lane < 64, low_out, 0.0))
            stage_tg[slot, :, D:] = jnp.where(lane < 32, chunk(15), last).astype(bf16)
            put_tg.start()
            put_ep.start()
            return carry

        lax.fori_loop(0, some, image, 0)
        for i in range(some - 2, some):
            rows = pl.ds(i * SEQP, SEQP)
            pltpu.make_async_copy(stage_tg.at[i % 2], tg_out.at[rows], tg_sem.at[i % 2]).wait()
            pltpu.make_async_copy(stage_ep.at[i % 2], ep_out.at[rows], ep_sem.at[i % 2]).wait()


def moe_call(token_list, tile_experts, picks, place, tables, places, w_up, w_down, b_up, a_down):
    half = w_up.shape[2]
    n = len(tables)
    n_copies = sum(len(spots) for spots in places)
    anywhere = pl.BlockSpec(memory_space=pl.ANY)
    inside = pl.BlockSpec(memory_space=pltpu.VMEM)
    return pl.pallas_call(
        lambda *refs: moe_kernel(places, *refs),
        grid_spec=pltpu.PrefetchScalarGridSpec(
            num_scalar_prefetch=4,
            grid=(1,),
            in_specs=[anywhere] * (n + 2) + [inside, inside],
            out_specs=[anywhere] * 8 + [inside, inside],
            scratch_shapes=[
                pltpu.VMEM((TOK, 16, 128), bf16),
                pltpu.VMEM((TOK, 8, 128), f32),
                pltpu.VMEM((TOK, 8, 128), f32),
                pltpu.VMEM((TILE, 8, 128), f32),
                pltpu.VMEM((TILE, 8, 128), f32),
                pltpu.VMEM((TILE, 8, 128), f32),
                pltpu.VMEM((TILE, 8, 128), f32),
                pltpu.VMEM((TILE, D + 128), bf16),
                pltpu.VMEM((TILE, D + 128), bf16),
                pltpu.VMEM((2, D, half), bf16),
                pltpu.VMEM((2, half, D), bf16),
                pltpu.VMEM((2, SEQP, D), bf16),
                pltpu.VMEM((2, SEQP, D + 128), bf16),
                pltpu.VMEM((half, ADAPT), f32),
                pltpu.VMEM((half, ADAPT), f32),
                pltpu.SemaphoreType.DMA((n_copies,)),
                pltpu.SemaphoreType.DMA((2,)),
                pltpu.SemaphoreType.DMA((2,)),
                pltpu.SemaphoreType.DMA((2,)),
                pltpu.SemaphoreType.DMA((2,)),
            ],
        ),
        out_shape=[
            *[jax.ShapeDtypeStruct((TOK // 4, D), bf16)] * 4,
            *[jax.ShapeDtypeStruct((TOK // 4, D + 128), bf16)] * 4,
            jax.ShapeDtypeStruct((half, ADAPT), bf16),
            jax.ShapeDtypeStruct((half, ADAPT), bf16),
        ],
        compiler_params=pltpu.CompilerParams(vmem_limit_bytes=58 * 1024 * 1024),
        cost_estimate=pl.CostEstimate(flops=20_000_000_000, bytes_accessed=60_000_000, transcendentals=10_000_000),
    )(token_list, tile_experts, picks, place, *tables, w_up, w_down, b_up, a_down)


def swapped(s):
    return ((s & 1) << 1) | (s >> 1)


def block_spot(block, row, col):
    from_row = block // 4
    s = (block % 4) ^ col
    return 4 * (from_row ^ row) + jnp.where(from_row == 0, swapped(s), s)


def routing(routes, row, col):
    token = jnp.arange(25 * 128, dtype=jnp.int32)[None, :]
    image = token // SEQ
    spot = block_spot(image // 2, row, col) * BLK + (image % 2) * SEQP + token % SEQ
    real = token < IMG_GRP * SEQ
    picked = jnp.pad(routes.T, ((0, 0), (0, 25 * 128 - IMG_GRP * SEQ)), constant_values=EXPERTS)
    beyond = EXPERTS * 4096 + DUMMY
    keys = jnp.where(real, picked * 4096 + spot, beyond).reshape(-1)
    experts = jnp.arange(EXPERTS, dtype=jnp.int32)
    count = jnp.sum((picked[None] == experts[:, None, None]).astype(jnp.int32), axis=(1, 2))
    tiles = (jnp.maximum(count, 1) + TILE - 1) // TILE
    extra = tiles * TILE - count
    filler = jnp.where(
        jnp.arange(256, dtype=jnp.int32)[None, :] < extra[:, None], (experts * 4096)[:, None] + DUMMY, beyond
    ).reshape(-1)
    ordered = lax.sort(jnp.concatenate([keys, filler])) & 4095
    ends = jnp.sum(jnp.where(experts[None, :] <= experts[:, None], tiles[None, :], 0), axis=1)
    steps = jnp.arange(max_tiles(), dtype=jnp.int32)
    owner = jnp.minimum(jnp.sum((ends[None, :] <= steps[:, None]).astype(jnp.int32), axis=1), EXPERTS - 1)
    return ordered, jnp.concatenate([owner, jnp.sum(tiles)[None]])


HEADS = 12
HEAD_DIM = 64


def pick_mask(pick):
    return (lane_iota((1, ADAPT)) // RANK) == pick


def norm_stats(values):
    centre = jnp.sum(values, axis=1, keepdims=True) * (1.0 / D)
    shifted = values - centre
    spread = jnp.sum(shifted * shifted, axis=1, keepdims=True) * (1.0 / D)
    inverse = lax.rsqrt(spread + 1e-06)
    return shifted * inverse, inverse


def norm_back(grad, gain, unit, inverse):
    scaled = grad * gain
    total = jnp.sum(scaled, axis=1, keepdims=True) * (1.0 / D)
    along = jnp.sum(scaled * unit, axis=1, keepdims=True) * (1.0 / D)
    return inverse * (scaled - total - unit * along)


def qkv_copies(place_ref, blocks, own_b, scratch, sem):
    w_qkv, a_qkv, b_qkv = scratch
    row, col = place_ref[0], place_ref[1]
    copies = []

    def copy(source, target):
        copies.append(pltpu.make_async_copy(source, target, sem.at[len(copies)]))

    for t in range(2):
        half_at = pl.multiple_of((row ^ t) * 384, 128)
        for s in range(4):
            block = blocks[4 * t + s]
            at = pl.multiple_of((col ^ s) * 192, 64)
            low_at = pl.multiple_of((col ^ s) * 192 + (row ^ t) * 96, 32)
            for p in range(3):
                copy(block.at[pl.ds(192 * p, 192)], w_qkv.at[p, pl.ds(at, 192), pl.ds(half_at, 384)])
                copy(block.at[pl.ds(576, 96), pl.ds(128 * p, 128)], a_qkv.at[p, pl.ds(low_at, 96), :])
        for p in range(3):
            source = own_b.at[p] if t == 0 else blocks[4].at[pl.ds(W_ROWS + 128 * p, 128)]
            copy(source, b_qkv.at[p, :, pl.ds(half_at, 384)])
    return copies


def out_copies(place_ref, far_block, own_a, out_w, scratch, sem):
    w_out, a_out = scratch
    row = place_ref[0]
    copies = []

    def copy(source, target):
        copies.append(pltpu.make_async_copy(source, target, sem.at[len(copies)]))

    for t in range(2):
        half_at = pl.multiple_of((row ^ t) * 384, 128)
        copy(out_w[t].at[pl.ds(0, 384)], w_out.at[pl.ds(half_at, 384), :])
        for j in range(3):
            if t == 0:
                source = own_a.at[pl.ds(128 * j, 128)]
            else:
                source = far_block.at[pl.ds(W_ROWS + 384, 128), pl.ds(128 * j, 128)]
            copy(source, a_out.at[pl.ds(half_at + 128 * j, 128), :])
    return copies


W_ROWS = 944
QKV_SCRATCH = [
    pltpu.VMEM((3, D, D), bf16),
    pltpu.VMEM((3, D, ADAPT), bf16),
    pltpu.VMEM((3, ADAPT, D), bf16),
    pltpu.SemaphoreType.DMA((54,)),
]
OUT_SCRATCH = [
    pltpu.VMEM((D, D), bf16),
    pltpu.VMEM((D, ADAPT), bf16),
    pltpu.SemaphoreType.DMA((8,)),
]


def split_kernel(place_ref, tokens_ref, cot_ref, own_out, one_out, two_out, three_out, left, right, stage, sem):
    rows = tokens_ref.shape[0]
    width = D // 4
    left[0:rows, 0:width] = tokens_ref[...].astype(f32)
    right[0:rows, 0:width] = cot_ref[...].astype(f32)
    lane = lane_iota((1, 128))
    real = lax.broadcasted_iota(jnp.int32, (SEQP, 1), 0) < SEQ
    for i in range(8):
        at = slice(SEQ * i, SEQ * i + SEQP)
        spot = slice(SEQP * (i % 2), SEQP * (i % 2) + SEQP)
        moved = pltpu.roll(right[at, :], 64, 1)
        middle = jnp.where(lane < 64, left[at, 128:256], moved[:, 0:128])
        stage[i // 2, spot, 0:128] = jnp.where(real, left[at, 0:128], 0.0).astype(bf16)
        stage[i // 2, spot, 128:256] = jnp.where(real, middle, 0.0).astype(bf16)
        stage[i // 2, spot, 256:384] = jnp.where(real, moved[:, 128:256], 0.0).astype(bf16)
    copies = [
        pltpu.make_async_copy(stage.at[place_ref[1] ^ s], out, sem.at[s])
        for s, out in enumerate((own_out, one_out, two_out, three_out))
    ]
    for copy in copies:
        copy.start()
    for copy in copies:
        copy.wait()


def split_call(place, tokens, cotangent):
    rows = tokens.shape[0]
    tall = -(-(SEQ * 7 + SEQP) // 8) * 8
    inside = pl.BlockSpec(memory_space=pltpu.VMEM)
    return pl.pallas_call(
        split_kernel,
        grid_spec=pltpu.PrefetchScalarGridSpec(
            num_scalar_prefetch=1,
            grid=(1,),
            in_specs=[inside, inside],
            out_specs=[ANYWHERE] * 4,
            scratch_shapes=[
                pltpu.VMEM((tall, 256), f32),
                pltpu.VMEM((tall, 256), f32),
                pltpu.VMEM((4, BLK, 384), bf16),
                pltpu.SemaphoreType.DMA((4,)),
            ],
        ),
        out_shape=[jax.ShapeDtypeStruct((BLK, 384), bf16)] * 4,
        compiler_params=pltpu.CompilerParams(vmem_limit_bytes=32 * 1024 * 1024),
        cost_estimate=pl.CostEstimate(flops=1_000_000_000, bytes_accessed=3_000_000, transcendentals=0),
    )(place, tokens, cotangent)


def finish_kernel(place_ref, mine, one, two, three, far, dp_sums, *refs):
    (
        a_qkv, b_qkv, a_out, b_out, a_router, b_router, a_up, b_up, a_down, b_down, wide, tall, every,
    ) = refs
    row, col = place_ref[0], place_ref[1]
    near_at = pl.multiple_of(row * 96, 32)
    far_at = pl.multiple_of((1 - row) * 96, 32)
    for p in range(4):
        ours = mine[96 * p : 96 * p + 96, :].astype(f32)
        theirs = far[96 * p : 96 * p + 96, :].astype(f32)
        if p < 3:
            a_qkv[p, pl.ds(near_at, 96), :] = ours
            a_qkv[p, pl.ds(far_at, 96), :] = theirs
        else:
            wide[pl.ds(near_at, 96), :] = ours
            wide[pl.ds(far_at, 96), :] = theirs
    b_out[...] = wide[...].T[:, : D // 4]
    share = BOTH_ROWS // 8
    for s, got in enumerate((mine, one, two, three)):
        base = 384 if s == 0 else 0
        at = pl.multiple_of((col ^ s) * 96, 32)
        for p in range(4):
            piece = got[base + 96 * p : base + 96 * p + 96, :].astype(f32)
            if p < 3:
                tall[p, pl.ds(at, 96), :] = piece
            else:
                a_out[pl.ds(at, 96), :] = piece
        ours = got[base + 384 : base + 384 + share, :].astype(f32)
        theirs = far[384 + share * s : 384 + share * s + share, :].astype(f32)
        every[pl.ds(pl.multiple_of((row * 4 + (col ^ s)) * share, 64), share), :] = ours
        every[pl.ds(pl.multiple_of(((1 - row) * 4 + (col ^ s)) * share, 64), share), :] = theirs
    for p in range(3):
        b_qkv[p] = tall[p].T
    a_router[...] = every[0:768, :]
    a_up[...] = every[768:1536, :]
    b_down[...] = every[1536:2304, :].T
    b_router[...] = every[2304:2432, :].T[:, :EXPERTS]
    b_up[...] = dp_sums[0:384, :].astype(f32).T
    a_down[...] = dp_sums[384:768, :].astype(f32)


def finish_call(place, mine, got, far, dp_sums):
    inside = pl.BlockSpec(memory_space=pltpu.VMEM)
    half = D // 2
    shapes = [
        (3, D // 4, ADAPT), (3, ADAPT, half), (half, ADAPT), (ADAPT, D // 4), (D, ADAPT), (ADAPT, EXPERTS),
        (D, ADAPT), (ADAPT, half), (half, ADAPT), (ADAPT, D),
    ]
    return pl.pallas_call(
        finish_kernel,
        grid_spec=pltpu.PrefetchScalarGridSpec(
            num_scalar_prefetch=1,
            grid=(1,),
            in_specs=[inside] * 6,
            out_specs=[inside] * 10,
            scratch_shapes=[
                pltpu.VMEM((256, 128), f32),
                pltpu.VMEM((3, half, 128), f32),
                pltpu.VMEM((BOTH_ROWS, 128), f32),
            ],
        ),
        out_shape=[jax.ShapeDtypeStruct(shape, f32) for shape in shapes],
        compiler_params=pltpu.CompilerParams(vmem_limit_bytes=32 * 1024 * 1024),
        cost_estimate=pl.CostEstimate(flops=1_000_000_000, bytes_accessed=4_000_000, transcendentals=0),
    )(place, mine, *got, far, dp_sums)


def merge_kernel(place_ref, *refs):
    blocks, refs = refs[:4], refs[4:]
    block_out, tokens_out, stage, tall, sem = refs
    copies = [
        pltpu.make_async_copy(block, stage.at[place_ref[1] ^ s], sem.at[s]) for s, block in enumerate(blocks)
    ]
    for copy in copies:
        copy.start()
    for copy in copies:
        copy.wait()
    width = D // 4
    rows = tokens_out.shape[0]
    for i in range(8):
        at = slice(SEQ * i, SEQ * i + SEQ)
        both = stage[i // 2, SEQP * (i % 2) : SEQP * (i % 2) + SEQP, :].astype(f32)[:SEQ]
        tokens_out[at, :] = both[:, :width]
        tall[at, :] = both[:, width:]
    block_out[...] = tall[0:rows, :].astype(bf16)


def merge_call(place, blocks, rows):
    width = D // 4
    inside = pl.BlockSpec(memory_space=pltpu.VMEM)
    return pl.pallas_call(
        merge_kernel,
        grid_spec=pltpu.PrefetchScalarGridSpec(
            num_scalar_prefetch=1,
            grid=(1,),
            in_specs=[ANYWHERE] * 4,
            out_specs=[inside, inside],
            scratch_shapes=[
                pltpu.VMEM((4, BLK, 2 * width), bf16),
                pltpu.VMEM((rows, width), f32),
                pltpu.SemaphoreType.DMA((4,)),
            ],
        ),
        out_shape=[jax.ShapeDtypeStruct((rows, width), bf16), jax.ShapeDtypeStruct((rows, width), f32)],
        compiler_params=pltpu.CompilerParams(vmem_limit_bytes=32 * 1024 * 1024),
        cost_estimate=pl.CostEstimate(flops=8_000_000_000, bytes_accessed=3_000_000, transcendentals=0),
    )(place, *blocks)


def place_weights(place_ref, blocks, own_b, own_a, out_w, w_qkv, a_qkv, b_qkv, w_out, a_out):
    row, col = place_ref[0], place_ref[1]
    for t in range(2):
        half_at = pl.multiple_of((row ^ t) * 384, 128)
        across = pl.ds(half_at, 384)
        for s in range(4):
            block = blocks[4 * t + s]
            at = pl.multiple_of((col ^ s) * 192, 64)
            low_at = pl.multiple_of((col ^ s) * 192 + (row ^ t) * 96, 32)
            for p in range(3):
                w_qkv[p, pl.ds(at, 192), across] = block[192 * p : 192 * p + 192, :]
                a_qkv[p, pl.ds(low_at, 96), :] = block[576:672, 128 * p : 128 * p + 128]
        w_out[across, :] = out_w[t][0:384, :]
        for p in range(3):
            down = pl.ds(pl.multiple_of(half_at + 128 * p, 128), 128)
            if t == 0:
                b_qkv[p, :, across] = own_b[p]
                a_out[down, :] = own_a[128 * p : 128 * p + 128, :]
            else:
                b_qkv[p, :, across] = blocks[4][W_ROWS + 128 * p : W_ROWS + 128 * p + 128, :]
                a_out[down, :] = blocks[4][W_ROWS + 384 : W_ROWS + 512, 128 * p : 128 * p + 128]


def two_masks(picks_ref):
    row = lax.broadcasted_iota(jnp.int32, (BLK, 1), 0)
    pick = jnp.where(row < SEQP, picks_ref[0], picks_ref[1])
    return (lane_iota((1, ADAPT)) // RANK) == pick, (row < SEQ) | ((row >= SEQP) & (row < SEQP + SEQ))


def both_heads(value):
    lane = lane_iota((1, 128))
    nothing = jnp.zeros_like(value)
    return jnp.concatenate(
        [jnp.where(lane < HEAD_DIM, value, nothing), jnp.where(lane < HEAD_DIM, nothing, value)], axis=0
    )


def attend_kernel(picks_ref, place_ref, *refs):
    blocks, refs = refs[:8], refs[8:]
    (
        own_b, own_a, out_near, out_far, x_ref, gain_one, gain_two, b_out,
        two_out, resid_out, normed_out, qkv_out, mixed_out, probs_out, lows_out,
        w_qkv, a_qkv, b_qkv, w_out, a_out,
    ) = refs
    place_weights(place_ref, blocks, own_b, own_a, (out_near, out_far), w_qkv, a_qkv, b_qkv, w_out, a_out)
    mask, real = two_masks(picks_ref)
    x = x_ref[...].astype(f32)
    unit, unused = norm_stats(x)
    normed = (unit * gain_one[...]).astype(bf16)
    normed_out[...] = normed
    for p in range(3):
        low = jnp.where(mask, dot(normed, a_qkv[p]), 0.0).astype(bf16)
        lows_out[:, 128 * p : 128 * p + 128] = low
        qkv_out[p] = (dot(normed, w_qkv[p]) + dot(low, b_qkv[p])).astype(bf16)
    lane = lane_iota((1, 128))
    key_lane = lane_iota((1, SEQP))
    for pair in range(HEADS // 2):
        at = slice(128 * pair, 128 * pair + 128)
        for image in range(2):
            rows = slice(SEQP * image, SEQP * image + SEQP)
            scores = dot_nt(both_heads(qkv_out[0, rows, at]), qkv_out[1, rows, at]) * (HEAD_DIM**-0.5)
            scores = jnp.where(key_lane < SEQ, scores, -1e30)
            power = jnp.exp(scores - jnp.max(scores, axis=1, keepdims=True))
            probs = (power / jnp.sum(power, axis=1, keepdims=True)).astype(bf16)
            probs_out[image, pair] = probs
            found = dot(probs, qkv_out[2, rows, at])
            mixed_out[rows, at] = jnp.where(lane < HEAD_DIM, found[:SEQP], found[SEQP:]).astype(bf16)
    mixed = mixed_out[...]
    low = jnp.where(mask, dot(mixed, a_out[...]), 0.0).astype(bf16)
    lows_out[:, 384:512] = low
    resid = x + dot(mixed, w_out[...]) + dot(low, b_out[...])
    resid_out[...] = resid
    unit, unused = norm_stats(resid)
    two_out[...] = jnp.where(real, unit * gain_two[...], 0.0).astype(bf16)


INSIDE = pl.BlockSpec(memory_space=pltpu.VMEM)


ANYWHERE = pl.BlockSpec(memory_space=pl.ANY)


def attend_call(picks, place, blocks, own_b, own_a, out_w, x, gain_one, gain_two, b_out):
    rows = x.shape[0]
    return pl.pallas_call(
        attend_kernel,
        grid_spec=pltpu.PrefetchScalarGridSpec(
            num_scalar_prefetch=2,
            grid=(1,),
            in_specs=[INSIDE] * (len(blocks) + 8),
            out_specs=[INSIDE] * 7,
            scratch_shapes=QKV_SCRATCH[:-1] + OUT_SCRATCH[:-1],
        ),
        out_shape=[
            jax.ShapeDtypeStruct((rows, D), bf16),
            jax.ShapeDtypeStruct((rows, D), f32),
            jax.ShapeDtypeStruct((rows, D), bf16),
            jax.ShapeDtypeStruct((3, rows, D), bf16),
            jax.ShapeDtypeStruct((rows, D), bf16),
            jax.ShapeDtypeStruct((2, HEADS // 2, BLK, SEQP), bf16),
            jax.ShapeDtypeStruct((rows, 512), bf16),
        ],
        compiler_params=pltpu.CompilerParams(vmem_limit_bytes=48 * 1024 * 1024),
        cost_estimate=pl.CostEstimate(flops=4_000_000_000, bytes_accessed=15_000_000, transcendentals=2_000_000),
    )(picks, place, *blocks, own_b, own_a, *out_w, x, gain_one, gain_two, b_out)


def out_back_kernel(picks_ref, place_ref, *refs):
    (
        far_block, own_a, out_near, out_far, gain_two, b_out, two_ref, resid_ref, mixed_ref, lows_ref,
        cot_ref, grad_a, grad_b, w_router, a_router, b_router, a_up, b_down,
        resid_grad_out, mixed_grad_out, base_out, both_out, a_part_out, b_part_out,
        w_out, a_out, sem,
    ) = refs
    copies = out_copies(place_ref, far_block, own_a, (out_near, out_far), (w_out, a_out), sem)
    for copy in copies:
        copy.start()
    mask, unused = two_masks(picks_ref)
    lane = lane_iota((1, 128))

    def add_part(row, value):
        both_out[row : row + value.shape[0], :] = value.astype(bf16)

    two = two_ref[...]
    received = grad_a[...].astype(f32) + grad_b[...].astype(f32)
    low_r = jnp.where(mask, dot(two, a_router[...]), 0.0).astype(bf16)
    logits = dot(two, w_router[...]) + dot(low_r, b_router[...])
    logits = jnp.where(lane < EXPERTS, logits, -1e30)
    power = jnp.exp(logits - jnp.max(logits, axis=1, keepdims=True))
    probs = power / jnp.sum(power, axis=1, keepdims=True)
    last = received[:, D:]
    grad_probs = jnp.where(lane < EXPERTS, last, 0.0)
    low_in = jnp.where(mask, repeat_lanes(jnp.where((lane >= 32) & (lane < 48), last, 0.0)), 0.0).astype(bf16)
    low_out = jnp.where(mask, repeat_lanes(jnp.where((lane >= 48) & (lane < 64), last, 0.0)), 0.0).astype(bf16)
    cot = cot_ref[...]
    resid = resid_ref[...]
    base_out[...] = resid + dot(low_out, b_down[...])
    add_part(768, dot_tn(two, low_in))
    add_part(1536, dot_tn(cot, low_out))
    grad_logits = probs * (grad_probs - jnp.sum(probs * grad_probs, axis=1, keepdims=True))
    grad_logits = grad_logits.astype(bf16)
    grad_low = jnp.where(mask, dot_nt(grad_logits, b_router[...]), 0.0).astype(bf16)
    grad_two = received[:, :D] + dot_nt(low_in, a_up[...])
    grad_two = grad_two + dot_nt(grad_logits, w_router[...]) + dot_nt(grad_low, a_router[...])
    add_part(0, dot_tn(two, grad_low))
    add_part(2304, dot_tn(grad_logits, low_r))
    unit, inverse = norm_stats(resid)
    grad_resid = cot.astype(f32) + norm_back(grad_two, gain_two[...], unit, inverse)
    resid_grad_out[...] = grad_resid
    grad_attn = grad_resid.astype(bf16)
    grad_low = jnp.where(mask, dot_nt(grad_attn, b_out[...]), 0.0).astype(bf16)
    for copy in copies:
        copy.wait()
    mixed_grad_out[...] = (dot_nt(grad_attn, w_out[...]) + dot_nt(grad_low, a_out[...])).astype(bf16)
    a_part_out[...] = dot_tn(mixed_ref[...], grad_low).astype(bf16)
    b_part_out[...] = dot_tn(grad_attn, lows_ref[:, 384:512]).astype(bf16)
    both_out[2432:BOTH_ROWS, :] = jnp.zeros((BOTH_ROWS - 2432, 128), bf16)


BOTH_ROWS = 2560


def out_back_call(picks, place, far_block, own_a, out_w, gain_two, b_out, two, resid, mixed, lows, cot, grad_a, grad_b,
                  w_router, a_router, b_router, a_up, b_down):
    rows = two.shape[0]
    return pl.pallas_call(
        out_back_kernel,
        grid_spec=pltpu.PrefetchScalarGridSpec(
            num_scalar_prefetch=2,
            grid=(1,),
            in_specs=[ANYWHERE] * 4 + [INSIDE] * 14,
            out_specs=[INSIDE] * 6,
            scratch_shapes=OUT_SCRATCH,
        ),
        out_shape=[
            jax.ShapeDtypeStruct((rows, D), f32),
            jax.ShapeDtypeStruct((rows, D), bf16),
            jax.ShapeDtypeStruct((rows, D), f32),
            jax.ShapeDtypeStruct((BOTH_ROWS, 128), bf16),
            jax.ShapeDtypeStruct((D, 128), bf16),
            jax.ShapeDtypeStruct((D, 128), bf16),
        ],
        compiler_params=pltpu.CompilerParams(vmem_limit_bytes=60 * 1024 * 1024),
        cost_estimate=pl.CostEstimate(flops=6_000_000_000, bytes_accessed=15_000_000, transcendentals=100_000),
    )(picks, place, far_block, own_a, *out_w, gain_two, b_out, two, resid, mixed, lows, cot, grad_a, grad_b,
      w_router, a_router, b_router, a_up, b_down)


def qkv_back_kernel(picks_ref, place_ref, *refs):
    blocks, refs = refs[:8], refs[8:]
    (
        own_b, x_hbm, gain_one, normed_hbm, qkv_ref, probs_ref, lows_hbm, resid_hbm, grad_mixed,
        tokens_out, a_part_out, b_part_out,
        w_qkv, a_qkv, b_qkv, sem, grads, x_ref, normed_ref, lows_ref, resid_grad, late_sem,
    ) = refs
    copies = qkv_copies(place_ref, blocks, own_b, (w_qkv, a_qkv, b_qkv), sem)
    late = ((x_hbm, x_ref), (normed_hbm, normed_ref), (lows_hbm, lows_ref), (resid_hbm, resid_grad))
    for k, (source, target) in enumerate(late):
        copies.append(pltpu.make_async_copy(source, target, late_sem.at[k]))
    for copy in copies:
        copy.start()
    mask, unused = two_masks(picks_ref)
    lane = lane_iota((1, 128))
    for pair in range(HEADS // 2):
        at = slice(128 * pair, 128 * pair + 128)
        for image in range(2):
            rows = slice(SEQP * image, SEQP * image + SEQP)
            grad_out = both_heads(grad_mixed[rows, at])
            weights = probs_ref[image, pair]
            weights_f = weights.astype(f32)
            grad_w = dot_nt(grad_out, qkv_ref[2, rows, at])
            inner = jnp.sum(weights_f * grad_w, axis=1, keepdims=True)
            grad_s = (weights_f * (grad_w - inner) * (HEAD_DIM**-0.5)).astype(bf16)
            found = dot(grad_s, qkv_ref[1, rows, at])
            grads[0, rows, at] = jnp.where(lane < HEAD_DIM, found[:SEQP], found[SEQP:]).astype(bf16)
            grads[1, rows, at] = dot_tn(grad_s, both_heads(qkv_ref[0, rows, at])).astype(bf16)
            grads[2, rows, at] = dot_tn(weights, grad_out).astype(bf16)
    for copy in copies:
        copy.wait()
    normed = normed_ref[...]
    grad_normed = jnp.zeros((BLK, D), f32)
    for p in range(3):
        piece = grads[p]
        grad_low = jnp.where(mask, dot_nt(piece, b_qkv[p]), 0.0).astype(bf16)
        grad_normed = grad_normed + dot_nt(piece, w_qkv[p]) + dot_nt(grad_low, a_qkv[p])
        a_part_out[D * p : D * p + D, :] = dot_tn(normed, grad_low).astype(bf16)
        b_part_out[D * p : D * p + D, :] = dot_tn(piece, lows_ref[:, 128 * p : 128 * p + 128]).astype(bf16)
    unit, inverse = norm_stats(x_ref[...].astype(f32))
    tokens_out[...] = (resid_grad[...] + norm_back(grad_normed, gain_one[...], unit, inverse)).astype(bf16)


def qkv_back_call(picks, place, blocks, own_b, x, gain_one, normed, qkv, probs, lows, resid_grad, grad_mixed):
    rows = x.shape[0]
    return pl.pallas_call(
        qkv_back_kernel,
        grid_spec=pltpu.PrefetchScalarGridSpec(
            num_scalar_prefetch=2,
            grid=(1,),
            in_specs=[ANYWHERE] * (len(blocks) + 2)
            + [INSIDE, ANYWHERE, INSIDE, INSIDE, ANYWHERE, ANYWHERE, INSIDE],
            out_specs=[INSIDE] * 3,
            scratch_shapes=QKV_SCRATCH
            + [
                pltpu.VMEM((3, BLK, D), bf16),
                pltpu.VMEM((BLK, D), bf16),
                pltpu.VMEM((BLK, D), bf16),
                pltpu.VMEM((BLK, 512), bf16),
                pltpu.VMEM((BLK, D), f32),
                pltpu.SemaphoreType.DMA((4,)),
            ],
        ),
        out_shape=[
            jax.ShapeDtypeStruct((rows, D), bf16),
            jax.ShapeDtypeStruct((3 * D, 128), bf16),
            jax.ShapeDtypeStruct((3 * D, 128), bf16),
        ],
        compiler_params=pltpu.CompilerParams(vmem_limit_bytes=60 * 1024 * 1024),
        cost_estimate=pl.CostEstimate(flops=9_000_000_000, bytes_accessed=15_000_000, transcendentals=1000),
    )(picks, place, *blocks, own_b, x, gain_one, normed, qkv, probs, lows, resid_grad, grad_mixed)


TABLES = (((0, 0), (1, 0)), ((0, 1), (0, 2), (1, 1), (1, 2)), ((0, 3), (1, 3)))


def across_row(value):
    return lax.ppermute(value, "row", [(0, 1), (1, 0)])


def across_col(value, step):
    return lax.ppermute(value, "col", [(i, i ^ step) for i in range(4)])


def by_place(blocks, col):
    found = []
    for place in range(4):
        value = blocks[place]
        for other in range(1, 4):
            value = jnp.where(col == other, blocks[place ^ other], value)
        found.append(value)
    return found


def across_chip(value, first, second):
    pairs = [(i, i ^ first) for i in range(4)] + [(4 + i, 4 + (i ^ second)) for i in range(4)]
    return lax.ppermute(value, ("row", "col"), pairs)


def gather_col(value, row):
    from_x = across_col(value, 1)
    from_y = across_col(value, 2)
    return [value, from_x, from_y, across_chip(jnp.where(row == 0, from_x, from_y), 2, 1)]


def added(*values):
    total = values[0].astype(f32)
    for value in values[1:]:
        total = total + value.astype(f32)
    return total


def last_exchange(kept_rows, got):
    sent = added(kept_rows[BLK:], got[BLK:]).astype(bf16)
    return added(kept_rows[:BLK], got[:BLK]).astype(bf16), across_chip(sent, 2, 1)


def at_place(value, axis, place):
    return lax.dynamic_index_in_dim(value, place, axis, keepdims=False)


def scatter_dp(value):
    place = lax.axis_index("dp")
    view = value.reshape(4, -1, 128)
    found = [at_place(view, 0, place)]
    for s in range(1, 4):
        found.append(across_dp(at_place(view, 0, place ^ s), s))
    return added(*found).astype(bf16)


def across_dp(value, step):
    return lax.ppermute(value, "dp", [(i, i ^ step) for i in range(4)])


def spread_dp(value):
    return jnp.concatenate(by_place([value] + [across_dp(value, s) for s in range(1, 4)], lax.axis_index("dp")))


def part_share(col_parts, row_parts, both_parts, place):
    col_parts = at_place(col_parts.reshape(4, 4, 2, 96, 128), 2, place)
    row_parts = at_place(row_parts.reshape(4, 2, 4, 96, 128), 1, place)
    both_parts = at_place(both_parts.reshape(2, 4, BOTH_ROWS // 8, 128), 0, place)
    col_parts = col_parts.swapaxes(0, 1).reshape(4, 384, 128)
    row_parts = row_parts.swapaxes(0, 1).reshape(4, 384, 128)
    return jnp.concatenate([col_parts, row_parts, both_parts], axis=1)


def exchange_col(value, col):
    return [at_place(value, 0, col)] + [across_col(at_place(value, 0, col ^ s), s) for s in range(1, 4)]


def to_features(first, second, col):
    width = D // 4
    pieces = []
    for p in range(4):
        at = slice(width * p, width * p + width)
        pieces.append(jnp.concatenate([first[:, at], second[:, at]], axis=1))
    sent = by_place(pieces, col)
    return [sent[0]] + [across_col(sent[s], s) for s in range(1, 4)]


def on_device(
    tokens, cotangent, routes, adapter_pick, gain_attn, gain_moe, w_qkv, w_out, w_router, w_up, w_down,
    a_qkv, b_qkv, a_out, b_out, a_router, b_router, a_up, b_up, a_down, b_down,
):
    row = lax.axis_index("row")
    col = lax.axis_index("col")
    me = row * 4 + col
    place = jnp.stack([row, col]).astype(jnp.int32)

    width = D // 4
    half = D // 2
    gains = []
    for gain in (gain_attn, gain_moe):
        left = gain
        for unused in range(3):
            lead = lax.reduce_precision(left, 8, 7)
            gains.append(lead.astype(bf16))
            left = left - lead
    small = jnp.concatenate([w_out, b_out, jnp.stack(gains), jnp.zeros((26, width), bf16)], axis=0)
    low = at_place(a_qkv.reshape(3, 2, 96, ADAPT), 1, row)
    packed = jnp.concatenate(
        [w_qkv.reshape(576, half), jnp.concatenate([low[0], low[1], low[2]], axis=1),
         jnp.concatenate([small[:272], small[272:]], axis=1)]
    )
    for_row = jnp.concatenate(
        [packed, b_qkv.reshape(half, half), jnp.concatenate([a_out[:128], a_out[128:256], a_out[256:]], axis=1)]
    )
    pairs = split_call(place, tokens, cotangent)
    from_x, from_y = across_col(packed, 1), across_col(packed, 2)
    near = [packed, from_x, from_y, across_chip(jnp.where(row == 0, from_x, from_y), 2, 1)]
    near[3], *pairs = lax.optimization_barrier((near[3], *pairs))
    pairs = by_place([pairs[0]] + [across_col(pairs[s], s) for s in range(1, 4)], col)
    x = jnp.concatenate([pair[:, :width] for pair in pairs], axis=1)
    cot = jnp.concatenate([pair[:, width:] for pair in pairs], axis=1)
    far = [across_row(for_row)] + [across_row(block) for block in near[1:]]
    blocks = near + far

    def assembled(group):
        parts = by_place([block[672:944] for block in group], col)
        return jnp.concatenate(
            [jnp.concatenate([part[:, :width] for part in parts], axis=1),
             jnp.concatenate([part[:, width:] for part in parts], axis=1)], axis=0
        )

    out_w = [assembled(near), assembled(far)]
    full_b_out = out_w[0][384:512]
    gain_rows = out_w[0][512:518].astype(f32)
    gain_one = jnp.sum(gain_rows[:3], axis=0, keepdims=True)
    gain_two = jnp.sum(gain_rows[3:], axis=0, keepdims=True)

    picks_group = lax.dynamic_slice_in_dim(adapter_pick, lax.axis_index("dp") * IMG_GRP, IMG_GRP)
    order = jnp.arange(IMG_GRP, dtype=jnp.int32)
    picks = jnp.take(picks_group, ((order // 2) ^ me) * 2 + order % 2)
    spot_picks = jnp.sum(
        jnp.where(block_spot(order // 2, row, col)[None, :] * 2 + order[None, :] % 2 == order[:, None], picks_group[None, :], 0), axis=1
    )
    token_list, tile_experts = routing(routes, row, col)
    wide_router = jnp.concatenate([w_router, w_router, jnp.zeros((D, 64), bf16)], axis=1)
    wide_b_router = jnp.concatenate([b_router, b_router, jnp.zeros((ADAPT, 64), bf16)], axis=1)
    slim_router = jnp.concatenate([w_router, jnp.zeros((D, 96), bf16)], axis=1)
    slim_b_router = jnp.concatenate([b_router, jnp.zeros((ADAPT, 96), bf16)], axis=1)

    x, token_list, tile_experts, wide_router, wide_b_router, slim_router, slim_b_router = lax.optimization_barrier(
        (x, token_list, tile_experts, wide_router, wide_b_router, slim_router, slim_b_router)
    )
    cot, unused = lax.optimization_barrier((cot, near[3]))
    two, resid, normed, qkv, mixed, probs, lows = attend_call(
        picks, place, blocks, b_qkv, a_out, out_w, x, gain_one, gain_two, full_b_out
    )
    cot_near = gather_col(cot, row)
    two_x, two_y = across_col(two, 1), across_col(two, 2)

    def table(spots, twos, cots):
        return table_call(
            jnp.stack([picks[8 * t + 2 * s + side] for t, s in spots for side in range(2)]),
            twos, cots, a_up, b_down, wide_router, a_router, wide_b_router,
        )

    cot_far = [across_row(block) for block in cot_near[:3]]
    tables = [table(TABLES[0], [two, across_row(two)], [cot, cot_far[0]])]
    two_x, two_y, tables[0] = lax.optimization_barrier((two_x, two_y, tables[0]))
    diag = across_chip(jnp.where(row == 0, two_x, two_y), 2, 1)
    tables.append(
        table(TABLES[1], [two_x, two_y, across_row(two_x), across_row(two_y)], [cot_near[1], cot_near[2], cot_far[1], cot_far[2]])
    )
    diag, cot_diag, *tables = lax.optimization_barrier((diag, cot_near[3], *tables))
    tables.append(table(TABLES[2], [diag, across_row(diag)], [cot_diag, across_row(cot_diag)]))
    *moved, part_b_up, part_a_down = moe_call(
        token_list, tile_experts, spot_picks, place, tables, TABLES, w_up, w_down, b_up, a_down
    )
    sums, grads = moved[:4], moved[4:]
    dp_parts = jnp.concatenate([part_b_up, part_a_down])
    grad_sent = added(grads[1], across_row(grads[3])).astype(bf16)
    grad_kept = added(grads[0], across_row(grads[2])).astype(bf16)
    grad_sent, dp_parts, *sums = lax.optimization_barrier((grad_sent, dp_parts, *sums))
    grad_got = across_chip(grad_sent, 1, 2)
    sum_kept, sum_sent = across_row(sums[2]), across_row(sums[3])
    sums = [
        added(near[at : at + BLK], far[at : at + BLK]).astype(bf16)
        for near, far in ((sums[0], sum_kept), (sums[1], sum_sent)) for at in (0, BLK)
    ]
    four_dp = lax.axis_size("dp") == 4
    dp_sums = scatter_dp(dp_parts) if four_dp else lax.psum(dp_parts, "dp")
    grad_got, dp_sums, *sums = lax.optimization_barrier((grad_got, dp_sums, *sums))
    grad_a, grad_b = last_exchange(grad_kept, grad_got)
    if four_dp:
        dp_sums = spread_dp(dp_sums)
    grad_a, grad_b, dp_sums, *sums = lax.optimization_barrier((grad_a, grad_b, dp_sums, *sums))
    sums = [sums[0], across_chip(sums[1], 2, 1), across_chip(sums[2], 1, 2), across_chip(sums[3], 3, 3)]
    resid_grad, mixed_grad, base, both_parts, part_a_out, part_b_out = out_back_call(
        picks, place, blocks[4], a_out, out_w, gain_two, full_b_out, two, resid, mixed, lows, cot, grad_a, grad_b,
        slim_router, a_router, slim_b_router, a_up, b_down,
    )
    grad_tokens, part_a_qkv, part_b_qkv = qkv_back_call(
        picks, place, blocks, b_qkv, x, gain_one, normed, qkv, probs, lows, resid_grad, mixed_grad
    )
    part_a_qkv, part_b_qkv, *sums = lax.optimization_barrier((part_a_qkv, part_b_qkv, *sums))
    col_parts = jnp.concatenate([part_a_qkv, part_b_out])
    row_parts = jnp.concatenate([part_b_qkv, part_a_out])
    theirs = across_row(part_share(col_parts, row_parts, both_parts, 1 - row))
    shared = added(part_share(col_parts, row_parts, both_parts, row), theirs).astype(bf16)
    found = exchange_col(shared, col)
    mine = added(*found).astype(bf16)
    mine, grad_tokens, base = lax.optimization_barrier((mine, grad_tokens, base))
    moves = to_features(grad_tokens, (base + added(*sums)).astype(bf16), col)
    mine = spread_dp(scatter_dp(mine)) if four_dp else lax.psum(mine, "dp")
    got = [across_col(mine[384:], s) for s in range(1, 4)]
    far = across_row(jnp.concatenate([mine[:384], mine[768:]] + [one[384:] for one in got]))
    block_out, grad_tokens = merge_call(place, moves, tokens.shape[0])
    far, block_out, grad_tokens = lax.optimization_barrier((far, block_out, grad_tokens))
    return (block_out, grad_tokens, *finish_call(place, mine, got, far, dp_sums))


def solution(mesh):
    return jax.shard_map(
        on_device,
        mesh=mesh,
        in_specs=(
            P(("dp", "row"), "col"),
            P(("dp", "row"), "col"),
            P("dp", None),
            P(),
            P("col"),
            P("col"),
            P(None, "col", "row"),
            P("row", "col"),
            P(),
            P(None, None, ("row", "col")),
            P(None, ("row", "col"), None),
            P(None, "col", None),
            P(None, None, "row"),
            P("row", None),
            P(None, "col"),
            P(),
            P(),
            P(),
            P(None, ("row", "col")),
            P(("row", "col"), None),
            P(),
        ),
        out_specs=(
            P(("dp", "row"), "col"),
            P(("dp", "row"), "col"),
            P(None, "col", None),
            P(None, None, "row"),
            P("row", None),
            P(None, "col"),
            P(),
            P(),
            P(),
            P(None, ("row", "col")),
            P(("row", "col"), None),
            P(),
        ),
        check_vma=False,
    )
```

```python
import jax
import jax.numpy as jnp
from jax import lax
from jax.experimental import pallas as pl
from jax.experimental.pallas import tpu as pltpu
from jax.sharding import PartitionSpec as P

D = 768
EXPERTS = 32
SEQ = 197
SEQP = 208
RANK = 16
ADAPT = 128
IMG_GRP = 16
TOK = IMG_GRP * SEQP
BLK = 2 * SEQP
DUMMY = SEQ
TILE = 160
f32 = jnp.float32
bf16 = jnp.bfloat16


def max_tiles():
    return (2 * IMG_GRP * SEQ) // TILE + EXPERTS + 1


def dot(left, right):
    return jnp.dot(left, right, preferred_element_type=f32)


def dot_nt(left, right):
    return lax.dot_general(left, right, (((1,), (1,)), ((), ())), preferred_element_type=f32)


def dot_tn(left, right):
    return lax.dot_general(left, right, (((0,), (0,)), ((), ())), preferred_element_type=f32)


def lane_iota(shape):
    return lax.broadcasted_iota(jnp.int32, shape, len(shape) - 1)


def repeat_lanes(value):
    for shift in (16, 32, 64):
        value = value + pltpu.roll(value, shift, 1)
    return value


def table_kernel(n_blocks, picks_ref, *refs):
    x_blocks = refs[:n_blocks]
    c_blocks = refs[n_blocks : 2 * n_blocks]
    a_up, b_down, w_router, a_router, b_router, table_out, xin, cin, rows_x, rows_c, sem = refs[2 * n_blocks :]
    image = pl.program_id(0)
    lane = lane_iota((1, 128))

    @pl.when(image == 0)
    def start():
        copies = []
        for blocks, place in ((x_blocks, xin), (c_blocks, cin)):
            for b, block in enumerate(blocks):
                copies.append(pltpu.make_async_copy(block, place.at[pl.ds(b * BLK, BLK)], sem.at[len(copies)]))
        for copy in copies:
            copy.start()
        for copy in copies:
            copy.wait()

    row = pl.multiple_of(image * SEQP, 16)
    mask = (lane // RANK) == picks_ref[image]
    x = xin[pl.ds(row, SEQP), :]
    c = cin[pl.ds(row, SEQP), :]
    flat_x = rows_x.reshape(SEQP * 8, 128)
    flat_c = rows_c.reshape(SEQP * 8, 128)
    low_x = jnp.where(mask, dot(x, a_up[...]), 0.0)
    low_c = jnp.where(mask, dot_nt(c, b_down[...]), 0.0)
    low_r = jnp.where(mask, dot(x, a_router[...]), 0.0).astype(bf16)
    logits = dot(x, w_router[...]) + dot(low_r, b_router[...])
    logits = jnp.where(lane < 2 * EXPERTS, logits, -1e30)
    power = jnp.exp(logits - jnp.max(logits, axis=1, keepdims=True))
    total = jnp.sum(jnp.where(lane < EXPERTS, power, 0.0), axis=1, keepdims=True)
    probs = power / total
    lead = probs.astype(bf16).astype(f32)
    probs = jnp.where(lane < EXPERTS, lead, probs - lead)
    for j in range(6):
        flat_x[pl.ds(j, SEQP, 8), :] = x[:, 128 * j : 128 * j + 128].astype(f32)
        flat_c[pl.ds(j, SEQP, 8), :] = c[:, 128 * j : 128 * j + 128].astype(f32)
    flat_x[pl.ds(6, SEQP, 8), :] = low_x
    flat_x[pl.ds(7, SEQP, 8), :] = probs
    flat_c[pl.ds(6, SEQP, 8), :] = low_c
    flat_c[pl.ds(7, SEQP, 8), :] = jnp.zeros((SEQP, 128), f32)
    table_out[...] = jnp.concatenate([rows_x[...], rows_c[...]], axis=1).astype(bf16)


def table_call(picks, x_blocks, c_blocks, a_up, b_down, w_router, a_router, b_router):
    n = len(x_blocks)

    def whole(*shape):
        return pl.BlockSpec(shape, lambda e, *_: (0,) * len(shape))

    anywhere = pl.BlockSpec(memory_space=pl.ANY)
    return pl.pallas_call(
        lambda *refs: table_kernel(n, *refs),
        grid_spec=pltpu.PrefetchScalarGridSpec(
            num_scalar_prefetch=1,
            grid=(2 * n,),
            in_specs=[anywhere] * (2 * n)
            + [whole(D, ADAPT), whole(ADAPT, D), whole(D, 128), whole(D, ADAPT), whole(ADAPT, 128)],
            out_specs=pl.BlockSpec((SEQP, 16, 128), lambda i, *_: (i, 0, 0)),
            scratch_shapes=[
                pltpu.VMEM((n * BLK, D), bf16),
                pltpu.VMEM((n * BLK, D), bf16),
                pltpu.VMEM((SEQP, 8, 128), f32),
                pltpu.VMEM((SEQP, 8, 128), f32),
                pltpu.SemaphoreType.DMA((2 * n,)),
            ],
        ),
        out_shape=jax.ShapeDtypeStruct((n * BLK, 16, 128), bf16),
        compiler_params=pltpu.CompilerParams(vmem_limit_bytes=32 * 1024 * 1024),
        cost_estimate=pl.CostEstimate(flops=n * 3_000_000_000, bytes_accessed=n * 3_000_000, transcendentals=n * 60_000),
    )(picks, *x_blocks, *c_blocks, a_up, b_down, w_router, a_router, b_router)


def moe_kernel(places, list_ref, expert_ref, picks_ref, place_ref, *refs):
    n = len(places)
    tables = refs[:n]
    ep_outs, tg_outs = refs[n + 4 : n + 8], refs[n + 8 : n + 12]
    refs = refs[: n + 4] + refs[n + 12 :]
    (
        w_up_hbm, w_down_hbm, b_up, a_down,
        gbu_bf, gad_bf,
        table, acc_e, acc_t, in_x, in_c, out_e, out_t, xb, cb, w_up, w_down, stage_ep, stage_tg,
        gbu_out, gad_out, in_sem, up_sem, down_sem, ep_sem, tg_sem,
    ) = refs[n:]
    acc_e_flat = acc_e.reshape(TOK * 8, 128)
    acc_t_flat = acc_t.reshape(TOK * 8, 128)
    in_x_flat = in_x.reshape(TILE * 8, 128)
    in_c_flat = in_c.reshape(TILE * 8, 128)
    out_e_flat = out_e.reshape(TILE * 8, 128)
    out_t_flat = out_t.reshape(TILE * 8, 128)
    lane = lane_iota((1, 128))
    n_tiles = expert_ref[max_tiles()]

    copies = []
    for piece, spots in zip(tables, places):
        for b, (t, s) in enumerate(spots):
            spot = 4 * t + jnp.where(place_ref[0] == t, swapped(s), s)
            copies.append(
                pltpu.make_async_copy(
                    piece.at[pl.ds(b * BLK, BLK)], table.at[pl.ds(pl.multiple_of(spot * BLK, 32), BLK)], in_sem.at[len(copies)]
                )
            )
    for copy in copies:
        copy.start()

    def weights(expert):
        slot = expert % 2
        return (
            pltpu.make_async_copy(w_up_hbm.at[expert], w_up.at[slot], up_sem.at[slot]),
            pltpu.make_async_copy(w_down_hbm.at[expert], w_down.at[slot], down_sem.at[slot]),
        )

    for copy in weights(0):
        copy.start()
    out_e[...] = jnp.zeros_like(out_e)
    out_t[...] = jnp.zeros_like(out_t)
    gbu_out[...] = jnp.zeros_like(gbu_out)
    gad_out[...] = jnp.zeros_like(gad_out)

    def clear(i, carry):
        acc_e[pl.ds(i * 64, 64)] = jnp.zeros((64, 8, 128), f32)
        acc_t[pl.ds(i * 64, 64)] = jnp.zeros((64, 8, 128), f32)
        return carry

    lax.fori_loop(0, TOK // 64, clear, 0)
    for copy in copies:
        copy.wait()

    def fetch(t):
        for i in range(TILE):
            both = table[list_ref[t * TILE + i]].astype(f32)
            in_x[i] = both[:8]
            in_c[i] = both[8:]

    def give(t):
        for b in range(TILE // 8):
            tokens = [list_ref[t * TILE + 8 * b + k] for k in range(8)]
            sums_e = [acc_e[tokens[k]] + out_e[8 * b + k] for k in range(8)]
            sums_t = [acc_t[tokens[k]] + out_t[8 * b + k] for k in range(8)]
            for k in range(8):
                acc_e[tokens[k]] = sums_e[k]
                acc_t[tokens[k]] = sums_t[k]

    fetch(0)

    def tile(t, carry):
        expert = expert_ref[t]
        slot = expert % 2

        @pl.when((t == 0) | (expert_ref[jnp.maximum(t - 1, 0)] != expert))
        def arrive():
            for copy in weights(expert):
                copy.wait()

            @pl.when(expert + 1 < EXPERTS)
            def ahead():
                for copy in weights(expert + 1):
                    copy.start()

        for j in range(7):
            xb[:, 128 * j : 128 * j + 128] = in_x_flat[pl.ds(j, TILE, 8), :].astype(bf16)
            cb[:, 128 * j : 128 * j + 128] = in_c_flat[pl.ds(j, TILE, 8), :].astype(bf16)
        spread = in_x_flat[pl.ds(7, TILE, 8), :]
        mine = (lane == expert) | (lane == expert + EXPERTS)
        gate = jnp.sum(jnp.where(mine, spread, 0.0), axis=1, keepdims=True)
        fetch(t + 1)
        give(jnp.maximum(t - 1, 0))
        hidden = dot(xb[:, :D], w_up[slot]) + dot(xb[:, D:], b_up[...])
        back = dot_nt(cb[:, :D], w_down[slot]) + dot_nt(cb[:, D:], a_down[...])
        cdf = 0.5 + 0.5 * lax.erf(hidden * 0.7071067811865476)
        slope = cdf + hidden * jnp.exp(hidden * hidden * -0.5) * 0.3989422804014327
        act = (hidden * cdf).astype(bf16)
        act_f = act.astype(f32)
        gate_grad = jnp.sum(act_f * back, axis=1, keepdims=True)
        grad_hidden = (gate * back * slope).astype(bf16)
        act_gate = (gate * act_f).astype(bf16)
        out_main = dot(act_gate, w_down[slot])
        out_low = dot(act_gate, a_down[...])
        in_main = dot_nt(grad_hidden, w_up[slot])
        in_low = dot_nt(grad_hidden, b_up[...])
        gbu_out[...] += dot_tn(grad_hidden, xb[:, D:])
        gad_out[...] += dot_tn(act_gate, cb[:, D:])
        for j in range(6):
            out_e_flat[pl.ds(j, TILE, 8), :] = out_main[:, 128 * j : 128 * j + 128]
            out_t_flat[pl.ds(j, TILE, 8), :] = in_main[:, 128 * j : 128 * j + 128]
        out_e_flat[pl.ds(6, TILE, 8), :] = out_low
        out_t_flat[pl.ds(6, TILE, 8), :] = in_low
        out_t_flat[pl.ds(7, TILE, 8), :] = jnp.where(lane == expert, gate_grad, 0.0)
        return carry

    lax.fori_loop(0, n_tiles, tile, 0)
    give(n_tiles - 1)

    gbu_bf[...] = gbu_out[...].astype(bf16)
    gad_bf[...] = gad_out[...].astype(bf16)
    some = IMG_GRP // 4
    for side, (ep_out, tg_out) in enumerate(zip(ep_outs, tg_outs)):

        def image(i, carry):
            slot = i % 2
            base = pl.multiple_of((i + side * some) * SEQP, 16) * 8
            mask = (lane // RANK) == picks_ref[i + side * some]
            rows = pl.ds(pl.multiple_of(i * SEQP, 16), SEQP)
            put_tg = pltpu.make_async_copy(stage_tg.at[slot], tg_out.at[rows], tg_sem.at[slot])
            put_ep = pltpu.make_async_copy(stage_ep.at[slot], ep_out.at[rows], ep_sem.at[slot])

            @pl.when(i >= 2)
            def drain():
                put_tg.wait()
                put_ep.wait()

            def chunk(j):
                flat = acc_e_flat if j < 8 else acc_t_flat
                return flat[pl.ds(base + j % 8, SEQP, 8), :]

            for j in range(6):
                at = slice(128 * j, 128 * j + 128)
                stage_tg[slot, :, at] = chunk(8 + j).astype(bf16)
                stage_ep[slot, :, at] = chunk(j).astype(bf16)
            low_in = repeat_lanes(jnp.where(mask, chunk(14), 0.0))
            low_out = repeat_lanes(jnp.where(mask, chunk(6), 0.0))
            last = jnp.where(lane < 48, low_in, jnp.where(lane < 64, low_out, 0.0))
            stage_tg[slot, :, D:] = jnp.where(lane < 32, chunk(15), last).astype(bf16)
            put_tg.start()
            put_ep.start()
            return carry

        lax.fori_loop(0, some, image, 0)
        for i in range(some - 2, some):
            rows = pl.ds(i * SEQP, SEQP)
            pltpu.make_async_copy(stage_tg.at[i % 2], tg_out.at[rows], tg_sem.at[i % 2]).wait()
            pltpu.make_async_copy(stage_ep.at[i % 2], ep_out.at[rows], ep_sem.at[i % 2]).wait()


def moe_call(token_list, tile_experts, picks, place, tables, places, w_up, w_down, b_up, a_down):
    half = w_up.shape[2]
    n = len(tables)
    n_copies = sum(len(spots) for spots in places)
    anywhere = pl.BlockSpec(memory_space=pl.ANY)
    inside = pl.BlockSpec(memory_space=pltpu.VMEM)
    return pl.pallas_call(
        lambda *refs: moe_kernel(places, *refs),
        grid_spec=pltpu.PrefetchScalarGridSpec(
            num_scalar_prefetch=4,
            grid=(1,),
            in_specs=[anywhere] * (n + 2) + [inside, inside],
            out_specs=[anywhere] * 8 + [inside, inside],
            scratch_shapes=[
                pltpu.VMEM((TOK, 16, 128), bf16),
                pltpu.VMEM((TOK, 8, 128), f32),
                pltpu.VMEM((TOK, 8, 128), f32),
                pltpu.VMEM((TILE, 8, 128), f32),
                pltpu.VMEM((TILE, 8, 128), f32),
                pltpu.VMEM((TILE, 8, 128), f32),
                pltpu.VMEM((TILE, 8, 128), f32),
                pltpu.VMEM((TILE, D + 128), bf16),
                pltpu.VMEM((TILE, D + 128), bf16),
                pltpu.VMEM((2, D, half), bf16),
                pltpu.VMEM((2, half, D), bf16),
                pltpu.VMEM((2, SEQP, D), bf16),
                pltpu.VMEM((2, SEQP, D + 128), bf16),
                pltpu.VMEM((half, ADAPT), f32),
                pltpu.VMEM((half, ADAPT), f32),
                pltpu.SemaphoreType.DMA((n_copies,)),
                pltpu.SemaphoreType.DMA((2,)),
                pltpu.SemaphoreType.DMA((2,)),
                pltpu.SemaphoreType.DMA((2,)),
                pltpu.SemaphoreType.DMA((2,)),
            ],
        ),
        out_shape=[
            *[jax.ShapeDtypeStruct((TOK // 4, D), bf16)] * 4,
            *[jax.ShapeDtypeStruct((TOK // 4, D + 128), bf16)] * 4,
            jax.ShapeDtypeStruct((half, ADAPT), bf16),
            jax.ShapeDtypeStruct((half, ADAPT), bf16),
        ],
        compiler_params=pltpu.CompilerParams(vmem_limit_bytes=58 * 1024 * 1024),
        cost_estimate=pl.CostEstimate(flops=20_000_000_000, bytes_accessed=60_000_000, transcendentals=10_000_000),
    )(token_list, tile_experts, picks, place, *tables, w_up, w_down, b_up, a_down)


def swapped(s):
    return ((s & 1) << 1) | (s >> 1)


def block_spot(block, row, col):
    from_row = block // 4
    s = (block % 4) ^ col
    return 4 * (from_row ^ row) + jnp.where(from_row == 0, swapped(s), s)


def routing(routes, row, col):
    token = jnp.arange(25 * 128, dtype=jnp.int32)[None, :]
    image = token // SEQ
    spot = block_spot(image // 2, row, col) * BLK + (image % 2) * SEQP + token % SEQ
    real = token < IMG_GRP * SEQ
    picked = jnp.pad(routes.T, ((0, 0), (0, 25 * 128 - IMG_GRP * SEQ)), constant_values=EXPERTS)
    beyond = EXPERTS * 4096 + DUMMY
    keys = jnp.where(real, picked * 4096 + spot, beyond).reshape(-1)
    experts = jnp.arange(EXPERTS, dtype=jnp.int32)
    count = jnp.sum((picked[None] == experts[:, None, None]).astype(jnp.int32), axis=(1, 2))
    tiles = (jnp.maximum(count, 1) + TILE - 1) // TILE
    extra = tiles * TILE - count
    filler = jnp.where(
        jnp.arange(256, dtype=jnp.int32)[None, :] < extra[:, None], (experts * 4096)[:, None] + DUMMY, beyond
    ).reshape(-1)
    ordered = lax.sort(jnp.concatenate([keys, filler])) & 4095
    ends = jnp.sum(jnp.where(experts[None, :] <= experts[:, None], tiles[None, :], 0), axis=1)
    steps = jnp.arange(max_tiles(), dtype=jnp.int32)
    owner = jnp.minimum(jnp.sum((ends[None, :] <= steps[:, None]).astype(jnp.int32), axis=1), EXPERTS - 1)
    return ordered, jnp.concatenate([owner, jnp.sum(tiles)[None]])


HEADS = 12
HEAD_DIM = 64


def pick_mask(pick):
    return (lane_iota((1, ADAPT)) // RANK) == pick


def norm_stats(values):
    centre = jnp.sum(values, axis=1, keepdims=True) * (1.0 / D)
    shifted = values - centre
    spread = jnp.sum(shifted * shifted, axis=1, keepdims=True) * (1.0 / D)
    inverse = lax.rsqrt(spread + 1e-06)
    return shifted * inverse, inverse


def norm_back(grad, gain, unit, inverse):
    scaled = grad * gain
    total = jnp.sum(scaled, axis=1, keepdims=True) * (1.0 / D)
    along = jnp.sum(scaled * unit, axis=1, keepdims=True) * (1.0 / D)
    return inverse * (scaled - total - unit * along)


def qkv_copies(place_ref, blocks, own_b, scratch, sem):
    w_qkv, a_qkv, b_qkv = scratch
    row, col = place_ref[0], place_ref[1]
    copies = []

    def copy(source, target):
        copies.append(pltpu.make_async_copy(source, target, sem.at[len(copies)]))

    for t in range(2):
        half_at = pl.multiple_of((row ^ t) * 384, 128)
        for s in range(4):
            block = blocks[4 * t + s]
            at = pl.multiple_of((col ^ s) * 192, 64)
            low_at = pl.multiple_of((col ^ s) * 192 + (row ^ t) * 96, 32)
            for p in range(3):
                copy(block.at[pl.ds(192 * p, 192)], w_qkv.at[p, pl.ds(at, 192), pl.ds(half_at, 384)])
                copy(block.at[pl.ds(576, 96), pl.ds(128 * p, 128)], a_qkv.at[p, pl.ds(low_at, 96), :])
        for p in range(3):
            source = own_b.at[p] if t == 0 else blocks[4].at[pl.ds(W_ROWS + 128 * p, 128)]
            copy(source, b_qkv.at[p, :, pl.ds(half_at, 384)])
    return copies


def out_copies(place_ref, far_block, own_a, out_w, scratch, sem):
    w_out, a_out = scratch
    row = place_ref[0]
    copies = []

    def copy(source, target):
        copies.append(pltpu.make_async_copy(source, target, sem.at[len(copies)]))

    for t in range(2):
        half_at = pl.multiple_of((row ^ t) * 384, 128)
        copy(out_w[t].at[pl.ds(0, 384)], w_out.at[pl.ds(half_at, 384), :])
        for j in range(3):
            if t == 0:
                source = own_a.at[pl.ds(128 * j, 128)]
            else:
                source = far_block.at[pl.ds(W_ROWS + 384, 128), pl.ds(128 * j, 128)]
            copy(source, a_out.at[pl.ds(half_at + 128 * j, 128), :])
    return copies


W_ROWS = 944
QKV_SCRATCH = [
    pltpu.VMEM((3, D, D), bf16),
    pltpu.VMEM((3, D, ADAPT), bf16),
    pltpu.VMEM((3, ADAPT, D), bf16),
    pltpu.SemaphoreType.DMA((54,)),
]
OUT_SCRATCH = [
    pltpu.VMEM((D, D), bf16),
    pltpu.VMEM((D, ADAPT), bf16),
    pltpu.SemaphoreType.DMA((8,)),
]


def split_kernel(place_ref, tokens_ref, cot_ref, own_out, one_out, two_out, three_out, left, right, stage, sem):
    rows = tokens_ref.shape[0]
    width = D // 4
    left[0:rows, 0:width] = tokens_ref[...].astype(f32)
    right[0:rows, 0:width] = cot_ref[...].astype(f32)
    lane = lane_iota((1, 128))
    real = lax.broadcasted_iota(jnp.int32, (SEQP, 1), 0) < SEQ
    for i in range(8):
        at = slice(SEQ * i, SEQ * i + SEQP)
        spot = slice(SEQP * (i % 2), SEQP * (i % 2) + SEQP)
        moved = pltpu.roll(right[at, :], 64, 1)
        middle = jnp.where(lane < 64, left[at, 128:256], moved[:, 0:128])
        stage[i // 2, spot, 0:128] = jnp.where(real, left[at, 0:128], 0.0).astype(bf16)
        stage[i // 2, spot, 128:256] = jnp.where(real, middle, 0.0).astype(bf16)
        stage[i // 2, spot, 256:384] = jnp.where(real, moved[:, 128:256], 0.0).astype(bf16)
    copies = [
        pltpu.make_async_copy(stage.at[place_ref[1] ^ s], out, sem.at[s])
        for s, out in enumerate((own_out, one_out, two_out, three_out))
    ]
    for copy in copies:
        copy.start()
    for copy in copies:
        copy.wait()


def split_call(place, tokens, cotangent):
    rows = tokens.shape[0]
    tall = -(-(SEQ * 7 + SEQP) // 8) * 8
    inside = pl.BlockSpec(memory_space=pltpu.VMEM)
    return pl.pallas_call(
        split_kernel,
        grid_spec=pltpu.PrefetchScalarGridSpec(
            num_scalar_prefetch=1,
            grid=(1,),
            in_specs=[inside, inside],
            out_specs=[ANYWHERE] * 4,
            scratch_shapes=[
                pltpu.VMEM((tall, 256), f32),
                pltpu.VMEM((tall, 256), f32),
                pltpu.VMEM((4, BLK, 384), bf16),
                pltpu.SemaphoreType.DMA((4,)),
            ],
        ),
        out_shape=[jax.ShapeDtypeStruct((BLK, 384), bf16)] * 4,
        compiler_params=pltpu.CompilerParams(vmem_limit_bytes=32 * 1024 * 1024),
        cost_estimate=pl.CostEstimate(flops=1_000_000_000, bytes_accessed=3_000_000, transcendentals=0),
    )(place, tokens, cotangent)


def finish_kernel(place_ref, mine, one, two, three, far, dp_sums, *refs):
    (
        a_qkv, b_qkv, a_out, b_out, a_router, b_router, a_up, b_up, a_down, b_down, wide, tall, every,
    ) = refs
    row, col = place_ref[0], place_ref[1]
    near_at = pl.multiple_of(row * 96, 32)
    far_at = pl.multiple_of((1 - row) * 96, 32)
    for p in range(4):
        ours = mine[96 * p : 96 * p + 96, :].astype(f32)
        theirs = far[96 * p : 96 * p + 96, :].astype(f32)
        if p < 3:
            a_qkv[p, pl.ds(near_at, 96), :] = ours
            a_qkv[p, pl.ds(far_at, 96), :] = theirs
        else:
            wide[pl.ds(near_at, 96), :] = ours
            wide[pl.ds(far_at, 96), :] = theirs
    b_out[...] = wide[...].T[:, : D // 4]
    share = BOTH_ROWS // 8
    for s, got in enumerate((mine, one, two, three)):
        base = 384 if s == 0 else 0
        at = pl.multiple_of((col ^ s) * 96, 32)
        for p in range(4):
            piece = got[base + 96 * p : base + 96 * p + 96, :].astype(f32)
            if p < 3:
                tall[p, pl.ds(at, 96), :] = piece
            else:
                a_out[pl.ds(at, 96), :] = piece
        ours = got[base + 384 : base + 384 + share, :].astype(f32)
        theirs = far[384 + share * s : 384 + share * s + share, :].astype(f32)
        every[pl.ds(pl.multiple_of((row * 4 + (col ^ s)) * share, 64), share), :] = ours
        every[pl.ds(pl.multiple_of(((1 - row) * 4 + (col ^ s)) * share, 64), share), :] = theirs
    for p in range(3):
        b_qkv[p] = tall[p].T
    a_router[...] = every[0:768, :]
    a_up[...] = every[768:1536, :]
    b_down[...] = every[1536:2304, :].T
    b_router[...] = every[2304:2432, :].T[:, :EXPERTS]
    b_up[...] = dp_sums[0:384, :].astype(f32).T
    a_down[...] = dp_sums[384:768, :].astype(f32)


def finish_call(place, mine, got, far, dp_sums):
    inside = pl.BlockSpec(memory_space=pltpu.VMEM)
    half = D // 2
    shapes = [
        (3, D // 4, ADAPT), (3, ADAPT, half), (half, ADAPT), (ADAPT, D // 4), (D, ADAPT), (ADAPT, EXPERTS),
        (D, ADAPT), (ADAPT, half), (half, ADAPT), (ADAPT, D),
    ]
    return pl.pallas_call(
        finish_kernel,
        grid_spec=pltpu.PrefetchScalarGridSpec(
            num_scalar_prefetch=1,
            grid=(1,),
            in_specs=[inside] * 6,
            out_specs=[inside] * 10,
            scratch_shapes=[
                pltpu.VMEM((256, 128), f32),
                pltpu.VMEM((3, half, 128), f32),
                pltpu.VMEM((BOTH_ROWS, 128), f32),
            ],
        ),
        out_shape=[jax.ShapeDtypeStruct(shape, f32) for shape in shapes],
        compiler_params=pltpu.CompilerParams(vmem_limit_bytes=32 * 1024 * 1024),
        cost_estimate=pl.CostEstimate(flops=1_000_000_000, bytes_accessed=4_000_000, transcendentals=0),
    )(place, mine, *got, far, dp_sums)


def merge_kernel(place_ref, *refs):
    blocks, refs = refs[:4], refs[4:]
    block_out, tokens_out, stage, tall, sem = refs
    copies = [
        pltpu.make_async_copy(block, stage.at[place_ref[1] ^ s], sem.at[s]) for s, block in enumerate(blocks)
    ]
    for copy in copies:
        copy.start()
    for copy in copies:
        copy.wait()
    width = D // 4
    rows = tokens_out.shape[0]
    for i in range(8):
        at = slice(SEQ * i, SEQ * i + SEQ)
        both = stage[i // 2, SEQP * (i % 2) : SEQP * (i % 2) + SEQP, :].astype(f32)[:SEQ]
        tokens_out[at, :] = both[:, :width]
        tall[at, :] = both[:, width:]
    block_out[...] = tall[0:rows, :].astype(bf16)


def merge_call(place, blocks, rows):
    width = D // 4
    inside = pl.BlockSpec(memory_space=pltpu.VMEM)
    return pl.pallas_call(
        merge_kernel,
        grid_spec=pltpu.PrefetchScalarGridSpec(
            num_scalar_prefetch=1,
            grid=(1,),
            in_specs=[ANYWHERE] * 4,
            out_specs=[inside, inside],
            scratch_shapes=[
                pltpu.VMEM((4, BLK, 2 * width), bf16),
                pltpu.VMEM((rows, width), f32),
                pltpu.SemaphoreType.DMA((4,)),
            ],
        ),
        out_shape=[jax.ShapeDtypeStruct((rows, width), bf16), jax.ShapeDtypeStruct((rows, width), f32)],
        compiler_params=pltpu.CompilerParams(vmem_limit_bytes=32 * 1024 * 1024),
        cost_estimate=pl.CostEstimate(flops=8_000_000_000, bytes_accessed=3_000_000, transcendentals=0),
    )(place, *blocks)


def place_weights(place_ref, blocks, own_b, own_a, out_w, w_qkv, a_qkv, b_qkv, w_out, a_out):
    row, col = place_ref[0], place_ref[1]
    for t in range(2):
        half_at = pl.multiple_of((row ^ t) * 384, 128)
        across = pl.ds(half_at, 384)
        for s in range(4):
            block = blocks[4 * t + s]
            at = pl.multiple_of((col ^ s) * 192, 64)
            low_at = pl.multiple_of((col ^ s) * 192 + (row ^ t) * 96, 32)
            for p in range(3):
                w_qkv[p, pl.ds(at, 192), across] = block[192 * p : 192 * p + 192, :]
                a_qkv[p, pl.ds(low_at, 96), :] = block[576:672, 128 * p : 128 * p + 128]
        w_out[across, :] = out_w[t][0:384, :]
        for p in range(3):
            down = pl.ds(pl.multiple_of(half_at + 128 * p, 128), 128)
            if t == 0:
                b_qkv[p, :, across] = own_b[p]
                a_out[down, :] = own_a[128 * p : 128 * p + 128, :]
            else:
                b_qkv[p, :, across] = blocks[4][W_ROWS + 128 * p : W_ROWS + 128 * p + 128, :]
                a_out[down, :] = blocks[4][W_ROWS + 384 : W_ROWS + 512, 128 * p : 128 * p + 128]


def two_masks(picks_ref):
    row = lax.broadcasted_iota(jnp.int32, (BLK, 1), 0)
    pick = jnp.where(row < SEQP, picks_ref[0], picks_ref[1])
    return (lane_iota((1, ADAPT)) // RANK) == pick, (row < SEQ) | ((row >= SEQP) & (row < SEQP + SEQ))


def both_heads(value):
    lane = lane_iota((1, 128))
    nothing = jnp.zeros_like(value)
    return jnp.concatenate(
        [jnp.where(lane < HEAD_DIM, value, nothing), jnp.where(lane < HEAD_DIM, nothing, value)], axis=0
    )


def attend_kernel(picks_ref, place_ref, *refs):
    blocks, refs = refs[:8], refs[8:]
    (
        own_b, own_a, out_near, out_far, x_ref, gain_one, gain_two, b_out,
        two_out, resid_out, normed_out, qkv_out, mixed_out, probs_out, lows_out,
        w_qkv, a_qkv, b_qkv, w_out, a_out,
    ) = refs
    place_weights(place_ref, blocks, own_b, own_a, (out_near, out_far), w_qkv, a_qkv, b_qkv, w_out, a_out)
    mask, real = two_masks(picks_ref)
    x = x_ref[...].astype(f32)
    unit, unused = norm_stats(x)
    normed = (unit * gain_one[...]).astype(bf16)
    normed_out[...] = normed
    for p in range(3):
        low = jnp.where(mask, dot(normed, a_qkv[p]), 0.0).astype(bf16)
        lows_out[:, 128 * p : 128 * p + 128] = low
        qkv_out[p] = (dot(normed, w_qkv[p]) + dot(low, b_qkv[p])).astype(bf16)
    lane = lane_iota((1, 128))
    key_lane = lane_iota((1, SEQP))
    for pair in range(HEADS // 2):
        at = slice(128 * pair, 128 * pair + 128)
        for image in range(2):
            rows = slice(SEQP * image, SEQP * image + SEQP)
            scores = dot_nt(both_heads(qkv_out[0, rows, at]), qkv_out[1, rows, at]) * (HEAD_DIM**-0.5)
            scores = jnp.where(key_lane < SEQ, scores, -1e30)
            power = jnp.exp(scores - jnp.max(scores, axis=1, keepdims=True))
            probs = (power / jnp.sum(power, axis=1, keepdims=True)).astype(bf16)
            probs_out[image, pair] = probs
            found = dot(probs, qkv_out[2, rows, at])
            mixed_out[rows, at] = jnp.where(lane < HEAD_DIM, found[:SEQP], found[SEQP:]).astype(bf16)
    mixed = mixed_out[...]
    low = jnp.where(mask, dot(mixed, a_out[...]), 0.0).astype(bf16)
    lows_out[:, 384:512] = low
    resid = x + dot(mixed, w_out[...]) + dot(low, b_out[...])
    resid_out[...] = resid
    unit, unused = norm_stats(resid)
    two_out[...] = jnp.where(real, unit * gain_two[...], 0.0).astype(bf16)


INSIDE = pl.BlockSpec(memory_space=pltpu.VMEM)


ANYWHERE = pl.BlockSpec(memory_space=pl.ANY)


def attend_call(picks, place, blocks, own_b, own_a, out_w, x, gain_one, gain_two, b_out):
    rows = x.shape[0]
    return pl.pallas_call(
        attend_kernel,
        grid_spec=pltpu.PrefetchScalarGridSpec(
            num_scalar_prefetch=2,
            grid=(1,),
            in_specs=[INSIDE] * (len(blocks) + 8),
            out_specs=[INSIDE] * 7,
            scratch_shapes=QKV_SCRATCH[:-1] + OUT_SCRATCH[:-1],
        ),
        out_shape=[
            jax.ShapeDtypeStruct((rows, D), bf16),
            jax.ShapeDtypeStruct((rows, D), f32),
            jax.ShapeDtypeStruct((rows, D), bf16),
            jax.ShapeDtypeStruct((3, rows, D), bf16),
            jax.ShapeDtypeStruct((rows, D), bf16),
            jax.ShapeDtypeStruct((2, HEADS // 2, BLK, SEQP), bf16),
            jax.ShapeDtypeStruct((rows, 512), bf16),
        ],
        compiler_params=pltpu.CompilerParams(vmem_limit_bytes=48 * 1024 * 1024),
        cost_estimate=pl.CostEstimate(flops=4_000_000_000, bytes_accessed=15_000_000, transcendentals=2_000_000),
    )(picks, place, *blocks, own_b, own_a, *out_w, x, gain_one, gain_two, b_out)


def out_back_kernel(picks_ref, place_ref, *refs):
    (
        far_block, own_a, out_near, out_far, gain_two, b_out, two_ref, resid_ref, mixed_ref, lows_ref,
        cot_ref, grad_a, grad_b, w_router, a_router, b_router, a_up, b_down,
        resid_grad_out, mixed_grad_out, base_out, both_out, a_part_out, b_part_out,
        w_out, a_out, sem,
    ) = refs
    copies = out_copies(place_ref, far_block, own_a, (out_near, out_far), (w_out, a_out), sem)
    for copy in copies:
        copy.start()
    mask, unused = two_masks(picks_ref)
    lane = lane_iota((1, 128))

    def add_part(row, value):
        both_out[row : row + value.shape[0], :] = value.astype(bf16)

    two = two_ref[...]
    received = grad_a[...].astype(f32) + grad_b[...].astype(f32)
    low_r = jnp.where(mask, dot(two, a_router[...]), 0.0).astype(bf16)
    logits = dot(two, w_router[...]) + dot(low_r, b_router[...])
    logits = jnp.where(lane < EXPERTS, logits, -1e30)
    power = jnp.exp(logits - jnp.max(logits, axis=1, keepdims=True))
    probs = power / jnp.sum(power, axis=1, keepdims=True)
    last = received[:, D:]
    grad_probs = jnp.where(lane < EXPERTS, last, 0.0)
    low_in = jnp.where(mask, repeat_lanes(jnp.where((lane >= 32) & (lane < 48), last, 0.0)), 0.0).astype(bf16)
    low_out = jnp.where(mask, repeat_lanes(jnp.where((lane >= 48) & (lane < 64), last, 0.0)), 0.0).astype(bf16)
    cot = cot_ref[...]
    resid = resid_ref[...]
    base_out[...] = resid + dot(low_out, b_down[...])
    add_part(768, dot_tn(two, low_in))
    add_part(1536, dot_tn(cot, low_out))
    grad_logits = probs * (grad_probs - jnp.sum(probs * grad_probs, axis=1, keepdims=True))
    grad_logits = grad_logits.astype(bf16)
    grad_low = jnp.where(mask, dot_nt(grad_logits, b_router[...]), 0.0).astype(bf16)
    grad_two = received[:, :D] + dot_nt(low_in, a_up[...])
    grad_two = grad_two + dot_nt(grad_logits, w_router[...]) + dot_nt(grad_low, a_router[...])
    add_part(0, dot_tn(two, grad_low))
    add_part(2304, dot_tn(grad_logits, low_r))
    unit, inverse = norm_stats(resid)
    grad_resid = cot.astype(f32) + norm_back(grad_two, gain_two[...], unit, inverse)
    resid_grad_out[...] = grad_resid
    grad_attn = grad_resid.astype(bf16)
    grad_low = jnp.where(mask, dot_nt(grad_attn, b_out[...]), 0.0).astype(bf16)
    for copy in copies:
        copy.wait()
    mixed_grad_out[...] = (dot_nt(grad_attn, w_out[...]) + dot_nt(grad_low, a_out[...])).astype(bf16)
    a_part_out[...] = dot_tn(mixed_ref[...], grad_low).astype(bf16)
    b_part_out[...] = dot_tn(grad_attn, lows_ref[:, 384:512]).astype(bf16)
    both_out[2432:BOTH_ROWS, :] = jnp.zeros((BOTH_ROWS - 2432, 128), bf16)


BOTH_ROWS = 2560


def out_back_call(picks, place, far_block, own_a, out_w, gain_two, b_out, two, resid, mixed, lows, cot, grad_a, grad_b,
                  w_router, a_router, b_router, a_up, b_down):
    rows = two.shape[0]
    return pl.pallas_call(
        out_back_kernel,
        grid_spec=pltpu.PrefetchScalarGridSpec(
            num_scalar_prefetch=2,
            grid=(1,),
            in_specs=[ANYWHERE] * 4 + [INSIDE] * 14,
            out_specs=[INSIDE] * 6,
            scratch_shapes=OUT_SCRATCH,
        ),
        out_shape=[
            jax.ShapeDtypeStruct((rows, D), f32),
            jax.ShapeDtypeStruct((rows, D), bf16),
            jax.ShapeDtypeStruct((rows, D), f32),
            jax.ShapeDtypeStruct((BOTH_ROWS, 128), bf16),
            jax.ShapeDtypeStruct((D, 128), bf16),
            jax.ShapeDtypeStruct((D, 128), bf16),
        ],
        compiler_params=pltpu.CompilerParams(vmem_limit_bytes=60 * 1024 * 1024),
        cost_estimate=pl.CostEstimate(flops=6_000_000_000, bytes_accessed=15_000_000, transcendentals=100_000),
    )(picks, place, far_block, own_a, *out_w, gain_two, b_out, two, resid, mixed, lows, cot, grad_a, grad_b,
      w_router, a_router, b_router, a_up, b_down)


def qkv_back_kernel(picks_ref, place_ref, *refs):
    blocks, refs = refs[:8], refs[8:]
    (
        own_b, x_hbm, gain_one, normed_hbm, qkv_ref, probs_ref, lows_hbm, resid_hbm, grad_mixed,
        tokens_out, a_part_out, b_part_out,
        w_qkv, a_qkv, b_qkv, sem, grads, x_ref, normed_ref, lows_ref, resid_grad, late_sem,
    ) = refs
    copies = qkv_copies(place_ref, blocks, own_b, (w_qkv, a_qkv, b_qkv), sem)
    late = ((x_hbm, x_ref), (normed_hbm, normed_ref), (lows_hbm, lows_ref), (resid_hbm, resid_grad))
    for k, (source, target) in enumerate(late):
        copies.append(pltpu.make_async_copy(source, target, late_sem.at[k]))
    for copy in copies:
        copy.start()
    mask, unused = two_masks(picks_ref)
    lane = lane_iota((1, 128))
    for pair in range(HEADS // 2):
        at = slice(128 * pair, 128 * pair + 128)
        for image in range(2):
            rows = slice(SEQP * image, SEQP * image + SEQP)
            grad_out = both_heads(grad_mixed[rows, at])
            weights = probs_ref[image, pair]
            weights_f = weights.astype(f32)
            grad_w = dot_nt(grad_out, qkv_ref[2, rows, at])
            inner = jnp.sum(weights_f * grad_w, axis=1, keepdims=True)
            grad_s = (weights_f * (grad_w - inner) * (HEAD_DIM**-0.5)).astype(bf16)
            found = dot(grad_s, qkv_ref[1, rows, at])
            grads[0, rows, at] = jnp.where(lane < HEAD_DIM, found[:SEQP], found[SEQP:]).astype(bf16)
            grads[1, rows, at] = dot_tn(grad_s, both_heads(qkv_ref[0, rows, at])).astype(bf16)
            grads[2, rows, at] = dot_tn(weights, grad_out).astype(bf16)
    for copy in copies:
        copy.wait()
    normed = normed_ref[...]
    grad_normed = jnp.zeros((BLK, D), f32)
    for p in range(3):
        piece = grads[p]
        grad_low = jnp.where(mask, dot_nt(piece, b_qkv[p]), 0.0).astype(bf16)
        grad_normed = grad_normed + dot_nt(piece, w_qkv[p]) + dot_nt(grad_low, a_qkv[p])
        a_part_out[D * p : D * p + D, :] = dot_tn(normed, grad_low).astype(bf16)
        b_part_out[D * p : D * p + D, :] = dot_tn(piece, lows_ref[:, 128 * p : 128 * p + 128]).astype(bf16)
    unit, inverse = norm_stats(x_ref[...].astype(f32))
    tokens_out[...] = (resid_grad[...] + norm_back(grad_normed, gain_one[...], unit, inverse)).astype(bf16)


def qkv_back_call(picks, place, blocks, own_b, x, gain_one, normed, qkv, probs, lows, resid_grad, grad_mixed):
    rows = x.shape[0]
    return pl.pallas_call(
        qkv_back_kernel,
        grid_spec=pltpu.PrefetchScalarGridSpec(
            num_scalar_prefetch=2,
            grid=(1,),
            in_specs=[ANYWHERE] * (len(blocks) + 2)
            + [INSIDE, ANYWHERE, INSIDE, INSIDE, ANYWHERE, ANYWHERE, INSIDE],
            out_specs=[INSIDE] * 3,
            scratch_shapes=QKV_SCRATCH
            + [
                pltpu.VMEM((3, BLK, D), bf16),
                pltpu.VMEM((BLK, D), bf16),
                pltpu.VMEM((BLK, D), bf16),
                pltpu.VMEM((BLK, 512), bf16),
                pltpu.VMEM((BLK, D), f32),
                pltpu.SemaphoreType.DMA((4,)),
            ],
        ),
        out_shape=[
            jax.ShapeDtypeStruct((rows, D), bf16),
            jax.ShapeDtypeStruct((3 * D, 128), bf16),
            jax.ShapeDtypeStruct((3 * D, 128), bf16),
        ],
        compiler_params=pltpu.CompilerParams(vmem_limit_bytes=60 * 1024 * 1024),
        cost_estimate=pl.CostEstimate(flops=9_000_000_000, bytes_accessed=15_000_000, transcendentals=1000),
    )(picks, place, *blocks, own_b, x, gain_one, normed, qkv, probs, lows, resid_grad, grad_mixed)


TABLES = (((0, 0), (1, 0)), ((0, 1), (0, 2), (1, 1), (1, 2)), ((0, 3), (1, 3)))


def across_row(value):
    return lax.ppermute(value, "row", [(0, 1), (1, 0)])


def across_col(value, step):
    return lax.ppermute(value, "col", [(i, i ^ step) for i in range(4)])


def by_place(blocks, col):
    found = []
    for place in range(4):
        value = blocks[place]
        for other in range(1, 4):
            value = jnp.where(col == other, blocks[place ^ other], value)
        found.append(value)
    return found


def across_chip(value, first, second):
    pairs = [(i, i ^ first) for i in range(4)] + [(4 + i, 4 + (i ^ second)) for i in range(4)]
    return lax.ppermute(value, ("row", "col"), pairs)


def gather_col(value, row):
    from_x = across_col(value, 1)
    from_y = across_col(value, 2)
    return [value, from_x, from_y, across_chip(jnp.where(row == 0, from_x, from_y), 2, 1)]


def added(*values):
    total = values[0].astype(f32)
    for value in values[1:]:
        total = total + value.astype(f32)
    return total


def last_exchange(kept_rows, got):
    sent = added(kept_rows[BLK:], got[BLK:]).astype(bf16)
    return added(kept_rows[:BLK], got[:BLK]).astype(bf16), across_chip(sent, 2, 1)


def at_place(value, axis, place):
    return lax.dynamic_index_in_dim(value, place, axis, keepdims=False)


def scatter_dp(value):
    place = lax.axis_index("dp")
    view = value.reshape(4, -1, 128)
    found = [at_place(view, 0, place)]
    for s in range(1, 4):
        found.append(across_dp(at_place(view, 0, place ^ s), s))
    return added(*found).astype(bf16)


def across_dp(value, step):
    return lax.ppermute(value, "dp", [(i, i ^ step) for i in range(4)])


def spread_dp(value):
    return jnp.concatenate(by_place([value] + [across_dp(value, s) for s in range(1, 4)], lax.axis_index("dp")))


def part_share(col_parts, row_parts, both_parts, place):
    col_parts = at_place(col_parts.reshape(4, 4, 2, 96, 128), 2, place)
    row_parts = at_place(row_parts.reshape(4, 2, 4, 96, 128), 1, place)
    both_parts = at_place(both_parts.reshape(2, 4, BOTH_ROWS // 8, 128), 0, place)
    col_parts = col_parts.swapaxes(0, 1).reshape(4, 384, 128)
    row_parts = row_parts.swapaxes(0, 1).reshape(4, 384, 128)
    return jnp.concatenate([col_parts, row_parts, both_parts], axis=1)


def exchange_col(value, col):
    return [at_place(value, 0, col)] + [across_col(at_place(value, 0, col ^ s), s) for s in range(1, 4)]


def to_features(first, second, col):
    width = D // 4
    pieces = []
    for p in range(4):
        at = slice(width * p, width * p + width)
        pieces.append(jnp.concatenate([first[:, at], second[:, at]], axis=1))
    sent = by_place(pieces, col)
    return [sent[0]] + [across_col(sent[s], s) for s in range(1, 4)]


def on_device(
    tokens, cotangent, routes, adapter_pick, gain_attn, gain_moe, w_qkv, w_out, w_router, w_up, w_down,
    a_qkv, b_qkv, a_out, b_out, a_router, b_router, a_up, b_up, a_down, b_down,
):
    row = lax.axis_index("row")
    col = lax.axis_index("col")
    me = row * 4 + col
    place = jnp.stack([row, col]).astype(jnp.int32)

    width = D // 4
    half = D // 2
    gains = []
    for gain in (gain_attn, gain_moe):
        left = gain
        for unused in range(3):
            lead = lax.reduce_precision(left, 8, 7)
            gains.append(lead.astype(bf16))
            left = left - lead
    small = jnp.concatenate([w_out, b_out, jnp.stack(gains), jnp.zeros((26, width), bf16)], axis=0)
    low = at_place(a_qkv.reshape(3, 2, 96, ADAPT), 1, row)
    packed = jnp.concatenate(
        [w_qkv.reshape(576, half), jnp.concatenate([low[0], low[1], low[2]], axis=1),
         jnp.concatenate([small[:272], small[272:]], axis=1)]
    )
    for_row = jnp.concatenate(
        [packed, b_qkv.reshape(half, half), jnp.concatenate([a_out[:128], a_out[128:256], a_out[256:]], axis=1)]
    )
    pairs = split_call(place, tokens, cotangent)
    from_x, from_y = across_col(packed, 1), across_col(packed, 2)
    chosen, *pairs = lax.optimization_barrier((jnp.where(row == 0, from_x, from_y), *pairs))
    near = [packed, from_x, from_y, across_chip(chosen, 2, 1)]
    pairs = by_place([pairs[0]] + [across_col(pairs[s], s) for s in range(1, 4)], col)
    x = jnp.concatenate([pair[:, :width] for pair in pairs], axis=1)
    cot = jnp.concatenate([pair[:, width:] for pair in pairs], axis=1)
    far = [across_row(for_row)] + [across_row(block) for block in near[1:]]
    blocks = near + far

    def assembled(group):
        parts = by_place([block[672:944] for block in group], col)
        return jnp.concatenate(
            [jnp.concatenate([part[:, :width] for part in parts], axis=1),
             jnp.concatenate([part[:, width:] for part in parts], axis=1)], axis=0
        )

    out_w = [assembled(near), assembled(far)]
    full_b_out = out_w[0][384:512]
    gain_rows = out_w[0][512:518].astype(f32)
    gain_one = jnp.sum(gain_rows[:3], axis=0, keepdims=True)
    gain_two = jnp.sum(gain_rows[3:], axis=0, keepdims=True)

    picks_group = lax.dynamic_slice_in_dim(adapter_pick, lax.axis_index("dp") * IMG_GRP, IMG_GRP)
    order = jnp.arange(IMG_GRP, dtype=jnp.int32)
    picks = jnp.take(picks_group, ((order // 2) ^ me) * 2 + order % 2)
    spot_picks = jnp.sum(
        jnp.where(block_spot(order // 2, row, col)[None, :] * 2 + order[None, :] % 2 == order[:, None], picks_group[None, :], 0), axis=1
    )
    token_list, tile_experts = routing(routes, row, col)
    wide_router = jnp.concatenate([w_router, w_router, jnp.zeros((D, 64), bf16)], axis=1)
    wide_b_router = jnp.concatenate([b_router, b_router, jnp.zeros((ADAPT, 64), bf16)], axis=1)
    slim_router = jnp.concatenate([w_router, jnp.zeros((D, 96), bf16)], axis=1)
    slim_b_router = jnp.concatenate([b_router, jnp.zeros((ADAPT, 96), bf16)], axis=1)

    x, token_list, tile_experts, wide_router, wide_b_router, slim_router, slim_b_router = lax.optimization_barrier(
        (x, token_list, tile_experts, wide_router, wide_b_router, slim_router, slim_b_router)
    )
    cot, unused = lax.optimization_barrier((cot, near[3]))
    two, resid, normed, qkv, mixed, probs, lows = attend_call(
        picks, place, blocks, b_qkv, a_out, out_w, x, gain_one, gain_two, full_b_out
    )
    cot_near = gather_col(cot, row)
    two_x, two_y = across_col(two, 1), across_col(two, 2)

    def table(spots, twos, cots):
        return table_call(
            jnp.stack([picks[8 * t + 2 * s + side] for t, s in spots for side in range(2)]),
            twos, cots, a_up, b_down, wide_router, a_router, wide_b_router,
        )

    cot_far = [across_row(block) for block in cot_near[:3]]
    tables = [table(TABLES[0], [two, across_row(two)], [cot, cot_far[0]])]
    two_x, two_y, tables[0] = lax.optimization_barrier((two_x, two_y, tables[0]))
    diag = across_chip(jnp.where(row == 0, two_x, two_y), 2, 1)
    tables.append(
        table(TABLES[1], [two_x, two_y, across_row(two_x), across_row(two_y)], [cot_near[1], cot_near[2], cot_far[1], cot_far[2]])
    )
    diag, cot_diag, *tables = lax.optimization_barrier((diag, cot_near[3], *tables))
    tables.append(table(TABLES[2], [diag, across_row(diag)], [cot_diag, across_row(cot_diag)]))
    *moved, part_b_up, part_a_down = moe_call(
        token_list, tile_experts, spot_picks, place, tables, TABLES, w_up, w_down, b_up, a_down
    )
    sums, grads = moved[:4], moved[4:]
    dp_parts = jnp.concatenate([part_b_up, part_a_down])
    grad_sent = added(grads[1], across_row(grads[3])).astype(bf16)
    grad_kept = added(grads[0], across_row(grads[2])).astype(bf16)
    grad_sent, dp_parts, *sums = lax.optimization_barrier((grad_sent, dp_parts, *sums))
    grad_got = across_chip(grad_sent, 1, 2)
    sum_kept, sum_sent = across_row(sums[2]), across_row(sums[3])
    sums = [
        added(near[at : at + BLK], far[at : at + BLK]).astype(bf16)
        for near, far in ((sums[0], sum_kept), (sums[1], sum_sent)) for at in (0, BLK)
    ]
    four_dp = lax.axis_size("dp") == 4
    dp_sums = scatter_dp(dp_parts) if four_dp else lax.psum(dp_parts, "dp")
    grad_got, dp_sums, *sums = lax.optimization_barrier((grad_got, dp_sums, *sums))
    grad_a, grad_b = last_exchange(grad_kept, grad_got)
    if four_dp:
        dp_sums = spread_dp(dp_sums)
    grad_a, grad_b, dp_sums, *sums = lax.optimization_barrier((grad_a, grad_b, dp_sums, *sums))
    sums = [sums[0], across_chip(sums[1], 2, 1), across_chip(sums[2], 1, 2), across_chip(sums[3], 3, 3)]
    resid_grad, mixed_grad, base, both_parts, part_a_out, part_b_out = out_back_call(
        picks, place, blocks[4], a_out, out_w, gain_two, full_b_out, two, resid, mixed, lows, cot, grad_a, grad_b,
        slim_router, a_router, slim_b_router, a_up, b_down,
    )
    grad_tokens, part_a_qkv, part_b_qkv = qkv_back_call(
        picks, place, blocks, b_qkv, x, gain_one, normed, qkv, probs, lows, resid_grad, mixed_grad
    )
    part_a_qkv, part_b_qkv, *sums = lax.optimization_barrier((part_a_qkv, part_b_qkv, *sums))
    col_parts = jnp.concatenate([part_a_qkv, part_b_out])
    row_parts = jnp.concatenate([part_b_qkv, part_a_out])
    theirs = across_row(part_share(col_parts, row_parts, both_parts, 1 - row))
    shared = added(part_share(col_parts, row_parts, both_parts, row), theirs).astype(bf16)
    found = exchange_col(shared, col)
    mine = added(*found).astype(bf16)
    mine, grad_tokens, base = lax.optimization_barrier((mine, grad_tokens, base))
    moves = to_features(grad_tokens, (base + added(*sums)).astype(bf16), col)
    mine = spread_dp(scatter_dp(mine)) if four_dp else lax.psum(mine, "dp")
    mine, moves[1] = lax.optimization_barrier((mine, moves[1]))
    got = [across_col(mine[384:], s) for s in range(1, 4)]
    far = across_row(jnp.concatenate([mine[:384], mine[768:]] + [one[384:] for one in got]))
    block_out, grad_tokens = merge_call(place, moves, tokens.shape[0])
    far, block_out, grad_tokens = lax.optimization_barrier((far, block_out, grad_tokens))
    return (block_out, grad_tokens, *finish_call(place, mine, got, far, dp_sums))


def solution(mesh):
    return jax.shard_map(
        on_device,
        mesh=mesh,
        in_specs=(
            P(("dp", "row"), "col"),
            P(("dp", "row"), "col"),
            P("dp", None),
            P(),
            P("col"),
            P("col"),
            P(None, "col", "row"),
            P("row", "col"),
            P(),
            P(None, None, ("row", "col")),
            P(None, ("row", "col"), None),
            P(None, "col", None),
            P(None, None, "row"),
            P("row", None),
            P(None, "col"),
            P(),
            P(),
            P(),
            P(None, ("row", "col")),
            P(("row", "col"), None),
            P(),
        ),
        out_specs=(
            P(("dp", "row"), "col"),
            P(("dp", "row"), "col"),
            P(None, "col", None),
            P(None, None, "row"),
            P("row", None),
            P(None, "col"),
            P(),
            P(),
            P(),
            P(None, ("row", "col")),
            P(("row", "col"), None),
            P(),
        ),
        check_vma=False,
    )
```

```python
import jax
import jax.numpy as jnp
from jax import lax
from jax.experimental import pallas as pl
from jax.experimental.pallas import tpu as pltpu
from jax.sharding import PartitionSpec as P

D = 768
EXPERTS = 32
SEQ = 197
SEQP = 208
RANK = 16
ADAPT = 128
IMG_GRP = 16
TOK = IMG_GRP * SEQP
BLK = 2 * SEQP
DUMMY = SEQ
TILE = 160
f32 = jnp.float32
bf16 = jnp.bfloat16


def max_tiles():
    return (2 * IMG_GRP * SEQ) // TILE + EXPERTS + 1


def dot(left, right):
    return jnp.dot(left, right, preferred_element_type=f32)


def dot_nt(left, right):
    return lax.dot_general(left, right, (((1,), (1,)), ((), ())), preferred_element_type=f32)


def dot_tn(left, right):
    return lax.dot_general(left, right, (((0,), (0,)), ((), ())), preferred_element_type=f32)


def lane_iota(shape):
    return lax.broadcasted_iota(jnp.int32, shape, len(shape) - 1)


def repeat_lanes(value):
    for shift in (16, 32, 64):
        value = value + pltpu.roll(value, shift, 1)
    return value


def table_kernel(n_blocks, picks_ref, *refs):
    x_blocks = refs[:n_blocks]
    c_blocks = refs[n_blocks : 2 * n_blocks]
    a_up, b_down, w_router, a_router, b_router, table_out, xin, cin, rows_x, rows_c, sem = refs[2 * n_blocks :]
    image = pl.program_id(0)
    lane = lane_iota((1, 128))

    @pl.when(image == 0)
    def start():
        copies = []
        for blocks, place in ((x_blocks, xin), (c_blocks, cin)):
            for b, block in enumerate(blocks):
                copies.append(pltpu.make_async_copy(block, place.at[pl.ds(b * BLK, BLK)], sem.at[len(copies)]))
        for copy in copies:
            copy.start()
        for copy in copies:
            copy.wait()

    row = pl.multiple_of(image * SEQP, 16)
    mask = (lane // RANK) == picks_ref[image]
    x = xin[pl.ds(row, SEQP), :]
    c = cin[pl.ds(row, SEQP), :]
    flat_x = rows_x.reshape(SEQP * 8, 128)
    flat_c = rows_c.reshape(SEQP * 8, 128)
    low_x = jnp.where(mask, dot(x, a_up[...]), 0.0)
    low_c = jnp.where(mask, dot_nt(c, b_down[...]), 0.0)
    low_r = jnp.where(mask, dot(x, a_router[...]), 0.0).astype(bf16)
    logits = dot(x, w_router[...]) + dot(low_r, b_router[...])
    logits = jnp.where(lane < 2 * EXPERTS, logits, -1e30)
    power = jnp.exp(logits - jnp.max(logits, axis=1, keepdims=True))
    total = jnp.sum(jnp.where(lane < EXPERTS, power, 0.0), axis=1, keepdims=True)
    probs = power / total
    lead = probs.astype(bf16).astype(f32)
    probs = jnp.where(lane < EXPERTS, lead, probs - lead)
    for j in range(6):
        flat_x[pl.ds(j, SEQP, 8), :] = x[:, 128 * j : 128 * j + 128].astype(f32)
        flat_c[pl.ds(j, SEQP, 8), :] = c[:, 128 * j : 128 * j + 128].astype(f32)
    flat_x[pl.ds(6, SEQP, 8), :] = low_x
    flat_x[pl.ds(7, SEQP, 8), :] = probs
    flat_c[pl.ds(6, SEQP, 8), :] = low_c
    flat_c[pl.ds(7, SEQP, 8), :] = jnp.zeros((SEQP, 128), f32)
    table_out[...] = jnp.concatenate([rows_x[...], rows_c[...]], axis=1).astype(bf16)


def table_call(picks, x_blocks, c_blocks, a_up, b_down, w_router, a_router, b_router):
    n = len(x_blocks)

    def whole(*shape):
        return pl.BlockSpec(shape, lambda e, *_: (0,) * len(shape))

    anywhere = pl.BlockSpec(memory_space=pl.ANY)
    return pl.pallas_call(
        lambda *refs: table_kernel(n, *refs),
        grid_spec=pltpu.PrefetchScalarGridSpec(
            num_scalar_prefetch=1,
            grid=(2 * n,),
            in_specs=[anywhere] * (2 * n)
            + [whole(D, ADAPT), whole(ADAPT, D), whole(D, 128), whole(D, ADAPT), whole(ADAPT, 128)],
            out_specs=pl.BlockSpec((SEQP, 16, 128), lambda i, *_: (i, 0, 0)),
            scratch_shapes=[
                pltpu.VMEM((n * BLK, D), bf16),
                pltpu.VMEM((n * BLK, D), bf16),
                pltpu.VMEM((SEQP, 8, 128), f32),
                pltpu.VMEM((SEQP, 8, 128), f32),
                pltpu.SemaphoreType.DMA((2 * n,)),
            ],
        ),
        out_shape=jax.ShapeDtypeStruct((n * BLK, 16, 128), bf16),
        compiler_params=pltpu.CompilerParams(vmem_limit_bytes=32 * 1024 * 1024),
        cost_estimate=pl.CostEstimate(flops=n * 3_000_000_000, bytes_accessed=n * 3_000_000, transcendentals=n * 60_000),
    )(picks, *x_blocks, *c_blocks, a_up, b_down, w_router, a_router, b_router)


def moe_kernel(places, list_ref, expert_ref, picks_ref, place_ref, *refs):
    n = len(places)
    tables = refs[:n]
    ep_outs, tg_outs = refs[n + 4 : n + 8], refs[n + 8 : n + 12]
    refs = refs[: n + 4] + refs[n + 12 :]
    (
        w_up_hbm, w_down_hbm, b_up, a_down,
        gbu_bf, gad_bf,
        table, acc_e, acc_t, in_x, in_c, out_e, out_t, xb, cb, w_up, w_down, stage_ep, stage_tg,
        gbu_out, gad_out, in_sem, up_sem, down_sem, ep_sem, tg_sem,
    ) = refs[n:]
    acc_e_flat = acc_e.reshape(TOK * 8, 128)
    acc_t_flat = acc_t.reshape(TOK * 8, 128)
    in_x_flat = in_x.reshape(TILE * 8, 128)
    in_c_flat = in_c.reshape(TILE * 8, 128)
    out_e_flat = out_e.reshape(TILE * 8, 128)
    out_t_flat = out_t.reshape(TILE * 8, 128)
    lane = lane_iota((1, 128))
    n_tiles = expert_ref[max_tiles()]

    copies = []
    for piece, spots in zip(tables, places):
        for b, (t, s) in enumerate(spots):
            spot = 4 * t + jnp.where(place_ref[0] == t, swapped(s), s)
            copies.append(
                pltpu.make_async_copy(
                    piece.at[pl.ds(b * BLK, BLK)], table.at[pl.ds(pl.multiple_of(spot * BLK, 32), BLK)], in_sem.at[len(copies)]
                )
            )
    for copy in copies:
        copy.start()

    def weights(expert):
        slot = expert % 2
        return (
            pltpu.make_async_copy(w_up_hbm.at[expert], w_up.at[slot], up_sem.at[slot]),
            pltpu.make_async_copy(w_down_hbm.at[expert], w_down.at[slot], down_sem.at[slot]),
        )

    for copy in weights(0):
        copy.start()
    out_e[...] = jnp.zeros_like(out_e)
    out_t[...] = jnp.zeros_like(out_t)
    gbu_out[...] = jnp.zeros_like(gbu_out)
    gad_out[...] = jnp.zeros_like(gad_out)

    def clear(i, carry):
        acc_e[pl.ds(i * 64, 64)] = jnp.zeros((64, 8, 128), f32)
        acc_t[pl.ds(i * 64, 64)] = jnp.zeros((64, 8, 128), f32)
        return carry

    lax.fori_loop(0, TOK // 64, clear, 0)
    for copy in copies:
        copy.wait()

    def fetch(t):
        for i in range(TILE):
            both = table[list_ref[t * TILE + i]].astype(f32)
            in_x[i] = both[:8]
            in_c[i] = both[8:]

    def give(t):
        for b in range(TILE // 8):
            tokens = [list_ref[t * TILE + 8 * b + k] for k in range(8)]
            sums_e = [acc_e[tokens[k]] + out_e[8 * b + k] for k in range(8)]
            sums_t = [acc_t[tokens[k]] + out_t[8 * b + k] for k in range(8)]
            for k in range(8):
                acc_e[tokens[k]] = sums_e[k]
                acc_t[tokens[k]] = sums_t[k]

    fetch(0)

    def tile(t, carry):
        expert = expert_ref[t]
        slot = expert % 2

        @pl.when((t == 0) | (expert_ref[jnp.maximum(t - 1, 0)] != expert))
        def arrive():
            for copy in weights(expert):
                copy.wait()

            @pl.when(expert + 1 < EXPERTS)
            def ahead():
                for copy in weights(expert + 1):
                    copy.start()

        for j in range(7):
            xb[:, 128 * j : 128 * j + 128] = in_x_flat[pl.ds(j, TILE, 8), :].astype(bf16)
            cb[:, 128 * j : 128 * j + 128] = in_c_flat[pl.ds(j, TILE, 8), :].astype(bf16)
        spread = in_x_flat[pl.ds(7, TILE, 8), :]
        mine = (lane == expert) | (lane == expert + EXPERTS)
        gate = jnp.sum(jnp.where(mine, spread, 0.0), axis=1, keepdims=True)
        fetch(t + 1)
        give(jnp.maximum(t - 1, 0))
        hidden = dot(xb[:, :D], w_up[slot]) + dot(xb[:, D:], b_up[...])
        back = dot_nt(cb[:, :D], w_down[slot]) + dot_nt(cb[:, D:], a_down[...])
        cdf = 0.5 + 0.5 * lax.erf(hidden * 0.7071067811865476)
        slope = cdf + hidden * jnp.exp(hidden * hidden * -0.5) * 0.3989422804014327
        act = (hidden * cdf).astype(bf16)
        act_f = act.astype(f32)
        gate_grad = jnp.sum(act_f * back, axis=1, keepdims=True)
        grad_hidden = (gate * back * slope).astype(bf16)
        act_gate = (gate * act_f).astype(bf16)
        out_main = dot(act_gate, w_down[slot])
        out_low = dot(act_gate, a_down[...])
        in_main = dot_nt(grad_hidden, w_up[slot])
        in_low = dot_nt(grad_hidden, b_up[...])
        gbu_out[...] += dot_tn(grad_hidden, xb[:, D:])
        gad_out[...] += dot_tn(act_gate, cb[:, D:])
        for j in range(6):
            out_e_flat[pl.ds(j, TILE, 8), :] = out_main[:, 128 * j : 128 * j + 128]
            out_t_flat[pl.ds(j, TILE, 8), :] = in_main[:, 128 * j : 128 * j + 128]
        out_e_flat[pl.ds(6, TILE, 8), :] = out_low
        out_t_flat[pl.ds(6, TILE, 8), :] = in_low
        out_t_flat[pl.ds(7, TILE, 8), :] = jnp.where(lane == expert, gate_grad, 0.0)
        return carry

    lax.fori_loop(0, n_tiles, tile, 0)
    give(n_tiles - 1)

    gbu_bf[...] = gbu_out[...].astype(bf16)
    gad_bf[...] = gad_out[...].astype(bf16)
    some = IMG_GRP // 4
    for side, (ep_out, tg_out) in enumerate(zip(ep_outs, tg_outs)):

        def image(i, carry):
            slot = i % 2
            base = pl.multiple_of((i + side * some) * SEQP, 16) * 8
            mask = (lane // RANK) == picks_ref[i + side * some]
            rows = pl.ds(pl.multiple_of(i * SEQP, 16), SEQP)
            put_tg = pltpu.make_async_copy(stage_tg.at[slot], tg_out.at[rows], tg_sem.at[slot])
            put_ep = pltpu.make_async_copy(stage_ep.at[slot], ep_out.at[rows], ep_sem.at[slot])

            @pl.when(i >= 2)
            def drain():
                put_tg.wait()
                put_ep.wait()

            def chunk(j):
                flat = acc_e_flat if j < 8 else acc_t_flat
                return flat[pl.ds(base + j % 8, SEQP, 8), :]

            for j in range(6):
                at = slice(128 * j, 128 * j + 128)
                stage_tg[slot, :, at] = chunk(8 + j).astype(bf16)
                stage_ep[slot, :, at] = chunk(j).astype(bf16)
            low_in = repeat_lanes(jnp.where(mask, chunk(14), 0.0))
            low_out = repeat_lanes(jnp.where(mask, chunk(6), 0.0))
            last = jnp.where(lane < 48, low_in, jnp.where(lane < 64, low_out, 0.0))
            stage_tg[slot, :, D:] = jnp.where(lane < 32, chunk(15), last).astype(bf16)
            put_tg.start()
            put_ep.start()
            return carry

        lax.fori_loop(0, some, image, 0)
        for i in range(some - 2, some):
            rows = pl.ds(i * SEQP, SEQP)
            pltpu.make_async_copy(stage_tg.at[i % 2], tg_out.at[rows], tg_sem.at[i % 2]).wait()
            pltpu.make_async_copy(stage_ep.at[i % 2], ep_out.at[rows], ep_sem.at[i % 2]).wait()


def moe_call(token_list, tile_experts, picks, place, tables, places, w_up, w_down, b_up, a_down):
    half = w_up.shape[2]
    n = len(tables)
    n_copies = sum(len(spots) for spots in places)
    anywhere = pl.BlockSpec(memory_space=pl.ANY)
    inside = pl.BlockSpec(memory_space=pltpu.VMEM)
    return pl.pallas_call(
        lambda *refs: moe_kernel(places, *refs),
        grid_spec=pltpu.PrefetchScalarGridSpec(
            num_scalar_prefetch=4,
            grid=(1,),
            in_specs=[anywhere] * (n + 2) + [inside, inside],
            out_specs=[anywhere] * 8 + [inside, inside],
            scratch_shapes=[
                pltpu.VMEM((TOK, 16, 128), bf16),
                pltpu.VMEM((TOK, 8, 128), f32),
                pltpu.VMEM((TOK, 8, 128), f32),
                pltpu.VMEM((TILE, 8, 128), f32),
                pltpu.VMEM((TILE, 8, 128), f32),
                pltpu.VMEM((TILE, 8, 128), f32),
                pltpu.VMEM((TILE, 8, 128), f32),
                pltpu.VMEM((TILE, D + 128), bf16),
                pltpu.VMEM((TILE, D + 128), bf16),
                pltpu.VMEM((2, D, half), bf16),
                pltpu.VMEM((2, half, D), bf16),
                pltpu.VMEM((2, SEQP, D), bf16),
                pltpu.VMEM((2, SEQP, D + 128), bf16),
                pltpu.VMEM((half, ADAPT), f32),
                pltpu.VMEM((half, ADAPT), f32),
                pltpu.SemaphoreType.DMA((n_copies,)),
                pltpu.SemaphoreType.DMA((2,)),
                pltpu.SemaphoreType.DMA((2,)),
                pltpu.SemaphoreType.DMA((2,)),
                pltpu.SemaphoreType.DMA((2,)),
            ],
        ),
        out_shape=[
            *[jax.ShapeDtypeStruct((TOK // 4, D), bf16)] * 4,
            *[jax.ShapeDtypeStruct((TOK // 4, D + 128), bf16)] * 4,
            jax.ShapeDtypeStruct((half, ADAPT), bf16),
            jax.ShapeDtypeStruct((half, ADAPT), bf16),
        ],
        compiler_params=pltpu.CompilerParams(vmem_limit_bytes=58 * 1024 * 1024),
        cost_estimate=pl.CostEstimate(flops=20_000_000_000, bytes_accessed=60_000_000, transcendentals=10_000_000),
    )(token_list, tile_experts, picks, place, *tables, w_up, w_down, b_up, a_down)


def swapped(s):
    return ((s & 1) << 1) | (s >> 1)


def block_spot(block, row, col):
    from_row = block // 4
    s = (block % 4) ^ col
    return 4 * (from_row ^ row) + jnp.where(from_row == 0, swapped(s), s)


def routing(routes, row, col):
    token = jnp.arange(25 * 128, dtype=jnp.int32)[None, :]
    image = token // SEQ
    spot = block_spot(image // 2, row, col) * BLK + (image % 2) * SEQP + token % SEQ
    real = token < IMG_GRP * SEQ
    picked = jnp.pad(routes.T, ((0, 0), (0, 25 * 128 - IMG_GRP * SEQ)), constant_values=EXPERTS)
    beyond = EXPERTS * 4096 + DUMMY
    keys = jnp.where(real, picked * 4096 + spot, beyond).reshape(-1)
    experts = jnp.arange(EXPERTS, dtype=jnp.int32)
    count = jnp.sum((picked[None] == experts[:, None, None]).astype(jnp.int32), axis=(1, 2))
    tiles = (jnp.maximum(count, 1) + TILE - 1) // TILE
    extra = tiles * TILE - count
    filler = jnp.where(
        jnp.arange(256, dtype=jnp.int32)[None, :] < extra[:, None], (experts * 4096)[:, None] + DUMMY, beyond
    ).reshape(-1)
    ordered = lax.sort(jnp.concatenate([keys, filler])) & 4095
    ends = jnp.sum(jnp.where(experts[None, :] <= experts[:, None], tiles[None, :], 0), axis=1)
    steps = jnp.arange(max_tiles(), dtype=jnp.int32)
    owner = jnp.minimum(jnp.sum((ends[None, :] <= steps[:, None]).astype(jnp.int32), axis=1), EXPERTS - 1)
    return ordered, jnp.concatenate([owner, jnp.sum(tiles)[None]])


HEADS = 12
HEAD_DIM = 64


def pick_mask(pick):
    return (lane_iota((1, ADAPT)) // RANK) == pick


def norm_stats(values):
    centre = jnp.sum(values, axis=1, keepdims=True) * (1.0 / D)
    shifted = values - centre
    spread = jnp.sum(shifted * shifted, axis=1, keepdims=True) * (1.0 / D)
    inverse = lax.rsqrt(spread + 1e-06)
    return shifted * inverse, inverse


def norm_back(grad, gain, unit, inverse):
    scaled = grad * gain
    total = jnp.sum(scaled, axis=1, keepdims=True) * (1.0 / D)
    along = jnp.sum(scaled * unit, axis=1, keepdims=True) * (1.0 / D)
    return inverse * (scaled - total - unit * along)


def qkv_copies(place_ref, blocks, own_b, scratch, sem):
    w_qkv, a_qkv, b_qkv = scratch
    row, col = place_ref[0], place_ref[1]
    copies = []

    def copy(source, target):
        copies.append(pltpu.make_async_copy(source, target, sem.at[len(copies)]))

    for t in range(2):
        half_at = pl.multiple_of((row ^ t) * 384, 128)
        for s in range(4):
            block = blocks[4 * t + s]
            at = pl.multiple_of((col ^ s) * 192, 64)
            low_at = pl.multiple_of((col ^ s) * 192 + (row ^ t) * 96, 32)
            for p in range(3):
                copy(block.at[pl.ds(192 * p, 192)], w_qkv.at[p, pl.ds(at, 192), pl.ds(half_at, 384)])
                copy(block.at[pl.ds(576, 96), pl.ds(128 * p, 128)], a_qkv.at[p, pl.ds(low_at, 96), :])
        for p in range(3):
            source = own_b.at[p] if t == 0 else blocks[4].at[pl.ds(W_ROWS + 128 * p, 128)]
            copy(source, b_qkv.at[p, :, pl.ds(half_at, 384)])
    return copies


def out_copies(place_ref, far_block, own_a, out_w, scratch, sem):
    w_out, a_out = scratch
    row = place_ref[0]
    copies = []

    def copy(source, target):
        copies.append(pltpu.make_async_copy(source, target, sem.at[len(copies)]))

    for t in range(2):
        half_at = pl.multiple_of((row ^ t) * 384, 128)
        copy(out_w[t].at[pl.ds(0, 384)], w_out.at[pl.ds(half_at, 384), :])
        for j in range(3):
            if t == 0:
                source = own_a.at[pl.ds(128 * j, 128)]
            else:
                source = far_block.at[pl.ds(W_ROWS + 384, 128), pl.ds(128 * j, 128)]
            copy(source, a_out.at[pl.ds(half_at + 128 * j, 128), :])
    return copies


W_ROWS = 944
QKV_SCRATCH = [
    pltpu.VMEM((3, D, D), bf16),
    pltpu.VMEM((3, D, ADAPT), bf16),
    pltpu.VMEM((3, ADAPT, D), bf16),
    pltpu.SemaphoreType.DMA((54,)),
]
OUT_SCRATCH = [
    pltpu.VMEM((D, D), bf16),
    pltpu.VMEM((D, ADAPT), bf16),
    pltpu.SemaphoreType.DMA((8,)),
]


def split_kernel(place_ref, tokens_ref, cot_ref, own_out, one_out, two_out, three_out, left, right, stage, sem):
    rows = tokens_ref.shape[0]
    width = D // 4
    left[0:rows, 0:width] = tokens_ref[...].astype(f32)
    right[0:rows, 0:width] = cot_ref[...].astype(f32)
    lane = lane_iota((1, 128))
    real = lax.broadcasted_iota(jnp.int32, (SEQP, 1), 0) < SEQ
    for i in range(8):
        at = slice(SEQ * i, SEQ * i + SEQP)
        spot = slice(SEQP * (i % 2), SEQP * (i % 2) + SEQP)
        moved = pltpu.roll(right[at, :], 64, 1)
        middle = jnp.where(lane < 64, left[at, 128:256], moved[:, 0:128])
        stage[i // 2, spot, 0:128] = jnp.where(real, left[at, 0:128], 0.0).astype(bf16)
        stage[i // 2, spot, 128:256] = jnp.where(real, middle, 0.0).astype(bf16)
        stage[i // 2, spot, 256:384] = jnp.where(real, moved[:, 128:256], 0.0).astype(bf16)
    copies = [
        pltpu.make_async_copy(stage.at[place_ref[1] ^ s], out, sem.at[s])
        for s, out in enumerate((own_out, one_out, two_out, three_out))
    ]
    for copy in copies:
        copy.start()
    for copy in copies:
        copy.wait()


def split_call(place, tokens, cotangent):
    rows = tokens.shape[0]
    tall = -(-(SEQ * 7 + SEQP) // 8) * 8
    inside = pl.BlockSpec(memory_space=pltpu.VMEM)
    return pl.pallas_call(
        split_kernel,
        grid_spec=pltpu.PrefetchScalarGridSpec(
            num_scalar_prefetch=1,
            grid=(1,),
            in_specs=[inside, inside],
            out_specs=[ANYWHERE] * 4,
            scratch_shapes=[
                pltpu.VMEM((tall, 256), f32),
                pltpu.VMEM((tall, 256), f32),
                pltpu.VMEM((4, BLK, 384), bf16),
                pltpu.SemaphoreType.DMA((4,)),
            ],
        ),
        out_shape=[jax.ShapeDtypeStruct((BLK, 384), bf16)] * 4,
        compiler_params=pltpu.CompilerParams(vmem_limit_bytes=32 * 1024 * 1024),
        cost_estimate=pl.CostEstimate(flops=1_000_000_000, bytes_accessed=3_000_000, transcendentals=0),
    )(place, tokens, cotangent)


def finish_kernel(place_ref, mine, one, two, three, far, dp_sums, *refs):
    (
        a_qkv, b_qkv, a_out, b_out, a_router, b_router, a_up, b_up, a_down, b_down, wide, tall, every,
    ) = refs
    row, col = place_ref[0], place_ref[1]
    near_at = pl.multiple_of(row * 96, 32)
    far_at = pl.multiple_of((1 - row) * 96, 32)
    for p in range(4):
        ours = mine[96 * p : 96 * p + 96, :].astype(f32)
        theirs = far[96 * p : 96 * p + 96, :].astype(f32)
        if p < 3:
            a_qkv[p, pl.ds(near_at, 96), :] = ours
            a_qkv[p, pl.ds(far_at, 96), :] = theirs
        else:
            wide[pl.ds(near_at, 96), :] = ours
            wide[pl.ds(far_at, 96), :] = theirs
    b_out[...] = wide[...].T[:, : D // 4]
    share = BOTH_ROWS // 8
    for s, got in enumerate((mine, one, two, three)):
        base = 384 if s == 0 else 0
        at = pl.multiple_of((col ^ s) * 96, 32)
        for p in range(4):
            piece = got[base + 96 * p : base + 96 * p + 96, :].astype(f32)
            if p < 3:
                tall[p, pl.ds(at, 96), :] = piece
            else:
                a_out[pl.ds(at, 96), :] = piece
        ours = got[base + 384 : base + 384 + share, :].astype(f32)
        theirs = far[384 + share * s : 384 + share * s + share, :].astype(f32)
        every[pl.ds(pl.multiple_of((row * 4 + (col ^ s)) * share, 64), share), :] = ours
        every[pl.ds(pl.multiple_of(((1 - row) * 4 + (col ^ s)) * share, 64), share), :] = theirs
    for p in range(3):
        b_qkv[p] = tall[p].T
    a_router[...] = every[0:768, :]
    a_up[...] = every[768:1536, :]
    b_down[...] = every[1536:2304, :].T
    b_router[...] = every[2304:2432, :].T[:, :EXPERTS]
    b_up[...] = dp_sums[0:384, :].astype(f32).T
    a_down[...] = dp_sums[384:768, :].astype(f32)


def finish_call(place, mine, got, far, dp_sums):
    inside = pl.BlockSpec(memory_space=pltpu.VMEM)
    half = D // 2
    shapes = [
        (3, D // 4, ADAPT), (3, ADAPT, half), (half, ADAPT), (ADAPT, D // 4), (D, ADAPT), (ADAPT, EXPERTS),
        (D, ADAPT), (ADAPT, half), (half, ADAPT), (ADAPT, D),
    ]
    return pl.pallas_call(
        finish_kernel,
        grid_spec=pltpu.PrefetchScalarGridSpec(
            num_scalar_prefetch=1,
            grid=(1,),
            in_specs=[inside] * 6,
            out_specs=[inside] * 10,
            scratch_shapes=[
                pltpu.VMEM((256, 128), f32),
                pltpu.VMEM((3, half, 128), f32),
                pltpu.VMEM((BOTH_ROWS, 128), f32),
            ],
        ),
        out_shape=[jax.ShapeDtypeStruct(shape, f32) for shape in shapes],
        compiler_params=pltpu.CompilerParams(vmem_limit_bytes=32 * 1024 * 1024),
        cost_estimate=pl.CostEstimate(flops=1_000_000_000, bytes_accessed=4_000_000, transcendentals=0),
    )(place, mine, *got, far, dp_sums)


def merge_kernel(place_ref, *refs):
    blocks, refs = refs[:4], refs[4:]
    block_out, tokens_out, stage, tall, sem = refs
    copies = [
        pltpu.make_async_copy(block, stage.at[place_ref[1] ^ s], sem.at[s]) for s, block in enumerate(blocks)
    ]
    for copy in copies:
        copy.start()
    for copy in copies:
        copy.wait()
    width = D // 4
    rows = tokens_out.shape[0]
    for i in range(8):
        at = slice(SEQ * i, SEQ * i + SEQ)
        both = stage[i // 2, SEQP * (i % 2) : SEQP * (i % 2) + SEQP, :].astype(f32)[:SEQ]
        tokens_out[at, :] = both[:, :width]
        tall[at, :] = both[:, width:]
    block_out[...] = tall[0:rows, :].astype(bf16)


def merge_call(place, blocks, rows):
    width = D // 4
    inside = pl.BlockSpec(memory_space=pltpu.VMEM)
    return pl.pallas_call(
        merge_kernel,
        grid_spec=pltpu.PrefetchScalarGridSpec(
            num_scalar_prefetch=1,
            grid=(1,),
            in_specs=[ANYWHERE] * 4,
            out_specs=[inside, inside],
            scratch_shapes=[
                pltpu.VMEM((4, BLK, 2 * width), bf16),
                pltpu.VMEM((rows, width), f32),
                pltpu.SemaphoreType.DMA((4,)),
            ],
        ),
        out_shape=[jax.ShapeDtypeStruct((rows, width), bf16), jax.ShapeDtypeStruct((rows, width), f32)],
        compiler_params=pltpu.CompilerParams(vmem_limit_bytes=32 * 1024 * 1024),
        cost_estimate=pl.CostEstimate(flops=8_000_000_000, bytes_accessed=3_000_000, transcendentals=0),
    )(place, *blocks)


def place_weights(place_ref, blocks, own_b, own_a, out_w, w_qkv, a_qkv, b_qkv, w_out, a_out):
    row, col = place_ref[0], place_ref[1]
    for t in range(2):
        half_at = pl.multiple_of((row ^ t) * 384, 128)
        across = pl.ds(half_at, 384)
        for s in range(4):
            block = blocks[4 * t + s]
            at = pl.multiple_of((col ^ s) * 192, 64)
            low_at = pl.multiple_of((col ^ s) * 192 + (row ^ t) * 96, 32)
            for p in range(3):
                w_qkv[p, pl.ds(at, 192), across] = block[192 * p : 192 * p + 192, :]
                a_qkv[p, pl.ds(low_at, 96), :] = block[576:672, 128 * p : 128 * p + 128]
        w_out[across, :] = out_w[t][0:384, :]
        for p in range(3):
            down = pl.ds(pl.multiple_of(half_at + 128 * p, 128), 128)
            if t == 0:
                b_qkv[p, :, across] = own_b[p]
                a_out[down, :] = own_a[128 * p : 128 * p + 128, :]
            else:
                b_qkv[p, :, across] = blocks[4][W_ROWS + 128 * p : W_ROWS + 128 * p + 128, :]
                a_out[down, :] = blocks[4][W_ROWS + 384 : W_ROWS + 512, 128 * p : 128 * p + 128]


def two_masks(picks_ref):
    row = lax.broadcasted_iota(jnp.int32, (BLK, 1), 0)
    pick = jnp.where(row < SEQP, picks_ref[0], picks_ref[1])
    return (lane_iota((1, ADAPT)) // RANK) == pick, (row < SEQ) | ((row >= SEQP) & (row < SEQP + SEQ))


def both_heads(value):
    lane = lane_iota((1, 128))
    nothing = jnp.zeros_like(value)
    return jnp.concatenate(
        [jnp.where(lane < HEAD_DIM, value, nothing), jnp.where(lane < HEAD_DIM, nothing, value)], axis=0
    )


def attend_kernel(picks_ref, place_ref, *refs):
    blocks, refs = refs[:8], refs[8:]
    (
        own_b, own_a, out_near, out_far, x_ref, gain_one, gain_two, b_out,
        two_out, resid_out, normed_out, qkv_out, mixed_out, probs_out, lows_out,
        w_qkv, a_qkv, b_qkv, w_out, a_out,
    ) = refs
    place_weights(place_ref, blocks, own_b, own_a, (out_near, out_far), w_qkv, a_qkv, b_qkv, w_out, a_out)
    mask, real = two_masks(picks_ref)
    x = x_ref[...].astype(f32)
    unit, unused = norm_stats(x)
    normed = (unit * gain_one[...]).astype(bf16)
    normed_out[...] = normed
    for p in range(3):
        low = jnp.where(mask, dot(normed, a_qkv[p]), 0.0).astype(bf16)
        lows_out[:, 128 * p : 128 * p + 128] = low
        qkv_out[p] = (dot(normed, w_qkv[p]) + dot(low, b_qkv[p])).astype(bf16)
    lane = lane_iota((1, 128))
    key_lane = lane_iota((1, SEQP))
    for pair in range(HEADS // 2):
        at = slice(128 * pair, 128 * pair + 128)
        for image in range(2):
            rows = slice(SEQP * image, SEQP * image + SEQP)
            scores = dot_nt(both_heads(qkv_out[0, rows, at]), qkv_out[1, rows, at]) * (HEAD_DIM**-0.5)
            scores = jnp.where(key_lane < SEQ, scores, -1e30)
            power = jnp.exp(scores - jnp.max(scores, axis=1, keepdims=True))
            probs = (power / jnp.sum(power, axis=1, keepdims=True)).astype(bf16)
            probs_out[image, pair] = probs
            found = dot(probs, qkv_out[2, rows, at])
            mixed_out[rows, at] = jnp.where(lane < HEAD_DIM, found[:SEQP], found[SEQP:]).astype(bf16)
    mixed = mixed_out[...]
    low = jnp.where(mask, dot(mixed, a_out[...]), 0.0).astype(bf16)
    lows_out[:, 384:512] = low
    resid = x + dot(mixed, w_out[...]) + dot(low, b_out[...])
    resid_out[...] = resid
    unit, unused = norm_stats(resid)
    two_out[...] = jnp.where(real, unit * gain_two[...], 0.0).astype(bf16)


INSIDE = pl.BlockSpec(memory_space=pltpu.VMEM)


ANYWHERE = pl.BlockSpec(memory_space=pl.ANY)


def attend_call(picks, place, blocks, own_b, own_a, out_w, x, gain_one, gain_two, b_out):
    rows = x.shape[0]
    return pl.pallas_call(
        attend_kernel,
        grid_spec=pltpu.PrefetchScalarGridSpec(
            num_scalar_prefetch=2,
            grid=(1,),
            in_specs=[INSIDE] * (len(blocks) + 8),
            out_specs=[INSIDE] * 7,
            scratch_shapes=QKV_SCRATCH[:-1] + OUT_SCRATCH[:-1],
        ),
        out_shape=[
            jax.ShapeDtypeStruct((rows, D), bf16),
            jax.ShapeDtypeStruct((rows, D), f32),
            jax.ShapeDtypeStruct((rows, D), bf16),
            jax.ShapeDtypeStruct((3, rows, D), bf16),
            jax.ShapeDtypeStruct((rows, D), bf16),
            jax.ShapeDtypeStruct((2, HEADS // 2, BLK, SEQP), bf16),
            jax.ShapeDtypeStruct((rows, 512), bf16),
        ],
        compiler_params=pltpu.CompilerParams(vmem_limit_bytes=48 * 1024 * 1024),
        cost_estimate=pl.CostEstimate(flops=4_000_000_000, bytes_accessed=15_000_000, transcendentals=2_000_000),
    )(picks, place, *blocks, own_b, own_a, *out_w, x, gain_one, gain_two, b_out)


def put_rows(part, p, value):
    value = value.astype(bf16)
    for r in range(2):
        for c in range(4):
            part[r, c, 96 * p : 96 * p + 96, :] = value[384 * r + 96 * c : 384 * r + 96 * c + 96, :]


def put_cols(part, p, value):
    value = value.astype(bf16)
    for r in range(2):
        for c in range(4):
            part[r, c, 96 * p : 96 * p + 96, :] = value[192 * c + 96 * r : 192 * c + 96 * r + 96, :]


def out_back_kernel(picks_ref, place_ref, *refs):
    (
        far_block, own_a, out_near, out_far, gain_two, b_out, two_ref, resid_ref, mixed_ref, lows_ref,
        cot_ref, grad_a, grad_b, w_router, a_router, b_router, a_up, b_down,
        resid_grad_out, mixed_grad_out, base_out, both_out, a_part_out, b_part_out,
        w_out, a_out, sem,
    ) = refs
    copies = out_copies(place_ref, far_block, own_a, (out_near, out_far), (w_out, a_out), sem)
    for copy in copies:
        copy.start()
    mask, unused = two_masks(picks_ref)
    lane = lane_iota((1, 128))

    def add_part(row, value):
        both_out[row : row + value.shape[0], :] = value.astype(bf16)

    two = two_ref[...]
    received = grad_a[...].astype(f32) + grad_b[...].astype(f32)
    low_r = jnp.where(mask, dot(two, a_router[...]), 0.0).astype(bf16)
    logits = dot(two, w_router[...]) + dot(low_r, b_router[...])
    logits = jnp.where(lane < EXPERTS, logits, -1e30)
    power = jnp.exp(logits - jnp.max(logits, axis=1, keepdims=True))
    probs = power / jnp.sum(power, axis=1, keepdims=True)
    last = received[:, D:]
    grad_probs = jnp.where(lane < EXPERTS, last, 0.0)
    low_in = jnp.where(mask, repeat_lanes(jnp.where((lane >= 32) & (lane < 48), last, 0.0)), 0.0).astype(bf16)
    low_out = jnp.where(mask, repeat_lanes(jnp.where((lane >= 48) & (lane < 64), last, 0.0)), 0.0).astype(bf16)
    cot = cot_ref[...]
    resid = resid_ref[...]
    base_out[...] = resid + dot(low_out, b_down[...])
    add_part(768, dot_tn(two, low_in))
    add_part(1536, dot_tn(cot, low_out))
    grad_logits = probs * (grad_probs - jnp.sum(probs * grad_probs, axis=1, keepdims=True))
    grad_logits = grad_logits.astype(bf16)
    grad_low = jnp.where(mask, dot_nt(grad_logits, b_router[...]), 0.0).astype(bf16)
    grad_two = received[:, :D] + dot_nt(low_in, a_up[...])
    grad_two = grad_two + dot_nt(grad_logits, w_router[...]) + dot_nt(grad_low, a_router[...])
    add_part(0, dot_tn(two, grad_low))
    add_part(2304, dot_tn(grad_logits, low_r))
    unit, inverse = norm_stats(resid)
    grad_resid = cot.astype(f32) + norm_back(grad_two, gain_two[...], unit, inverse)
    resid_grad_out[...] = grad_resid
    grad_attn = grad_resid.astype(bf16)
    grad_low = jnp.where(mask, dot_nt(grad_attn, b_out[...]), 0.0).astype(bf16)
    for copy in copies:
        copy.wait()
    mixed_grad_out[...] = (dot_nt(grad_attn, w_out[...]) + dot_nt(grad_low, a_out[...])).astype(bf16)
    put_rows(a_part_out, 0, dot_tn(mixed_ref[...], grad_low))
    put_cols(b_part_out, 0, dot_tn(grad_attn, lows_ref[:, 384:512]))
    both_out[2432:BOTH_ROWS, :] = jnp.zeros((BOTH_ROWS - 2432, 128), bf16)


BOTH_ROWS = 2560


def out_back_call(picks, place, far_block, own_a, out_w, gain_two, b_out, two, resid, mixed, lows, cot, grad_a, grad_b,
                  w_router, a_router, b_router, a_up, b_down):
    rows = two.shape[0]
    return pl.pallas_call(
        out_back_kernel,
        grid_spec=pltpu.PrefetchScalarGridSpec(
            num_scalar_prefetch=2,
            grid=(1,),
            in_specs=[ANYWHERE] * 4 + [INSIDE] * 14,
            out_specs=[INSIDE] * 6,
            scratch_shapes=OUT_SCRATCH,
        ),
        out_shape=[
            jax.ShapeDtypeStruct((rows, D), f32),
            jax.ShapeDtypeStruct((rows, D), bf16),
            jax.ShapeDtypeStruct((rows, D), f32),
            jax.ShapeDtypeStruct((BOTH_ROWS, 128), bf16),
            jax.ShapeDtypeStruct((2, 4, 96, 128), bf16),
            jax.ShapeDtypeStruct((2, 4, 96, 128), bf16),
        ],
        compiler_params=pltpu.CompilerParams(vmem_limit_bytes=60 * 1024 * 1024),
        cost_estimate=pl.CostEstimate(flops=6_000_000_000, bytes_accessed=15_000_000, transcendentals=100_000),
    )(picks, place, far_block, own_a, *out_w, gain_two, b_out, two, resid, mixed, lows, cot, grad_a, grad_b,
      w_router, a_router, b_router, a_up, b_down)


def qkv_back_kernel(picks_ref, place_ref, *refs):
    blocks, refs = refs[:8], refs[8:]
    (
        own_b, x_hbm, gain_one, normed_hbm, qkv_ref, probs_ref, lows_hbm, resid_hbm, grad_mixed,
        tokens_out, a_part_out, b_part_out,
        w_qkv, a_qkv, b_qkv, sem, grads, x_ref, normed_ref, lows_ref, resid_grad, late_sem,
    ) = refs
    copies = qkv_copies(place_ref, blocks, own_b, (w_qkv, a_qkv, b_qkv), sem)
    late = ((x_hbm, x_ref), (normed_hbm, normed_ref), (lows_hbm, lows_ref), (resid_hbm, resid_grad))
    for k, (source, target) in enumerate(late):
        copies.append(pltpu.make_async_copy(source, target, late_sem.at[k]))
    for copy in copies:
        copy.start()
    mask, unused = two_masks(picks_ref)
    lane = lane_iota((1, 128))
    for pair in range(HEADS // 2):
        at = slice(128 * pair, 128 * pair + 128)
        for image in range(2):
            rows = slice(SEQP * image, SEQP * image + SEQP)
            grad_out = both_heads(grad_mixed[rows, at])
            weights = probs_ref[image, pair]
            weights_f = weights.astype(f32)
            grad_w = dot_nt(grad_out, qkv_ref[2, rows, at])
            inner = jnp.sum(weights_f * grad_w, axis=1, keepdims=True)
            grad_s = (weights_f * (grad_w - inner) * (HEAD_DIM**-0.5)).astype(bf16)
            found = dot(grad_s, qkv_ref[1, rows, at])
            grads[0, rows, at] = jnp.where(lane < HEAD_DIM, found[:SEQP], found[SEQP:]).astype(bf16)
            grads[1, rows, at] = dot_tn(grad_s, both_heads(qkv_ref[0, rows, at])).astype(bf16)
            grads[2, rows, at] = dot_tn(weights, grad_out).astype(bf16)
    for copy in copies:
        copy.wait()
    normed = normed_ref[...]
    grad_normed = jnp.zeros((BLK, D), f32)
    for p in range(3):
        piece = grads[p]
        grad_low = jnp.where(mask, dot_nt(piece, b_qkv[p]), 0.0).astype(bf16)
        grad_normed = grad_normed + dot_nt(piece, w_qkv[p]) + dot_nt(grad_low, a_qkv[p])
        put_cols(a_part_out, p, dot_tn(normed, grad_low))
        put_rows(b_part_out, p, dot_tn(piece, lows_ref[:, 128 * p : 128 * p + 128]))
    unit, inverse = norm_stats(x_ref[...].astype(f32))
    tokens_out[...] = (resid_grad[...] + norm_back(grad_normed, gain_one[...], unit, inverse)).astype(bf16)


def qkv_back_call(picks, place, blocks, own_b, x, gain_one, normed, qkv, probs, lows, resid_grad, grad_mixed):
    rows = x.shape[0]
    return pl.pallas_call(
        qkv_back_kernel,
        grid_spec=pltpu.PrefetchScalarGridSpec(
            num_scalar_prefetch=2,
            grid=(1,),
            in_specs=[ANYWHERE] * (len(blocks) + 2)
            + [INSIDE, ANYWHERE, INSIDE, INSIDE, ANYWHERE, ANYWHERE, INSIDE],
            out_specs=[INSIDE] * 3,
            scratch_shapes=QKV_SCRATCH
            + [
                pltpu.VMEM((3, BLK, D), bf16),
                pltpu.VMEM((BLK, D), bf16),
                pltpu.VMEM((BLK, D), bf16),
                pltpu.VMEM((BLK, 512), bf16),
                pltpu.VMEM((BLK, D), f32),
                pltpu.SemaphoreType.DMA((4,)),
            ],
        ),
        out_shape=[
            jax.ShapeDtypeStruct((rows, D), bf16),
            jax.ShapeDtypeStruct((2, 4, 288, 128), bf16),
            jax.ShapeDtypeStruct((2, 4, 288, 128), bf16),
        ],
        compiler_params=pltpu.CompilerParams(vmem_limit_bytes=60 * 1024 * 1024),
        cost_estimate=pl.CostEstimate(flops=9_000_000_000, bytes_accessed=15_000_000, transcendentals=1000),
    )(picks, place, *blocks, own_b, x, gain_one, normed, qkv, probs, lows, resid_grad, grad_mixed)


TABLES = (((0, 0), (1, 0)), ((0, 1), (0, 2), (1, 1), (1, 2)), ((0, 3), (1, 3)))


def across_row(value):
    return lax.ppermute(value, "row", [(0, 1), (1, 0)])


def across_col(value, step):
    return lax.ppermute(value, "col", [(i, i ^ step) for i in range(4)])


def by_place(blocks, col):
    found = []
    for place in range(4):
        value = blocks[place]
        for other in range(1, 4):
            value = jnp.where(col == other, blocks[place ^ other], value)
        found.append(value)
    return found


def across_chip(value, first, second):
    pairs = [(i, i ^ first) for i in range(4)] + [(4 + i, 4 + (i ^ second)) for i in range(4)]
    return lax.ppermute(value, ("row", "col"), pairs)


def gather_col(value, row):
    from_x = across_col(value, 1)
    from_y = across_col(value, 2)
    return [value, from_x, from_y, across_chip(jnp.where(row == 0, from_x, from_y), 2, 1)]


def added(*values):
    total = values[0].astype(f32)
    for value in values[1:]:
        total = total + value.astype(f32)
    return total


def last_exchange(kept_rows, got):
    sent = added(kept_rows[BLK:], got[BLK:]).astype(bf16)
    return added(kept_rows[:BLK], got[:BLK]).astype(bf16), across_chip(sent, 2, 1)


def at_place(value, axis, place):
    return lax.dynamic_index_in_dim(value, place, axis, keepdims=False)


def scatter_dp(value):
    place = lax.axis_index("dp")
    view = value.reshape(4, -1, 128)
    found = [at_place(view, 0, place)]
    for s in range(1, 4):
        found.append(across_dp(at_place(view, 0, place ^ s), s))
    return added(*found).astype(bf16)


def across_dp(value, step):
    return lax.ppermute(value, "dp", [(i, i ^ step) for i in range(4)])


def spread_dp(value):
    return jnp.concatenate(by_place([value] + [across_dp(value, s) for s in range(1, 4)], lax.axis_index("dp")))


def part_share(parts, place):
    return jnp.concatenate([at_place(part, 0, place) for part in parts], axis=1)


def exchange_col(value, col):
    return [at_place(value, 0, col)] + [across_col(at_place(value, 0, col ^ s), s) for s in range(1, 4)]


def to_features(first, second, col):
    width = D // 4
    pieces = []
    for p in range(4):
        at = slice(width * p, width * p + width)
        pieces.append(jnp.concatenate([first[:, at], second[:, at]], axis=1))
    sent = by_place(pieces, col)
    return [sent[0]] + [across_col(sent[s], s) for s in range(1, 4)]


def on_device(
    tokens, cotangent, routes, adapter_pick, gain_attn, gain_moe, w_qkv, w_out, w_router, w_up, w_down,
    a_qkv, b_qkv, a_out, b_out, a_router, b_router, a_up, b_up, a_down, b_down,
):
    row = lax.axis_index("row")
    col = lax.axis_index("col")
    me = row * 4 + col
    place = jnp.stack([row, col]).astype(jnp.int32)

    width = D // 4
    half = D // 2
    gains = []
    for gain in (gain_attn, gain_moe):
        left = gain
        for unused in range(3):
            lead = lax.reduce_precision(left, 8, 7)
            gains.append(lead.astype(bf16))
            left = left - lead
    small = jnp.concatenate([w_out, b_out, jnp.stack(gains), jnp.zeros((26, width), bf16)], axis=0)
    low = at_place(a_qkv.reshape(3, 2, 96, ADAPT), 1, row)
    packed = jnp.concatenate(
        [w_qkv.reshape(576, half), jnp.concatenate([low[0], low[1], low[2]], axis=1),
         jnp.concatenate([small[:272], small[272:]], axis=1)]
    )
    for_row = jnp.concatenate(
        [packed, b_qkv.reshape(half, half), jnp.concatenate([a_out[:128], a_out[128:256], a_out[256:]], axis=1)]
    )
    pairs = split_call(place, tokens, cotangent)
    from_x, from_y = across_col(packed, 1), across_col(packed, 2)
    chosen, *pairs = lax.optimization_barrier((jnp.where(row == 0, from_x, from_y), *pairs))
    near = [packed, from_x, from_y, across_chip(chosen, 2, 1)]
    pairs = by_place([pairs[0]] + [across_col(pairs[s], s) for s in range(1, 4)], col)
    x = jnp.concatenate([pair[:, :width] for pair in pairs], axis=1)
    cot = jnp.concatenate([pair[:, width:] for pair in pairs], axis=1)
    far = [across_row(for_row)] + [across_row(block) for block in near[1:]]
    blocks = near + far

    def assembled(group):
        parts = by_place([block[672:944] for block in group], col)
        return jnp.concatenate(
            [jnp.concatenate([part[:, :width] for part in parts], axis=1),
             jnp.concatenate([part[:, width:] for part in parts], axis=1)], axis=0
        )

    out_w = [assembled(near), assembled(far)]
    full_b_out = out_w[0][384:512]
    gain_rows = out_w[0][512:518].astype(f32)
    gain_one = jnp.sum(gain_rows[:3], axis=0, keepdims=True)
    gain_two = jnp.sum(gain_rows[3:], axis=0, keepdims=True)

    picks_group = lax.dynamic_slice_in_dim(adapter_pick, lax.axis_index("dp") * IMG_GRP, IMG_GRP)
    order = jnp.arange(IMG_GRP, dtype=jnp.int32)
    picks = jnp.take(picks_group, ((order // 2) ^ me) * 2 + order % 2)
    spot_picks = jnp.sum(
        jnp.where(block_spot(order // 2, row, col)[None, :] * 2 + order[None, :] % 2 == order[:, None], picks_group[None, :], 0), axis=1
    )
    token_list, tile_experts = routing(routes, row, col)
    wide_router = jnp.concatenate([w_router, w_router, jnp.zeros((D, 64), bf16)], axis=1)
    wide_b_router = jnp.concatenate([b_router, b_router, jnp.zeros((ADAPT, 64), bf16)], axis=1)
    slim_router = jnp.concatenate([w_router, jnp.zeros((D, 96), bf16)], axis=1)
    slim_b_router = jnp.concatenate([b_router, jnp.zeros((ADAPT, 96), bf16)], axis=1)

    x, token_list, tile_experts, wide_router, wide_b_router, slim_router, slim_b_router = lax.optimization_barrier(
        (x, token_list, tile_experts, wide_router, wide_b_router, slim_router, slim_b_router)
    )
    cot, unused = lax.optimization_barrier((cot, near[3]))
    two, resid, normed, qkv, mixed, probs, lows = attend_call(
        picks, place, blocks, b_qkv, a_out, out_w, x, gain_one, gain_two, full_b_out
    )
    cot_near = gather_col(cot, row)
    two_x, two_y = across_col(two, 1), across_col(two, 2)

    def table(spots, twos, cots):
        return table_call(
            jnp.stack([picks[8 * t + 2 * s + side] for t, s in spots for side in range(2)]),
            twos, cots, a_up, b_down, wide_router, a_router, wide_b_router,
        )

    cot_far = [across_row(block) for block in cot_near[:3]]
    tables = [table(TABLES[0], [two, across_row(two)], [cot, cot_far[0]])]
    two_x, two_y, tables[0] = lax.optimization_barrier((two_x, two_y, tables[0]))
    diag = across_chip(jnp.where(row == 0, two_x, two_y), 2, 1)
    tables.append(
        table(TABLES[1], [two_x, two_y, across_row(two_x), across_row(two_y)], [cot_near[1], cot_near[2], cot_far[1], cot_far[2]])
    )
    diag, cot_diag, *tables = lax.optimization_barrier((diag, cot_near[3], *tables))
    tables.append(table(TABLES[2], [diag, across_row(diag)], [cot_diag, across_row(cot_diag)]))
    *moved, part_b_up, part_a_down = moe_call(
        token_list, tile_experts, spot_picks, place, tables, TABLES, w_up, w_down, b_up, a_down
    )
    sums, grads = moved[:4], moved[4:]
    dp_parts = jnp.concatenate([part_b_up, part_a_down])
    grad_sent = added(grads[1], across_row(grads[3])).astype(bf16)
    grad_kept = added(grads[0], across_row(grads[2])).astype(bf16)
    grad_sent, dp_parts, *sums = lax.optimization_barrier((grad_sent, dp_parts, *sums))
    grad_got = across_chip(grad_sent, 1, 2)
    sum_kept, sum_sent = across_row(sums[2]), across_row(sums[3])
    sums = [
        added(near[at : at + BLK], far[at : at + BLK]).astype(bf16)
        for near, far in ((sums[0], sum_kept), (sums[1], sum_sent)) for at in (0, BLK)
    ]
    four_dp = lax.axis_size("dp") == 4
    dp_sums = scatter_dp(dp_parts) if four_dp else lax.psum(dp_parts, "dp")
    grad_got, dp_sums, *sums = lax.optimization_barrier((grad_got, dp_sums, *sums))
    grad_a, grad_b = last_exchange(grad_kept, grad_got)
    if four_dp:
        dp_sums = spread_dp(dp_sums)
    grad_a, grad_b, dp_sums, *sums = lax.optimization_barrier((grad_a, grad_b, dp_sums, *sums))
    sums = [sums[0], across_chip(sums[1], 2, 1), across_chip(sums[2], 1, 2), across_chip(sums[3], 3, 3)]
    resid_grad, mixed_grad, base, both_parts, part_a_out, part_b_out = out_back_call(
        picks, place, blocks[4], a_out, out_w, gain_two, full_b_out, two, resid, mixed, lows, cot, grad_a, grad_b,
        slim_router, a_router, slim_b_router, a_up, b_down,
    )
    grad_tokens, part_a_qkv, part_b_qkv = qkv_back_call(
        picks, place, blocks, b_qkv, x, gain_one, normed, qkv, probs, lows, resid_grad, mixed_grad
    )
    part_a_qkv, part_b_qkv, *sums = lax.optimization_barrier((part_a_qkv, part_b_qkv, *sums))
    parts = (part_a_qkv, part_b_out, part_b_qkv, part_a_out, both_parts.reshape(2, 4, BOTH_ROWS // 8, 128))
    theirs = across_row(part_share(parts, 1 - row))
    shared = added(part_share(parts, row), theirs).astype(bf16)
    found = exchange_col(shared, col)
    mine = added(*found).astype(bf16)
    mine, grad_tokens, base = lax.optimization_barrier((mine, grad_tokens, base))
    moves = to_features(grad_tokens, (base + added(*sums)).astype(bf16), col)
    mine = spread_dp(scatter_dp(mine)) if four_dp else lax.psum(mine, "dp")
    got = [across_col(mine[384:], s) for s in range(1, 4)]
    far = across_row(jnp.concatenate([mine[:384], mine[768:]] + [one[384:] for one in got]))
    block_out, grad_tokens = merge_call(place, moves, tokens.shape[0])
    far, block_out, grad_tokens = lax.optimization_barrier((far, block_out, grad_tokens))
    return (block_out, grad_tokens, *finish_call(place, mine, got, far, dp_sums))


def solution(mesh):
    return jax.shard_map(
        on_device,
        mesh=mesh,
        in_specs=(
            P(("dp", "row"), "col"),
            P(("dp", "row"), "col"),
            P("dp", None),
            P(),
            P("col"),
            P("col"),
            P(None, "col", "row"),
            P("row", "col"),
            P(),
            P(None, None, ("row", "col")),
            P(None, ("row", "col"), None),
            P(None, "col", None),
            P(None, None, "row"),
            P("row", None),
            P(None, "col"),
            P(),
            P(),
            P(),
            P(None, ("row", "col")),
            P(("row", "col"), None),
            P(),
        ),
        out_specs=(
            P(("dp", "row"), "col"),
            P(("dp", "row"), "col"),
            P(None, "col", None),
            P(None, None, "row"),
            P("row", None),
            P(None, "col"),
            P(),
            P(),
            P(),
            P(None, ("row", "col")),
            P(("row", "col"), None),
            P(),
        ),
        check_vma=False,
    )
```

```python
import jax
import jax.numpy as jnp
from jax import lax
from jax.experimental import pallas as pl
from jax.experimental.pallas import tpu as pltpu
from jax.sharding import PartitionSpec as P

D = 768
EXPERTS = 32
SEQ = 197
SEQP = 208
RANK = 16
ADAPT = 128
IMG_GRP = 16
TOK = IMG_GRP * SEQP
BLK = 2 * SEQP
DUMMY = SEQ
TILE = 160
f32 = jnp.float32
bf16 = jnp.bfloat16


def max_tiles():
    return (2 * IMG_GRP * SEQ) // TILE + EXPERTS + 1


def dot(left, right):
    return jnp.dot(left, right, preferred_element_type=f32)


def dot_nt(left, right):
    return lax.dot_general(left, right, (((1,), (1,)), ((), ())), preferred_element_type=f32)


def dot_tn(left, right):
    return lax.dot_general(left, right, (((0,), (0,)), ((), ())), preferred_element_type=f32)


def lane_iota(shape):
    return lax.broadcasted_iota(jnp.int32, shape, len(shape) - 1)


def repeat_lanes(value):
    for shift in (16, 32, 64):
        value = value + pltpu.roll(value, shift, 1)
    return value


def table_kernel(n_blocks, picks_ref, *refs):
    x_blocks = refs[:n_blocks]
    c_blocks = refs[n_blocks : 2 * n_blocks]
    a_up, b_down, w_router, a_router, b_router, table_out, xin, cin, rows_x, rows_c, sem = refs[2 * n_blocks :]
    image = pl.program_id(0)
    lane = lane_iota((1, 128))

    @pl.when(image == 0)
    def start():
        copies = []
        for blocks, place in ((x_blocks, xin), (c_blocks, cin)):
            for b, block in enumerate(blocks):
                copies.append(pltpu.make_async_copy(block, place.at[pl.ds(b * BLK, BLK)], sem.at[len(copies)]))
        for copy in copies:
            copy.start()
        for copy in copies:
            copy.wait()

    row = pl.multiple_of(image * SEQP, 16)
    mask = (lane // RANK) == picks_ref[image]
    x = xin[pl.ds(row, SEQP), :]
    c = cin[pl.ds(row, SEQP), :]
    flat_x = rows_x.reshape(SEQP * 8, 128)
    flat_c = rows_c.reshape(SEQP * 8, 128)
    low_x = jnp.where(mask, dot(x, a_up[...]), 0.0)
    low_c = jnp.where(mask, dot_nt(c, b_down[...]), 0.0)
    low_r = jnp.where(mask, dot(x, a_router[...]), 0.0).astype(bf16)
    logits = dot(x, w_router[...]) + dot(low_r, b_router[...])
    logits = jnp.where(lane < 2 * EXPERTS, logits, -1e30)
    power = jnp.exp(logits - jnp.max(logits, axis=1, keepdims=True))
    total = jnp.sum(jnp.where(lane < EXPERTS, power, 0.0), axis=1, keepdims=True)
    probs = power / total
    lead = probs.astype(bf16).astype(f32)
    probs = jnp.where(lane < EXPERTS, lead, probs - lead)
    for j in range(6):
        flat_x[pl.ds(j, SEQP, 8), :] = x[:, 128 * j : 128 * j + 128].astype(f32)
        flat_c[pl.ds(j, SEQP, 8), :] = c[:, 128 * j : 128 * j + 128].astype(f32)
    flat_x[pl.ds(6, SEQP, 8), :] = low_x
    flat_x[pl.ds(7, SEQP, 8), :] = probs
    flat_c[pl.ds(6, SEQP, 8), :] = low_c
    flat_c[pl.ds(7, SEQP, 8), :] = jnp.zeros((SEQP, 128), f32)
    table_out[...] = jnp.concatenate([rows_x[...], rows_c[...]], axis=1).astype(bf16)


def table_call(picks, x_blocks, c_blocks, a_up, b_down, w_router, a_router, b_router):
    n = len(x_blocks)

    def whole(*shape):
        return pl.BlockSpec(shape, lambda e, *_: (0,) * len(shape))

    anywhere = pl.BlockSpec(memory_space=pl.ANY)
    return pl.pallas_call(
        lambda *refs: table_kernel(n, *refs),
        grid_spec=pltpu.PrefetchScalarGridSpec(
            num_scalar_prefetch=1,
            grid=(2 * n,),
            in_specs=[anywhere] * (2 * n)
            + [whole(D, ADAPT), whole(ADAPT, D), whole(D, 128), whole(D, ADAPT), whole(ADAPT, 128)],
            out_specs=pl.BlockSpec((SEQP, 16, 128), lambda i, *_: (i, 0, 0)),
            scratch_shapes=[
                pltpu.VMEM((n * BLK, D), bf16),
                pltpu.VMEM((n * BLK, D), bf16),
                pltpu.VMEM((SEQP, 8, 128), f32),
                pltpu.VMEM((SEQP, 8, 128), f32),
                pltpu.SemaphoreType.DMA((2 * n,)),
            ],
        ),
        out_shape=jax.ShapeDtypeStruct((n * BLK, 16, 128), bf16),
        compiler_params=pltpu.CompilerParams(vmem_limit_bytes=32 * 1024 * 1024),
        cost_estimate=pl.CostEstimate(flops=n * 3_000_000_000, bytes_accessed=n * 3_000_000, transcendentals=n * 60_000),
    )(picks, *x_blocks, *c_blocks, a_up, b_down, w_router, a_router, b_router)


def moe_kernel(places, list_ref, expert_ref, picks_ref, place_ref, *refs):
    n = len(places)
    tables = refs[:n]
    ep_outs, tg_outs = refs[n + 4 : n + 8], refs[n + 8 : n + 12]
    refs = refs[: n + 4] + refs[n + 12 :]
    (
        w_up_hbm, w_down_hbm, b_up, a_down,
        gbu_bf, gad_bf,
        table, acc_e, acc_t, in_x, in_c, out_e, out_t, xb, cb, w_up, w_down, stage_ep, stage_tg,
        gbu_out, gad_out, in_sem, up_sem, down_sem, ep_sem, tg_sem,
    ) = refs[n:]
    acc_e_flat = acc_e.reshape(TOK * 8, 128)
    acc_t_flat = acc_t.reshape(TOK * 8, 128)
    in_x_flat = in_x.reshape(TILE * 8, 128)
    in_c_flat = in_c.reshape(TILE * 8, 128)
    out_e_flat = out_e.reshape(TILE * 8, 128)
    out_t_flat = out_t.reshape(TILE * 8, 128)
    lane = lane_iota((1, 128))
    n_tiles = expert_ref[max_tiles()]

    copies = []
    for piece, spots in zip(tables, places):
        for b, (t, s) in enumerate(spots):
            spot = 4 * t + jnp.where(place_ref[0] == t, swapped(s), s)
            copies.append(
                pltpu.make_async_copy(
                    piece.at[pl.ds(b * BLK, BLK)], table.at[pl.ds(pl.multiple_of(spot * BLK, 32), BLK)], in_sem.at[len(copies)]
                )
            )
    for copy in copies:
        copy.start()

    def weights(expert):
        slot = expert % 2
        return (
            pltpu.make_async_copy(w_up_hbm.at[expert], w_up.at[slot], up_sem.at[slot]),
            pltpu.make_async_copy(w_down_hbm.at[expert], w_down.at[slot], down_sem.at[slot]),
        )

    for copy in weights(0):
        copy.start()
    out_e[...] = jnp.zeros_like(out_e)
    out_t[...] = jnp.zeros_like(out_t)
    gbu_out[...] = jnp.zeros_like(gbu_out)
    gad_out[...] = jnp.zeros_like(gad_out)

    def clear(i, carry):
        acc_e[pl.ds(i * 64, 64)] = jnp.zeros((64, 8, 128), f32)
        acc_t[pl.ds(i * 64, 64)] = jnp.zeros((64, 8, 128), f32)
        return carry

    lax.fori_loop(0, TOK // 64, clear, 0)
    for copy in copies:
        copy.wait()

    def fetch(t):
        for i in range(TILE):
            both = table[list_ref[t * TILE + i]].astype(f32)
            in_x[i] = both[:8]
            in_c[i] = both[8:]

    def give(t):
        for b in range(TILE // 8):
            tokens = [list_ref[t * TILE + 8 * b + k] for k in range(8)]
            sums_e = [acc_e[tokens[k]] + out_e[8 * b + k] for k in range(8)]
            sums_t = [acc_t[tokens[k]] + out_t[8 * b + k] for k in range(8)]
            for k in range(8):
                acc_e[tokens[k]] = sums_e[k]
                acc_t[tokens[k]] = sums_t[k]

    fetch(0)

    def tile(t, carry):
        expert = expert_ref[t]
        slot = expert % 2

        @pl.when((t == 0) | (expert_ref[jnp.maximum(t - 1, 0)] != expert))
        def arrive():
            for copy in weights(expert):
                copy.wait()

            @pl.when(expert + 1 < EXPERTS)
            def ahead():
                for copy in weights(expert + 1):
                    copy.start()

        for j in range(7):
            xb[:, 128 * j : 128 * j + 128] = in_x_flat[pl.ds(j, TILE, 8), :].astype(bf16)
            cb[:, 128 * j : 128 * j + 128] = in_c_flat[pl.ds(j, TILE, 8), :].astype(bf16)
        spread = in_x_flat[pl.ds(7, TILE, 8), :]
        mine = (lane == expert) | (lane == expert + EXPERTS)
        gate = jnp.sum(jnp.where(mine, spread, 0.0), axis=1, keepdims=True)
        fetch(t + 1)
        give(jnp.maximum(t - 1, 0))
        hidden = dot(xb[:, :D], w_up[slot]) + dot(xb[:, D:], b_up[...])
        back = dot_nt(cb[:, :D], w_down[slot]) + dot_nt(cb[:, D:], a_down[...])
        cdf = 0.5 + 0.5 * lax.erf(hidden * 0.7071067811865476)
        slope = cdf + hidden * jnp.exp(hidden * hidden * -0.5) * 0.3989422804014327
        act = (hidden * cdf).astype(bf16)
        act_f = act.astype(f32)
        gate_grad = jnp.sum(act_f * back, axis=1, keepdims=True)
        grad_hidden = (gate * back * slope).astype(bf16)
        act_gate = (gate * act_f).astype(bf16)
        out_main = dot(act_gate, w_down[slot])
        out_low = dot(act_gate, a_down[...])
        in_main = dot_nt(grad_hidden, w_up[slot])
        in_low = dot_nt(grad_hidden, b_up[...])
        gbu_out[...] += dot_tn(grad_hidden, xb[:, D:])
        gad_out[...] += dot_tn(act_gate, cb[:, D:])
        for j in range(6):
            out_e_flat[pl.ds(j, TILE, 8), :] = out_main[:, 128 * j : 128 * j + 128]
            out_t_flat[pl.ds(j, TILE, 8), :] = in_main[:, 128 * j : 128 * j + 128]
        out_e_flat[pl.ds(6, TILE, 8), :] = out_low
        out_t_flat[pl.ds(6, TILE, 8), :] = in_low
        out_t_flat[pl.ds(7, TILE, 8), :] = jnp.where(lane == expert, gate_grad, 0.0)
        return carry

    lax.fori_loop(0, n_tiles, tile, 0)
    give(n_tiles - 1)

    gbu_bf[...] = gbu_out[...].astype(bf16)
    gad_bf[...] = gad_out[...].astype(bf16)
    some = IMG_GRP // 4
    for side, (ep_out, tg_out) in enumerate(zip(ep_outs, tg_outs)):

        def image(i, carry):
            slot = i % 2
            base = pl.multiple_of((i + side * some) * SEQP, 16) * 8
            mask = (lane // RANK) == picks_ref[i + side * some]
            rows = pl.ds(pl.multiple_of(i * SEQP, 16), SEQP)
            put_tg = pltpu.make_async_copy(stage_tg.at[slot], tg_out.at[rows], tg_sem.at[slot])
            put_ep = pltpu.make_async_copy(stage_ep.at[slot], ep_out.at[rows], ep_sem.at[slot])

            @pl.when(i >= 2)
            def drain():
                put_tg.wait()
                put_ep.wait()

            def chunk(j):
                flat = acc_e_flat if j < 8 else acc_t_flat
                return flat[pl.ds(base + j % 8, SEQP, 8), :]

            for j in range(6):
                at = slice(128 * j, 128 * j + 128)
                stage_tg[slot, :, at] = chunk(8 + j).astype(bf16)
                stage_ep[slot, :, at] = chunk(j).astype(bf16)
            low_in = repeat_lanes(jnp.where(mask, chunk(14), 0.0))
            low_out = repeat_lanes(jnp.where(mask, chunk(6), 0.0))
            last = jnp.where(lane < 48, low_in, jnp.where(lane < 64, low_out, 0.0))
            stage_tg[slot, :, D:] = jnp.where(lane < 32, chunk(15), last).astype(bf16)
            put_tg.start()
            put_ep.start()
            return carry

        lax.fori_loop(0, some, image, 0)
        for i in range(some - 2, some):
            rows = pl.ds(i * SEQP, SEQP)
            pltpu.make_async_copy(stage_tg.at[i % 2], tg_out.at[rows], tg_sem.at[i % 2]).wait()
            pltpu.make_async_copy(stage_ep.at[i % 2], ep_out.at[rows], ep_sem.at[i % 2]).wait()


def moe_call(token_list, tile_experts, picks, place, tables, places, w_up, w_down, b_up, a_down):
    half = w_up.shape[2]
    n = len(tables)
    n_copies = sum(len(spots) for spots in places)
    anywhere = pl.BlockSpec(memory_space=pl.ANY)
    inside = pl.BlockSpec(memory_space=pltpu.VMEM)
    return pl.pallas_call(
        lambda *refs: moe_kernel(places, *refs),
        grid_spec=pltpu.PrefetchScalarGridSpec(
            num_scalar_prefetch=4,
            grid=(1,),
            in_specs=[anywhere] * (n + 2) + [inside, inside],
            out_specs=[anywhere] * 8 + [inside, inside],
            scratch_shapes=[
                pltpu.VMEM((TOK, 16, 128), bf16),
                pltpu.VMEM((TOK, 8, 128), f32),
                pltpu.VMEM((TOK, 8, 128), f32),
                pltpu.VMEM((TILE, 8, 128), f32),
                pltpu.VMEM((TILE, 8, 128), f32),
                pltpu.VMEM((TILE, 8, 128), f32),
                pltpu.VMEM((TILE, 8, 128), f32),
                pltpu.VMEM((TILE, D + 128), bf16),
                pltpu.VMEM((TILE, D + 128), bf16),
                pltpu.VMEM((2, D, half), bf16),
                pltpu.VMEM((2, half, D), bf16),
                pltpu.VMEM((2, SEQP, D), bf16),
                pltpu.VMEM((2, SEQP, D + 128), bf16),
                pltpu.VMEM((half, ADAPT), f32),
                pltpu.VMEM((half, ADAPT), f32),
                pltpu.SemaphoreType.DMA((n_copies,)),
                pltpu.SemaphoreType.DMA((2,)),
                pltpu.SemaphoreType.DMA((2,)),
                pltpu.SemaphoreType.DMA((2,)),
                pltpu.SemaphoreType.DMA((2,)),
            ],
        ),
        out_shape=[
            *[jax.ShapeDtypeStruct((TOK // 4, D), bf16)] * 4,
            *[jax.ShapeDtypeStruct((TOK // 4, D + 128), bf16)] * 4,
            jax.ShapeDtypeStruct((half, ADAPT), bf16),
            jax.ShapeDtypeStruct((half, ADAPT), bf16),
        ],
        compiler_params=pltpu.CompilerParams(vmem_limit_bytes=58 * 1024 * 1024),
        cost_estimate=pl.CostEstimate(flops=20_000_000_000, bytes_accessed=60_000_000, transcendentals=10_000_000),
    )(token_list, tile_experts, picks, place, *tables, w_up, w_down, b_up, a_down)


def swapped(s):
    return ((s & 1) << 1) | (s >> 1)


def block_spot(block, row, col):
    from_row = block // 4
    s = (block % 4) ^ col
    return 4 * (from_row ^ row) + jnp.where(from_row == 0, swapped(s), s)


def routing(routes, row, col):
    token = jnp.arange(25 * 128, dtype=jnp.int32)[None, :]
    image = token // SEQ
    spot = block_spot(image // 2, row, col) * BLK + (image % 2) * SEQP + token % SEQ
    real = token < IMG_GRP * SEQ
    picked = jnp.pad(routes.T, ((0, 0), (0, 25 * 128 - IMG_GRP * SEQ)), constant_values=EXPERTS)
    beyond = EXPERTS * 4096 + DUMMY
    keys = jnp.where(real, picked * 4096 + spot, beyond).reshape(-1)
    experts = jnp.arange(EXPERTS, dtype=jnp.int32)
    count = jnp.sum((picked[None] == experts[:, None, None]).astype(jnp.int32), axis=(1, 2))
    tiles = (jnp.maximum(count, 1) + TILE - 1) // TILE
    extra = tiles * TILE - count
    filler = jnp.where(
        jnp.arange(256, dtype=jnp.int32)[None, :] < extra[:, None], (experts * 4096)[:, None] + DUMMY, beyond
    ).reshape(-1)
    ordered = lax.sort(jnp.concatenate([keys, filler])) & 4095
    ends = jnp.sum(jnp.where(experts[None, :] <= experts[:, None], tiles[None, :], 0), axis=1)
    steps = jnp.arange(max_tiles(), dtype=jnp.int32)
    owner = jnp.minimum(jnp.sum((ends[None, :] <= steps[:, None]).astype(jnp.int32), axis=1), EXPERTS - 1)
    return ordered, jnp.concatenate([owner, jnp.sum(tiles)[None]])


HEADS = 12
HEAD_DIM = 64


def pick_mask(pick):
    return (lane_iota((1, ADAPT)) // RANK) == pick


def norm_stats(values):
    centre = jnp.sum(values, axis=1, keepdims=True) * (1.0 / D)
    shifted = values - centre
    spread = jnp.sum(shifted * shifted, axis=1, keepdims=True) * (1.0 / D)
    inverse = lax.rsqrt(spread + 1e-06)
    return shifted * inverse, inverse


def norm_back(grad, gain, unit, inverse):
    scaled = grad * gain
    total = jnp.sum(scaled, axis=1, keepdims=True) * (1.0 / D)
    along = jnp.sum(scaled * unit, axis=1, keepdims=True) * (1.0 / D)
    return inverse * (scaled - total - unit * along)


def qkv_copies(place_ref, blocks, own_b, scratch, sem):
    w_qkv, a_qkv, b_qkv = scratch
    row, col = place_ref[0], place_ref[1]
    copies = []

    def copy(source, target):
        copies.append(pltpu.make_async_copy(source, target, sem.at[len(copies)]))

    for t in range(2):
        half_at = pl.multiple_of((row ^ t) * 384, 128)
        for s in range(4):
            block = blocks[4 * t + s]
            at = pl.multiple_of((col ^ s) * 192, 64)
            low_at = pl.multiple_of((col ^ s) * 192 + (row ^ t) * 96, 32)
            for p in range(3):
                copy(block.at[pl.ds(192 * p, 192)], w_qkv.at[p, pl.ds(at, 192), pl.ds(half_at, 384)])
                copy(block.at[pl.ds(576, 96), pl.ds(128 * p, 128)], a_qkv.at[p, pl.ds(low_at, 96), :])
        for p in range(3):
            source = own_b.at[p] if t == 0 else blocks[4].at[pl.ds(W_ROWS + 128 * p, 128)]
            copy(source, b_qkv.at[p, :, pl.ds(half_at, 384)])
    return copies


def out_copies(place_ref, far_block, own_a, out_w, scratch, sem):
    w_out, a_out = scratch
    row = place_ref[0]
    copies = []

    def copy(source, target):
        copies.append(pltpu.make_async_copy(source, target, sem.at[len(copies)]))

    for t in range(2):
        half_at = pl.multiple_of((row ^ t) * 384, 128)
        copy(out_w[t].at[pl.ds(0, 384)], w_out.at[pl.ds(half_at, 384), :])
        for j in range(3):
            if t == 0:
                source = own_a.at[pl.ds(128 * j, 128)]
            else:
                source = far_block.at[pl.ds(W_ROWS + 384, 128), pl.ds(128 * j, 128)]
            copy(source, a_out.at[pl.ds(half_at + 128 * j, 128), :])
    return copies


W_ROWS = 944
QKV_SCRATCH = [
    pltpu.VMEM((3, D, D), bf16),
    pltpu.VMEM((3, D, ADAPT), bf16),
    pltpu.VMEM((3, ADAPT, D), bf16),
    pltpu.SemaphoreType.DMA((54,)),
]
OUT_SCRATCH = [
    pltpu.VMEM((D, D), bf16),
    pltpu.VMEM((D, ADAPT), bf16),
    pltpu.SemaphoreType.DMA((8,)),
]


def split_kernel(place_ref, tokens_ref, cot_ref, own_out, one_out, two_out, three_out, left, right, stage, sem):
    rows = tokens_ref.shape[0]
    width = D // 4
    left[0:rows, 0:width] = tokens_ref[...].astype(f32)
    right[0:rows, 0:width] = cot_ref[...].astype(f32)
    lane = lane_iota((1, 128))
    real = lax.broadcasted_iota(jnp.int32, (SEQP, 1), 0) < SEQ
    for i in range(8):
        at = slice(SEQ * i, SEQ * i + SEQP)
        spot = slice(SEQP * (i % 2), SEQP * (i % 2) + SEQP)
        moved = pltpu.roll(right[at, :], 64, 1)
        middle = jnp.where(lane < 64, left[at, 128:256], moved[:, 0:128])
        stage[i // 2, spot, 0:128] = jnp.where(real, left[at, 0:128], 0.0).astype(bf16)
        stage[i // 2, spot, 128:256] = jnp.where(real, middle, 0.0).astype(bf16)
        stage[i // 2, spot, 256:384] = jnp.where(real, moved[:, 128:256], 0.0).astype(bf16)
    copies = [
        pltpu.make_async_copy(stage.at[place_ref[1] ^ s], out, sem.at[s])
        for s, out in enumerate((own_out, one_out, two_out, three_out))
    ]
    for copy in copies:
        copy.start()
    for copy in copies:
        copy.wait()


def split_call(place, tokens, cotangent):
    rows = tokens.shape[0]
    tall = -(-(SEQ * 7 + SEQP) // 8) * 8
    inside = pl.BlockSpec(memory_space=pltpu.VMEM)
    return pl.pallas_call(
        split_kernel,
        grid_spec=pltpu.PrefetchScalarGridSpec(
            num_scalar_prefetch=1,
            grid=(1,),
            in_specs=[inside, inside],
            out_specs=[ANYWHERE] * 4,
            scratch_shapes=[
                pltpu.VMEM((tall, 256), f32),
                pltpu.VMEM((tall, 256), f32),
                pltpu.VMEM((4, BLK, 384), bf16),
                pltpu.SemaphoreType.DMA((4,)),
            ],
        ),
        out_shape=[jax.ShapeDtypeStruct((BLK, 384), bf16)] * 4,
        compiler_params=pltpu.CompilerParams(vmem_limit_bytes=32 * 1024 * 1024),
        cost_estimate=pl.CostEstimate(flops=1_000_000_000, bytes_accessed=3_000_000, transcendentals=0),
    )(place, tokens, cotangent)


def finish_kernel(place_ref, mine, one, two, three, far, dp_sums, *refs):
    (
        a_qkv, b_qkv, a_out, b_out, a_router, b_router, a_up, b_up, a_down, b_down, wide, tall, every,
    ) = refs
    row, col = place_ref[0], place_ref[1]
    near_at = pl.multiple_of(row * 96, 32)
    far_at = pl.multiple_of((1 - row) * 96, 32)
    for p in range(4):
        ours = mine[96 * p : 96 * p + 96, :].astype(f32)
        theirs = far[96 * p : 96 * p + 96, :].astype(f32)
        if p < 3:
            a_qkv[p, pl.ds(near_at, 96), :] = ours
            a_qkv[p, pl.ds(far_at, 96), :] = theirs
        else:
            wide[pl.ds(near_at, 96), :] = ours
            wide[pl.ds(far_at, 96), :] = theirs
    b_out[...] = wide[...].T[:, : D // 4]
    share = BOTH_ROWS // 8
    for s, got in enumerate((mine, one, two, three)):
        base = 384 if s == 0 else 0
        at = pl.multiple_of((col ^ s) * 96, 32)
        for p in range(4):
            piece = got[base + 96 * p : base + 96 * p + 96, :].astype(f32)
            if p < 3:
                tall[p, pl.ds(at, 96), :] = piece
            else:
                a_out[pl.ds(at, 96), :] = piece
        ours = got[base + 384 : base + 384 + share, :].astype(f32)
        theirs = far[384 + share * s : 384 + share * s + share, :].astype(f32)
        every[pl.ds(pl.multiple_of((row * 4 + (col ^ s)) * share, 64), share), :] = ours
        every[pl.ds(pl.multiple_of(((1 - row) * 4 + (col ^ s)) * share, 64), share), :] = theirs
    for p in range(3):
        b_qkv[p] = tall[p].T
    a_router[...] = every[0:768, :]
    a_up[...] = every[768:1536, :]
    b_down[...] = every[1536:2304, :].T
    b_router[...] = every[2304:2432, :].T[:, :EXPERTS]
    b_up[...] = dp_sums[0:384, :].astype(f32).T
    a_down[...] = dp_sums[384:768, :].astype(f32)


def finish_call(place, mine, got, far, dp_sums):
    inside = pl.BlockSpec(memory_space=pltpu.VMEM)
    half = D // 2
    shapes = [
        (3, D // 4, ADAPT), (3, ADAPT, half), (half, ADAPT), (ADAPT, D // 4), (D, ADAPT), (ADAPT, EXPERTS),
        (D, ADAPT), (ADAPT, half), (half, ADAPT), (ADAPT, D),
    ]
    return pl.pallas_call(
        finish_kernel,
        grid_spec=pltpu.PrefetchScalarGridSpec(
            num_scalar_prefetch=1,
            grid=(1,),
            in_specs=[inside] * 6,
            out_specs=[inside] * 10,
            scratch_shapes=[
                pltpu.VMEM((256, 128), f32),
                pltpu.VMEM((3, half, 128), f32),
                pltpu.VMEM((BOTH_ROWS, 128), f32),
            ],
        ),
        out_shape=[jax.ShapeDtypeStruct(shape, f32) for shape in shapes],
        compiler_params=pltpu.CompilerParams(vmem_limit_bytes=32 * 1024 * 1024),
        cost_estimate=pl.CostEstimate(flops=1_000_000_000, bytes_accessed=4_000_000, transcendentals=0),
    )(place, mine, *got, far, dp_sums)


def merge_kernel(place_ref, *refs):
    blocks, refs = refs[:4], refs[4:]
    block_out, tokens_out, stage, tall, sem = refs
    copies = [
        pltpu.make_async_copy(block, stage.at[place_ref[1] ^ s], sem.at[s]) for s, block in enumerate(blocks)
    ]
    for copy in copies:
        copy.start()
    for copy in copies:
        copy.wait()
    width = D // 4
    rows = tokens_out.shape[0]
    for i in range(8):
        at = slice(SEQ * i, SEQ * i + SEQ)
        both = stage[i // 2, SEQP * (i % 2) : SEQP * (i % 2) + SEQP, :].astype(f32)[:SEQ]
        tokens_out[at, :] = both[:, :width]
        tall[at, :] = both[:, width:]
    block_out[...] = tall[0:rows, :].astype(bf16)


def merge_call(place, blocks, rows):
    width = D // 4
    inside = pl.BlockSpec(memory_space=pltpu.VMEM)
    return pl.pallas_call(
        merge_kernel,
        grid_spec=pltpu.PrefetchScalarGridSpec(
            num_scalar_prefetch=1,
            grid=(1,),
            in_specs=[ANYWHERE] * 4,
            out_specs=[inside, inside],
            scratch_shapes=[
                pltpu.VMEM((4, BLK, 2 * width), bf16),
                pltpu.VMEM((rows, width), f32),
                pltpu.SemaphoreType.DMA((4,)),
            ],
        ),
        out_shape=[jax.ShapeDtypeStruct((rows, width), bf16), jax.ShapeDtypeStruct((rows, width), f32)],
        compiler_params=pltpu.CompilerParams(vmem_limit_bytes=32 * 1024 * 1024),
        cost_estimate=pl.CostEstimate(flops=8_000_000_000, bytes_accessed=3_000_000, transcendentals=0),
    )(place, *blocks)


def place_weights(place_ref, blocks, own_b, own_a, out_w, w_qkv, a_qkv, b_qkv, w_out, a_out):
    row, col = place_ref[0], place_ref[1]
    for t in range(2):
        half_at = pl.multiple_of((row ^ t) * 384, 128)
        across = pl.ds(half_at, 384)
        for s in range(4):
            block = blocks[4 * t + s]
            at = pl.multiple_of((col ^ s) * 192, 64)
            low_at = pl.multiple_of((col ^ s) * 192 + (row ^ t) * 96, 32)
            for p in range(3):
                w_qkv[p, pl.ds(at, 192), across] = block[192 * p : 192 * p + 192, :]
                a_qkv[p, pl.ds(low_at, 96), :] = block[576:672, 128 * p : 128 * p + 128]
        w_out[across, :] = out_w[t][0:384, :]
        for p in range(3):
            down = pl.ds(pl.multiple_of(half_at + 128 * p, 128), 128)
            if t == 0:
                b_qkv[p, :, across] = own_b[p]
                a_out[down, :] = own_a[128 * p : 128 * p + 128, :]
            else:
                b_qkv[p, :, across] = blocks[4][W_ROWS + 128 * p : W_ROWS + 128 * p + 128, :]
                a_out[down, :] = blocks[4][W_ROWS + 384 : W_ROWS + 512, 128 * p : 128 * p + 128]


def two_masks(picks_ref):
    row = lax.broadcasted_iota(jnp.int32, (BLK, 1), 0)
    pick = jnp.where(row < SEQP, picks_ref[0], picks_ref[1])
    return (lane_iota((1, ADAPT)) // RANK) == pick, (row < SEQ) | ((row >= SEQP) & (row < SEQP + SEQ))


def both_heads(value):
    lane = lane_iota((1, 128))
    nothing = jnp.zeros_like(value)
    return jnp.concatenate(
        [jnp.where(lane < HEAD_DIM, value, nothing), jnp.where(lane < HEAD_DIM, nothing, value)], axis=0
    )


def attend_kernel(picks_ref, place_ref, *refs):
    blocks, refs = refs[:8], refs[8:]
    (
        own_b, own_a, out_near, out_far, x_ref, gain_one, gain_two, b_out,
        two_out, resid_out, normed_out, qkv_out, mixed_out, probs_out, lows_out,
        w_qkv, a_qkv, b_qkv, w_out, a_out,
    ) = refs
    place_weights(place_ref, blocks, own_b, own_a, (out_near, out_far), w_qkv, a_qkv, b_qkv, w_out, a_out)
    mask, real = two_masks(picks_ref)
    x = x_ref[...].astype(f32)
    unit, unused = norm_stats(x)
    normed = (unit * gain_one[...]).astype(bf16)
    normed_out[...] = normed
    for p in range(3):
        low = jnp.where(mask, dot(normed, a_qkv[p]), 0.0).astype(bf16)
        lows_out[:, 128 * p : 128 * p + 128] = low
        qkv_out[p] = (dot(normed, w_qkv[p]) + dot(low, b_qkv[p])).astype(bf16)
    lane = lane_iota((1, 128))
    key_lane = lane_iota((1, SEQP))
    for pair in range(HEADS // 2):
        at = slice(128 * pair, 128 * pair + 128)
        for image in range(2):
            rows = slice(SEQP * image, SEQP * image + SEQP)
            scores = dot_nt(both_heads(qkv_out[0, rows, at]), qkv_out[1, rows, at]) * (HEAD_DIM**-0.5)
            scores = jnp.where(key_lane < SEQ, scores, -1e30)
            power = jnp.exp(scores - jnp.max(scores, axis=1, keepdims=True))
            probs = (power / jnp.sum(power, axis=1, keepdims=True)).astype(bf16)
            probs_out[image, pair] = probs
            found = dot(probs, qkv_out[2, rows, at])
            mixed_out[rows, at] = jnp.where(lane < HEAD_DIM, found[:SEQP], found[SEQP:]).astype(bf16)
    mixed = mixed_out[...]
    low = jnp.where(mask, dot(mixed, a_out[...]), 0.0).astype(bf16)
    lows_out[:, 384:512] = low
    resid = x + dot(mixed, w_out[...]) + dot(low, b_out[...])
    resid_out[...] = resid
    unit, unused = norm_stats(resid)
    two_out[...] = jnp.where(real, unit * gain_two[...], 0.0).astype(bf16)


INSIDE = pl.BlockSpec(memory_space=pltpu.VMEM)


ANYWHERE = pl.BlockSpec(memory_space=pl.ANY)


def attend_call(picks, place, blocks, own_b, own_a, out_w, x, gain_one, gain_two, b_out):
    rows = x.shape[0]
    return pl.pallas_call(
        attend_kernel,
        grid_spec=pltpu.PrefetchScalarGridSpec(
            num_scalar_prefetch=2,
            grid=(1,),
            in_specs=[INSIDE] * (len(blocks) + 8),
            out_specs=[INSIDE] * 7,
            scratch_shapes=QKV_SCRATCH[:-1] + OUT_SCRATCH[:-1],
        ),
        out_shape=[
            jax.ShapeDtypeStruct((rows, D), bf16),
            jax.ShapeDtypeStruct((rows, D), f32),
            jax.ShapeDtypeStruct((rows, D), bf16),
            jax.ShapeDtypeStruct((3, rows, D), bf16),
            jax.ShapeDtypeStruct((rows, D), bf16),
            jax.ShapeDtypeStruct((2, HEADS // 2, BLK, SEQP), bf16),
            jax.ShapeDtypeStruct((rows, 512), bf16),
        ],
        compiler_params=pltpu.CompilerParams(vmem_limit_bytes=48 * 1024 * 1024),
        cost_estimate=pl.CostEstimate(flops=4_000_000_000, bytes_accessed=15_000_000, transcendentals=2_000_000),
    )(picks, place, *blocks, own_b, own_a, *out_w, x, gain_one, gain_two, b_out)


def put_rows(part, p, value):
    value = value.astype(bf16)
    for r in range(2):
        for c in range(4):
            part[r, c, 96 * p : 96 * p + 96, :] = value[384 * r + 96 * c : 384 * r + 96 * c + 96, :]


def put_cols(part, p, value):
    value = value.astype(bf16)
    for r in range(2):
        for c in range(4):
            part[r, c, 96 * p : 96 * p + 96, :] = value[192 * c + 96 * r : 192 * c + 96 * r + 96, :]


def out_back_kernel(picks_ref, place_ref, *refs):
    (
        far_block, own_a, out_near, out_far, gain_two, b_out, two_ref, resid_ref, mixed_ref, lows_ref,
        cot_ref, grad_a, grad_b, w_router, a_router, b_router, a_up, b_down,
        resid_grad_out, mixed_grad_out, base_out, both_out, a_part_out, b_part_out,
        w_out, a_out, sem,
    ) = refs
    copies = out_copies(place_ref, far_block, own_a, (out_near, out_far), (w_out, a_out), sem)
    for copy in copies:
        copy.start()
    mask, unused = two_masks(picks_ref)
    lane = lane_iota((1, 128))

    def add_part(row, value):
        both_out[row : row + value.shape[0], :] = value.astype(bf16)

    two = two_ref[...]
    received = grad_a[...].astype(f32) + grad_b[...].astype(f32)
    low_r = jnp.where(mask, dot(two, a_router[...]), 0.0).astype(bf16)
    logits = dot(two, w_router[...]) + dot(low_r, b_router[...])
    logits = jnp.where(lane < EXPERTS, logits, -1e30)
    power = jnp.exp(logits - jnp.max(logits, axis=1, keepdims=True))
    probs = power / jnp.sum(power, axis=1, keepdims=True)
    last = received[:, D:]
    grad_probs = jnp.where(lane < EXPERTS, last, 0.0)
    low_in = jnp.where(mask, repeat_lanes(jnp.where((lane >= 32) & (lane < 48), last, 0.0)), 0.0).astype(bf16)
    low_out = jnp.where(mask, repeat_lanes(jnp.where((lane >= 48) & (lane < 64), last, 0.0)), 0.0).astype(bf16)
    cot = cot_ref[...]
    resid = resid_ref[...]
    base_out[...] = resid + dot(low_out, b_down[...])
    add_part(768, dot_tn(two, low_in))
    add_part(1536, dot_tn(cot, low_out))
    grad_logits = probs * (grad_probs - jnp.sum(probs * grad_probs, axis=1, keepdims=True))
    grad_logits = grad_logits.astype(bf16)
    grad_low = jnp.where(mask, dot_nt(grad_logits, b_router[...]), 0.0).astype(bf16)
    grad_two = received[:, :D] + dot_nt(low_in, a_up[...])
    grad_two = grad_two + dot_nt(grad_logits, w_router[...]) + dot_nt(grad_low, a_router[...])
    add_part(0, dot_tn(two, grad_low))
    add_part(2304, dot_tn(grad_logits, low_r))
    unit, inverse = norm_stats(resid)
    grad_resid = cot.astype(f32) + norm_back(grad_two, gain_two[...], unit, inverse)
    resid_grad_out[...] = grad_resid
    grad_attn = grad_resid.astype(bf16)
    grad_low = jnp.where(mask, dot_nt(grad_attn, b_out[...]), 0.0).astype(bf16)
    for copy in copies:
        copy.wait()
    mixed_grad_out[...] = (dot_nt(grad_attn, w_out[...]) + dot_nt(grad_low, a_out[...])).astype(bf16)
    put_rows(a_part_out, 0, dot_tn(mixed_ref[...], grad_low))
    put_cols(b_part_out, 0, dot_tn(grad_attn, lows_ref[:, 384:512]))
    both_out[2432:BOTH_ROWS, :] = jnp.zeros((BOTH_ROWS - 2432, 128), bf16)


BOTH_ROWS = 2560


def out_back_call(picks, place, far_block, own_a, out_w, gain_two, b_out, two, resid, mixed, lows, cot, grad_a, grad_b,
                  w_router, a_router, b_router, a_up, b_down):
    rows = two.shape[0]
    return pl.pallas_call(
        out_back_kernel,
        grid_spec=pltpu.PrefetchScalarGridSpec(
            num_scalar_prefetch=2,
            grid=(1,),
            in_specs=[ANYWHERE] * 4 + [INSIDE] * 14,
            out_specs=[INSIDE] * 6,
            scratch_shapes=OUT_SCRATCH,
        ),
        out_shape=[
            jax.ShapeDtypeStruct((rows, D), f32),
            jax.ShapeDtypeStruct((rows, D), bf16),
            jax.ShapeDtypeStruct((rows, D), f32),
            jax.ShapeDtypeStruct((BOTH_ROWS, 128), bf16),
            jax.ShapeDtypeStruct((2, 4, 96, 128), bf16),
            jax.ShapeDtypeStruct((2, 4, 96, 128), bf16),
        ],
        compiler_params=pltpu.CompilerParams(vmem_limit_bytes=60 * 1024 * 1024),
        cost_estimate=pl.CostEstimate(flops=6_000_000_000, bytes_accessed=15_000_000, transcendentals=100_000),
    )(picks, place, far_block, own_a, *out_w, gain_two, b_out, two, resid, mixed, lows, cot, grad_a, grad_b,
      w_router, a_router, b_router, a_up, b_down)


def qkv_back_kernel(picks_ref, place_ref, *refs):
    blocks, refs = refs[:8], refs[8:]
    (
        own_b, x_hbm, gain_one, normed_hbm, qkv_ref, probs_ref, lows_hbm, resid_hbm, grad_mixed,
        tokens_out, a_part_out, b_part_out,
        w_qkv, a_qkv, b_qkv, sem, grads, x_ref, normed_ref, lows_ref, resid_grad, late_sem,
    ) = refs
    copies = qkv_copies(place_ref, blocks, own_b, (w_qkv, a_qkv, b_qkv), sem)
    late = ((x_hbm, x_ref), (normed_hbm, normed_ref), (lows_hbm, lows_ref), (resid_hbm, resid_grad))
    for k, (source, target) in enumerate(late):
        copies.append(pltpu.make_async_copy(source, target, late_sem.at[k]))
    for copy in copies:
        copy.start()
    mask, unused = two_masks(picks_ref)
    lane = lane_iota((1, 128))
    for pair in range(HEADS // 2):
        at = slice(128 * pair, 128 * pair + 128)
        for image in range(2):
            rows = slice(SEQP * image, SEQP * image + SEQP)
            grad_out = both_heads(grad_mixed[rows, at])
            weights = probs_ref[image, pair]
            weights_f = weights.astype(f32)
            grad_w = dot_nt(grad_out, qkv_ref[2, rows, at])
            inner = jnp.sum(weights_f * grad_w, axis=1, keepdims=True)
            grad_s = (weights_f * (grad_w - inner) * (HEAD_DIM**-0.5)).astype(bf16)
            found = dot(grad_s, qkv_ref[1, rows, at])
            grads[0, rows, at] = jnp.where(lane < HEAD_DIM, found[:SEQP], found[SEQP:]).astype(bf16)
            grads[1, rows, at] = dot_tn(grad_s, both_heads(qkv_ref[0, rows, at])).astype(bf16)
            grads[2, rows, at] = dot_tn(weights, grad_out).astype(bf16)
    for copy in copies:
        copy.wait()
    normed = normed_ref[...]
    grad_normed = jnp.zeros((BLK, D), f32)
    for p in range(3):
        piece = grads[p]
        grad_low = jnp.where(mask, dot_nt(piece, b_qkv[p]), 0.0).astype(bf16)
        grad_normed = grad_normed + dot_nt(piece, w_qkv[p]) + dot_nt(grad_low, a_qkv[p])
        put_cols(a_part_out, p, dot_tn(normed, grad_low))
        put_rows(b_part_out, p, dot_tn(piece, lows_ref[:, 128 * p : 128 * p + 128]))
    unit, inverse = norm_stats(x_ref[...].astype(f32))
    tokens_out[...] = (resid_grad[...] + norm_back(grad_normed, gain_one[...], unit, inverse)).astype(bf16)


def qkv_back_call(picks, place, blocks, own_b, x, gain_one, normed, qkv, probs, lows, resid_grad, grad_mixed):
    rows = x.shape[0]
    return pl.pallas_call(
        qkv_back_kernel,
        grid_spec=pltpu.PrefetchScalarGridSpec(
            num_scalar_prefetch=2,
            grid=(1,),
            in_specs=[ANYWHERE] * (len(blocks) + 2)
            + [INSIDE, ANYWHERE, INSIDE, INSIDE, ANYWHERE, ANYWHERE, INSIDE],
            out_specs=[INSIDE] * 3,
            scratch_shapes=QKV_SCRATCH
            + [
                pltpu.VMEM((3, BLK, D), bf16),
                pltpu.VMEM((BLK, D), bf16),
                pltpu.VMEM((BLK, D), bf16),
                pltpu.VMEM((BLK, 512), bf16),
                pltpu.VMEM((BLK, D), f32),
                pltpu.SemaphoreType.DMA((4,)),
            ],
        ),
        out_shape=[
            jax.ShapeDtypeStruct((rows, D), bf16),
            jax.ShapeDtypeStruct((2, 4, 288, 128), bf16),
            jax.ShapeDtypeStruct((2, 4, 288, 128), bf16),
        ],
        compiler_params=pltpu.CompilerParams(vmem_limit_bytes=60 * 1024 * 1024),
        cost_estimate=pl.CostEstimate(flops=9_000_000_000, bytes_accessed=15_000_000, transcendentals=1000),
    )(picks, place, *blocks, own_b, x, gain_one, normed, qkv, probs, lows, resid_grad, grad_mixed)


TABLES = (((0, 0), (1, 0)), ((0, 1), (0, 2), (1, 1), (1, 2)), ((0, 3), (1, 3)))


def across_row(value):
    return lax.ppermute(value, "row", [(0, 1), (1, 0)])


def across_col(value, step):
    return lax.ppermute(value, "col", [(i, i ^ step) for i in range(4)])


def by_place(blocks, col):
    found = []
    for place in range(4):
        value = blocks[place]
        for other in range(1, 4):
            value = jnp.where(col == other, blocks[place ^ other], value)
        found.append(value)
    return found


def across_chip(value, first, second):
    pairs = [(i, i ^ first) for i in range(4)] + [(4 + i, 4 + (i ^ second)) for i in range(4)]
    return lax.ppermute(value, ("row", "col"), pairs)


def gather_col(value, row):
    from_x = across_col(value, 1)
    from_y = across_col(value, 2)
    return [value, from_x, from_y, across_chip(jnp.where(row == 0, from_x, from_y), 2, 1)]


def added(*values):
    total = values[0].astype(f32)
    for value in values[1:]:
        total = total + value.astype(f32)
    return total


def last_exchange(kept_rows, got):
    sent = added(kept_rows[BLK:], got[BLK:]).astype(bf16)
    return added(kept_rows[:BLK], got[:BLK]).astype(bf16), across_chip(sent, 2, 1)


def at_place(value, axis, place):
    return lax.dynamic_index_in_dim(value, place, axis, keepdims=False)


def scatter_dp(value):
    place = lax.axis_index("dp")
    view = value.reshape(4, -1, 128)
    found = [at_place(view, 0, place)]
    for s in range(1, 4):
        found.append(across_dp(at_place(view, 0, place ^ s), s))
    return added(*found).astype(bf16)


def across_dp(value, step):
    return lax.ppermute(value, "dp", [(i, i ^ step) for i in range(4)])


def spread_dp(value):
    return jnp.concatenate(by_place([value] + [across_dp(value, s) for s in range(1, 4)], lax.axis_index("dp")))


def part_share(parts, place):
    return jnp.concatenate([at_place(part, 0, place) for part in parts], axis=1)


def exchange_col(value, col):
    return [at_place(value, 0, col)] + [across_col(at_place(value, 0, col ^ s), s) for s in range(1, 4)]


def to_features(first, second, col):
    width = D // 4
    pieces = []
    for p in range(4):
        at = slice(width * p, width * p + width)
        pieces.append(jnp.concatenate([first[:, at], second[:, at]], axis=1))
    sent = by_place(pieces, col)
    return [sent[0]] + [across_col(sent[s], s) for s in range(1, 4)]


def on_device(
    tokens, cotangent, routes, adapter_pick, gain_attn, gain_moe, w_qkv, w_out, w_router, w_up, w_down,
    a_qkv, b_qkv, a_out, b_out, a_router, b_router, a_up, b_up, a_down, b_down,
):
    row = lax.axis_index("row")
    col = lax.axis_index("col")
    me = row * 4 + col
    place = jnp.stack([row, col]).astype(jnp.int32)

    width = D // 4
    half = D // 2
    gains = []
    for gain in (gain_attn, gain_moe):
        left = gain
        for unused in range(3):
            lead = lax.reduce_precision(left, 8, 7)
            gains.append(lead.astype(bf16))
            left = left - lead
    small = jnp.concatenate([w_out, b_out, jnp.stack(gains), jnp.zeros((26, width), bf16)], axis=0)
    low = at_place(a_qkv.reshape(3, 2, 96, ADAPT), 1, row)
    packed = jnp.concatenate(
        [w_qkv.reshape(576, half), jnp.concatenate([low[0], low[1], low[2]], axis=1),
         jnp.concatenate([small[:272], small[272:]], axis=1)]
    )
    for_row = jnp.concatenate(
        [packed, b_qkv.reshape(half, half), jnp.concatenate([a_out[:128], a_out[128:256], a_out[256:]], axis=1)]
    )
    pairs = split_call(place, tokens, cotangent)
    from_x, from_y = across_col(packed, 1), across_col(packed, 2)
    chosen, routes, *pairs = lax.optimization_barrier((jnp.where(row == 0, from_x, from_y), routes, *pairs))
    near = [packed, from_x, from_y, across_chip(chosen, 2, 1)]
    pairs = by_place([pairs[0]] + [across_col(pairs[s], s) for s in range(1, 4)], col)
    x = jnp.concatenate([pair[:, :width] for pair in pairs], axis=1)
    cot = jnp.concatenate([pair[:, width:] for pair in pairs], axis=1)
    far = [across_row(for_row)] + [across_row(block) for block in near[1:]]
    blocks = near + far

    def assembled(group):
        parts = by_place([block[672:944] for block in group], col)
        return jnp.concatenate(
            [jnp.concatenate([part[:, :width] for part in parts], axis=1),
             jnp.concatenate([part[:, width:] for part in parts], axis=1)], axis=0
        )

    out_w = [assembled(near), assembled(far)]
    full_b_out = out_w[0][384:512]
    gain_rows = out_w[0][512:518].astype(f32)
    gain_one = jnp.sum(gain_rows[:3], axis=0, keepdims=True)
    gain_two = jnp.sum(gain_rows[3:], axis=0, keepdims=True)

    picks_group = lax.dynamic_slice_in_dim(adapter_pick, lax.axis_index("dp") * IMG_GRP, IMG_GRP)
    order = jnp.arange(IMG_GRP, dtype=jnp.int32)
    picks = jnp.take(picks_group, ((order // 2) ^ me) * 2 + order % 2)
    spot_picks = jnp.sum(
        jnp.where(block_spot(order // 2, row, col)[None, :] * 2 + order[None, :] % 2 == order[:, None], picks_group[None, :], 0), axis=1
    )
    token_list, tile_experts = routing(routes, row, col)
    wide_router = jnp.concatenate([w_router, w_router, jnp.zeros((D, 64), bf16)], axis=1)
    wide_b_router = jnp.concatenate([b_router, b_router, jnp.zeros((ADAPT, 64), bf16)], axis=1)
    slim_router = jnp.concatenate([w_router, jnp.zeros((D, 96), bf16)], axis=1)
    slim_b_router = jnp.concatenate([b_router, jnp.zeros((ADAPT, 96), bf16)], axis=1)

    x, token_list, tile_experts, wide_router, wide_b_router, slim_router, slim_b_router = lax.optimization_barrier(
        (x, token_list, tile_experts, wide_router, wide_b_router, slim_router, slim_b_router)
    )
    cot, unused = lax.optimization_barrier((cot, near[3]))
    two, resid, normed, qkv, mixed, probs, lows = attend_call(
        picks, place, blocks, b_qkv, a_out, out_w, x, gain_one, gain_two, full_b_out
    )
    cot_near = gather_col(cot, row)
    two_x, two_y = across_col(two, 1), across_col(two, 2)

    def table(spots, twos, cots):
        return table_call(
            jnp.stack([picks[8 * t + 2 * s + side] for t, s in spots for side in range(2)]),
            twos, cots, a_up, b_down, wide_router, a_router, wide_b_router,
        )

    cot_far = [across_row(block) for block in cot_near[:3]]
    tables = [table(TABLES[0], [two, across_row(two)], [cot, cot_far[0]])]
    two_x, two_y, tables[0] = lax.optimization_barrier((two_x, two_y, tables[0]))
    diag = across_chip(jnp.where(row == 0, two_x, two_y), 2, 1)
    tables.append(
        table(TABLES[1], [two_x, two_y, across_row(two_x), across_row(two_y)], [cot_near[1], cot_near[2], cot_far[1], cot_far[2]])
    )
    diag, cot_diag, *tables = lax.optimization_barrier((diag, cot_near[3], *tables))
    tables.append(table(TABLES[2], [diag, across_row(diag)], [cot_diag, across_row(cot_diag)]))
    *moved, part_b_up, part_a_down = moe_call(
        token_list, tile_experts, spot_picks, place, tables, TABLES, w_up, w_down, b_up, a_down
    )
    sums, grads = moved[:4], moved[4:]
    dp_parts = jnp.concatenate([part_b_up, part_a_down])
    grad_sent = added(grads[1], across_row(grads[3])).astype(bf16)
    grad_kept = added(grads[0], across_row(grads[2])).astype(bf16)
    grad_sent, dp_parts, *sums = lax.optimization_barrier((grad_sent, dp_parts, *sums))
    grad_got = across_chip(grad_sent, 1, 2)
    sum_kept, sum_sent = across_row(sums[2]), across_row(sums[3])
    sums = [
        added(near[at : at + BLK], far[at : at + BLK]).astype(bf16)
        for near, far in ((sums[0], sum_kept), (sums[1], sum_sent)) for at in (0, BLK)
    ]
    four_dp = lax.axis_size("dp") == 4
    dp_sums = scatter_dp(dp_parts) if four_dp else lax.psum(dp_parts, "dp")
    grad_got, dp_sums, *sums = lax.optimization_barrier((grad_got, dp_sums, *sums))
    grad_a, grad_b = last_exchange(grad_kept, grad_got)
    if four_dp:
        dp_sums = spread_dp(dp_sums)
    grad_a, grad_b, dp_sums, *sums = lax.optimization_barrier((grad_a, grad_b, dp_sums, *sums))
    sums = [sums[0], across_chip(sums[1], 2, 1), across_chip(sums[2], 1, 2), across_chip(sums[3], 3, 3)]
    resid_grad, mixed_grad, base, both_parts, part_a_out, part_b_out = out_back_call(
        picks, place, blocks[4], a_out, out_w, gain_two, full_b_out, two, resid, mixed, lows, cot, grad_a, grad_b,
        slim_router, a_router, slim_b_router, a_up, b_down,
    )
    grad_tokens, part_a_qkv, part_b_qkv = qkv_back_call(
        picks, place, blocks, b_qkv, x, gain_one, normed, qkv, probs, lows, resid_grad, mixed_grad
    )
    part_a_qkv, part_b_qkv, *sums = lax.optimization_barrier((part_a_qkv, part_b_qkv, *sums))
    parts = (part_a_qkv, part_b_out, part_b_qkv, part_a_out, both_parts.reshape(2, 4, BOTH_ROWS // 8, 128))
    theirs = across_row(part_share(parts, 1 - row))
    shared = added(part_share(parts, row), theirs).astype(bf16)
    found = exchange_col(shared, col)
    mine = added(*found).astype(bf16)
    mine, grad_tokens, base = lax.optimization_barrier((mine, grad_tokens, base))
    moves = to_features(grad_tokens, (base + added(*sums)).astype(bf16), col)
    mine = spread_dp(scatter_dp(mine)) if four_dp else lax.psum(mine, "dp")
    got = [across_col(mine[384:], s) for s in range(1, 4)]
    far = across_row(jnp.concatenate([mine[:384], mine[768:]] + [one[384:] for one in got]))
    block_out, grad_tokens = merge_call(place, moves, tokens.shape[0])
    far, block_out, grad_tokens = lax.optimization_barrier((far, block_out, grad_tokens))
    return (block_out, grad_tokens, *finish_call(place, mine, got, far, dp_sums))


def solution(mesh):
    return jax.shard_map(
        on_device,
        mesh=mesh,
        in_specs=(
            P(("dp", "row"), "col"),
            P(("dp", "row"), "col"),
            P("dp", None),
            P(),
            P("col"),
            P("col"),
            P(None, "col", "row"),
            P("row", "col"),
            P(),
            P(None, None, ("row", "col")),
            P(None, ("row", "col"), None),
            P(None, "col", None),
            P(None, None, "row"),
            P("row", None),
            P(None, "col"),
            P(),
            P(),
            P(),
            P(None, ("row", "col")),
            P(("row", "col"), None),
            P(),
        ),
        out_specs=(
            P(("dp", "row"), "col"),
            P(("dp", "row"), "col"),
            P(None, "col", None),
            P(None, None, "row"),
            P("row", None),
            P(None, "col"),
            P(),
            P(),
            P(),
            P(None, ("row", "col")),
            P(("row", "col"), None),
            P(),
        ),
        check_vma=False,
    )
```

```python
import jax
import jax.numpy as jnp
from jax import lax
from jax.experimental import pallas as pl
from jax.experimental.pallas import tpu as pltpu
from jax.sharding import PartitionSpec as P

D = 768
EXPERTS = 32
SEQ = 197
SEQP = 208
RANK = 16
ADAPT = 128
IMG_GRP = 16
TOK = IMG_GRP * SEQP
BLK = 2 * SEQP
DUMMY = SEQ
TILE = 128
f32 = jnp.float32
bf16 = jnp.bfloat16


def max_tiles():
    return (2 * IMG_GRP * SEQ) // TILE + EXPERTS + 1


def dot(left, right):
    return jnp.dot(left, right, preferred_element_type=f32)


def dot_nt(left, right):
    return lax.dot_general(left, right, (((1,), (1,)), ((), ())), preferred_element_type=f32)


def dot_tn(left, right):
    return lax.dot_general(left, right, (((0,), (0,)), ((), ())), preferred_element_type=f32)


def lane_iota(shape):
    return lax.broadcasted_iota(jnp.int32, shape, len(shape) - 1)


def repeat_lanes(value):
    for shift in (16, 32, 64):
        value = value + pltpu.roll(value, shift, 1)
    return value


def table_kernel(n_blocks, picks_ref, *refs):
    x_blocks = refs[:n_blocks]
    c_blocks = refs[n_blocks : 2 * n_blocks]
    a_up, b_down, w_router, a_router, b_router, table_out, xin, cin, rows_x, rows_c, sem = refs[2 * n_blocks :]
    image = pl.program_id(0)
    lane = lane_iota((1, 128))

    @pl.when(image == 0)
    def start():
        copies = []
        for blocks, place in ((x_blocks, xin), (c_blocks, cin)):
            for b, block in enumerate(blocks):
                copies.append(pltpu.make_async_copy(block, place.at[pl.ds(b * BLK, BLK)], sem.at[len(copies)]))
        for copy in copies:
            copy.start()
        for copy in copies:
            copy.wait()

    row = pl.multiple_of(image * SEQP, 16)
    mask = (lane // RANK) == picks_ref[image]
    x = xin[pl.ds(row, SEQP), :]
    c = cin[pl.ds(row, SEQP), :]
    flat_x = rows_x.reshape(SEQP * 8, 128)
    flat_c = rows_c.reshape(SEQP * 8, 128)
    low_x = jnp.where(mask, dot(x, a_up[...]), 0.0)
    low_c = jnp.where(mask, dot_nt(c, b_down[...]), 0.0)
    low_r = jnp.where(mask, dot(x, a_router[...]), 0.0).astype(bf16)
    logits = dot(x, w_router[...]) + dot(low_r, b_router[...])
    logits = jnp.where(lane < 2 * EXPERTS, logits, -1e30)
    power = jnp.exp(logits - jnp.max(logits, axis=1, keepdims=True))
    total = jnp.sum(jnp.where(lane < EXPERTS, power, 0.0), axis=1, keepdims=True)
    probs = power / total
    lead = probs.astype(bf16).astype(f32)
    probs = jnp.where(lane < EXPERTS, lead, probs - lead)
    for j in range(6):
        flat_x[pl.ds(j, SEQP, 8), :] = x[:, 128 * j : 128 * j + 128].astype(f32)
        flat_c[pl.ds(j, SEQP, 8), :] = c[:, 128 * j : 128 * j + 128].astype(f32)
    flat_x[pl.ds(6, SEQP, 8), :] = low_x
    flat_x[pl.ds(7, SEQP, 8), :] = probs
    flat_c[pl.ds(6, SEQP, 8), :] = low_c
    flat_c[pl.ds(7, SEQP, 8), :] = jnp.zeros((SEQP, 128), f32)
    table_out[...] = jnp.concatenate([rows_x[...], rows_c[...]], axis=1).astype(bf16)


def table_call(picks, x_blocks, c_blocks, a_up, b_down, w_router, a_router, b_router):
    n = len(x_blocks)

    def whole(*shape):
        return pl.BlockSpec(shape, lambda e, *_: (0,) * len(shape))

    anywhere = pl.BlockSpec(memory_space=pl.ANY)
    return pl.pallas_call(
        lambda *refs: table_kernel(n, *refs),
        grid_spec=pltpu.PrefetchScalarGridSpec(
            num_scalar_prefetch=1,
            grid=(2 * n,),
            in_specs=[anywhere] * (2 * n)
            + [whole(D, ADAPT), whole(ADAPT, D), whole(D, 128), whole(D, ADAPT), whole(ADAPT, 128)],
            out_specs=pl.BlockSpec((SEQP, 16, 128), lambda i, *_: (i, 0, 0)),
            scratch_shapes=[
                pltpu.VMEM((n * BLK, D), bf16),
                pltpu.VMEM((n * BLK, D), bf16),
                pltpu.VMEM((SEQP, 8, 128), f32),
                pltpu.VMEM((SEQP, 8, 128), f32),
                pltpu.SemaphoreType.DMA((2 * n,)),
            ],
        ),
        out_shape=jax.ShapeDtypeStruct((n * BLK, 16, 128), bf16),
        compiler_params=pltpu.CompilerParams(vmem_limit_bytes=32 * 1024 * 1024),
        cost_estimate=pl.CostEstimate(flops=n * 3_000_000_000, bytes_accessed=n * 3_000_000, transcendentals=n * 60_000),
    )(picks, *x_blocks, *c_blocks, a_up, b_down, w_router, a_router, b_router)


def moe_kernel(places, list_ref, expert_ref, picks_ref, place_ref, *refs):
    n = len(places)
    tables = refs[:n]
    ep_outs, tg_outs = refs[n + 4 : n + 8], refs[n + 8 : n + 12]
    refs = refs[: n + 4] + refs[n + 12 :]
    (
        w_up_hbm, w_down_hbm, b_up, a_down,
        gbu_bf, gad_bf,
        table, acc_e, acc_t, in_x, in_c, out_e, out_t, xb, cb, w_up, w_down, stage_ep, stage_tg,
        gbu_out, gad_out, in_sem, up_sem, down_sem, ep_sem, tg_sem,
    ) = refs[n:]
    acc_e_flat = acc_e.reshape(TOK * 8, 128)
    acc_t_flat = acc_t.reshape(TOK * 8, 128)
    in_x_flat = in_x.reshape(TILE * 8, 128)
    in_c_flat = in_c.reshape(TILE * 8, 128)
    out_e_flat = out_e.reshape(TILE * 8, 128)
    out_t_flat = out_t.reshape(TILE * 8, 128)
    lane = lane_iota((1, 128))
    n_tiles = expert_ref[max_tiles()]

    copies = []
    for piece, spots in zip(tables, places):
        for b, (t, s) in enumerate(spots):
            spot = 4 * t + jnp.where(place_ref[0] == t, swapped(s), s)
            copies.append(
                pltpu.make_async_copy(
                    piece.at[pl.ds(b * BLK, BLK)], table.at[pl.ds(pl.multiple_of(spot * BLK, 32), BLK)], in_sem.at[len(copies)]
                )
            )
    for copy in copies:
        copy.start()

    def weights(expert):
        slot = expert % 2
        return (
            pltpu.make_async_copy(w_up_hbm.at[expert], w_up.at[slot], up_sem.at[slot]),
            pltpu.make_async_copy(w_down_hbm.at[expert], w_down.at[slot], down_sem.at[slot]),
        )

    for copy in weights(0):
        copy.start()
    out_e[...] = jnp.zeros_like(out_e)
    out_t[...] = jnp.zeros_like(out_t)
    gbu_out[...] = jnp.zeros_like(gbu_out)
    gad_out[...] = jnp.zeros_like(gad_out)

    def clear(i, carry):
        acc_e[pl.ds(i * 64, 64)] = jnp.zeros((64, 8, 128), f32)
        acc_t[pl.ds(i * 64, 64)] = jnp.zeros((64, 8, 128), f32)
        return carry

    lax.fori_loop(0, TOK // 64, clear, 0)
    for copy in copies:
        copy.wait()

    def fetch(t):
        for i in range(TILE):
            both = table[list_ref[t * TILE + i]].astype(f32)
            in_x[i] = both[:8]
            in_c[i] = both[8:]

    def give(t):
        for b in range(TILE // 8):
            tokens = [list_ref[t * TILE + 8 * b + k] for k in range(8)]
            sums_e = [acc_e[tokens[k]] + out_e[8 * b + k] for k in range(8)]
            sums_t = [acc_t[tokens[k]] + out_t[8 * b + k] for k in range(8)]
            for k in range(8):
                acc_e[tokens[k]] = sums_e[k]
                acc_t[tokens[k]] = sums_t[k]

    fetch(0)

    def tile(t, carry):
        expert = expert_ref[t]
        slot = expert % 2

        @pl.when((t == 0) | (expert_ref[jnp.maximum(t - 1, 0)] != expert))
        def arrive():
            for copy in weights(expert):
                copy.wait()

            @pl.when(expert + 1 < EXPERTS)
            def ahead():
                for copy in weights(expert + 1):
                    copy.start()

        for j in range(7):
            xb[:, 128 * j : 128 * j + 128] = in_x_flat[pl.ds(j, TILE, 8), :].astype(bf16)
            cb[:, 128 * j : 128 * j + 128] = in_c_flat[pl.ds(j, TILE, 8), :].astype(bf16)
        spread = in_x_flat[pl.ds(7, TILE, 8), :]
        mine = (lane == expert) | (lane == expert + EXPERTS)
        gate = jnp.sum(jnp.where(mine, spread, 0.0), axis=1, keepdims=True)
        fetch(t + 1)
        give(jnp.maximum(t - 1, 0))
        hidden = dot(xb[:, :D], w_up[slot]) + dot(xb[:, D:], b_up[...])
        back = dot_nt(cb[:, :D], w_down[slot]) + dot_nt(cb[:, D:], a_down[...])
        cdf = 0.5 + 0.5 * lax.erf(hidden * 0.7071067811865476)
        slope = cdf + hidden * jnp.exp(hidden * hidden * -0.5) * 0.3989422804014327
        act = (hidden * cdf).astype(bf16)
        act_f = act.astype(f32)
        gate_grad = jnp.sum(act_f * back, axis=1, keepdims=True)
        grad_hidden = (gate * back * slope).astype(bf16)
        act_gate = (gate * act_f).astype(bf16)
        out_main = dot(act_gate, w_down[slot])
        out_low = dot(act_gate, a_down[...])
        in_main = dot_nt(grad_hidden, w_up[slot])
        in_low = dot_nt(grad_hidden, b_up[...])
        gbu_out[...] += dot_tn(grad_hidden, xb[:, D:])
        gad_out[...] += dot_tn(act_gate, cb[:, D:])
        for j in range(6):
            out_e_flat[pl.ds(j, TILE, 8), :] = out_main[:, 128 * j : 128 * j + 128]
            out_t_flat[pl.ds(j, TILE, 8), :] = in_main[:, 128 * j : 128 * j + 128]
        out_e_flat[pl.ds(6, TILE, 8), :] = out_low
        out_t_flat[pl.ds(6, TILE, 8), :] = in_low
        out_t_flat[pl.ds(7, TILE, 8), :] = jnp.where(lane == expert, gate_grad, 0.0)
        return carry

    lax.fori_loop(0, n_tiles, tile, 0)
    give(n_tiles - 1)

    gbu_bf[...] = gbu_out[...].astype(bf16)
    gad_bf[...] = gad_out[...].astype(bf16)
    some = IMG_GRP // 4
    for side, (ep_out, tg_out) in enumerate(zip(ep_outs, tg_outs)):

        def image(i, carry):
            slot = i % 2
            base = pl.multiple_of((i + side * some) * SEQP, 16) * 8
            mask = (lane // RANK) == picks_ref[i + side * some]
            rows = pl.ds(pl.multiple_of(i * SEQP, 16), SEQP)
            put_tg = pltpu.make_async_copy(stage_tg.at[slot], tg_out.at[rows], tg_sem.at[slot])
            put_ep = pltpu.make_async_copy(stage_ep.at[slot], ep_out.at[rows], ep_sem.at[slot])

            @pl.when(i >= 2)
            def drain():
                put_tg.wait()
                put_ep.wait()

            def chunk(j):
                flat = acc_e_flat if j < 8 else acc_t_flat
                return flat[pl.ds(base + j % 8, SEQP, 8), :]

            for j in range(6):
                at = slice(128 * j, 128 * j + 128)
                stage_tg[slot, :, at] = chunk(8 + j).astype(bf16)
                stage_ep[slot, :, at] = chunk(j).astype(bf16)
            low_in = repeat_lanes(jnp.where(mask, chunk(14), 0.0))
            low_out = repeat_lanes(jnp.where(mask, chunk(6), 0.0))
            last = jnp.where(lane < 48, low_in, jnp.where(lane < 64, low_out, 0.0))
            stage_tg[slot, :, D:] = jnp.where(lane < 32, chunk(15), last).astype(bf16)
            put_tg.start()
            put_ep.start()
            return carry

        lax.fori_loop(0, some, image, 0)
        for i in range(some - 2, some):
            rows = pl.ds(i * SEQP, SEQP)
            pltpu.make_async_copy(stage_tg.at[i % 2], tg_out.at[rows], tg_sem.at[i % 2]).wait()
            pltpu.make_async_copy(stage_ep.at[i % 2], ep_out.at[rows], ep_sem.at[i % 2]).wait()


def moe_call(token_list, tile_experts, picks, place, tables, places, w_up, w_down, b_up, a_down):
    half = w_up.shape[2]
    n = len(tables)
    n_copies = sum(len(spots) for spots in places)
    anywhere = pl.BlockSpec(memory_space=pl.ANY)
    inside = pl.BlockSpec(memory_space=pltpu.VMEM)
    return pl.pallas_call(
        lambda *refs: moe_kernel(places, *refs),
        grid_spec=pltpu.PrefetchScalarGridSpec(
            num_scalar_prefetch=4,
            grid=(1,),
            in_specs=[anywhere] * (n + 2) + [inside, inside],
            out_specs=[anywhere] * 8 + [inside, inside],
            scratch_shapes=[
                pltpu.VMEM((TOK, 16, 128), bf16),
                pltpu.VMEM((TOK, 8, 128), f32),
                pltpu.VMEM((TOK, 8, 128), f32),
                pltpu.VMEM((TILE, 8, 128), f32),
                pltpu.VMEM((TILE, 8, 128), f32),
                pltpu.VMEM((TILE, 8, 128), f32),
                pltpu.VMEM((TILE, 8, 128), f32),
                pltpu.VMEM((TILE, D + 128), bf16),
                pltpu.VMEM((TILE, D + 128), bf16),
                pltpu.VMEM((2, D, half), bf16),
                pltpu.VMEM((2, half, D), bf16),
                pltpu.VMEM((2, SEQP, D), bf16),
                pltpu.VMEM((2, SEQP, D + 128), bf16),
                pltpu.VMEM((half, ADAPT), f32),
                pltpu.VMEM((half, ADAPT), f32),
                pltpu.SemaphoreType.DMA((n_copies,)),
                pltpu.SemaphoreType.DMA((2,)),
                pltpu.SemaphoreType.DMA((2,)),
                pltpu.SemaphoreType.DMA((2,)),
                pltpu.SemaphoreType.DMA((2,)),
            ],
        ),
        out_shape=[
            *[jax.ShapeDtypeStruct((TOK // 4, D), bf16)] * 4,
            *[jax.ShapeDtypeStruct((TOK // 4, D + 128), bf16)] * 4,
            jax.ShapeDtypeStruct((half, ADAPT), bf16),
            jax.ShapeDtypeStruct((half, ADAPT), bf16),
        ],
        compiler_params=pltpu.CompilerParams(vmem_limit_bytes=58 * 1024 * 1024),
        cost_estimate=pl.CostEstimate(flops=20_000_000_000, bytes_accessed=60_000_000, transcendentals=10_000_000),
    )(token_list, tile_experts, picks, place, *tables, w_up, w_down, b_up, a_down)


def swapped(s):
    return ((s & 1) << 1) | (s >> 1)


def block_spot(block, row, col):
    from_row = block // 4
    s = (block % 4) ^ col
    return 4 * (from_row ^ row) + jnp.where(from_row == 0, swapped(s), s)


def routing(routes, row, col):
    token = jnp.arange(25 * 128, dtype=jnp.int32)[None, :]
    image = token // SEQ
    spot = block_spot(image // 2, row, col) * BLK + (image % 2) * SEQP + token % SEQ
    real = token < IMG_GRP * SEQ
    picked = jnp.pad(routes.T, ((0, 0), (0, 25 * 128 - IMG_GRP * SEQ)), constant_values=EXPERTS)
    beyond = EXPERTS * 4096 + DUMMY
    keys = jnp.where(real, picked * 4096 + spot, beyond).reshape(-1)
    experts = jnp.arange(EXPERTS, dtype=jnp.int32)
    count = jnp.sum((picked[None] == experts[:, None, None]).astype(jnp.int32), axis=(1, 2))
    tiles = (jnp.maximum(count, 1) + TILE - 1) // TILE
    extra = tiles * TILE - count
    filler = jnp.where(
        jnp.arange(256, dtype=jnp.int32)[None, :] < extra[:, None], (experts * 4096)[:, None] + DUMMY, beyond
    ).reshape(-1)
    ordered = lax.sort(jnp.concatenate([keys, filler])) & 4095
    ends = jnp.sum(jnp.where(experts[None, :] <= experts[:, None], tiles[None, :], 0), axis=1)
    steps = jnp.arange(max_tiles(), dtype=jnp.int32)
    owner = jnp.minimum(jnp.sum((ends[None, :] <= steps[:, None]).astype(jnp.int32), axis=1), EXPERTS - 1)
    return ordered, jnp.concatenate([owner, jnp.sum(tiles)[None]])


HEADS = 12
HEAD_DIM = 64


def pick_mask(pick):
    return (lane_iota((1, ADAPT)) // RANK) == pick


def norm_stats(values):
    centre = jnp.sum(values, axis=1, keepdims=True) * (1.0 / D)
    shifted = values - centre
    spread = jnp.sum(shifted * shifted, axis=1, keepdims=True) * (1.0 / D)
    inverse = lax.rsqrt(spread + 1e-06)
    return shifted * inverse, inverse


def norm_back(grad, gain, unit, inverse):
    scaled = grad * gain
    total = jnp.sum(scaled, axis=1, keepdims=True) * (1.0 / D)
    along = jnp.sum(scaled * unit, axis=1, keepdims=True) * (1.0 / D)
    return inverse * (scaled - total - unit * along)


def qkv_copies(place_ref, blocks, own_b, scratch, sem):
    w_qkv, a_qkv, b_qkv = scratch
    row, col = place_ref[0], place_ref[1]
    copies = []

    def copy(source, target):
        copies.append(pltpu.make_async_copy(source, target, sem.at[len(copies)]))

    for t in range(2):
        half_at = pl.multiple_of((row ^ t) * 384, 128)
        for s in range(4):
            block = blocks[4 * t + s]
            at = pl.multiple_of((col ^ s) * 192, 64)
            low_at = pl.multiple_of((col ^ s) * 192 + (row ^ t) * 96, 32)
            for p in range(3):
                copy(block.at[pl.ds(192 * p, 192)], w_qkv.at[p, pl.ds(at, 192), pl.ds(half_at, 384)])
                copy(block.at[pl.ds(576, 96), pl.ds(128 * p, 128)], a_qkv.at[p, pl.ds(low_at, 96), :])
        for p in range(3):
            source = own_b.at[p] if t == 0 else blocks[4].at[pl.ds(W_ROWS + 128 * p, 128)]
            copy(source, b_qkv.at[p, :, pl.ds(half_at, 384)])
    return copies


def out_copies(place_ref, far_block, own_a, out_w, scratch, sem):
    w_out, a_out = scratch
    row = place_ref[0]
    copies = []

    def copy(source, target):
        copies.append(pltpu.make_async_copy(source, target, sem.at[len(copies)]))

    for t in range(2):
        half_at = pl.multiple_of((row ^ t) * 384, 128)
        copy(out_w[t].at[pl.ds(0, 384)], w_out.at[pl.ds(half_at, 384), :])
        for j in range(3):
            if t == 0:
                source = own_a.at[pl.ds(128 * j, 128)]
            else:
                source = far_block.at[pl.ds(W_ROWS + 384, 128), pl.ds(128 * j, 128)]
            copy(source, a_out.at[pl.ds(half_at + 128 * j, 128), :])
    return copies


W_ROWS = 944
QKV_SCRATCH = [
    pltpu.VMEM((3, D, D), bf16),
    pltpu.VMEM((3, D, ADAPT), bf16),
    pltpu.VMEM((3, ADAPT, D), bf16),
    pltpu.SemaphoreType.DMA((54,)),
]
OUT_SCRATCH = [
    pltpu.VMEM((D, D), bf16),
    pltpu.VMEM((D, ADAPT), bf16),
    pltpu.SemaphoreType.DMA((8,)),
]


def split_kernel(place_ref, tokens_ref, cot_ref, own_out, one_out, two_out, three_out, left, right, stage, sem):
    rows = tokens_ref.shape[0]
    width = D // 4
    left[0:rows, 0:width] = tokens_ref[...].astype(f32)
    right[0:rows, 0:width] = cot_ref[...].astype(f32)
    lane = lane_iota((1, 128))
    real = lax.broadcasted_iota(jnp.int32, (SEQP, 1), 0) < SEQ
    for i in range(8):
        at = slice(SEQ * i, SEQ * i + SEQP)
        spot = slice(SEQP * (i % 2), SEQP * (i % 2) + SEQP)
        moved = pltpu.roll(right[at, :], 64, 1)
        middle = jnp.where(lane < 64, left[at, 128:256], moved[:, 0:128])
        stage[i // 2, spot, 0:128] = jnp.where(real, left[at, 0:128], 0.0).astype(bf16)
        stage[i // 2, spot, 128:256] = jnp.where(real, middle, 0.0).astype(bf16)
        stage[i // 2, spot, 256:384] = jnp.where(real, moved[:, 128:256], 0.0).astype(bf16)
    copies = [
        pltpu.make_async_copy(stage.at[place_ref[1] ^ s], out, sem.at[s])
        for s, out in enumerate((own_out, one_out, two_out, three_out))
    ]
    for copy in copies:
        copy.start()
    for copy in copies:
        copy.wait()


def split_call(place, tokens, cotangent):
    rows = tokens.shape[0]
    tall = -(-(SEQ * 7 + SEQP) // 8) * 8
    inside = pl.BlockSpec(memory_space=pltpu.VMEM)
    return pl.pallas_call(
        split_kernel,
        grid_spec=pltpu.PrefetchScalarGridSpec(
            num_scalar_prefetch=1,
            grid=(1,),
            in_specs=[inside, inside],
            out_specs=[ANYWHERE] * 4,
            scratch_shapes=[
                pltpu.VMEM((tall, 256), f32),
                pltpu.VMEM((tall, 256), f32),
                pltpu.VMEM((4, BLK, 384), bf16),
                pltpu.SemaphoreType.DMA((4,)),
            ],
        ),
        out_shape=[jax.ShapeDtypeStruct((BLK, 384), bf16)] * 4,
        compiler_params=pltpu.CompilerParams(vmem_limit_bytes=32 * 1024 * 1024),
        cost_estimate=pl.CostEstimate(flops=1_000_000_000, bytes_accessed=3_000_000, transcendentals=0),
    )(place, tokens, cotangent)


def finish_kernel(place_ref, mine, one, two, three, far, dp_sums, *refs):
    (
        a_qkv, b_qkv, a_out, b_out, a_router, b_router, a_up, b_up, a_down, b_down, wide, tall, every,
    ) = refs
    row, col = place_ref[0], place_ref[1]
    near_at = pl.multiple_of(row * 96, 32)
    far_at = pl.multiple_of((1 - row) * 96, 32)
    for p in range(4):
        ours = mine[96 * p : 96 * p + 96, :].astype(f32)
        theirs = far[96 * p : 96 * p + 96, :].astype(f32)
        if p < 3:
            a_qkv[p, pl.ds(near_at, 96), :] = ours
            a_qkv[p, pl.ds(far_at, 96), :] = theirs
        else:
            wide[pl.ds(near_at, 96), :] = ours
            wide[pl.ds(far_at, 96), :] = theirs
    b_out[...] = wide[...].T[:, : D // 4]
    share = BOTH_ROWS // 8
    for s, got in enumerate((mine, one, two, three)):
        base = 384 if s == 0 else 0
        at = pl.multiple_of((col ^ s) * 96, 32)
        for p in range(4):
            piece = got[base + 96 * p : base + 96 * p + 96, :].astype(f32)
            if p < 3:
                tall[p, pl.ds(at, 96), :] = piece
            else:
                a_out[pl.ds(at, 96), :] = piece
        ours = got[base + 384 : base + 384 + share, :].astype(f32)
        theirs = far[384 + share * s : 384 + share * s + share, :].astype(f32)
        every[pl.ds(pl.multiple_of((row * 4 + (col ^ s)) * share, 64), share), :] = ours
        every[pl.ds(pl.multiple_of(((1 - row) * 4 + (col ^ s)) * share, 64), share), :] = theirs
    for p in range(3):
        b_qkv[p] = tall[p].T
    a_router[...] = every[0:768, :]
    a_up[...] = every[768:1536, :]
    b_down[...] = every[1536:2304, :].T
    b_router[...] = every[2304:2432, :].T[:, :EXPERTS]
    b_up[...] = dp_sums[0:384, :].astype(f32).T
    a_down[...] = dp_sums[384:768, :].astype(f32)


def finish_call(place, mine, got, far, dp_sums):
    inside = pl.BlockSpec(memory_space=pltpu.VMEM)
    half = D // 2
    shapes = [
        (3, D // 4, ADAPT), (3, ADAPT, half), (half, ADAPT), (ADAPT, D // 4), (D, ADAPT), (ADAPT, EXPERTS),
        (D, ADAPT), (ADAPT, half), (half, ADAPT), (ADAPT, D),
    ]
    return pl.pallas_call(
        finish_kernel,
        grid_spec=pltpu.PrefetchScalarGridSpec(
            num_scalar_prefetch=1,
            grid=(1,),
            in_specs=[inside] * 6,
            out_specs=[inside] * 10,
            scratch_shapes=[
                pltpu.VMEM((256, 128), f32),
                pltpu.VMEM((3, half, 128), f32),
                pltpu.VMEM((BOTH_ROWS, 128), f32),
            ],
        ),
        out_shape=[jax.ShapeDtypeStruct(shape, f32) for shape in shapes],
        compiler_params=pltpu.CompilerParams(vmem_limit_bytes=32 * 1024 * 1024),
        cost_estimate=pl.CostEstimate(flops=1_000_000_000, bytes_accessed=4_000_000, transcendentals=0),
    )(place, mine, *got, far, dp_sums)


def merge_kernel(place_ref, *refs):
    blocks, refs = refs[:4], refs[4:]
    block_out, tokens_out, stage, tall, sem = refs
    copies = [
        pltpu.make_async_copy(block, stage.at[place_ref[1] ^ s], sem.at[s]) for s, block in enumerate(blocks)
    ]
    for copy in copies:
        copy.start()
    for copy in copies:
        copy.wait()
    width = D // 4
    rows = tokens_out.shape[0]
    for i in range(8):
        at = slice(SEQ * i, SEQ * i + SEQ)
        both = stage[i // 2, SEQP * (i % 2) : SEQP * (i % 2) + SEQP, :].astype(f32)[:SEQ]
        tokens_out[at, :] = both[:, :width]
        tall[at, :] = both[:, width:]
    block_out[...] = tall[0:rows, :].astype(bf16)


def merge_call(place, blocks, rows):
    width = D // 4
    inside = pl.BlockSpec(memory_space=pltpu.VMEM)
    return pl.pallas_call(
        merge_kernel,
        grid_spec=pltpu.PrefetchScalarGridSpec(
            num_scalar_prefetch=1,
            grid=(1,),
            in_specs=[ANYWHERE] * 4,
            out_specs=[inside, inside],
            scratch_shapes=[
                pltpu.VMEM((4, BLK, 2 * width), bf16),
                pltpu.VMEM((rows, width), f32),
                pltpu.SemaphoreType.DMA((4,)),
            ],
        ),
        out_shape=[jax.ShapeDtypeStruct((rows, width), bf16), jax.ShapeDtypeStruct((rows, width), f32)],
        compiler_params=pltpu.CompilerParams(vmem_limit_bytes=32 * 1024 * 1024),
        cost_estimate=pl.CostEstimate(flops=8_000_000_000, bytes_accessed=3_000_000, transcendentals=0),
    )(place, *blocks)


def place_weights(place_ref, blocks, own_b, own_a, out_w, w_qkv, a_qkv, b_qkv, w_out, a_out):
    row, col = place_ref[0], place_ref[1]
    for t in range(2):
        half_at = pl.multiple_of((row ^ t) * 384, 128)
        across = pl.ds(half_at, 384)
        for s in range(4):
            block = blocks[4 * t + s]
            at = pl.multiple_of((col ^ s) * 192, 64)
            low_at = pl.multiple_of((col ^ s) * 192 + (row ^ t) * 96, 32)
            for p in range(3):
                w_qkv[p, pl.ds(at, 192), across] = block[192 * p : 192 * p + 192, :]
                a_qkv[p, pl.ds(low_at, 96), :] = block[576:672, 128 * p : 128 * p + 128]
        w_out[across, :] = out_w[t][0:384, :]
        for p in range(3):
            down = pl.ds(pl.multiple_of(half_at + 128 * p, 128), 128)
            if t == 0:
                b_qkv[p, :, across] = own_b[p]
                a_out[down, :] = own_a[128 * p : 128 * p + 128, :]
            else:
                b_qkv[p, :, across] = blocks[4][W_ROWS + 128 * p : W_ROWS + 128 * p + 128, :]
                a_out[down, :] = blocks[4][W_ROWS + 384 : W_ROWS + 512, 128 * p : 128 * p + 128]


def two_masks(picks_ref):
    row = lax.broadcasted_iota(jnp.int32, (BLK, 1), 0)
    pick = jnp.where(row < SEQP, picks_ref[0], picks_ref[1])
    return (lane_iota((1, ADAPT)) // RANK) == pick, (row < SEQ) | ((row >= SEQP) & (row < SEQP + SEQ))


def both_heads(value):
    lane = lane_iota((1, 128))
    nothing = jnp.zeros_like(value)
    return jnp.concatenate(
        [jnp.where(lane < HEAD_DIM, value, nothing), jnp.where(lane < HEAD_DIM, nothing, value)], axis=0
    )


def attend_kernel(picks_ref, place_ref, *refs):
    blocks, refs = refs[:8], refs[8:]
    (
        own_b, own_a, out_near, out_far, x_ref, gain_one, gain_two, b_out,
        two_out, resid_out, normed_out, qkv_out, mixed_out, probs_out, lows_out,
        w_qkv, a_qkv, b_qkv, w_out, a_out,
    ) = refs
    place_weights(place_ref, blocks, own_b, own_a, (out_near, out_far), w_qkv, a_qkv, b_qkv, w_out, a_out)
    mask, real = two_masks(picks_ref)
    x = x_ref[...].astype(f32)
    unit, unused = norm_stats(x)
    normed = (unit * gain_one[...]).astype(bf16)
    normed_out[...] = normed
    for p in range(3):
        low = jnp.where(mask, dot(normed, a_qkv[p]), 0.0).astype(bf16)
        lows_out[:, 128 * p : 128 * p + 128] = low
        qkv_out[p] = (dot(normed, w_qkv[p]) + dot(low, b_qkv[p])).astype(bf16)
    lane = lane_iota((1, 128))
    key_lane = lane_iota((1, SEQP))
    for pair in range(HEADS // 2):
        at = slice(128 * pair, 128 * pair + 128)
        for image in range(2):
            rows = slice(SEQP * image, SEQP * image + SEQP)
            scores = dot_nt(both_heads(qkv_out[0, rows, at]), qkv_out[1, rows, at]) * (HEAD_DIM**-0.5)
            scores = jnp.where(key_lane < SEQ, scores, -1e30)
            power = jnp.exp(scores - jnp.max(scores, axis=1, keepdims=True))
            probs = (power / jnp.sum(power, axis=1, keepdims=True)).astype(bf16)
            probs_out[image, pair] = probs
            found = dot(probs, qkv_out[2, rows, at])
            mixed_out[rows, at] = jnp.where(lane < HEAD_DIM, found[:SEQP], found[SEQP:]).astype(bf16)
    mixed = mixed_out[...]
    low = jnp.where(mask, dot(mixed, a_out[...]), 0.0).astype(bf16)
    lows_out[:, 384:512] = low
    resid = x + dot(mixed, w_out[...]) + dot(low, b_out[...])
    resid_out[...] = resid
    unit, unused = norm_stats(resid)
    two_out[...] = jnp.where(real, unit * gain_two[...], 0.0).astype(bf16)


INSIDE = pl.BlockSpec(memory_space=pltpu.VMEM)


ANYWHERE = pl.BlockSpec(memory_space=pl.ANY)


def attend_call(picks, place, blocks, own_b, own_a, out_w, x, gain_one, gain_two, b_out):
    rows = x.shape[0]
    return pl.pallas_call(
        attend_kernel,
        grid_spec=pltpu.PrefetchScalarGridSpec(
            num_scalar_prefetch=2,
            grid=(1,),
            in_specs=[INSIDE] * (len(blocks) + 8),
            out_specs=[INSIDE] * 7,
            scratch_shapes=QKV_SCRATCH[:-1] + OUT_SCRATCH[:-1],
        ),
        out_shape=[
            jax.ShapeDtypeStruct((rows, D), bf16),
            jax.ShapeDtypeStruct((rows, D), f32),
            jax.ShapeDtypeStruct((rows, D), bf16),
            jax.ShapeDtypeStruct((3, rows, D), bf16),
            jax.ShapeDtypeStruct((rows, D), bf16),
            jax.ShapeDtypeStruct((2, HEADS // 2, BLK, SEQP), bf16),
            jax.ShapeDtypeStruct((rows, 512), bf16),
        ],
        compiler_params=pltpu.CompilerParams(vmem_limit_bytes=48 * 1024 * 1024),
        cost_estimate=pl.CostEstimate(flops=4_000_000_000, bytes_accessed=15_000_000, transcendentals=2_000_000),
    )(picks, place, *blocks, own_b, own_a, *out_w, x, gain_one, gain_two, b_out)


def put_rows(part, p, value):
    value = value.astype(bf16)
    for r in range(2):
        for c in range(4):
            part[r, c, 96 * p : 96 * p + 96, :] = value[384 * r + 96 * c : 384 * r + 96 * c + 96, :]


def put_cols(part, p, value):
    value = value.astype(bf16)
    for r in range(2):
        for c in range(4):
            part[r, c, 96 * p : 96 * p + 96, :] = value[192 * c + 96 * r : 192 * c + 96 * r + 96, :]


def out_back_kernel(picks_ref, place_ref, *refs):
    (
        far_block, own_a, out_near, out_far, gain_two, b_out, two_ref, resid_ref, mixed_ref, lows_ref,
        cot_ref, grad_a, grad_b, w_router, a_router, b_router, a_up, b_down,
        resid_grad_out, mixed_grad_out, base_out, both_out, a_part_out, b_part_out,
        w_out, a_out, sem,
    ) = refs
    copies = out_copies(place_ref, far_block, own_a, (out_near, out_far), (w_out, a_out), sem)
    for copy in copies:
        copy.start()
    mask, unused = two_masks(picks_ref)
    lane = lane_iota((1, 128))

    def add_part(row, value):
        both_out[row : row + value.shape[0], :] = value.astype(bf16)

    two = two_ref[...]
    received = grad_a[...].astype(f32) + grad_b[...].astype(f32)
    low_r = jnp.where(mask, dot(two, a_router[...]), 0.0).astype(bf16)
    logits = dot(two, w_router[...]) + dot(low_r, b_router[...])
    logits = jnp.where(lane < EXPERTS, logits, -1e30)
    power = jnp.exp(logits - jnp.max(logits, axis=1, keepdims=True))
    probs = power / jnp.sum(power, axis=1, keepdims=True)
    last = received[:, D:]
    grad_probs = jnp.where(lane < EXPERTS, last, 0.0)
    low_in = jnp.where(mask, repeat_lanes(jnp.where((lane >= 32) & (lane < 48), last, 0.0)), 0.0).astype(bf16)
    low_out = jnp.where(mask, repeat_lanes(jnp.where((lane >= 48) & (lane < 64), last, 0.0)), 0.0).astype(bf16)
    cot = cot_ref[...]
    resid = resid_ref[...]
    base_out[...] = resid + dot(low_out, b_down[...])
    add_part(768, dot_tn(two, low_in))
    add_part(1536, dot_tn(cot, low_out))
    grad_logits = probs * (grad_probs - jnp.sum(probs * grad_probs, axis=1, keepdims=True))
    grad_logits = grad_logits.astype(bf16)
    grad_low = jnp.where(mask, dot_nt(grad_logits, b_router[...]), 0.0).astype(bf16)
    grad_two = received[:, :D] + dot_nt(low_in, a_up[...])
    grad_two = grad_two + dot_nt(grad_logits, w_router[...]) + dot_nt(grad_low, a_router[...])
    add_part(0, dot_tn(two, grad_low))
    add_part(2304, dot_tn(grad_logits, low_r))
    unit, inverse = norm_stats(resid)
    grad_resid = cot.astype(f32) + norm_back(grad_two, gain_two[...], unit, inverse)
    resid_grad_out[...] = grad_resid
    grad_attn = grad_resid.astype(bf16)
    grad_low = jnp.where(mask, dot_nt(grad_attn, b_out[...]), 0.0).astype(bf16)
    for copy in copies:
        copy.wait()
    mixed_grad_out[...] = (dot_nt(grad_attn, w_out[...]) + dot_nt(grad_low, a_out[...])).astype(bf16)
    put_rows(a_part_out, 0, dot_tn(mixed_ref[...], grad_low))
    put_cols(b_part_out, 0, dot_tn(grad_attn, lows_ref[:, 384:512]))
    both_out[2432:BOTH_ROWS, :] = jnp.zeros((BOTH_ROWS - 2432, 128), bf16)


BOTH_ROWS = 2560


def out_back_call(picks, place, far_block, own_a, out_w, gain_two, b_out, two, resid, mixed, lows, cot, grad_a, grad_b,
                  w_router, a_router, b_router, a_up, b_down):
    rows = two.shape[0]
    return pl.pallas_call(
        out_back_kernel,
        grid_spec=pltpu.PrefetchScalarGridSpec(
            num_scalar_prefetch=2,
            grid=(1,),
            in_specs=[ANYWHERE] * 4 + [INSIDE] * 14,
            out_specs=[INSIDE] * 6,
            scratch_shapes=OUT_SCRATCH,
        ),
        out_shape=[
            jax.ShapeDtypeStruct((rows, D), f32),
            jax.ShapeDtypeStruct((rows, D), bf16),
            jax.ShapeDtypeStruct((rows, D), f32),
            jax.ShapeDtypeStruct((BOTH_ROWS, 128), bf16),
            jax.ShapeDtypeStruct((2, 4, 96, 128), bf16),
            jax.ShapeDtypeStruct((2, 4, 96, 128), bf16),
        ],
        compiler_params=pltpu.CompilerParams(vmem_limit_bytes=60 * 1024 * 1024),
        cost_estimate=pl.CostEstimate(flops=6_000_000_000, bytes_accessed=15_000_000, transcendentals=100_000),
    )(picks, place, far_block, own_a, *out_w, gain_two, b_out, two, resid, mixed, lows, cot, grad_a, grad_b,
      w_router, a_router, b_router, a_up, b_down)


def qkv_back_kernel(picks_ref, place_ref, *refs):
    blocks, refs = refs[:8], refs[8:]
    (
        own_b, x_hbm, gain_one, normed_hbm, qkv_ref, probs_ref, lows_hbm, resid_hbm, grad_mixed,
        tokens_out, a_part_out, b_part_out,
        w_qkv, a_qkv, b_qkv, sem, grads, x_ref, normed_ref, lows_ref, resid_grad, late_sem,
    ) = refs
    copies = qkv_copies(place_ref, blocks, own_b, (w_qkv, a_qkv, b_qkv), sem)
    late = ((x_hbm, x_ref), (normed_hbm, normed_ref), (lows_hbm, lows_ref), (resid_hbm, resid_grad))
    for k, (source, target) in enumerate(late):
        copies.append(pltpu.make_async_copy(source, target, late_sem.at[k]))
    for copy in copies:
        copy.start()
    mask, unused = two_masks(picks_ref)
    lane = lane_iota((1, 128))
    for pair in range(HEADS // 2):
        at = slice(128 * pair, 128 * pair + 128)
        for image in range(2):
            rows = slice(SEQP * image, SEQP * image + SEQP)
            grad_out = both_heads(grad_mixed[rows, at])
            weights = probs_ref[image, pair]
            weights_f = weights.astype(f32)
            grad_w = dot_nt(grad_out, qkv_ref[2, rows, at])
            inner = jnp.sum(weights_f * grad_w, axis=1, keepdims=True)
            grad_s = (weights_f * (grad_w - inner) * (HEAD_DIM**-0.5)).astype(bf16)
            found = dot(grad_s, qkv_ref[1, rows, at])
            grads[0, rows, at] = jnp.where(lane < HEAD_DIM, found[:SEQP], found[SEQP:]).astype(bf16)
            grads[1, rows, at] = dot_tn(grad_s, both_heads(qkv_ref[0, rows, at])).astype(bf16)
            grads[2, rows, at] = dot_tn(weights, grad_out).astype(bf16)
    for copy in copies:
        copy.wait()
    normed = normed_ref[...]
    grad_normed = jnp.zeros((BLK, D), f32)
    for p in range(3):
        piece = grads[p]
        grad_low = jnp.where(mask, dot_nt(piece, b_qkv[p]), 0.0).astype(bf16)
        grad_normed = grad_normed + dot_nt(piece, w_qkv[p]) + dot_nt(grad_low, a_qkv[p])
        put_cols(a_part_out, p, dot_tn(normed, grad_low))
        put_rows(b_part_out, p, dot_tn(piece, lows_ref[:, 128 * p : 128 * p + 128]))
    unit, inverse = norm_stats(x_ref[...].astype(f32))
    tokens_out[...] = (resid_grad[...] + norm_back(grad_normed, gain_one[...], unit, inverse)).astype(bf16)


def qkv_back_call(picks, place, blocks, own_b, x, gain_one, normed, qkv, probs, lows, resid_grad, grad_mixed):
    rows = x.shape[0]
    return pl.pallas_call(
        qkv_back_kernel,
        grid_spec=pltpu.PrefetchScalarGridSpec(
            num_scalar_prefetch=2,
            grid=(1,),
            in_specs=[ANYWHERE] * (len(blocks) + 2)
            + [INSIDE, ANYWHERE, INSIDE, INSIDE, ANYWHERE, ANYWHERE, INSIDE],
            out_specs=[INSIDE] * 3,
            scratch_shapes=QKV_SCRATCH
            + [
                pltpu.VMEM((3, BLK, D), bf16),
                pltpu.VMEM((BLK, D), bf16),
                pltpu.VMEM((BLK, D), bf16),
                pltpu.VMEM((BLK, 512), bf16),
                pltpu.VMEM((BLK, D), f32),
                pltpu.SemaphoreType.DMA((4,)),
            ],
        ),
        out_shape=[
            jax.ShapeDtypeStruct((rows, D), bf16),
            jax.ShapeDtypeStruct((2, 4, 288, 128), bf16),
            jax.ShapeDtypeStruct((2, 4, 288, 128), bf16),
        ],
        compiler_params=pltpu.CompilerParams(vmem_limit_bytes=60 * 1024 * 1024),
        cost_estimate=pl.CostEstimate(flops=9_000_000_000, bytes_accessed=15_000_000, transcendentals=1000),
    )(picks, place, *blocks, own_b, x, gain_one, normed, qkv, probs, lows, resid_grad, grad_mixed)


TABLES = (((0, 0), (1, 0)), ((0, 1), (0, 2), (1, 1), (1, 2)), ((0, 3), (1, 3)))


def across_row(value):
    return lax.ppermute(value, "row", [(0, 1), (1, 0)])


def across_col(value, step):
    return lax.ppermute(value, "col", [(i, i ^ step) for i in range(4)])


def by_place(blocks, col):
    found = []
    for place in range(4):
        value = blocks[place]
        for other in range(1, 4):
            value = jnp.where(col == other, blocks[place ^ other], value)
        found.append(value)
    return found


def across_chip(value, first, second):
    pairs = [(i, i ^ first) for i in range(4)] + [(4 + i, 4 + (i ^ second)) for i in range(4)]
    return lax.ppermute(value, ("row", "col"), pairs)


def gather_col(value, row):
    from_x = across_col(value, 1)
    from_y = across_col(value, 2)
    return [value, from_x, from_y, across_chip(jnp.where(row == 0, from_x, from_y), 2, 1)]


def added(*values):
    total = values[0].astype(f32)
    for value in values[1:]:
        total = total + value.astype(f32)
    return total


def last_exchange(kept_rows, got):
    sent = added(kept_rows[BLK:], got[BLK:]).astype(bf16)
    return added(kept_rows[:BLK], got[:BLK]).astype(bf16), across_chip(sent, 2, 1)


def at_place(value, axis, place):
    return lax.dynamic_index_in_dim(value, place, axis, keepdims=False)


def scatter_dp(value):
    place = lax.axis_index("dp")
    view = value.reshape(4, -1, 128)
    found = [at_place(view, 0, place)]
    for s in range(1, 4):
        found.append(across_dp(at_place(view, 0, place ^ s), s))
    return added(*found).astype(bf16)


def across_dp(value, step):
    return lax.ppermute(value, "dp", [(i, i ^ step) for i in range(4)])


def spread_dp(value):
    return jnp.concatenate(by_place([value] + [across_dp(value, s) for s in range(1, 4)], lax.axis_index("dp")))


def part_share(parts, place):
    return jnp.concatenate([at_place(part, 0, place) for part in parts], axis=1)


def exchange_col(value, col):
    return [at_place(value, 0, col)] + [across_col(at_place(value, 0, col ^ s), s) for s in range(1, 4)]


def to_features(first, second, col):
    width = D // 4
    pieces = []
    for p in range(4):
        at = slice(width * p, width * p + width)
        pieces.append(jnp.concatenate([first[:, at], second[:, at]], axis=1))
    sent = by_place(pieces, col)
    return [sent[0]] + [across_col(sent[s], s) for s in range(1, 4)]


def on_device(
    tokens, cotangent, routes, adapter_pick, gain_attn, gain_moe, w_qkv, w_out, w_router, w_up, w_down,
    a_qkv, b_qkv, a_out, b_out, a_router, b_router, a_up, b_up, a_down, b_down,
):
    row = lax.axis_index("row")
    col = lax.axis_index("col")
    me = row * 4 + col
    place = jnp.stack([row, col]).astype(jnp.int32)

    width = D // 4
    half = D // 2
    gains = []
    for gain in (gain_attn, gain_moe):
        left = gain
        for unused in range(3):
            lead = lax.reduce_precision(left, 8, 7)
            gains.append(lead.astype(bf16))
            left = left - lead
    small = jnp.concatenate([w_out, b_out, jnp.stack(gains), jnp.zeros((26, width), bf16)], axis=0)
    low = at_place(a_qkv.reshape(3, 2, 96, ADAPT), 1, row)
    packed = jnp.concatenate(
        [w_qkv.reshape(576, half), jnp.concatenate([low[0], low[1], low[2]], axis=1),
         jnp.concatenate([small[:272], small[272:]], axis=1)]
    )
    for_row = jnp.concatenate(
        [packed, b_qkv.reshape(half, half), jnp.concatenate([a_out[:128], a_out[128:256], a_out[256:]], axis=1)]
    )
    pairs = split_call(place, tokens, cotangent)
    from_x, from_y = across_col(packed, 1), across_col(packed, 2)
    chosen, *pairs = lax.optimization_barrier((jnp.where(row == 0, from_x, from_y), *pairs))
    near = [packed, from_x, from_y, across_chip(chosen, 2, 1)]
    pairs = by_place([pairs[0]] + [across_col(pairs[s], s) for s in range(1, 4)], col)
    x = jnp.concatenate([pair[:, :width] for pair in pairs], axis=1)
    cot = jnp.concatenate([pair[:, width:] for pair in pairs], axis=1)
    far = [across_row(for_row)] + [across_row(block) for block in near[1:]]
    blocks = near + far

    def assembled(group):
        parts = by_place([block[672:944] for block in group], col)
        return jnp.concatenate(
            [jnp.concatenate([part[:, :width] for part in parts], axis=1),
             jnp.concatenate([part[:, width:] for part in parts], axis=1)], axis=0
        )

    out_w = [assembled(near), assembled(far)]
    full_b_out = out_w[0][384:512]
    gain_rows = out_w[0][512:518].astype(f32)
    gain_one = jnp.sum(gain_rows[:3], axis=0, keepdims=True)
    gain_two = jnp.sum(gain_rows[3:], axis=0, keepdims=True)

    picks_group = lax.dynamic_slice_in_dim(adapter_pick, lax.axis_index("dp") * IMG_GRP, IMG_GRP)
    order = jnp.arange(IMG_GRP, dtype=jnp.int32)
    picks = jnp.take(picks_group, ((order // 2) ^ me) * 2 + order % 2)
    spot_picks = jnp.sum(
        jnp.where(block_spot(order // 2, row, col)[None, :] * 2 + order[None, :] % 2 == order[:, None], picks_group[None, :], 0), axis=1
    )
    token_list, tile_experts = routing(routes, row, col)
    wide_router = jnp.concatenate([w_router, w_router, jnp.zeros((D, 64), bf16)], axis=1)
    wide_b_router = jnp.concatenate([b_router, b_router, jnp.zeros((ADAPT, 64), bf16)], axis=1)
    slim_router = jnp.concatenate([w_router, jnp.zeros((D, 96), bf16)], axis=1)
    slim_b_router = jnp.concatenate([b_router, jnp.zeros((ADAPT, 96), bf16)], axis=1)

    x, token_list, tile_experts, wide_router, wide_b_router, slim_router, slim_b_router = lax.optimization_barrier(
        (x, token_list, tile_experts, wide_router, wide_b_router, slim_router, slim_b_router)
    )
    cot, unused = lax.optimization_barrier((cot, near[3]))
    two, resid, normed, qkv, mixed, probs, lows = attend_call(
        picks, place, blocks, b_qkv, a_out, out_w, x, gain_one, gain_two, full_b_out
    )
    cot_near = gather_col(cot, row)
    two_x, two_y = across_col(two, 1), across_col(two, 2)

    def table(spots, twos, cots):
        return table_call(
            jnp.stack([picks[8 * t + 2 * s + side] for t, s in spots for side in range(2)]),
            twos, cots, a_up, b_down, wide_router, a_router, wide_b_router,
        )

    cot_far = [across_row(block) for block in cot_near[:3]]
    tables = [table(TABLES[0], [two, across_row(two)], [cot, cot_far[0]])]
    two_x, two_y, tables[0] = lax.optimization_barrier((two_x, two_y, tables[0]))
    diag = across_chip(jnp.where(row == 0, two_x, two_y), 2, 1)
    tables.append(
        table(TABLES[1], [two_x, two_y, across_row(two_x), across_row(two_y)], [cot_near[1], cot_near[2], cot_far[1], cot_far[2]])
    )
    diag, cot_diag, *tables = lax.optimization_barrier((diag, cot_near[3], *tables))
    tables.append(table(TABLES[2], [diag, across_row(diag)], [cot_diag, across_row(cot_diag)]))
    *moved, part_b_up, part_a_down = moe_call(
        token_list, tile_experts, spot_picks, place, tables, TABLES, w_up, w_down, b_up, a_down
    )
    sums, grads = moved[:4], moved[4:]
    dp_parts = jnp.concatenate([part_b_up, part_a_down])
    grad_sent = added(grads[1], across_row(grads[3])).astype(bf16)
    grad_kept = added(grads[0], across_row(grads[2])).astype(bf16)
    grad_sent, dp_parts, *sums = lax.optimization_barrier((grad_sent, dp_parts, *sums))
    grad_got = across_chip(grad_sent, 1, 2)
    sum_kept, sum_sent = across_row(sums[2]), across_row(sums[3])
    sums = [
        added(near[at : at + BLK], far[at : at + BLK]).astype(bf16)
        for near, far in ((sums[0], sum_kept), (sums[1], sum_sent)) for at in (0, BLK)
    ]
    four_dp = lax.axis_size("dp") == 4
    dp_sums = scatter_dp(dp_parts) if four_dp else lax.psum(dp_parts, "dp")
    grad_got, dp_sums, *sums = lax.optimization_barrier((grad_got, dp_sums, *sums))
    grad_a, grad_b = last_exchange(grad_kept, grad_got)
    if four_dp:
        dp_sums = spread_dp(dp_sums)
    grad_a, grad_b, dp_sums, *sums = lax.optimization_barrier((grad_a, grad_b, dp_sums, *sums))
    sums = [sums[0], across_chip(sums[1], 2, 1), across_chip(sums[2], 1, 2), across_chip(sums[3], 3, 3)]
    resid_grad, mixed_grad, base, both_parts, part_a_out, part_b_out = out_back_call(
        picks, place, blocks[4], a_out, out_w, gain_two, full_b_out, two, resid, mixed, lows, cot, grad_a, grad_b,
        slim_router, a_router, slim_b_router, a_up, b_down,
    )
    grad_tokens, part_a_qkv, part_b_qkv = qkv_back_call(
        picks, place, blocks, b_qkv, x, gain_one, normed, qkv, probs, lows, resid_grad, mixed_grad
    )
    part_a_qkv, part_b_qkv, *sums = lax.optimization_barrier((part_a_qkv, part_b_qkv, *sums))
    parts = (part_a_qkv, part_b_out, part_b_qkv, part_a_out, both_parts.reshape(2, 4, BOTH_ROWS // 8, 128))
    theirs = across_row(part_share(parts, 1 - row))
    shared = added(part_share(parts, row), theirs).astype(bf16)
    found = exchange_col(shared, col)
    mine = added(*found).astype(bf16)
    mine, grad_tokens, base = lax.optimization_barrier((mine, grad_tokens, base))
    moves = to_features(grad_tokens, (base + added(*sums)).astype(bf16), col)
    mine = spread_dp(scatter_dp(mine)) if four_dp else lax.psum(mine, "dp")
    got = [across_col(mine[384:], s) for s in range(1, 4)]
    far = across_row(jnp.concatenate([mine[:384], mine[768:]] + [one[384:] for one in got]))
    block_out, grad_tokens = merge_call(place, moves, tokens.shape[0])
    far, block_out, grad_tokens = lax.optimization_barrier((far, block_out, grad_tokens))
    return (block_out, grad_tokens, *finish_call(place, mine, got, far, dp_sums))


def solution(mesh):
    return jax.shard_map(
        on_device,
        mesh=mesh,
        in_specs=(
            P(("dp", "row"), "col"),
            P(("dp", "row"), "col"),
            P("dp", None),
            P(),
            P("col"),
            P("col"),
            P(None, "col", "row"),
            P("row", "col"),
            P(),
            P(None, None, ("row", "col")),
            P(None, ("row", "col"), None),
            P(None, "col", None),
            P(None, None, "row"),
            P("row", None),
            P(None, "col"),
            P(),
            P(),
            P(),
            P(None, ("row", "col")),
            P(("row", "col"), None),
            P(),
        ),
        out_specs=(
            P(("dp", "row"), "col"),
            P(("dp", "row"), "col"),
            P(None, "col", None),
            P(None, None, "row"),
            P("row", None),
            P(None, "col"),
            P(),
            P(),
            P(),
            P(None, ("row", "col")),
            P(("row", "col"), None),
            P(),
        ),
        check_vma=False,
    )
```
